32 devices in a mesh: row: 4 (over z), head: 8 (over y, x, core).
Axes of the slice: x: 2, y: 2, z: 4, core: 2. Of those that a mesh axis runs over, the one named last changes fastest.
Arguments:
- layer_in: bfloat16 [8192, 2048], P(('row', 'head')), may hold values from -6 to 6
- cotangent: bfloat16 [8192, 2048], P(('row', 'head')), may hold values from -6 to 6
- mix_gain: bfloat16 [2048], P(('row', 'head')), may hold values from 0.5 to 1.5
- ffn_gain: bfloat16 [2048], P(('row', 'head')), may hold values from 0.5 to 1.5
- x_weight: bfloat16 [2048, 2736], P('row', 'head'), may hold values from -0.125 to 0.125
- y_weight: bfloat16 [2048, 2736], P('row', 'head'), may hold values from -0.125 to 0.125
- out_weight: bfloat16 [2048, 2736], P('row', 'head'), may hold values from -0.4375 to 0.4375
- conv_weight: float32 [4, 2736], P(None, 'head'), may hold values from -3 to 3
- conv_bias: float32 [2736], P('head'), may hold values from -3 to 3
- rate_weight: bfloat16 [16, 171, 171], P('head'), may hold values from -0.4375 to 0.4375
- rate_bias: float32 [2736], P('head'), may hold values from -3 to 3
- entry_weight: bfloat16 [16, 171, 171], P('head'), may hold values from -0.4375 to 0.4375
- entry_bias: float32 [2736], P('head'), may hold values from -3 to 3
- decay_param: float32 [2736], P('head'), may hold values from 2 to 6
- gate_weight: bfloat16 [2048, 6144], P('row', 'head'), may hold values from -0.125 to 0.125
- up_weight: bfloat16 [2048, 6144], P('row', 'head'), may hold values from -0.125 to 0.125
- down_weight: bfloat16 [2048, 6144], P('row', 'head'), may hold values from -0.109375 to 0.109375
- resets: int32 [4, 2048], P('row'), may hold values 0 or 1
Outputs:
- layer_out: bfloat16 [8192, 2048], P(('row', 'head'))
- layer_in_grad: bfloat16 [8192, 2048], P(('row', 'head'))
- mix_gain_grad: float32 [2048], P(('row', 'head'))
- ffn_gain_grad: float32 [2048], P(('row', 'head'))
- x_weight_grad: float32 [2048, 2736], P('row', 'head')
- y_weight_grad: float32 [2048, 2736], P('row', 'head')
- out_weight_grad: float32 [2048, 2736], P('row', 'head')
- conv_weight_grad: float32 [4, 2736], P(None, 'head')
- conv_bias_grad: float32 [2736], P('head')
- rate_weight_grad: float32 [16, 171, 171], P('head')
- rate_bias_grad: float32 [2736], P('head')
- entry_weight_grad: float32 [16, 171, 171], P('head')
- entry_bias_grad: float32 [2736], P('head')
- decay_param_grad: float32 [2736], P('head')
- gate_weight_grad: float32 [2048, 6144], P('row', 'head')
- up_weight_grad: float32 [2048, 6144], P('row', 'head')
- down_weight_grad: float32 [2048, 6144], P('row', 'head')
The draws below stay inside these ranges and needn't reach their ends.
Inputs may be any that keep to these rules, and one draw needn't show every extreme that they name: resets[s, t] = 1 marks a document that starts at position t of sequence s; position 0 starts a document whatever resets holds there.
All inputs are finite; a program needn't handle non-finite values. No bound on the sum of `resets` on one device may be relied on, other than what follows from the above.
Results may differ from the reference program's by a relative error of at most 0.015.
Values may be sent and summed in bfloat16 or wider, within the bound.
A program may use at most 576 MiB of HBM per device.

```python
import jax
import jax.numpy as jnp
from jax import lax

D = 2048
HEADS = 16
HEAD_W = 171
FF = 6144
TAPS = 4
SEQ_LEN = 2048
SEQS_ROW = 1
RW = 2736
SEQS = 4
TOKENS = 8192
N_ROW = 4


def set_ends(values, stream_key, low, top_value):
    shape = values.shape
    place = [jax.random.randint(jax.random.fold_in(stream_key, axis), (), 0, shape[axis]) for axis in range(len(shape))]
    values = values.at[tuple(place)].set(low)
    longest = shape.index(max(shape))
    place[longest] = (place[longest] + 1) % shape[longest]
    return values.at[tuple(place)].set(top_value)


def levels(key, extent, pieces, smallest, high):
    level = 1.0
    for dim, blocks in pieces:
        heights = jax.random.uniform(jax.random.fold_in(jax.random.fold_in(key, 6), dim), (blocks,), jnp.float32, smallest / len(pieces), high / len(pieces))
        level = level * jnp.repeat(jnp.exp(heights), extent[dim] // blocks).reshape((-1,) + (1,) * (len(extent) - 1 - dim))
    return level


def gaussian(key, shape, spread, bound, split=(), held_as=jnp.bfloat16):
    level = levels(key, shape, split, -0.22, 0.18) if split else 1.0
    array = jax.random.normal(key, shape, jnp.float32) * spread * level
    return jnp.minimum(jnp.maximum(array, -bound), bound).astype(held_as)


def setup_inputs(seed: int = 0) -> dict:
    arg_keys = jax.random.split(jax.random.key(seed), 19)
    layer_in = gaussian(arg_keys[0], (TOKENS, D), 1.0, 6.0, ((0, 32),))
    cotangent = gaussian(arg_keys[1], (TOKENS, D), 1.0, 6.0, ((0, 32),))
    mix_gain = jnp.clip(1.0 + 0.1 * jax.random.normal(arg_keys[2], (D,), jnp.float32), 0.5, 1.5).astype(jnp.bfloat16)
    ffn_gain = jnp.clip(1.0 + 0.1 * jax.random.normal(arg_keys[3], (D,), jnp.float32), 0.5, 1.5).astype(jnp.bfloat16)
    x_weight = gaussian(arg_keys[4], (D, RW), D ** -0.5, 0.125, ((0, 4), (1, 8)))
    y_weight = gaussian(arg_keys[5], (D, RW), D ** -0.5, 0.125, ((0, 4), (1, 8)))
    out_weight = gaussian(arg_keys[6], (D, RW), (RW // 16) ** -0.5, 0.4375, ((0, 4), (1, 8)))
    conv_weight = gaussian(arg_keys[7], (TAPS, RW), 0.5, 3.0, ((1, 8),), jnp.float32)
    conv_bias = gaussian(arg_keys[8], (RW,), 0.5, 3.0, ((0, 8),), jnp.float32)
    rate_weight = gaussian(arg_keys[9], (HEADS, HEAD_W, HEAD_W), HEAD_W ** -0.5, 0.4375, ((0, 8),))
    rate_bias = gaussian(arg_keys[10], (RW,), 0.5, 3.0, ((0, 8),), jnp.float32)
    entry_weight = gaussian(arg_keys[11], (HEADS, HEAD_W, HEAD_W), HEAD_W ** -0.5, 0.4375, ((0, 8),))
    entry_bias = gaussian(arg_keys[12], (RW,), 0.5, 3.0, ((0, 8),), jnp.float32)
    decay_param = jnp.clip(2.0 + 4.0 * jax.random.uniform(arg_keys[13], (RW,), jnp.float32) ** levels(arg_keys[13], (RW,), ((0, 8),), -0.2, 0.2), 2.0, 6.0)
    gate_weight = gaussian(arg_keys[14], (D, FF), D ** -0.5, 0.125, ((0, 4), (1, 8)))
    up_weight = gaussian(arg_keys[15], (D, FF), D ** -0.5, 0.125, ((0, 4), (1, 8)))
    down_weight = gaussian(arg_keys[16], (D, FF), (FF // 2) ** -0.5, 0.109375, ((0, 4), (1, 8)))
    resets = set_ends((jax.random.randint(arg_keys[17], (SEQS, SEQ_LEN), 0, max(SEQ_LEN // 16, 8)) < 1).astype(jnp.int32), jax.random.fold_in(arg_keys[17], 1), 0, 1)
    return dict(layer_in=layer_in, cotangent=cotangent, mix_gain=mix_gain, ffn_gain=ffn_gain, x_weight=x_weight, y_weight=y_weight, out_weight=out_weight, conv_weight=conv_weight, conv_bias=conv_bias, rate_weight=rate_weight, rate_bias=rate_bias, entry_weight=entry_weight, entry_bias=entry_bias, decay_param=decay_param, gate_weight=gate_weight, up_weight=up_weight, down_weight=down_weight, resets=resets)


@jax.custom_vjp
def low(v):
    return lax.optimization_barrier(v.astype(jnp.bfloat16)).astype(jnp.float32)

@jax.custom_vjp
def low_back(v):
    return v

def low_keep(v):
    return (low(v), None)

def low_pass(kept, grad):
    return (grad,)

def back_keep(v):
    return (v, None)

def back_low(kept, grad):
    return (low(grad),)
low.defvjp(low_keep, low_pass)
low_back.defvjp(back_keep, back_low)
EPSILON = 1e-06

def product(left, right):
    return jnp.dot(left, right, precision=lax.Precision.HIGHEST, preferred_element_type=jnp.float32)

def product_trans(left, right):
    return lax.dot_general(left, right, (((1,), (1,)), ((), ())), precision=lax.Precision.HIGHEST, preferred_element_type=jnp.float32)

def norm_apply(rows, gain):
    return rows * lax.rsqrt(lax.optimization_barrier(jnp.mean(rows * rows, axis=-1, keepdims=True)) + EPSILON) * gain

def combine(earlier, later):
    return (earlier[0] * later[0], later[0] * earlier[1] + later[1])

def recurrence(inputs, conv_weight, conv_bias, rate_weight, rate_bias, entry_weight, entry_bias, decay_param, resets):
    seqs_here, length, channels = inputs.shape
    heads_here = rate_weight.shape[0]
    position = lax.broadcasted_iota(jnp.int32, (seqs_here, length), 1)
    starts = jnp.maximum(resets, (position == 0).astype(jnp.int32)).astype(jnp.float32)
    carried = 1.0 - starts
    convolved = conv_weight[0] * inputs + conv_bias
    within = jnp.ones_like(carried)
    for offset in range(1, conv_weight.shape[0]):
        within = within * jnp.pad(carried, ((0, 0), (offset - 1, 0)))[:, :length]
        shifted = jnp.pad(inputs, ((0, 0), (offset, 0), (0, 0)))[:, :length]
        convolved = convolved + conv_weight[offset] * within[:, :, None] * shifted
    conv_low = low(convolved).reshape(seqs_here, length, heads_here, -1)
    pre_rate = low_back(jnp.einsum('slhi,hij->slhj', conv_low, rate_weight, precision=lax.Precision.HIGHEST)).reshape(seqs_here, length, channels) + rate_bias
    pre_entry = low_back(jnp.einsum('slhi,hij->slhj', conv_low, entry_weight, precision=lax.Precision.HIGHEST)).reshape(seqs_here, length, channels) + entry_bias
    log_decay = -8.0 * jax.nn.sigmoid(pre_rate) * jax.nn.softplus(-decay_param)
    decays = jnp.exp(log_decay) * carried[:, :, None]
    scaling = starts[:, :, None] + carried[:, :, None] * jnp.sqrt(-jnp.expm1(2.0 * log_decay))
    driven = scaling * jax.nn.sigmoid(pre_entry) * convolved
    unused, states = lax.associative_scan(combine, (decays, driven), axis=1)
    return states

def layer(inputs, params, resets):
    mix_gain, ffn_gain, x_weight, y_weight, out_weight, conv_weight, conv_bias, rate_weight, rate_bias, entry_weight, entry_bias, decay_param, gate_weight, up_weight, down_weight = params
    normed = low(norm_apply(inputs, mix_gain))
    branch_x = low_back(low(product(normed, x_weight)))
    branch_y = low_back(product(normed, y_weight))
    states = recurrence(branch_x.reshape(SEQS_ROW, SEQ_LEN, -1), conv_weight, conv_bias, rate_weight, rate_bias, entry_weight, entry_bias, decay_param, resets)
    states = low_back(low(states.reshape(inputs.shape[0], -1)))
    mixed = low(states * jax.nn.gelu(branch_y))
    residual = inputs + low_back(product_trans(mixed, out_weight))
    normed_two = low(norm_apply(residual, ffn_gain))
    gates = low_back(product(normed_two, gate_weight))
    ups = low_back(product(normed_two, up_weight))
    hidden = low(jax.nn.gelu(gates) * ups)
    return residual + product_trans(hidden, down_weight)

def reference(layer_in, cotangent, mix_gain, ffn_gain, x_weight, y_weight, out_weight, conv_weight, conv_bias, rate_weight, rate_bias, entry_weight, entry_bias, decay_param, gate_weight, up_weight, down_weight, resets):
    weights = tuple((item.astype(jnp.float32) for item in (mix_gain, ffn_gain, x_weight, y_weight, out_weight, conv_weight, conv_bias, rate_weight, rate_bias, entry_weight, entry_bias, decay_param, gate_weight, up_weight, down_weight)))
    groups = N_ROW
    block_in = layer_in.astype(jnp.float32).reshape(groups, SEQS_ROW * SEQ_LEN, D)
    block_cot = cotangent.astype(jnp.float32).reshape(groups, SEQS_ROW * SEQ_LEN, D)
    block_resets = resets.reshape(groups, SEQS_ROW, SEQ_LEN)

    def group_step(totals, item):
        rows_in, rows_cot, rows_resets = item

        def forward(inputs, *params):
            return layer(inputs, params, rows_resets)
        result, backward = jax.vjp(forward, rows_in, *weights)
        grads = backward(rows_cot)
        totals = tuple((total + grad for total, grad in zip(totals, grads[1:])))
        return (totals, (result.astype(jnp.bfloat16), grads[0].astype(jnp.bfloat16)))
    zeros = tuple((jnp.zeros(item.shape, jnp.float32) for item in weights))
    totals, (results, in_grads) = lax.scan(group_step, zeros, (block_in, block_cot, block_resets))
    return (results.reshape(TOKENS, D), in_grads.reshape(TOKENS, D), totals[0], totals[1], totals[2], totals[3], totals[4], totals[5], totals[6], totals[7], totals[8], totals[9], totals[10], totals[11], totals[12], totals[13], totals[14])
```

```python
import jax
import jax.numpy as jnp
from jax import lax
from jax.experimental import pallas as pl
from jax.experimental.pallas import tpu as pltpu
from jax.sharding import PartitionSpec as P

EPSILON = 1e-06
ROWS = 256
GELU_A = 0.7978845608028654
GELU_B = 0.044715
CHUNK = 16


def gelu_only(x):
    return 0.5 * x * (1.0 + jnp.tanh(GELU_A * (x + GELU_B * x * x * x)))


def gelu_both(x):
    square = x * x
    bent = jnp.tanh(GELU_A * x * (1.0 + GELU_B * square))
    half = 0.5 * (1.0 + bent)
    slope = half + 0.5 * x * (1.0 - bent * bent) * (GELU_A * (1.0 + 3.0 * GELU_B * square))
    return x * half, slope


def one_minus_exp(x, exp_x):
    series = 1.0 + x * (1.0 / 7.0)
    for order in (6.0, 5.0, 4.0, 3.0, 2.0):
        series = 1.0 + x * (1.0 / order) * series
    return jnp.where(x > -0.25, -x * series, 1.0 - exp_x)


def dot_plain(left, right):
    return jnp.dot(left, right, preferred_element_type=jnp.float32)


def contract_last(left, right):
    return lax.dot_general(
        left, right, (((1,), (1,)), ((), ())), preferred_element_type=jnp.float32
    )


def contract_first(left, right):
    return lax.dot_general(
        left, right, (((0,), (0,)), ((), ())), preferred_element_type=jnp.float32
    )


def conv_rows(window, keep, taps, shift):
    rows = window.shape[0] - 8
    total = taps[0:1] * window[8:] + shift
    for offset in range(1, 4):
        total = total + taps[offset : offset + 1] * (
            keep[:, offset : offset + 1] * window[8 - offset : 8 - offset + rows]
        )
    return total


def scan_down(decays, driven, carry):
    rows = decays.shape[0]
    place = lax.broadcasted_iota(jnp.int32, decays.shape, 0)
    step = 1
    while step < rows:
        inside = place >= step
        driven = jnp.where(inside, decays * pltpu.roll(driven, step, 0) + driven, driven)
        decays = jnp.where(inside, decays * pltpu.roll(decays, step, 0), decays)
        step *= 2
    return decays * carry + driven


def scan_up(decays, driven, carry):
    rows = decays.shape[0]
    place = lax.broadcasted_iota(jnp.int32, decays.shape, 0)
    step = 1
    while step < rows:
        inside = place < rows - step
        driven = jnp.where(inside, decays * pltpu.roll(driven, rows - step, 0) + driven, driven)
        decays = jnp.where(inside, decays * pltpu.roll(decays, rows - step, 0), decays)
        step *= 2
    return decays * carry + driven


def forward_body(
    normed_ref, xw_ref, yw_ref, ow_ref, taps_ref, vec_ref, wr_ref, we_ref, keep_ref,
    u_ref, by_ref, before_ref, states_ref, mixed_ref, part_ref,
    window, conv, conv_low, rate, entry, carry,
):
    rows = normed_ref.shape[0]

    @pl.when(pl.program_id(0) == 0)
    def _():
        window[0:8, :] = jnp.zeros_like(window[0:8, :])
        carry[...] = jnp.zeros_like(carry)

    branch_x = dot_plain(normed_ref[...], xw_ref[...]).astype(jnp.bfloat16)
    u_ref[...] = branch_x
    window[pl.ds(8, rows), :] = branch_x.astype(jnp.float32)
    by_ref[...] = dot_plain(normed_ref[...], yw_ref[...])

    def conv_step(j, unused):
        at = pl.multiple_of(j * CHUNK, CHUNK)
        made = conv_rows(
            window[pl.ds(at, CHUNK + 8), :], keep_ref[pl.ds(at, CHUNK), :],
            taps_ref[...], vec_ref[0:1, :],
        )
        conv[pl.ds(at, CHUNK), :] = made
        conv_low[pl.ds(at, CHUNK), :] = made.astype(jnp.bfloat16)
        return unused

    lax.fori_loop(0, rows // CHUNK, conv_step, 0)
    window[0:8, :] = window[pl.ds(rows, 8), :]
    rate[...] = dot_plain(conv_low[...], wr_ref[...]) + vec_ref[1:2, :]
    entry[...] = dot_plain(conv_low[...], we_ref[...]) + vec_ref[2:3, :]

    def scan_step(j, before):
        at = pl.multiple_of(j * CHUNK, CHUNK)
        here = pl.ds(at, CHUNK)
        carried = keep_ref[here, 0:1]
        log_decay = jax.nn.sigmoid(rate[here, :]) * vec_ref[3:4, :]
        exp_decay = jnp.exp(log_decay)
        drop = jnp.sqrt(one_minus_exp(2.0 * log_decay, exp_decay * exp_decay))
        scaling = (1.0 - carried) + carried * drop
        driven = scaling * jax.nn.sigmoid(entry[here, :]) * conv[here, :]
        states = scan_down(exp_decay * carried, driven, before)
        first = lax.broadcasted_iota(jnp.int32, states.shape, 0) == 0
        before_ref[here, :] = jnp.where(first, before, pltpu.roll(states, 1, 0))
        states_low = states.astype(jnp.bfloat16)
        states_ref[here, :] = states_low
        mixed_ref[here, :] = (
            states_low.astype(jnp.float32) * gelu_only(by_ref[here, :])
        ).astype(jnp.bfloat16)
        return states[CHUNK - 1 : CHUNK, :]

    carry[0:1, :] = lax.fori_loop(0, rows // CHUNK, scan_step, carry[0:1, :])
    part_ref[...] = contract_last(mixed_ref[...], ow_ref[...]).astype(jnp.bfloat16)


def backward_body(
    d_res_ref, xw_ref, yw_ref, ow_ref, taps_ref, vec_ref, wr_ref, we_ref, keep_ref,
    u_ref, u_prev_ref, by_ref, before_ref, states_ref,
    d_bx_ref, d_by_ref, part_ref, taps_out, vec_out, wr_out, we_out,
    window, conv, conv_low, rate, entry, d_mixed, d_conv, g_rate, g_entry, carry, sums,
):
    rows = d_res_ref.shape[0]
    step_id = pl.program_id(0)

    @pl.when(step_id == 0)
    def _():
        d_conv[pl.ds(rows, 8), :] = jnp.zeros_like(d_conv[pl.ds(rows, 8), :])
        carry[...] = jnp.zeros_like(carry)
        sums[...] = jnp.zeros_like(sums)
        wr_out[...] = jnp.zeros_like(wr_out)
        we_out[...] = jnp.zeros_like(we_out)

    @pl.when(step_id > 0)
    def _():
        d_conv[pl.ds(rows, 8), :] = d_conv[0:8, :]

    d_mixed[...] = dot_plain(d_res_ref[...], ow_ref[...])
    window[0:8, :] = u_prev_ref[8:16, :].astype(jnp.float32)
    window[pl.ds(8, rows), :] = u_ref[...].astype(jnp.float32)

    def conv_step(j, unused):
        at = pl.multiple_of(j * CHUNK, CHUNK)
        made = conv_rows(
            window[pl.ds(at, CHUNK + 8), :], keep_ref[pl.ds(at, CHUNK), :],
            taps_ref[...], vec_ref[0:1, :],
        )
        conv[pl.ds(at, CHUNK), :] = made
        conv_low[pl.ds(at, CHUNK), :] = made.astype(jnp.bfloat16)
        return unused

    lax.fori_loop(0, rows // CHUNK, conv_step, 0)
    rate[...] = dot_plain(conv_low[...], wr_ref[...]) + vec_ref[1:2, :]
    entry[...] = dot_plain(conv_low[...], we_ref[...]) + vec_ref[2:3, :]

    def fold(value):
        return value[0:8, :] + value[8:16, :]

    def scan_step(j, after):
        at = pl.multiple_of(rows - CHUNK - j * CHUNK, CHUNK)
        here = pl.ds(at, CHUNK)
        carried = keep_ref[here, 0:1]
        rate_gate = jax.nn.sigmoid(rate[here, :])
        entry_gate = jax.nn.sigmoid(entry[here, :])
        log_decay = rate_gate * vec_ref[3:4, :]
        exp_decay = jnp.exp(log_decay)
        exp_twice = exp_decay * exp_decay
        drop = jnp.sqrt(one_minus_exp(2.0 * log_decay, exp_twice))
        scaling = (1.0 - carried) + carried * drop
        decays = exp_decay * carried
        gelu_y, slope_y = gelu_both(by_ref[here, :])
        through = d_mixed[here, :]
        d_states = (through * gelu_y).astype(jnp.bfloat16).astype(jnp.float32)
        d_by_ref[here, :] = (
            through * states_ref[here, :].astype(jnp.float32) * slope_y
        ).astype(jnp.bfloat16)
        passed = scan_up(decays, decays * d_states, after)
        last = lax.broadcasted_iota(jnp.int32, passed.shape, 0) == CHUNK - 1
        adjoint = d_states + jnp.where(last, after, pltpu.roll(passed, CHUNK - 1, 0))
        convolved = conv[here, :]
        gated = adjoint * entry_gate
        g_log = adjoint * before_ref[here, :] * decays - gated * convolved * (
            carried * (exp_twice / drop)
        )
        g_pre_rate = g_log * vec_ref[3:4, :] * (rate_gate * (1.0 - rate_gate))
        direct = gated * scaling
        g_pre_entry = direct * convolved * (1.0 - entry_gate)
        d_conv[here, :] = direct
        g_rate[here, :] = g_pre_rate.astype(jnp.bfloat16)
        g_entry[here, :] = g_pre_entry.astype(jnp.bfloat16)
        sums[8:16, :] += fold(g_pre_rate)
        sums[16:24, :] += fold(g_pre_entry)
        sums[24:32, :] += fold(g_log * rate_gate)
        return passed[0:1, :]

    carry[0:1, :] = lax.fori_loop(0, rows // CHUNK, scan_step, carry[0:1, :])
    wr_out[...] += contract_first(conv_low[...], g_rate[...])
    we_out[...] += contract_first(conv_low[...], g_entry[...])
    d_conv[0:rows, :] += contract_last(g_rate[...], wr_ref[...]) + contract_last(
        g_entry[...], we_ref[...]
    )

    def back_step(j, unused):
        at = pl.multiple_of(j * CHUNK, CHUNK)
        here = pl.ds(at, CHUNK)
        keep = keep_ref[here, :]
        ahead = d_conv[pl.ds(at, CHUNK + 8), :]
        behind = window[pl.ds(at, CHUNK + 8), :]
        now = ahead[0:CHUNK]
        total = taps_ref[0:1, :] * now
        sums[0:8, :] += fold(now)
        sums[32:40, :] += fold(now * behind[8:])
        for offset in range(1, 4):
            total = total + taps_ref[offset : offset + 1, :] * (
                keep[:, 3 + offset : 4 + offset] * ahead[offset : offset + CHUNK]
            )
            base = 32 + 8 * offset
            sums[base : base + 8, :] += fold(
                now * (keep[:, offset : offset + 1] * behind[8 - offset : 8 - offset + CHUNK])
            )
        d_bx_ref[here, :] = total.astype(jnp.bfloat16)
        return unused

    lax.fori_loop(0, rows // CHUNK, back_step, 0)
    part_ref[...] = (
        contract_last(d_bx_ref[...], xw_ref[...]) + contract_last(d_by_ref[...], yw_ref[...])
    ).astype(jnp.bfloat16)

    @pl.when(step_id == pl.num_programs(0) - 1)
    def _():
        vec_out[...] = jnp.zeros_like(vec_out)
        for place in range(4):
            vec_out[place : place + 1, :] = jnp.sum(
                sums[8 * place : 8 * place + 8, :], axis=0, keepdims=True
            )
            taps_out[place : place + 1, :] = jnp.sum(
                sums[32 + 8 * place : 40 + 8 * place, :], axis=0, keepdims=True
            )


def whole(shape):
    return pl.BlockSpec(shape, lambda i: (0,) * len(shape))


def mixer_forward(normed, xw, yw, ow, taps, vec, wr, we, keep, rows):
    length, width = normed.shape
    chans = xw.shape[1]
    tile = lambda columns: pl.BlockSpec((rows, columns), lambda i: (i, 0))
    return pl.pallas_call(
        forward_body,
        grid=(length // rows,),
        in_specs=[
            tile(width), whole(xw.shape), whole(yw.shape), whole(ow.shape), whole(taps.shape),
            whole(vec.shape), whole(wr.shape), whole(we.shape), tile(keep.shape[1]),
        ],
        out_specs=[tile(chans)] * 5 + [tile(width)],
        out_shape=[
            jax.ShapeDtypeStruct((length, chans), jnp.bfloat16),
            jax.ShapeDtypeStruct((length, chans), jnp.float32),
            jax.ShapeDtypeStruct((length, chans), jnp.float32),
            jax.ShapeDtypeStruct((length, chans), jnp.bfloat16),
            jax.ShapeDtypeStruct((length, chans), jnp.bfloat16),
            jax.ShapeDtypeStruct((length, width), jnp.bfloat16),
        ],
        scratch_shapes=[
            pltpu.VMEM((rows + 8, chans), jnp.float32),
            pltpu.VMEM((rows, chans), jnp.float32),
            pltpu.VMEM((rows, chans), jnp.bfloat16),
            pltpu.VMEM((rows, chans), jnp.float32),
            pltpu.VMEM((rows, chans), jnp.float32),
            pltpu.VMEM((8, chans), jnp.float32),
        ],
        compiler_params=pltpu.CompilerParams(vmem_limit_bytes=48 * 2**20),
        cost_estimate=pl.CostEstimate(
            flops=6 * length * width * chans,
            bytes_accessed=4 * length * width + 30 * length * chans,
            transcendentals=6 * length * chans,
        ),
        name="mixer_forward",
    )(normed, xw, yw, ow, taps, vec, wr, we, keep)


def mixer_backward(d_res, xw, yw, ow, taps, vec, wr, we, keep, u, by, before, states, rows):
    length, width = d_res.shape
    chans = xw.shape[1]
    blocks = length // rows
    tile = lambda columns: pl.BlockSpec((rows, columns), lambda i: (blocks - 1 - i, 0))
    ahead = pl.BlockSpec(
        (16, chans), lambda i: (jnp.maximum((blocks - 1 - i) * (rows // 16) - 1, 0), 0)
    )
    return pl.pallas_call(
        backward_body,
        grid=(blocks,),
        in_specs=[
            tile(width), whole(xw.shape), whole(yw.shape), whole(ow.shape), whole(taps.shape),
            whole(vec.shape), whole(wr.shape), whole(we.shape), tile(keep.shape[1]),
            tile(chans), ahead, tile(chans), tile(chans), tile(chans),
        ],
        out_specs=[
            tile(chans), tile(chans), tile(width), whole(taps.shape), whole(vec.shape),
            whole(wr.shape), whole(we.shape),
        ],
        out_shape=[
            jax.ShapeDtypeStruct((length, chans), jnp.bfloat16),
            jax.ShapeDtypeStruct((length, chans), jnp.bfloat16),
            jax.ShapeDtypeStruct((length, width), jnp.bfloat16),
            jax.ShapeDtypeStruct(taps.shape, jnp.float32),
            jax.ShapeDtypeStruct(vec.shape, jnp.float32),
            jax.ShapeDtypeStruct(wr.shape, jnp.float32),
            jax.ShapeDtypeStruct(we.shape, jnp.float32),
        ],
        scratch_shapes=[
            pltpu.VMEM((rows + 8, chans), jnp.float32),
            pltpu.VMEM((rows, chans), jnp.float32),
            pltpu.VMEM((rows, chans), jnp.bfloat16),
            pltpu.VMEM((rows, chans), jnp.float32),
            pltpu.VMEM((rows, chans), jnp.float32),
            pltpu.VMEM((rows, chans), jnp.float32),
            pltpu.VMEM((rows + 8, chans), jnp.float32),
            pltpu.VMEM((rows, chans), jnp.bfloat16),
            pltpu.VMEM((rows, chans), jnp.bfloat16),
            pltpu.VMEM((8, chans), jnp.float32),
            pltpu.VMEM((64, chans), jnp.float32),
        ],
        compiler_params=pltpu.CompilerParams(vmem_limit_bytes=48 * 2**20),
        cost_estimate=pl.CostEstimate(
            flops=6 * length * width * chans,
            bytes_accessed=4 * length * width + 30 * length * chans,
            transcendentals=6 * length * chans,
        ),
        name="mixer_backward",
    )(d_res, xw, yw, ow, taps, vec, wr, we, keep, u, u, by, before, states)


def keep_columns(resets):
    length = resets.shape[1]
    position = lax.broadcasted_iota(jnp.int32, resets.shape, 1)
    starts = jnp.maximum(resets, (position == 0).astype(jnp.int32)).astype(jnp.float32)
    carried = (1.0 - starts).reshape(-1)
    seqs = resets.shape[0]

    def back(values, by):
        values = values.reshape(seqs, length)
        return jnp.pad(values, ((0, 0), (by, 0)))[:, :length].reshape(-1)

    def ahead(values, by):
        values = values.reshape(seqs, length)
        return jnp.pad(values, ((0, 0), (0, by)))[:, by:].reshape(-1)

    one = carried
    two = one * back(carried, 1)
    three = two * back(carried, 2)
    return jnp.stack(
        [carried, one, two, three, ahead(one, 1), ahead(two, 2), ahead(three, 3), carried], axis=1
    )


def block_diagonal(blocks, chans):
    heads, width, unused = blocks.shape
    rows = [
        jnp.pad(blocks[h], ((0, 0), (h * width, chans - (h + 1) * width))) for h in range(heads)
    ]
    full = jnp.concatenate(rows, axis=0)
    return jnp.pad(full, ((0, chans - heads * width), (0, 0)))


def diagonal_blocks(full, heads, width):
    return jnp.stack(
        [full[h * width : (h + 1) * width, h * width : (h + 1) * width] for h in range(heads)]
    )


def norm_apply(rows, gain):
    return rows * lax.rsqrt(jnp.mean(rows * rows, axis=-1, keepdims=True) + EPSILON) * gain


def gather(values, axis_name, axis):
    return lax.all_gather(values, axis_name, axis=axis, tiled=True)


def scatter(values, axis_name, axis):
    return lax.psum_scatter(values, axis_name, scatter_dimension=axis, tiled=True)


def shards(
    layer_in,
    cotangent,
    mix_gain,
    ffn_gain,
    x_weight,
    y_weight,
    out_weight,
    conv_weight,
    conv_bias,
    rate_weight,
    rate_bias,
    entry_weight,
    entry_bias,
    decay_param,
    gate_weight,
    up_weight,
    down_weight,
    resets,
):
    heads, head_width = rate_weight.shape[:2]
    used = conv_bias.shape[0]
    chans = -(-used // 128) * 128
    widen = lambda values: jnp.pad(values, ((0, 0), (0, chans - used)))
    mix_full = gather(mix_gain, ("row", "head"), 0)
    ffn_full = gather(ffn_gain, ("row", "head"), 0)
    x_rows = gather(widen(x_weight), "row", 0)
    y_rows = gather(widen(y_weight), "row", 0)
    out_rows = gather(widen(out_weight), "row", 0)
    gate_rows = gather(gate_weight, "row", 0)
    up_rows = gather(up_weight, "row", 0)
    down_rows = gather(down_weight, "row", 0)

    spare = (0, chans - used)
    decay_wide = jnp.pad(decay_param, spare, constant_values=2.0)
    blank = jnp.zeros((chans,), jnp.float32)
    vec = jnp.stack(
        [
            jnp.pad(conv_bias, spare),
            jnp.pad(rate_bias, spare),
            jnp.pad(entry_bias, spare),
            -8.0 * jax.nn.softplus(-decay_wide),
            blank,
            blank,
            blank,
            blank,
        ]
    )
    taps = widen(conv_weight)
    wr = block_diagonal(rate_weight, chans)
    we = block_diagonal(entry_weight, chans)
    keep = keep_columns(resets)

    inputs = layer_in.astype(jnp.float32)
    normed_f, norm_back_one = jax.vjp(norm_apply, inputs, mix_full.astype(jnp.float32))
    normed_group = gather(normed_f.astype(jnp.bfloat16), "head", 0)
    u, by, before, states, mixed, part = mixer_forward(
        normed_group, x_rows, y_rows, out_rows, taps, vec, wr, we, keep, ROWS
    )
    residual = inputs + scatter(part, "head", 0).astype(jnp.float32)
    normed_two_f, norm_back_two = jax.vjp(norm_apply, residual, ffn_full.astype(jnp.float32))
    cot_group = gather(cotangent, "head", 0)
    two_group = gather(normed_two_f.astype(jnp.bfloat16), "head", 0)
    gates = dot_plain(two_group, gate_rows)
    ups = dot_plain(two_group, up_rows)
    activated, slope = gelu_both(gates)
    hidden = (activated * ups).astype(jnp.bfloat16)
    ffn_part = contract_last(hidden, down_rows).astype(jnp.bfloat16)
    d_hidden = dot_plain(cot_group, down_rows)
    d_gates = (d_hidden * ups * slope).astype(jnp.bfloat16)
    d_ups = (d_hidden * activated).astype(jnp.bfloat16)
    d_two_part = (contract_last(d_gates, gate_rows) + contract_last(d_ups, up_rows)).astype(
        jnp.bfloat16
    )
    gate_grad = scatter(contract_first(two_group, d_gates).astype(jnp.bfloat16), "row", 0)
    up_grad = scatter(contract_first(two_group, d_ups).astype(jnp.bfloat16), "row", 0)
    down_grad = scatter(contract_first(cot_group, hidden).astype(jnp.bfloat16), "row", 0)
    layer_out = (residual + scatter(ffn_part, "head", 0).astype(jnp.float32)).astype(jnp.bfloat16)
    d_two = scatter(d_two_part, "head", 0).astype(jnp.float32)
    d_resid_norm, d_ffn_gain = norm_back_two(d_two)
    d_residual = cotangent.astype(jnp.float32) + d_resid_norm
    d_res_group = gather(d_residual.astype(jnp.bfloat16), "head", 0)
    d_bx, d_by, d_part, d_taps, d_vec, d_wr, d_we = mixer_backward(
        d_res_group, x_rows, y_rows, out_rows, taps, vec, wr, we, keep, u, by, before, states, ROWS
    )
    out_grad = scatter(contract_first(d_res_group, mixed).astype(jnp.bfloat16), "row", 0)
    x_grad = scatter(contract_first(normed_group, d_bx).astype(jnp.bfloat16), "row", 0)
    y_grad = scatter(contract_first(normed_group, d_by).astype(jnp.bfloat16), "row", 0)
    d_normed = scatter(d_part, "head", 0).astype(jnp.float32)
    d_inputs, d_mix_gain = norm_back_one(d_normed)
    layer_in_grad = (d_inputs + d_residual).astype(jnp.bfloat16)

    small = [
        d_taps[:, :used],
        d_vec[0, :used],
        diagonal_blocks(d_wr, heads, head_width),
        d_vec[1, :used],
        diagonal_blocks(d_we, heads, head_width),
        d_vec[2, :used],
        d_vec[3, :used] * (8.0 * jax.nn.sigmoid(-decay_param)),
    ]
    small = [lax.psum(item.astype(jnp.bfloat16), "row").astype(jnp.float32) for item in small]
    mix_part = scatter(d_mix_gain, ("row", "head"), 0)
    ffn_part_grad = scatter(d_ffn_gain, ("row", "head"), 0)
    wide = lambda values: values[:, :used].astype(jnp.float32)
    return (
        layer_out,
        layer_in_grad,
        mix_part,
        ffn_part_grad,
        wide(x_grad),
        wide(y_grad),
        wide(out_grad),
        *small,
        gate_grad.astype(jnp.float32),
        up_grad.astype(jnp.float32),
        down_grad.astype(jnp.float32),
    )


def solution(mesh):
    return jax.shard_map(
        shards,
        mesh=mesh,
        in_specs=(
            P(("row", "head"), None),
            P(("row", "head"), None),
            P(("row", "head")),
            P(("row", "head")),
            P("row", "head"),
            P("row", "head"),
            P("row", "head"),
            P(None, "head"),
            P("head"),
            P("head", None, None),
            P("head"),
            P("head", None, None),
            P("head"),
            P("head"),
            P("row", "head"),
            P("row", "head"),
            P("row", "head"),
            P("row", None),
        ),
        out_specs=(
            P(("row", "head"), None),
            P(("row", "head"), None),
            P(("row", "head")),
            P(("row", "head")),
            P("row", "head"),
            P("row", "head"),
            P("row", "head"),
            P(None, "head"),
            P("head"),
            P("head", None, None),
            P("head"),
            P("head", None, None),
            P("head"),
            P("head"),
            P("row", "head"),
            P("row", "head"),
            P("row", "head"),
        ),
        check_vma=False,
    )
```

```python
import jax
import jax.numpy as jnp
from jax import lax
from jax.experimental import pallas as pl
from jax.experimental.pallas import tpu as pltpu
from jax.sharding import PartitionSpec as P

EPSILON = 1e-06
ROWS = 256
GELU_A = 0.7978845608028654
GELU_B = 0.044715
CHUNK = 16


def gelu_only(x):
    return 0.5 * x * (1.0 + jnp.tanh(GELU_A * (x + GELU_B * x * x * x)))


def gelu_both(x):
    square = x * x
    bent = jnp.tanh(GELU_A * x * (1.0 + GELU_B * square))
    half = 0.5 * (1.0 + bent)
    slope = half + 0.5 * x * (1.0 - bent * bent) * (GELU_A * (1.0 + 3.0 * GELU_B * square))
    return x * half, slope


def one_minus_exp(x, exp_x):
    series = 1.0 + x * (1.0 / 7.0)
    for order in (6.0, 5.0, 4.0, 3.0, 2.0):
        series = 1.0 + x * (1.0 / order) * series
    return jnp.where(x > -0.25, -x * series, 1.0 - exp_x)


def dot_plain(left, right):
    return jnp.dot(left, right, preferred_element_type=jnp.float32)


def contract_last(left, right):
    return lax.dot_general(
        left, right, (((1,), (1,)), ((), ())), preferred_element_type=jnp.float32
    )


def contract_first(left, right):
    return lax.dot_general(
        left, right, (((0,), (0,)), ((), ())), preferred_element_type=jnp.float32
    )


def conv_rows(window, keep, taps, shift):
    rows = window.shape[0] - 8
    total = taps[0:1] * window[8:] + shift
    for offset in range(1, 4):
        total = total + taps[offset : offset + 1] * (
            keep[:, offset : offset + 1] * window[8 - offset : 8 - offset + rows]
        )
    return total


def scan_down(decays, driven, carry):
    rows = decays.shape[0]
    place = lax.broadcasted_iota(jnp.int32, decays.shape, 0)
    step = 1
    while step < rows:
        inside = place >= step
        driven = jnp.where(inside, decays * pltpu.roll(driven, step, 0) + driven, driven)
        decays = jnp.where(inside, decays * pltpu.roll(decays, step, 0), decays)
        step *= 2
    return decays * carry + driven


def scan_up(decays, driven, carry):
    rows = decays.shape[0]
    place = lax.broadcasted_iota(jnp.int32, decays.shape, 0)
    step = 1
    while step < rows:
        inside = place < rows - step
        driven = jnp.where(inside, decays * pltpu.roll(driven, rows - step, 0) + driven, driven)
        decays = jnp.where(inside, decays * pltpu.roll(decays, rows - step, 0), decays)
        step *= 2
    return decays * carry + driven


def forward_step(
    normed_ref, xw_ref, yw_ref, ow_ref, taps_ref, vec_ref, wr_ref, we_ref, keep_ref,
    u_ref, by_ref, before_ref, states_ref, mixed_ref,
    window, conv, conv_low, rate, entry, carry,
):
    rows = normed_ref.shape[0]

    @pl.when(pl.program_id(0) == 0)
    def _():
        window[0:8, :] = jnp.zeros_like(window[0:8, :])
        carry[...] = jnp.zeros_like(carry)

    branch_x = dot_plain(normed_ref[...], xw_ref[...]).astype(jnp.bfloat16)
    u_ref[...] = branch_x
    window[pl.ds(8, rows), :] = branch_x.astype(jnp.float32)
    by_ref[...] = dot_plain(normed_ref[...], yw_ref[...])

    def conv_step(j, unused):
        at = pl.multiple_of(j * CHUNK, CHUNK)
        made = conv_rows(
            window[pl.ds(at, CHUNK + 8), :], keep_ref[pl.ds(at, CHUNK), :],
            taps_ref[...], vec_ref[0:1, :],
        )
        conv[pl.ds(at, CHUNK), :] = made
        conv_low[pl.ds(at, CHUNK), :] = made.astype(jnp.bfloat16)
        return unused

    lax.fori_loop(0, rows // CHUNK, conv_step, 0)
    window[0:8, :] = window[pl.ds(rows, 8), :]
    rate[...] = dot_plain(conv_low[...], wr_ref[...]) + vec_ref[1:2, :]
    entry[...] = dot_plain(conv_low[...], we_ref[...]) + vec_ref[2:3, :]

    def scan_step(j, before):
        at = pl.multiple_of(j * CHUNK, CHUNK)
        here = pl.ds(at, CHUNK)
        carried = keep_ref[here, 0:1]
        log_decay = jax.nn.sigmoid(rate[here, :]) * vec_ref[3:4, :]
        exp_decay = jnp.exp(log_decay)
        drop = jnp.sqrt(one_minus_exp(2.0 * log_decay, exp_decay * exp_decay))
        scaling = (1.0 - carried) + carried * drop
        driven = scaling * jax.nn.sigmoid(entry[here, :]) * conv[here, :]
        states = scan_down(exp_decay * carried, driven, before)
        first = lax.broadcasted_iota(jnp.int32, states.shape, 0) == 0
        before_ref[here, :] = jnp.where(first, before, pltpu.roll(states, 1, 0))
        states_low = states.astype(jnp.bfloat16)
        states_ref[here, :] = states_low
        mixed_ref[here, :] = (
            states_low.astype(jnp.float32) * gelu_only(by_ref[here, :])
        ).astype(jnp.bfloat16)
        return states[CHUNK - 1 : CHUNK, :]

    carry[0:1, :] = lax.fori_loop(0, rows // CHUNK, scan_step, carry[0:1, :])
    return contract_last(mixed_ref[...], ow_ref[...]).astype(jnp.bfloat16)


def forward_body(
    normed_ref, xw_ref, yw_ref, ow_ref, taps_ref, vec_ref, wr_ref, we_ref, keep_ref,
    u_ref, by_ref, before_ref, states_ref, mixed_ref, part_ref, *scratch,
):
    part_ref[...] = forward_step(
        normed_ref, xw_ref, yw_ref, ow_ref, taps_ref, vec_ref, wr_ref, we_ref, keep_ref,
        u_ref, by_ref, before_ref, states_ref, mixed_ref, *scratch,
    )


def backward_body(
    d_res_ref, xw_ref, yw_ref, ow_ref, taps_ref, vec_ref, wr_ref, we_ref, keep_ref,
    u_ref, u_prev_ref, by_ref, before_ref, states_ref,
    d_bx_ref, d_by_ref, part_ref, taps_out, vec_out, wr_out, we_out,
    window, conv, conv_low, rate, entry, d_mixed, d_conv, g_rate, g_entry, carry, sums,
):
    rows = d_res_ref.shape[0]
    step_id = pl.program_id(0)

    @pl.when(step_id == 0)
    def _():
        d_conv[pl.ds(rows, 8), :] = jnp.zeros_like(d_conv[pl.ds(rows, 8), :])
        carry[...] = jnp.zeros_like(carry)
        sums[...] = jnp.zeros_like(sums)
        wr_out[...] = jnp.zeros_like(wr_out)
        we_out[...] = jnp.zeros_like(we_out)

    @pl.when(step_id > 0)
    def _():
        d_conv[pl.ds(rows, 8), :] = d_conv[0:8, :]

    d_mixed[...] = dot_plain(d_res_ref[...], ow_ref[...])
    window[0:8, :] = u_prev_ref[8:16, :].astype(jnp.float32)
    window[pl.ds(8, rows), :] = u_ref[...].astype(jnp.float32)

    def conv_step(j, unused):
        at = pl.multiple_of(j * CHUNK, CHUNK)
        made = conv_rows(
            window[pl.ds(at, CHUNK + 8), :], keep_ref[pl.ds(at, CHUNK), :],
            taps_ref[...], vec_ref[0:1, :],
        )
        conv[pl.ds(at, CHUNK), :] = made
        conv_low[pl.ds(at, CHUNK), :] = made.astype(jnp.bfloat16)
        return unused

    lax.fori_loop(0, rows // CHUNK, conv_step, 0)
    rate[...] = dot_plain(conv_low[...], wr_ref[...]) + vec_ref[1:2, :]
    entry[...] = dot_plain(conv_low[...], we_ref[...]) + vec_ref[2:3, :]

    def fold(value):
        return value[0:8, :] + value[8:16, :]

    def scan_step(j, after):
        at = pl.multiple_of(rows - CHUNK - j * CHUNK, CHUNK)
        here = pl.ds(at, CHUNK)
        carried = keep_ref[here, 0:1]
        rate_gate = jax.nn.sigmoid(rate[here, :])
        entry_gate = jax.nn.sigmoid(entry[here, :])
        log_decay = rate_gate * vec_ref[3:4, :]
        exp_decay = jnp.exp(log_decay)
        exp_twice = exp_decay * exp_decay
        drop = jnp.sqrt(one_minus_exp(2.0 * log_decay, exp_twice))
        scaling = (1.0 - carried) + carried * drop
        decays = exp_decay * carried
        gelu_y, slope_y = gelu_both(by_ref[here, :])
        through = d_mixed[here, :]
        d_states = (through * gelu_y).astype(jnp.bfloat16).astype(jnp.float32)
        d_by_ref[here, :] = (
            through * states_ref[here, :].astype(jnp.float32) * slope_y
        ).astype(jnp.bfloat16)
        passed = scan_up(decays, decays * d_states, after)
        last = lax.broadcasted_iota(jnp.int32, passed.shape, 0) == CHUNK - 1
        adjoint = d_states + jnp.where(last, after, pltpu.roll(passed, CHUNK - 1, 0))
        convolved = conv[here, :]
        gated = adjoint * entry_gate
        g_log = adjoint * before_ref[here, :] * decays - gated * convolved * (
            carried * (exp_twice / drop)
        )
        g_pre_rate = g_log * vec_ref[3:4, :] * (rate_gate * (1.0 - rate_gate))
        direct = gated * scaling
        g_pre_entry = direct * convolved * (1.0 - entry_gate)
        d_conv[here, :] = direct
        g_rate[here, :] = g_pre_rate.astype(jnp.bfloat16)
        g_entry[here, :] = g_pre_entry.astype(jnp.bfloat16)
        sums[8:16, :] += fold(g_pre_rate)
        sums[16:24, :] += fold(g_pre_entry)
        sums[24:32, :] += fold(g_log * rate_gate)
        return passed[0:1, :]

    carry[0:1, :] = lax.fori_loop(0, rows // CHUNK, scan_step, carry[0:1, :])
    wr_out[...] += contract_first(conv_low[...], g_rate[...])
    we_out[...] += contract_first(conv_low[...], g_entry[...])
    d_conv[0:rows, :] += contract_last(g_rate[...], wr_ref[...]) + contract_last(
        g_entry[...], we_ref[...]
    )

    def back_step(j, unused):
        at = pl.multiple_of(j * CHUNK, CHUNK)
        here = pl.ds(at, CHUNK)
        keep = keep_ref[here, :]
        ahead = d_conv[pl.ds(at, CHUNK + 8), :]
        behind = window[pl.ds(at, CHUNK + 8), :]
        now = ahead[0:CHUNK]
        total = taps_ref[0:1, :] * now
        sums[0:8, :] += fold(now)
        sums[32:40, :] += fold(now * behind[8:])
        for offset in range(1, 4):
            total = total + taps_ref[offset : offset + 1, :] * (
                keep[:, 3 + offset : 4 + offset] * ahead[offset : offset + CHUNK]
            )
            base = 32 + 8 * offset
            sums[base : base + 8, :] += fold(
                now * (keep[:, offset : offset + 1] * behind[8 - offset : 8 - offset + CHUNK])
            )
        d_bx_ref[here, :] = total.astype(jnp.bfloat16)
        return unused

    lax.fori_loop(0, rows // CHUNK, back_step, 0)
    part_ref[...] = (
        contract_last(d_bx_ref[...], xw_ref[...]) + contract_last(d_by_ref[...], yw_ref[...])
    ).astype(jnp.bfloat16)

    @pl.when(step_id == pl.num_programs(0) - 1)
    def _():
        vec_out[...] = jnp.zeros_like(vec_out)
        for place in range(4):
            vec_out[place : place + 1, :] = jnp.sum(
                sums[8 * place : 8 * place + 8, :], axis=0, keepdims=True
            )
            taps_out[place : place + 1, :] = jnp.sum(
                sums[32 + 8 * place : 40 + 8 * place, :], axis=0, keepdims=True
            )


def whole(shape):
    return pl.BlockSpec(shape, lambda i: (0,) * len(shape))


def mixer_forward(normed, xw, yw, ow, taps, vec, wr, we, keep, rows):
    length, width = normed.shape
    chans = xw.shape[1]
    tile = lambda columns: pl.BlockSpec((rows, columns), lambda i: (i, 0))
    return pl.pallas_call(
        forward_body,
        grid=(length // rows,),
        in_specs=[
            tile(width), whole(xw.shape), whole(yw.shape), whole(ow.shape), whole(taps.shape),
            whole(vec.shape), whole(wr.shape), whole(we.shape), tile(keep.shape[1]),
        ],
        out_specs=[tile(chans)] * 5 + [tile(width)],
        out_shape=[
            jax.ShapeDtypeStruct((length, chans), jnp.bfloat16),
            jax.ShapeDtypeStruct((length, chans), jnp.float32),
            jax.ShapeDtypeStruct((length, chans), jnp.float32),
            jax.ShapeDtypeStruct((length, chans), jnp.bfloat16),
            jax.ShapeDtypeStruct((length, chans), jnp.bfloat16),
            jax.ShapeDtypeStruct((length, width), jnp.bfloat16),
        ],
        scratch_shapes=[
            pltpu.VMEM((rows + 8, chans), jnp.float32),
            pltpu.VMEM((rows, chans), jnp.float32),
            pltpu.VMEM((rows, chans), jnp.bfloat16),
            pltpu.VMEM((rows, chans), jnp.float32),
            pltpu.VMEM((rows, chans), jnp.float32),
            pltpu.VMEM((8, chans), jnp.float32),
        ],
        compiler_params=pltpu.CompilerParams(vmem_limit_bytes=48 * 2**20),
        cost_estimate=pl.CostEstimate(
            flops=6 * length * width * chans,
            bytes_accessed=4 * length * width + 30 * length * chans,
            transcendentals=6 * length * chans,
        ),
        name="mixer_forward",
    )(normed, xw, yw, ow, taps, vec, wr, we, keep)


def mixer_backward(d_res, xw, yw, ow, taps, vec, wr, we, keep, u, by, before, states, rows):
    length, width = d_res.shape
    chans = xw.shape[1]
    blocks = length // rows
    tile = lambda columns: pl.BlockSpec((rows, columns), lambda i: (blocks - 1 - i, 0))
    ahead = pl.BlockSpec(
        (16, chans), lambda i: (jnp.maximum((blocks - 1 - i) * (rows // 16) - 1, 0), 0)
    )
    return pl.pallas_call(
        backward_body,
        grid=(blocks,),
        in_specs=[
            tile(width), whole(xw.shape), whole(yw.shape), whole(ow.shape), whole(taps.shape),
            whole(vec.shape), whole(wr.shape), whole(we.shape), tile(keep.shape[1]),
            tile(chans), ahead, tile(chans), tile(chans), tile(chans),
        ],
        out_specs=[
            tile(chans), tile(chans), tile(width), whole(taps.shape), whole(vec.shape),
            whole(wr.shape), whole(we.shape),
        ],
        out_shape=[
            jax.ShapeDtypeStruct((length, chans), jnp.bfloat16),
            jax.ShapeDtypeStruct((length, chans), jnp.bfloat16),
            jax.ShapeDtypeStruct((length, width), jnp.bfloat16),
            jax.ShapeDtypeStruct(taps.shape, jnp.float32),
            jax.ShapeDtypeStruct(vec.shape, jnp.float32),
            jax.ShapeDtypeStruct(wr.shape, jnp.float32),
            jax.ShapeDtypeStruct(we.shape, jnp.float32),
        ],
        scratch_shapes=[
            pltpu.VMEM((rows + 8, chans), jnp.float32),
            pltpu.VMEM((rows, chans), jnp.float32),
            pltpu.VMEM((rows, chans), jnp.bfloat16),
            pltpu.VMEM((rows, chans), jnp.float32),
            pltpu.VMEM((rows, chans), jnp.float32),
            pltpu.VMEM((rows, chans), jnp.float32),
            pltpu.VMEM((rows + 8, chans), jnp.float32),
            pltpu.VMEM((rows, chans), jnp.bfloat16),
            pltpu.VMEM((rows, chans), jnp.bfloat16),
            pltpu.VMEM((8, chans), jnp.float32),
            pltpu.VMEM((64, chans), jnp.float32),
        ],
        compiler_params=pltpu.CompilerParams(vmem_limit_bytes=48 * 2**20),
        cost_estimate=pl.CostEstimate(
            flops=6 * length * width * chans,
            bytes_accessed=4 * length * width + 30 * length * chans,
            transcendentals=6 * length * chans,
        ),
        name="mixer_backward",
    )(d_res, xw, yw, ow, taps, vec, wr, we, keep, u, u, by, before, states)


def keep_columns(resets):
    length = resets.shape[1]
    position = lax.broadcasted_iota(jnp.int32, resets.shape, 1)
    starts = jnp.maximum(resets, (position == 0).astype(jnp.int32)).astype(jnp.float32)
    carried = (1.0 - starts).reshape(-1)
    seqs = resets.shape[0]

    def back(values, by):
        values = values.reshape(seqs, length)
        return jnp.pad(values, ((0, 0), (by, 0)))[:, :length].reshape(-1)

    def ahead(values, by):
        values = values.reshape(seqs, length)
        return jnp.pad(values, ((0, 0), (0, by)))[:, by:].reshape(-1)

    one = carried
    two = one * back(carried, 1)
    three = two * back(carried, 2)
    return jnp.stack(
        [carried, one, two, three, ahead(one, 1), ahead(two, 2), ahead(three, 3), carried], axis=1
    )


def block_diagonal(blocks, chans):
    heads, width, unused = blocks.shape
    rows = [
        jnp.pad(blocks[h], ((0, 0), (h * width, chans - (h + 1) * width))) for h in range(heads)
    ]
    full = jnp.concatenate(rows, axis=0)
    return jnp.pad(full, ((0, chans - heads * width), (0, 0)))


def diagonal_blocks(full, heads, width):
    return jnp.stack(
        [full[h * width : (h + 1) * width, h * width : (h + 1) * width] for h in range(heads)]
    )


MESH = pl.DeviceIdType.MESH
ANYWHERE = pl.BlockSpec(memory_space=pl.ANY)
IN_VMEM = pl.BlockSpec(memory_space=pltpu.VMEM)
LINE = 4
PLANE = 8
PIECES = 4


def send_to(src, dst, sent, arrived, axis, target):
    return pltpu.make_async_remote_copy(
        src_ref=src,
        dst_ref=dst,
        send_sem=sent,
        recv_sem=arrived,
        device_id={axis: target},
        device_id_type=MESH,
    )


def sibling_of(h):
    return h + 1 - 2 * lax.rem(h, 2)


def across_of(h):
    return h + 2 - 4 * lax.rem(lax.div(h, 2), 2)


def along_of(h):
    return lax.rem(h + 4, PLANE)


def meet(row_line, plane):
    r, h = lax.axis_index("row"), lax.axis_index("head")
    barrier = pltpu.get_barrier_semaphore()
    count = 0
    if row_line:
        for step in range(1, LINE):
            pl.semaphore_signal(
                barrier, inc=1, device_id={"row": lax.rem(r + step, LINE)}, device_id_type=MESH
            )
        count += LINE - 1
    if plane == "all":
        for step in range(1, PLANE):
            pl.semaphore_signal(
                barrier, inc=1, device_id={"head": lax.rem(h + step, PLANE)}, device_id_type=MESH
            )
        count += PLANE - 1
    if plane == "near":
        for target in (sibling_of(h), across_of(h), along_of(h), across_of(along_of(h))):
            pl.semaphore_signal(barrier, inc=1, device_id={"head": target}, device_id_type=MESH)
        count += 4
    pl.semaphore_wait(barrier, count)


class LineGather:
    semaphores = (
        pltpu.SemaphoreType.DMA((LINE,)),
        pltpu.SemaphoreType.DMA((LINE,)),
        pltpu.SemaphoreType.DMA((2,)),
    )

    def __init__(self, shard, full, sent, arrived, other):
        self.r = lax.axis_index("row")
        self.shard, self.full, self.sent, self.arrived, self.other = (
            shard, full, sent, arrived, other,
        )

    def near(self, t):
        gap = self.r - t
        return (gap != 0) & (gap < 3) & (gap > -3)

    def own(self, t):
        return send_to(
            self.shard, self.full.at[self.r], self.sent.at[t], self.arrived.at[self.r], "row", t
        )

    def handed(self, origin, target):
        return send_to(
            self.full.at[origin], self.full.at[origin], self.other.at[0], self.arrived.at[origin],
            "row", target,
        )

    def local(self):
        return pltpu.make_async_copy(self.shard, self.full.at[self.r], self.other.at[1])

    def start(self):
        for t in range(LINE):

            @pl.when(self.near(t))
            def _(t=t):
                self.own(t).start()

        self.local().start()

    def forward(self):
        for me, origin, target in ((2, 0, 3), (1, 3, 0)):

            @pl.when(self.r == me)
            def _(origin=origin, target=target):
                copy = self.handed(origin, target)
                copy.wait_recv()
                copy.start()

    def finish(self):
        r = self.r
        for t in range(LINE):
            known = (r == t) | ((r == 2) & (t == 0)) | ((r == 1) & (t == 3))

            @pl.when(jnp.logical_not(known))
            def _(t=t):
                self.handed(t, t).wait_recv()

            @pl.when(self.near(t))
            def _(t=t):
                self.own(t).wait_send()

        for me, origin, target in ((2, 0, 3), (1, 3, 0)):

            @pl.when(r == me)
            def _(origin=origin, target=target):
                self.handed(origin, target).wait_send()

        self.local().wait()


class LineReduce:
    semaphores = (
        pltpu.SemaphoreType.DMA((LINE,)),
        pltpu.SemaphoreType.DMA((LINE,)),
        pltpu.SemaphoreType.DMA((2,)),
    )

    def __init__(self, parts, landed, passed, sent, arrived, other):
        self.r = lax.axis_index("row")
        self.parts, self.landed, self.passed = parts, landed, passed
        self.sent, self.arrived, self.other = sent, arrived, other

    def to_pass(self, me, origin, via):
        return send_to(
            self.parts.at[origin], self.passed, self.sent.at[origin], self.other.at[0], "row", via
        )

    def direct(self, t):
        return send_to(
            self.parts.at[t], self.landed.at[self.r], self.sent.at[t], self.arrived.at[self.r],
            "row", t,
        )

    def plain(self, t):
        r = self.r
        ends = ((r == 0) & (t == 3)) | ((r == 3) & (t == 0))
        added = ((r == 1) & (t == 3)) | ((r == 2) & (t == 0))
        return jnp.logical_not(ends | added | (r == t))

    def start(self):
        for me, end, via in ((0, 3, 1), (3, 0, 2)):

            @pl.when(self.r == me)
            def _(me=me, end=end, via=via):
                self.to_pass(me, end, via).start()

        for t in range(LINE):

            @pl.when(self.plain(t))
            def _(t=t):
                self.direct(t).start()

    def forward(self):
        for me, end in ((1, 3), (2, 0)):

            @pl.when(self.r == me)
            def _(me=me, end=end):
                self.to_pass(me, end, end).wait_recv()
                rows = self.passed.shape[0]
                step = 64

                def add(i, unused):
                    at = pl.ds(pl.multiple_of(i * step, step), step)
                    self.parts[end, at, :] = (
                        self.parts[end, at, :].astype(jnp.float32)
                        + self.passed[at, :].astype(jnp.float32)
                    ).astype(jnp.bfloat16)
                    return unused

                lax.fori_loop(0, rows // step, add, 0)
                self.direct(end).start()

    def finish(self, write):
        r = self.r
        for t in range(LINE):

            @pl.when(jnp.logical_not(unsent_to(r, t)))
            def _(t=t):
                send_to(
                    self.parts.at[t], self.landed.at[t], self.sent.at[t], self.arrived.at[t],
                    "row", t,
                ).wait_recv()

        rows = self.passed.shape[0]
        step = 64

        def add(i, unused):
            at = pl.ds(pl.multiple_of(i * step, step), step)
            total = self.parts[r, at, :].astype(jnp.float32)
            for t in range(LINE):
                total = total + jnp.where(
                    unsent_to(r, t), 0.0, self.landed[t, at, :].astype(jnp.float32)
                )
            write(at, total)
            return unused

        lax.fori_loop(0, rows // step, add, 0)
        for me, end, via in ((0, 3, 1), (3, 0, 2)):

            @pl.when(r == me)
            def _(me=me, end=end, via=via):
                self.to_pass(me, end, via).wait_send()

        for t in range(LINE):

            @pl.when(jnp.logical_not(unsent_to(r, t)))
            def _(t=t):
                self.direct(t).wait_send()


def unsent_to(r, t):
    return ((r == 0) & (t == 3)) | ((r == 3) & (t == 0)) | (r == t)


class PlaneGather:
    semaphores = (
        pltpu.SemaphoreType.DMA((PIECES, 7)),
        pltpu.SemaphoreType.DMA((PIECES, 7)),
        pltpu.SemaphoreType.DMA((1,)),
    )
    first = tuple(range(PIECES // 2))
    second = tuple(range(PIECES // 2, PIECES))

    def __init__(self, block, full, sent, arrived, other):
        h = lax.axis_index("head")
        self.h, self.side, self.x, self.y = h, sibling_of(h), across_of(h), along_of(h)
        self.far = across_of(self.y)
        self.block, self.full = block, full
        self.sent, self.arrived, self.other = sent, arrived, other
        self.rows = block.shape[0] // PIECES

    def piece(self, owner, c):
        return self.full.at[owner, pl.ds(c * self.rows, self.rows)]

    def own(self, c, lane, target):
        return send_to(
            self.block.at[pl.ds(c * self.rows, self.rows)], self.piece(self.h, c),
            self.sent.at[c, lane], self.arrived.at[c, lane], "head", target,
        )

    def hand(self, owner, c, lane, target):
        return send_to(
            self.piece(owner, c), self.piece(owner, c), self.sent.at[c, lane],
            self.arrived.at[c, lane], "head", target,
        )

    def local(self):
        return pltpu.make_async_copy(self.block, self.full.at[self.h], self.other.at[0])

    def start(self):
        for a, b in zip(self.first, self.second):
            self.own(a, 1, self.x).start()
            self.own(b, 2, self.y).start()
        for a, b in zip(self.first, self.second):
            self.own(b, 1, self.x).start()
            self.own(a, 2, self.y).start()
        for c in range(PIECES):
            self.own(c, 0, self.side).start()
        self.local().start()

    def relay(self, place):
        a, b = self.first[place], self.second[place]
        self.hand(self.x, a, 1, self.x).wait_recv()
        self.hand(self.x, a, 3, self.y).start()
        self.hand(self.x, a, 4, self.side).start()
        self.hand(self.y, b, 2, self.y).wait_recv()
        self.hand(self.y, b, 3, self.x).start()
        self.hand(self.y, b, 5, self.side).start()

    def rest(self):
        for a, b in zip(self.first, self.second):
            self.hand(self.x, b, 1, self.x).wait_recv()
            self.hand(self.x, b, 4, self.side).start()
            self.hand(self.y, a, 2, self.y).wait_recv()
            self.hand(self.y, a, 5, self.side).start()

    def end(self):
        for pair in zip(self.first, self.second):
            for c in pair:
                self.hand(self.far, c, 3, self.side).wait_recv()
                self.hand(self.far, c, 6, self.side).start()
        side = self.side
        for c in range(PIECES):
            for owner, lane in (
                (side, 0), (across_of(side), 4), (along_of(side), 5),
                (across_of(along_of(side)), 6),
            ):
                self.hand(owner, c, lane, side).wait_recv()
        for c in range(PIECES):
            for lane in range(7):
                self.own(c, lane, side).wait_send()
        self.local().wait()


class PlaneReduce:
    semaphores = (
        pltpu.SemaphoreType.DMA((4,)),
        pltpu.SemaphoreType.DMA((4,)),
        pltpu.SemaphoreType.DMA((4,)),
        pltpu.SemaphoreType.DMA((3,)),
    )

    @staticmethod
    def buffers(rows, width):
        return [
            pltpu.VMEM((4, rows, width), jnp.bfloat16),
            pltpu.VMEM((4, rows, width), jnp.bfloat16),
            pltpu.VMEM((4, rows, width), jnp.bfloat16),
            pltpu.VMEM((3, rows, width), jnp.bfloat16),
        ]

    def __init__(self, staged, beside, mine, landed, side_sent, side_arrived, sent, arrived):
        h = lax.axis_index("head")
        self.h, self.core, self.chip = h, lax.rem(h, 2), lax.div(h, 2)
        self.staged, self.beside, self.mine, self.landed = staged, beside, mine, landed
        self.side_sent, self.side_arrived = side_sent, side_arrived
        self.sent, self.arrived = sent, arrived

    def aside(self, chip):
        return send_to(
            self.staged.at[chip], self.beside.at[chip], self.side_sent.at[chip],
            self.side_arrived.at[chip], "head", sibling_of(self.h),
        )

    def place(self, chip):
        flip_x = lax.rem(chip + self.chip, 2)
        flip_y = lax.rem(lax.div(chip, 2) + lax.div(self.chip, 2), 2)
        return flip_x + 2 * flip_y - 1

    def across(self, chip):
        at = self.place(chip)
        return send_to(
            self.mine.at[chip], self.landed.at[at], self.sent.at[chip], self.arrived.at[at],
            "head", 2 * chip + self.core,
        )

    def put(self, block, value):
        chip, core = lax.div(block, 2), lax.rem(block, 2)

        @pl.when(core == self.core)
        def _():
            self.mine[chip] = value

        @pl.when(core != self.core)
        def _():
            self.staged[chip] = value
            self.aside(chip).start()

    def pass_on(self, block):
        chip, core = lax.div(block, 2), lax.rem(block, 2)

        @pl.when(core == self.core)
        def _():
            self.aside(chip).wait_recv()
            rows = self.mine.shape[1]
            step = 32

            def add(i, unused):
                at = pl.ds(pl.multiple_of(i * step, step), step)
                self.mine[chip, at, :] = (
                    self.mine[chip, at, :].astype(jnp.float32)
                    + self.beside[chip, at, :].astype(jnp.float32)
                ).astype(jnp.bfloat16)
                return unused

            lax.fori_loop(0, rows // step, add, 0)

            @pl.when(chip != self.chip)
            def _():
                self.across(chip).start()

    def arrive(self):
        for at in range(3):
            send_to(
                self.landed.at[at], self.landed.at[at], self.sent.at[0], self.arrived.at[at],
                "head", self.h,
            ).wait_recv()

    def total(self, at):
        value = self.mine[self.chip, at, :].astype(jnp.float32)
        for place in range(3):
            value = value + self.landed[place, at, :].astype(jnp.float32)
        return value

    def finish(self):
        for chip in range(4):
            self.aside(chip).wait_send()

            @pl.when(chip != self.chip)
            def _(chip=chip):
                self.across(chip).wait_send()


def norm_apply(rows, gain):
    return rows * lax.rsqrt(jnp.mean(rows * rows, axis=-1, keepdims=True) + EPSILON) * gain


def gather(values, axis_name, axis):
    return lax.all_gather(values, axis_name, axis=axis, tiled=True)


def scatter(values, axis_name, axis):
    return lax.psum_scatter(values, axis_name, scatter_dimension=axis, tiled=True)

def norm_rows(rows, gain):
    return rows * lax.rsqrt(jnp.mean(rows * rows, axis=-1, keepdims=True) + EPSILON) * gain


def open_body(
    x_ref, tile_ref, xs, ys, zs, full, xf, yf, zf, gains_ref,
    normed, column, spread, gain_sent, gain_arrived, wide_sent, wide_arrived, *semaphores,
):
    r, h = lax.axis_index("row"), lax.axis_index("head")
    lines = [
        LineGather(src, dst, *semaphores[3 * k : 3 * k + 3])
        for k, (src, dst) in enumerate(((xs, xf), (ys, yf), (zs, zf)))
    ]
    plane = PlaneGather(normed, full, *semaphores[9:12])
    meet(True, "all")

    def up_line(t):
        return send_to(
            column.at[r], column.at[r], gain_sent.at[t], gain_arrived.at[r], "row", t
        )

    def from_line(t):
        return send_to(
            column.at[t], column.at[t], gain_sent.at[t], gain_arrived.at[t], "row", t
        )

    def over_plane(step, owner):
        return send_to(
            column, spread.at[owner], wide_sent.at[step], wide_arrived.at[owner], "head",
            lax.rem(h + step, PLANE),
        )

    column[r] = tile_ref[...]
    for step in range(1, LINE):
        up_line(lax.rem(r + step, LINE)).start()
    for line in lines:
        line.start()
    for step in range(1, LINE):
        from_line(lax.rem(r + step, LINE)).wait_recv()
    for step in range(1, PLANE):
        over_plane(step, h).start()
    spread[h] = column[...]
    for step in range(1, PLANE):
        over_plane(step, lax.rem(h + step, PLANE)).wait_recv()

    share = tile_ref.shape[1] // 2
    low = lax.broadcasted_iota(jnp.int32, (1, 2 * share), 1) < share
    for line_place in range(LINE):
        for pair in range(PLANE // 2):
            even = spread[2 * pair, line_place][0:1, :]
            odd = spread[2 * pair + 1, line_place][0:1, :]
            at = (line_place * (PLANE // 2) + pair) * 2 * share
            gains_ref[0:1, at : at + 2 * share] = jnp.where(low, even, pltpu.roll(odd, share, 1))
            gains_ref[1:2, at : at + 2 * share] = jnp.where(low, pltpu.roll(even, share, 1), odd)

    def make(i, unused):
        at = pl.ds(pl.multiple_of(i * CHUNK, CHUNK), CHUNK)
        normed[at, :] = norm_rows(x_ref[at, :].astype(jnp.float32), gains_ref[0:1, :]).astype(
            jnp.bfloat16
        )
        return unused

    lax.fori_loop(0, x_ref.shape[0] // CHUNK, make, 0)
    plane.start()
    plane.relay(0)
    lines[0].forward()
    plane.relay(1)
    plane.rest()
    plane.end()
    for line in lines[1:]:
        line.forward()
    for line in lines:
        line.finish()
    for step in range(1, LINE):
        up_line(lax.rem(r + step, LINE)).wait_send()
    for step in range(1, PLANE):
        over_plane(step, h).wait_send()


def open_block(layer_in, tile, weights):
    rows, width = layer_in.shape
    return pl.pallas_call(
        open_body,
        in_specs=[IN_VMEM, IN_VMEM] + [ANYWHERE] * 3,
        out_specs=[ANYWHERE] * 4 + [IN_VMEM],
        out_shape=[jax.ShapeDtypeStruct((PLANE, rows, width), jnp.bfloat16)]
        + [jax.ShapeDtypeStruct((LINE,) + item.shape, item.dtype) for item in weights]
        + [jax.ShapeDtypeStruct((2, width), jnp.float32)],
        scratch_shapes=[
            pltpu.VMEM((rows, width), jnp.bfloat16),
            pltpu.VMEM((LINE,) + tile.shape, jnp.float32),
            pltpu.VMEM((PLANE, LINE) + tile.shape, jnp.float32),
            pltpu.SemaphoreType.DMA((LINE,)),
            pltpu.SemaphoreType.DMA((LINE,)),
            pltpu.SemaphoreType.DMA((PLANE,)),
            pltpu.SemaphoreType.DMA((PLANE,)),
            *(LineGather.semaphores * 3),
            *PlaneGather.semaphores,
        ],
        compiler_params=pltpu.CompilerParams(
            collective_id=0, has_side_effects=True, vmem_limit_bytes=24 * 2**20
        ),
        name="open_block",
    )(layer_in, tile, *weights)


def forward_linked_body(
    normed_ref, xw_ref, yw_ref, ow_ref, taps_ref, vec_ref, wr_ref, we_ref, keep_ref,
    x_ref, gain_ref, shard,
    u_ref, by_ref, before_ref, states_ref, mixed_ref, residual_ref, two_ref, gathered,
    window, conv, conv_low, rate, entry, carry, *links,
):
    step = pl.program_id(0)
    plane = PlaneReduce(*links[:8])
    line = LineGather(shard, gathered, *links[8:11])

    @pl.when(step == 0)
    def _():
        meet(True, "near")
        line.start()

    @pl.when(step > 0)
    def _():
        plane.pass_on(step - 1)

    value = forward_step(
        normed_ref, xw_ref, yw_ref, ow_ref, taps_ref, vec_ref, wr_ref, we_ref, keep_ref,
        u_ref, by_ref, before_ref, states_ref, mixed_ref,
        window, conv, conv_low, rate, entry, carry,
    )
    plane.put(step, value)

    @pl.when(step == 6)
    def _():
        line.forward()

    @pl.when(step == PLANE - 1)
    def _():
        plane.pass_on(step)
        plane.arrive()

        def make(i, unused):
            at = pl.ds(pl.multiple_of(i * CHUNK, CHUNK), CHUNK)
            residual = x_ref[at, :].astype(jnp.float32) + plane.total(at)
            residual_ref[at, :] = residual
            two_ref[at, :] = norm_rows(residual, gain_ref[...]).astype(jnp.bfloat16)
            return unused

        lax.fori_loop(0, x_ref.shape[0] // CHUNK, make, 0)
        plane.finish()
        line.finish()


def forward_linked(normed, xw, yw, ow, taps, vec, wr, we, keep, layer_in, gain, shard):
    length, width = normed.shape
    chans = xw.shape[1]
    rows = length // PLANE
    tile = lambda columns: pl.BlockSpec((rows, columns), lambda i: (i, 0))
    return pl.pallas_call(
        forward_linked_body,
        grid=(PLANE,),
        in_specs=[
            tile(width), whole(xw.shape), whole(yw.shape), whole(ow.shape), whole(taps.shape),
            whole(vec.shape), whole(wr.shape), whole(we.shape), tile(keep.shape[1]),
            whole(layer_in.shape), whole(gain.shape), ANYWHERE,
        ],
        out_specs=[tile(chans)] * 5 + [whole((rows, width))] * 2 + [ANYWHERE],
        out_shape=[
            jax.ShapeDtypeStruct((length, chans), jnp.bfloat16),
            jax.ShapeDtypeStruct((length, chans), jnp.float32),
            jax.ShapeDtypeStruct((length, chans), jnp.float32),
            jax.ShapeDtypeStruct((length, chans), jnp.bfloat16),
            jax.ShapeDtypeStruct((length, chans), jnp.bfloat16),
            jax.ShapeDtypeStruct((rows, width), jnp.float32),
            jax.ShapeDtypeStruct((rows, width), jnp.bfloat16),
            jax.ShapeDtypeStruct((LINE,) + shard.shape, shard.dtype),
        ],
        scratch_shapes=[
            pltpu.VMEM((rows + 8, chans), jnp.float32),
            pltpu.VMEM((rows, chans), jnp.float32),
            pltpu.VMEM((rows, chans), jnp.bfloat16),
            pltpu.VMEM((rows, chans), jnp.float32),
            pltpu.VMEM((rows, chans), jnp.float32),
            pltpu.VMEM((8, chans), jnp.float32),
            *PlaneReduce.buffers(rows, width),
            *PlaneReduce.semaphores,
            *LineGather.semaphores,
        ],
        compiler_params=pltpu.CompilerParams(
            collective_id=1, has_side_effects=True, vmem_limit_bytes=56 * 2**20
        ),
        name="mixer_forward_linked",
    )(normed, xw, yw, ow, taps, vec, wr, we, keep, layer_in, gain, shard)


def spread_body(block, shard, full, gathered, *semaphores):
    plane = PlaneGather(block, full, *semaphores[:3])
    line = LineGather(shard, gathered, *semaphores[3:6])
    meet(True, "near")
    line.start()
    plane.start()
    plane.relay(0)
    plane.relay(1)
    plane.rest()
    line.forward()
    plane.end()
    line.finish()


def spread(block, shard, place):
    return pl.pallas_call(
        spread_body,
        in_specs=[ANYWHERE] * 2,
        out_specs=[ANYWHERE] * 2,
        out_shape=[
            jax.ShapeDtypeStruct((PLANE,) + block.shape, block.dtype),
            jax.ShapeDtypeStruct((LINE,) + shard.shape, shard.dtype),
        ],
        scratch_shapes=[*PlaneGather.semaphores, *LineGather.semaphores],
        compiler_params=pltpu.CompilerParams(collective_id=place, has_side_effects=True),
        name="spread",
    )(block, shard)


def ffn_up_body(
    two_ref, gate_ref, up_ref, cot, shard,
    gates_ref, ups_ref, hidden_ref, full, gathered, *semaphores,
):
    step = pl.program_id(0)
    plane = PlaneGather(cot, full, *semaphores[:3])
    line = LineGather(shard, gathered, *semaphores[3:6])

    @pl.when(step == 0)
    def _():
        meet(True, "near")
        line.start()
        plane.start()

    @pl.when(step == 3)
    def _():
        plane.relay(0)

    @pl.when(step == 5)
    def _():
        plane.relay(1)

    gates = dot_plain(two_ref[...], gate_ref[...])
    ups = dot_plain(two_ref[...], up_ref[...])
    gates_ref[...] = gates
    ups_ref[...] = ups
    rows = gates_ref.shape[0]

    def make(i, unused):
        at = pl.ds(pl.multiple_of(i * CHUNK, CHUNK), CHUNK)
        hidden_ref[at, :] = (gelu_only(gates_ref[at, :]) * ups_ref[at, :]).astype(jnp.bfloat16)
        return unused

    lax.fori_loop(0, rows // CHUNK, make, 0)

    @pl.when(step == PLANE - 1)
    def _():
        plane.rest()
        line.forward()
        plane.end()
        line.finish()


def ffn_up(two, gate, up, cot, shard):
    length, width = two.shape
    units = gate.shape[1]
    rows = length // PLANE
    tile = lambda columns: pl.BlockSpec((rows, columns), lambda i: (i, 0))
    return pl.pallas_call(
        ffn_up_body,
        grid=(PLANE,),
        in_specs=[tile(width), whole(gate.shape), whole(up.shape), ANYWHERE, ANYWHERE],
        out_specs=[tile(units)] * 3 + [ANYWHERE] * 2,
        out_shape=[
            jax.ShapeDtypeStruct((length, units), jnp.float32),
            jax.ShapeDtypeStruct((length, units), jnp.float32),
            jax.ShapeDtypeStruct((length, units), jnp.bfloat16),
            jax.ShapeDtypeStruct((PLANE,) + cot.shape, cot.dtype),
            jax.ShapeDtypeStruct((LINE,) + shard.shape, shard.dtype),
        ],
        scratch_shapes=[*PlaneGather.semaphores, *LineGather.semaphores],
        compiler_params=pltpu.CompilerParams(
            collective_id=3, has_side_effects=True, vmem_limit_bytes=40 * 2**20
        ),
        name="ffn_up",
    )(two, gate, up, cot, shard)


def mixer_params(
    conv_weight, conv_bias, rate_weight, rate_bias, entry_weight, entry_bias, decay_param, chans
):
    used = conv_bias.shape[0]
    spare = (0, chans - used)
    decay_wide = jnp.pad(decay_param, spare, constant_values=2.0)
    blank = jnp.zeros((chans,), jnp.float32)
    vec = jnp.stack(
        [
            jnp.pad(conv_bias, spare),
            jnp.pad(rate_bias, spare),
            jnp.pad(entry_bias, spare),
            -8.0 * jax.nn.softplus(-decay_wide),
            blank,
            blank,
            blank,
            blank,
        ]
    )
    taps = jnp.pad(conv_weight, ((0, 0), spare))
    return taps, vec, block_diagonal(rate_weight, chans), block_diagonal(entry_weight, chans)


def shards(
    layer_in,
    cotangent,
    mix_gain,
    ffn_gain,
    x_weight,
    y_weight,
    out_weight,
    conv_weight,
    conv_bias,
    rate_weight,
    rate_bias,
    entry_weight,
    entry_bias,
    decay_param,
    gate_weight,
    up_weight,
    down_weight,
    resets,
):
    heads, head_width = rate_weight.shape[:2]
    used = conv_bias.shape[0]
    chans = -(-used // 128) * 128
    widen = lambda values: jnp.pad(values, ((0, 0), (0, chans - used)))
    mix_full = gather(mix_gain, ("row", "head"), 0)
    ffn_full = gather(ffn_gain, ("row", "head"), 0)
    x_rows = gather(widen(x_weight), "row", 0)
    y_rows = gather(widen(y_weight), "row", 0)
    out_rows = gather(widen(out_weight), "row", 0)
    gate_rows = gather(gate_weight, "row", 0)
    up_rows = gather(up_weight, "row", 0)
    down_rows = gather(down_weight, "row", 0)

    taps, vec, wr, we = mixer_params(
        conv_weight, conv_bias, rate_weight, rate_bias, entry_weight, entry_bias, decay_param, chans
    )
    keep = keep_columns(resets)

    inputs = layer_in.astype(jnp.float32)
    normed_f, norm_back_one = jax.vjp(norm_apply, inputs, mix_full.astype(jnp.float32))
    normed_group = gather(normed_f.astype(jnp.bfloat16), "head", 0)
    u, by, before, states, mixed, part = mixer_forward(
        normed_group, x_rows, y_rows, out_rows, taps, vec, wr, we, keep, ROWS
    )
    residual = inputs + scatter(part, "head", 0).astype(jnp.float32)
    normed_two_f, norm_back_two = jax.vjp(norm_apply, residual, ffn_full.astype(jnp.float32))
    cot_group = gather(cotangent, "head", 0)
    two_group = gather(normed_two_f.astype(jnp.bfloat16), "head", 0)
    gates = dot_plain(two_group, gate_rows)
    ups = dot_plain(two_group, up_rows)
    activated, slope = gelu_both(gates)
    hidden = (activated * ups).astype(jnp.bfloat16)
    ffn_part = contract_last(hidden, down_rows).astype(jnp.bfloat16)
    d_hidden = dot_plain(cot_group, down_rows)
    d_gates = (d_hidden * ups * slope).astype(jnp.bfloat16)
    d_ups = (d_hidden * activated).astype(jnp.bfloat16)
    d_two_part = (contract_last(d_gates, gate_rows) + contract_last(d_ups, up_rows)).astype(
        jnp.bfloat16
    )
    gate_grad = scatter(contract_first(two_group, d_gates).astype(jnp.bfloat16), "row", 0)
    up_grad = scatter(contract_first(two_group, d_ups).astype(jnp.bfloat16), "row", 0)
    down_grad = scatter(contract_first(cot_group, hidden).astype(jnp.bfloat16), "row", 0)
    layer_out = (residual + scatter(ffn_part, "head", 0).astype(jnp.float32)).astype(jnp.bfloat16)
    d_two = scatter(d_two_part, "head", 0).astype(jnp.float32)
    d_resid_norm, d_ffn_gain = norm_back_two(d_two)
    d_residual = cotangent.astype(jnp.float32) + d_resid_norm
    d_res_group = gather(d_residual.astype(jnp.bfloat16), "head", 0)
    d_bx, d_by, d_part, d_taps, d_vec, d_wr, d_we = mixer_backward(
        d_res_group, x_rows, y_rows, out_rows, taps, vec, wr, we, keep, u, by, before, states, ROWS
    )
    out_grad = scatter(contract_first(d_res_group, mixed).astype(jnp.bfloat16), "row", 0)
    x_grad = scatter(contract_first(normed_group, d_bx).astype(jnp.bfloat16), "row", 0)
    y_grad = scatter(contract_first(normed_group, d_by).astype(jnp.bfloat16), "row", 0)
    d_normed = scatter(d_part, "head", 0).astype(jnp.float32)
    d_inputs, d_mix_gain = norm_back_one(d_normed)
    layer_in_grad = (d_inputs + d_residual).astype(jnp.bfloat16)

    small = [
        d_taps[:, :used],
        d_vec[0, :used],
        diagonal_blocks(d_wr, heads, head_width),
        d_vec[1, :used],
        diagonal_blocks(d_we, heads, head_width),
        d_vec[2, :used],
        d_vec[3, :used] * (8.0 * jax.nn.sigmoid(-decay_param)),
    ]
    small = [lax.psum(item.astype(jnp.bfloat16), "row").astype(jnp.float32) for item in small]
    mix_part = scatter(d_mix_gain, ("row", "head"), 0)
    ffn_part_grad = scatter(d_ffn_gain, ("row", "head"), 0)
    wide = lambda values: values[:, :used].astype(jnp.float32)
    return (
        layer_out,
        layer_in_grad,
        mix_part,
        ffn_part_grad,
        wide(x_grad),
        wide(y_grad),
        wide(out_grad),
        *small,
        gate_grad.astype(jnp.float32),
        up_grad.astype(jnp.float32),
        down_grad.astype(jnp.float32),
    )

def shards_linked(
    layer_in,
    cotangent,
    mix_gain,
    ffn_gain,
    x_weight,
    y_weight,
    out_weight,
    conv_weight,
    conv_bias,
    rate_weight,
    rate_bias,
    entry_weight,
    entry_bias,
    decay_param,
    gate_weight,
    up_weight,
    down_weight,
    resets,
):
    heads, head_width = rate_weight.shape[:2]
    used = conv_bias.shape[0]
    chans = -(-used // 128) * 128
    widen = lambda values: jnp.pad(values, ((0, 0), (0, chans - used)))
    flat = lambda values: values.reshape((-1, values.shape[-1]))
    taps, vec, wr, we = mixer_params(
        conv_weight, conv_bias, rate_weight, rate_bias, entry_weight, entry_bias, decay_param, chans
    )
    keep = keep_columns(resets)
    own_gains = jnp.concatenate([mix_gain, ffn_gain]).astype(jnp.float32)
    tile = jnp.broadcast_to(own_gains, (8, own_gains.shape[0]))

    normed_group, x_rows, y_rows, out_rows, gains = open_block(
        layer_in, tile, (widen(x_weight), widen(y_weight), widen(out_weight))
    )
    normed_group, x_rows, y_rows, out_rows = map(flat, (normed_group, x_rows, y_rows, out_rows))
    u, by, before, states, mixed, residual, normed_two, gate_rows = forward_linked(
        normed_group, x_rows, y_rows, out_rows, taps, vec, wr, we, keep, layer_in, gains[1:2],
        gate_weight,
    )
    two_group, up_rows = spread(normed_two, up_weight, 2)
    gate_rows, two_group, up_rows = map(flat, (gate_rows, two_group, up_rows))
    gates, ups, hidden, cot_group, down_rows = ffn_up(
        two_group, gate_rows, up_rows, cotangent, down_weight
    )
    cot_group, down_rows = map(flat, (cot_group, down_rows))

    inputs = layer_in.astype(jnp.float32)
    normed_f, norm_back_one = jax.vjp(norm_apply, inputs, gains[0])
    normed_two_f, norm_back_two = jax.vjp(norm_apply, residual, gains[1])
    activated, slope = gelu_both(gates)
    ffn_part = contract_last(hidden, down_rows).astype(jnp.bfloat16)
    d_hidden = dot_plain(cot_group, down_rows)
    d_gates = (d_hidden * ups * slope).astype(jnp.bfloat16)
    d_ups = (d_hidden * activated).astype(jnp.bfloat16)
    d_two_part = (contract_last(d_gates, gate_rows) + contract_last(d_ups, up_rows)).astype(
        jnp.bfloat16
    )
    gate_grad = scatter(contract_first(two_group, d_gates).astype(jnp.bfloat16), "row", 0)
    up_grad = scatter(contract_first(two_group, d_ups).astype(jnp.bfloat16), "row", 0)
    down_grad = scatter(contract_first(cot_group, hidden).astype(jnp.bfloat16), "row", 0)
    layer_out = (residual + scatter(ffn_part, "head", 0).astype(jnp.float32)).astype(jnp.bfloat16)
    d_two = scatter(d_two_part, "head", 0).astype(jnp.float32)
    d_resid_norm, d_ffn_gain = norm_back_two(d_two)
    d_residual = cotangent.astype(jnp.float32) + d_resid_norm
    d_res_group = gather(d_residual.astype(jnp.bfloat16), "head", 0)
    d_bx, d_by, d_part, d_taps, d_vec, d_wr, d_we = mixer_backward(
        d_res_group, x_rows, y_rows, out_rows, taps, vec, wr, we, keep, u, by, before, states, ROWS
    )
    out_grad = scatter(contract_first(d_res_group, mixed).astype(jnp.bfloat16), "row", 0)
    x_grad = scatter(contract_first(normed_group, d_bx).astype(jnp.bfloat16), "row", 0)
    y_grad = scatter(contract_first(normed_group, d_by).astype(jnp.bfloat16), "row", 0)
    d_normed = scatter(d_part, "head", 0).astype(jnp.float32)
    d_inputs, d_mix_gain = norm_back_one(d_normed)
    layer_in_grad = (d_inputs + d_residual).astype(jnp.bfloat16)

    small = [
        d_taps[:, :used],
        d_vec[0, :used],
        diagonal_blocks(d_wr, heads, head_width),
        d_vec[1, :used],
        diagonal_blocks(d_we, heads, head_width),
        d_vec[2, :used],
        d_vec[3, :used] * (8.0 * jax.nn.sigmoid(-decay_param)),
    ]
    small = [lax.psum(item.astype(jnp.bfloat16), "row").astype(jnp.float32) for item in small]
    mix_part = scatter(d_mix_gain, ("row", "head"), 0)
    ffn_part_grad = scatter(d_ffn_gain, ("row", "head"), 0)
    wide = lambda values: values[:, :used].astype(jnp.float32)
    return (
        layer_out,
        layer_in_grad,
        mix_part,
        ffn_part_grad,
        wide(x_grad),
        wide(y_grad),
        wide(out_grad),
        *small,
        gate_grad.astype(jnp.float32),
        up_grad.astype(jnp.float32),
        down_grad.astype(jnp.float32),
    )


def solution(mesh):
    linked = mesh.shape["row"] == LINE and mesh.shape["head"] == PLANE
    return jax.shard_map(
        shards_linked if linked else shards,
        mesh=mesh,
        in_specs=(
            P(("row", "head"), None),
            P(("row", "head"), None),
            P(("row", "head")),
            P(("row", "head")),
            P("row", "head"),
            P("row", "head"),
            P("row", "head"),
            P(None, "head"),
            P("head"),
            P("head", None, None),
            P("head"),
            P("head", None, None),
            P("head"),
            P("head"),
            P("row", "head"),
            P("row", "head"),
            P("row", "head"),
            P("row", None),
        ),
        out_specs=(
            P(("row", "head"), None),
            P(("row", "head"), None),
            P(("row", "head")),
            P(("row", "head")),
            P("row", "head"),
            P("row", "head"),
            P("row", "head"),
            P(None, "head"),
            P("head"),
            P("head", None, None),
            P("head"),
            P("head", None, None),
            P("head"),
            P("head"),
            P("row", "head"),
            P("row", "head"),
            P("row", "head"),
        ),
        check_vma=False,
    )
```

```python
import jax
import jax.numpy as jnp
from jax import lax
from jax.experimental import pallas as pl
from jax.experimental.pallas import tpu as pltpu
from jax.sharding import PartitionSpec as P

EPSILON = 1e-06
ROWS = 256
GELU_A = 0.7978845608028654
GELU_B = 0.044715
CHUNK = 16


def gelu_only(x):
    return 0.5 * x * (1.0 + jnp.tanh(GELU_A * (x + GELU_B * x * x * x)))


def gelu_both(x):
    square = x * x
    bent = jnp.tanh(GELU_A * x * (1.0 + GELU_B * square))
    half = 0.5 * (1.0 + bent)
    slope = half + 0.5 * x * (1.0 - bent * bent) * (GELU_A * (1.0 + 3.0 * GELU_B * square))
    return x * half, slope


def one_minus_exp(x, exp_x):
    series = 1.0 + x * (1.0 / 7.0)
    for order in (6.0, 5.0, 4.0, 3.0, 2.0):
        series = 1.0 + x * (1.0 / order) * series
    return jnp.where(x > -0.25, -x * series, 1.0 - exp_x)


def dot_plain(left, right):
    return jnp.dot(left, right, preferred_element_type=jnp.float32)


def contract_last(left, right):
    return lax.dot_general(
        left, right, (((1,), (1,)), ((), ())), preferred_element_type=jnp.float32
    )


def contract_first(left, right):
    return lax.dot_general(
        left, right, (((0,), (0,)), ((), ())), preferred_element_type=jnp.float32
    )


def conv_rows(window, keep, taps, shift):
    rows = window.shape[0] - 8
    total = taps[0:1] * window[8:] + shift
    for offset in range(1, 4):
        total = total + taps[offset : offset + 1] * (
            keep[:, offset : offset + 1] * window[8 - offset : 8 - offset + rows]
        )
    return total


def scan_down(decays, driven, carry):
    rows = decays.shape[0]
    place = lax.broadcasted_iota(jnp.int32, decays.shape, 0)
    step = 1
    while step < rows:
        inside = place >= step
        driven = jnp.where(inside, decays * pltpu.roll(driven, step, 0) + driven, driven)
        decays = jnp.where(inside, decays * pltpu.roll(decays, step, 0), decays)
        step *= 2
    return decays * carry + driven


def scan_up(decays, driven, carry):
    rows = decays.shape[0]
    place = lax.broadcasted_iota(jnp.int32, decays.shape, 0)
    step = 1
    while step < rows:
        inside = place < rows - step
        driven = jnp.where(inside, decays * pltpu.roll(driven, rows - step, 0) + driven, driven)
        decays = jnp.where(inside, decays * pltpu.roll(decays, rows - step, 0), decays)
        step *= 2
    return decays * carry + driven


def forward_step(
    normed_ref, xw_ref, yw_ref, ow_ref, taps_ref, vec_ref, wr_ref, we_ref, keep_ref,
    u_ref, by_ref, before_ref, states_ref, mixed_ref,
    window, conv, conv_low, rate, entry, carry,
):
    rows = normed_ref.shape[0]

    @pl.when(pl.program_id(0) == 0)
    def _():
        window[0:8, :] = jnp.zeros_like(window[0:8, :])
        carry[...] = jnp.zeros_like(carry)

    branch_x = dot_plain(normed_ref[...], xw_ref[...]).astype(jnp.bfloat16)
    u_ref[...] = branch_x
    window[pl.ds(8, rows), :] = branch_x.astype(jnp.float32)
    by_ref[...] = dot_plain(normed_ref[...], yw_ref[...])

    def conv_step(j, unused):
        at = pl.multiple_of(j * CHUNK, CHUNK)
        made = conv_rows(
            window[pl.ds(at, CHUNK + 8), :], keep_ref[pl.ds(at, CHUNK), :],
            taps_ref[...], vec_ref[0:1, :],
        )
        conv[pl.ds(at, CHUNK), :] = made
        conv_low[pl.ds(at, CHUNK), :] = made.astype(jnp.bfloat16)
        return unused

    lax.fori_loop(0, rows // CHUNK, conv_step, 0)
    window[0:8, :] = window[pl.ds(rows, 8), :]
    rate[...] = dot_plain(conv_low[...], wr_ref[...]) + vec_ref[1:2, :]
    entry[...] = dot_plain(conv_low[...], we_ref[...]) + vec_ref[2:3, :]

    def scan_step(j, before):
        at = pl.multiple_of(j * CHUNK, CHUNK)
        here = pl.ds(at, CHUNK)
        carried = keep_ref[here, 0:1]
        log_decay = jax.nn.sigmoid(rate[here, :]) * vec_ref[3:4, :]
        exp_decay = jnp.exp(log_decay)
        drop = jnp.sqrt(one_minus_exp(2.0 * log_decay, exp_decay * exp_decay))
        scaling = (1.0 - carried) + carried * drop
        driven = scaling * jax.nn.sigmoid(entry[here, :]) * conv[here, :]
        states = scan_down(exp_decay * carried, driven, before)
        first = lax.broadcasted_iota(jnp.int32, states.shape, 0) == 0
        before_ref[here, :] = jnp.where(first, before, pltpu.roll(states, 1, 0))
        states_low = states.astype(jnp.bfloat16)
        states_ref[here, :] = states_low
        mixed_ref[here, :] = (
            states_low.astype(jnp.float32) * gelu_only(by_ref[here, :])
        ).astype(jnp.bfloat16)
        return states[CHUNK - 1 : CHUNK, :]

    carry[0:1, :] = lax.fori_loop(0, rows // CHUNK, scan_step, carry[0:1, :])
    return contract_last(mixed_ref[...], ow_ref[...]).astype(jnp.bfloat16)


def forward_body(
    normed_ref, xw_ref, yw_ref, ow_ref, taps_ref, vec_ref, wr_ref, we_ref, keep_ref,
    u_ref, by_ref, before_ref, states_ref, mixed_ref, part_ref, *scratch,
):
    part_ref[...] = forward_step(
        normed_ref, xw_ref, yw_ref, ow_ref, taps_ref, vec_ref, wr_ref, we_ref, keep_ref,
        u_ref, by_ref, before_ref, states_ref, mixed_ref, *scratch,
    )


def backward_step(
    d_res_ref, xw_ref, yw_ref, ow_ref, taps_ref, vec_ref, wr_ref, we_ref, keep_ref,
    u_ref, u_prev_ref, by_ref, before_ref, states_ref,
    d_bx_ref, d_by_ref, taps_out, vec_out, wr_out, we_out,
    window, conv, conv_low, rate, entry, d_mixed, d_conv, g_rate, g_entry, carry, sums,
):
    rows = d_res_ref.shape[0]
    step_id = pl.program_id(0)

    @pl.when(step_id == 0)
    def _():
        d_conv[pl.ds(rows, 8), :] = jnp.zeros_like(d_conv[pl.ds(rows, 8), :])
        carry[...] = jnp.zeros_like(carry)
        sums[...] = jnp.zeros_like(sums)
        wr_out[...] = jnp.zeros_like(wr_out)
        we_out[...] = jnp.zeros_like(we_out)

    @pl.when(step_id > 0)
    def _():
        d_conv[pl.ds(rows, 8), :] = d_conv[0:8, :]

    d_mixed[...] = dot_plain(d_res_ref[...], ow_ref[...])
    window[0:8, :] = u_prev_ref[8:16, :].astype(jnp.float32)
    window[pl.ds(8, rows), :] = u_ref[...].astype(jnp.float32)

    def conv_step(j, unused):
        at = pl.multiple_of(j * CHUNK, CHUNK)
        made = conv_rows(
            window[pl.ds(at, CHUNK + 8), :], keep_ref[pl.ds(at, CHUNK), :],
            taps_ref[...], vec_ref[0:1, :],
        )
        conv[pl.ds(at, CHUNK), :] = made
        conv_low[pl.ds(at, CHUNK), :] = made.astype(jnp.bfloat16)
        return unused

    lax.fori_loop(0, rows // CHUNK, conv_step, 0)
    rate[...] = dot_plain(conv_low[...], wr_ref[...]) + vec_ref[1:2, :]
    entry[...] = dot_plain(conv_low[...], we_ref[...]) + vec_ref[2:3, :]

    def fold(value):
        return value[0:8, :] + value[8:16, :]

    def scan_step(j, after):
        at = pl.multiple_of(rows - CHUNK - j * CHUNK, CHUNK)
        here = pl.ds(at, CHUNK)
        carried = keep_ref[here, 0:1]
        rate_gate = jax.nn.sigmoid(rate[here, :])
        entry_gate = jax.nn.sigmoid(entry[here, :])
        log_decay = rate_gate * vec_ref[3:4, :]
        exp_decay = jnp.exp(log_decay)
        exp_twice = exp_decay * exp_decay
        drop = jnp.sqrt(one_minus_exp(2.0 * log_decay, exp_twice))
        scaling = (1.0 - carried) + carried * drop
        decays = exp_decay * carried
        gelu_y, slope_y = gelu_both(by_ref[here, :])
        through = d_mixed[here, :]
        d_states = (through * gelu_y).astype(jnp.bfloat16).astype(jnp.float32)
        d_by_ref[here, :] = (
            through * states_ref[here, :].astype(jnp.float32) * slope_y
        ).astype(jnp.bfloat16)
        passed = scan_up(decays, decays * d_states, after)
        last = lax.broadcasted_iota(jnp.int32, passed.shape, 0) == CHUNK - 1
        adjoint = d_states + jnp.where(last, after, pltpu.roll(passed, CHUNK - 1, 0))
        convolved = conv[here, :]
        gated = adjoint * entry_gate
        g_log = adjoint * before_ref[here, :] * decays - gated * convolved * (
            carried * (exp_twice / drop)
        )
        g_pre_rate = g_log * vec_ref[3:4, :] * (rate_gate * (1.0 - rate_gate))
        direct = gated * scaling
        g_pre_entry = direct * convolved * (1.0 - entry_gate)
        d_conv[here, :] = direct
        g_rate[here, :] = g_pre_rate.astype(jnp.bfloat16)
        g_entry[here, :] = g_pre_entry.astype(jnp.bfloat16)
        sums[8:16, :] += fold(g_pre_rate)
        sums[16:24, :] += fold(g_pre_entry)
        sums[24:32, :] += fold(g_log * rate_gate)
        return passed[0:1, :]

    carry[0:1, :] = lax.fori_loop(0, rows // CHUNK, scan_step, carry[0:1, :])
    wr_out[...] += contract_first(conv_low[...], g_rate[...])
    we_out[...] += contract_first(conv_low[...], g_entry[...])
    d_conv[0:rows, :] += contract_last(g_rate[...], wr_ref[...]) + contract_last(
        g_entry[...], we_ref[...]
    )

    def back_step(j, unused):
        at = pl.multiple_of(j * CHUNK, CHUNK)
        here = pl.ds(at, CHUNK)
        keep = keep_ref[here, :]
        ahead = d_conv[pl.ds(at, CHUNK + 8), :]
        behind = window[pl.ds(at, CHUNK + 8), :]
        now = ahead[0:CHUNK]
        total = taps_ref[0:1, :] * now
        sums[0:8, :] += fold(now)
        sums[32:40, :] += fold(now * behind[8:])
        for offset in range(1, 4):
            total = total + taps_ref[offset : offset + 1, :] * (
                keep[:, 3 + offset : 4 + offset] * ahead[offset : offset + CHUNK]
            )
            base = 32 + 8 * offset
            sums[base : base + 8, :] += fold(
                now * (keep[:, offset : offset + 1] * behind[8 - offset : 8 - offset + CHUNK])
            )
        d_bx_ref[here, :] = total.astype(jnp.bfloat16)
        return unused

    lax.fori_loop(0, rows // CHUNK, back_step, 0)

    @pl.when(step_id == pl.num_programs(0) - 1)
    def _():
        vec_out[...] = jnp.zeros_like(vec_out)
        for place in range(4):
            vec_out[place : place + 1, :] = jnp.sum(
                sums[8 * place : 8 * place + 8, :], axis=0, keepdims=True
            )
            taps_out[place : place + 1, :] = jnp.sum(
                sums[32 + 8 * place : 40 + 8 * place, :], axis=0, keepdims=True
            )

    return (
        contract_last(d_bx_ref[...], xw_ref[...]) + contract_last(d_by_ref[...], yw_ref[...])
    ).astype(jnp.bfloat16)


def backward_body(
    d_res_ref, xw_ref, yw_ref, ow_ref, taps_ref, vec_ref, wr_ref, we_ref, keep_ref,
    u_ref, u_prev_ref, by_ref, before_ref, states_ref,
    d_bx_ref, d_by_ref, part_ref, *rest,
):
    part_ref[...] = backward_step(
        d_res_ref, xw_ref, yw_ref, ow_ref, taps_ref, vec_ref, wr_ref, we_ref, keep_ref,
        u_ref, u_prev_ref, by_ref, before_ref, states_ref, d_bx_ref, d_by_ref, *rest,
    )


def whole(shape):
    return pl.BlockSpec(shape, lambda i: (0,) * len(shape))


def mixer_forward(normed, xw, yw, ow, taps, vec, wr, we, keep, rows):
    length, width = normed.shape
    chans = xw.shape[1]
    tile = lambda columns: pl.BlockSpec((rows, columns), lambda i: (i, 0))
    return pl.pallas_call(
        forward_body,
        grid=(length // rows,),
        in_specs=[
            tile(width), whole(xw.shape), whole(yw.shape), whole(ow.shape), whole(taps.shape),
            whole(vec.shape), whole(wr.shape), whole(we.shape), tile(keep.shape[1]),
        ],
        out_specs=[tile(chans)] * 5 + [tile(width)],
        out_shape=[
            jax.ShapeDtypeStruct((length, chans), jnp.bfloat16),
            jax.ShapeDtypeStruct((length, chans), jnp.float32),
            jax.ShapeDtypeStruct((length, chans), jnp.float32),
            jax.ShapeDtypeStruct((length, chans), jnp.bfloat16),
            jax.ShapeDtypeStruct((length, chans), jnp.bfloat16),
            jax.ShapeDtypeStruct((length, width), jnp.bfloat16),
        ],
        scratch_shapes=[
            pltpu.VMEM((rows + 8, chans), jnp.float32),
            pltpu.VMEM((rows, chans), jnp.float32),
            pltpu.VMEM((rows, chans), jnp.bfloat16),
            pltpu.VMEM((rows, chans), jnp.float32),
            pltpu.VMEM((rows, chans), jnp.float32),
            pltpu.VMEM((8, chans), jnp.float32),
        ],
        compiler_params=pltpu.CompilerParams(vmem_limit_bytes=48 * 2**20),
        cost_estimate=pl.CostEstimate(
            flops=6 * length * width * chans,
            bytes_accessed=4 * length * width + 30 * length * chans,
            transcendentals=6 * length * chans,
        ),
        name="mixer_forward",
    )(normed, xw, yw, ow, taps, vec, wr, we, keep)


def mixer_backward(d_res, xw, yw, ow, taps, vec, wr, we, keep, u, by, before, states, rows):
    length, width = d_res.shape
    chans = xw.shape[1]
    blocks = length // rows
    tile = lambda columns: pl.BlockSpec((rows, columns), lambda i: (blocks - 1 - i, 0))
    ahead = pl.BlockSpec(
        (16, chans), lambda i: (jnp.maximum((blocks - 1 - i) * (rows // 16) - 1, 0), 0)
    )
    return pl.pallas_call(
        backward_body,
        grid=(blocks,),
        in_specs=[
            tile(width), whole(xw.shape), whole(yw.shape), whole(ow.shape), whole(taps.shape),
            whole(vec.shape), whole(wr.shape), whole(we.shape), tile(keep.shape[1]),
            tile(chans), ahead, tile(chans), tile(chans), tile(chans),
        ],
        out_specs=[
            tile(chans), tile(chans), tile(width), whole(taps.shape), whole(vec.shape),
            whole(wr.shape), whole(we.shape),
        ],
        out_shape=[
            jax.ShapeDtypeStruct((length, chans), jnp.bfloat16),
            jax.ShapeDtypeStruct((length, chans), jnp.bfloat16),
            jax.ShapeDtypeStruct((length, width), jnp.bfloat16),
            jax.ShapeDtypeStruct(taps.shape, jnp.float32),
            jax.ShapeDtypeStruct(vec.shape, jnp.float32),
            jax.ShapeDtypeStruct(wr.shape, jnp.float32),
            jax.ShapeDtypeStruct(we.shape, jnp.float32),
        ],
        scratch_shapes=[
            pltpu.VMEM((rows + 8, chans), jnp.float32),
            pltpu.VMEM((rows, chans), jnp.float32),
            pltpu.VMEM((rows, chans), jnp.bfloat16),
            pltpu.VMEM((rows, chans), jnp.float32),
            pltpu.VMEM((rows, chans), jnp.float32),
            pltpu.VMEM((rows, chans), jnp.float32),
            pltpu.VMEM((rows + 8, chans), jnp.float32),
            pltpu.VMEM((rows, chans), jnp.bfloat16),
            pltpu.VMEM((rows, chans), jnp.bfloat16),
            pltpu.VMEM((8, chans), jnp.float32),
            pltpu.VMEM((64, chans), jnp.float32),
        ],
        compiler_params=pltpu.CompilerParams(vmem_limit_bytes=48 * 2**20),
        cost_estimate=pl.CostEstimate(
            flops=6 * length * width * chans,
            bytes_accessed=4 * length * width + 30 * length * chans,
            transcendentals=6 * length * chans,
        ),
        name="mixer_backward",
    )(d_res, xw, yw, ow, taps, vec, wr, we, keep, u, u, by, before, states)


def keep_columns(resets):
    length = resets.shape[1]
    position = lax.broadcasted_iota(jnp.int32, resets.shape, 1)
    starts = jnp.maximum(resets, (position == 0).astype(jnp.int32)).astype(jnp.float32)
    carried = (1.0 - starts).reshape(-1)
    seqs = resets.shape[0]

    def back(values, by):
        values = values.reshape(seqs, length)
        return jnp.pad(values, ((0, 0), (by, 0)))[:, :length].reshape(-1)

    def ahead(values, by):
        values = values.reshape(seqs, length)
        return jnp.pad(values, ((0, 0), (0, by)))[:, by:].reshape(-1)

    one = carried
    two = one * back(carried, 1)
    three = two * back(carried, 2)
    return jnp.stack(
        [carried, one, two, three, ahead(one, 1), ahead(two, 2), ahead(three, 3), carried], axis=1
    )


def block_diagonal(blocks, chans):
    heads, width, unused = blocks.shape
    rows = [
        jnp.pad(blocks[h], ((0, 0), (h * width, chans - (h + 1) * width))) for h in range(heads)
    ]
    full = jnp.concatenate(rows, axis=0)
    return jnp.pad(full, ((0, chans - heads * width), (0, 0)))


def diagonal_blocks(full, heads, width):
    return jnp.stack(
        [full[h * width : (h + 1) * width, h * width : (h + 1) * width] for h in range(heads)]
    )


MESH = pl.DeviceIdType.MESH
ANYWHERE = pl.BlockSpec(memory_space=pl.ANY)
IN_VMEM = pl.BlockSpec(memory_space=pltpu.VMEM)
LINE = 4
PLANE = 8
PIECES = 4


def send_to(src, dst, sent, arrived, axis, target):
    return pltpu.make_async_remote_copy(
        src_ref=src,
        dst_ref=dst,
        send_sem=sent,
        recv_sem=arrived,
        device_id={axis: target},
        device_id_type=MESH,
    )


def sibling_of(h):
    return h + 1 - 2 * lax.rem(h, 2)


def across_of(h):
    return h + 2 - 4 * lax.rem(lax.div(h, 2), 2)


def along_of(h):
    return lax.rem(h + 4, PLANE)


def meet(row_line, plane):
    r, h = lax.axis_index("row"), lax.axis_index("head")
    barrier = pltpu.get_barrier_semaphore()
    count = 0
    if row_line:
        for step in range(1, LINE):
            pl.semaphore_signal(
                barrier, inc=1, device_id={"row": lax.rem(r + step, LINE)}, device_id_type=MESH
            )
        count += LINE - 1
    if plane == "all":
        for step in range(1, PLANE):
            pl.semaphore_signal(
                barrier, inc=1, device_id={"head": lax.rem(h + step, PLANE)}, device_id_type=MESH
            )
        count += PLANE - 1
    if plane == "near":
        for target in (sibling_of(h), across_of(h), along_of(h), across_of(along_of(h))):
            pl.semaphore_signal(barrier, inc=1, device_id={"head": target}, device_id_type=MESH)
        count += 4
    pl.semaphore_wait(barrier, count)


class LineGather:
    semaphores = (
        pltpu.SemaphoreType.DMA((LINE,)),
        pltpu.SemaphoreType.DMA((LINE,)),
        pltpu.SemaphoreType.DMA((2,)),
    )

    def __init__(self, shard, full, sent, arrived, other):
        self.r = lax.axis_index("row")
        self.shard, self.full, self.sent, self.arrived, self.other = (
            shard, full, sent, arrived, other,
        )

    def near(self, t):
        gap = self.r - t
        return (gap != 0) & (gap < 3) & (gap > -3)

    def own(self, t):
        return send_to(
            self.shard, self.full.at[self.r], self.sent.at[t], self.arrived.at[self.r], "row", t
        )

    def handed(self, origin, target):
        return send_to(
            self.full.at[origin], self.full.at[origin], self.other.at[0], self.arrived.at[origin],
            "row", target,
        )

    def local(self):
        return pltpu.make_async_copy(self.shard, self.full.at[self.r], self.other.at[1])

    def start(self):
        for t in range(LINE):

            @pl.when(self.near(t))
            def _(t=t):
                self.own(t).start()

        self.local().start()

    def forward(self):
        for me, origin, target in ((2, 0, 3), (1, 3, 0)):

            @pl.when(self.r == me)
            def _(origin=origin, target=target):
                copy = self.handed(origin, target)
                copy.wait_recv()
                copy.start()

    def finish(self):
        r = self.r
        for t in range(LINE):
            known = (r == t) | ((r == 2) & (t == 0)) | ((r == 1) & (t == 3))

            @pl.when(jnp.logical_not(known))
            def _(t=t):
                self.handed(t, t).wait_recv()

            @pl.when(self.near(t))
            def _(t=t):
                self.own(t).wait_send()

        for me, origin, target in ((2, 0, 3), (1, 3, 0)):

            @pl.when(r == me)
            def _(origin=origin, target=target):
                self.handed(origin, target).wait_send()

        self.local().wait()


class LineReduce:
    semaphores = (
        pltpu.SemaphoreType.DMA((LINE,)),
        pltpu.SemaphoreType.DMA((LINE,)),
        pltpu.SemaphoreType.DMA((2,)),
    )

    @staticmethod
    def buffers(rows, width):
        return [
            pltpu.VMEM((LINE, rows, width), jnp.bfloat16),
            pltpu.VMEM((rows, width), jnp.bfloat16),
        ]

    def __init__(self, parts, landed, passed, sent, arrived, other):
        self.r = lax.axis_index("row")
        self.parts, self.landed, self.passed = parts, landed, passed
        self.sent, self.arrived, self.other = sent, arrived, other

    def to_pass(self, me, origin, via):
        return send_to(
            self.parts.at[origin], self.passed, self.sent.at[origin], self.other.at[0], "row", via
        )

    def direct(self, t):
        return send_to(
            self.parts.at[t], self.landed.at[self.r], self.sent.at[t], self.arrived.at[self.r],
            "row", t,
        )

    def added(self, t):
        return send_to(
            self.passed, self.landed.at[self.r], self.sent.at[t], self.arrived.at[self.r], "row", t
        )

    def plain(self, t):
        r = self.r
        ends = ((r == 0) & (t == 3)) | ((r == 3) & (t == 0))
        added = ((r == 1) & (t == 3)) | ((r == 2) & (t == 0))
        return jnp.logical_not(ends | added | (r == t))

    def start(self):
        for me, end, via in ((0, 3, 1), (3, 0, 2)):

            @pl.when(self.r == me)
            def _(me=me, end=end, via=via):
                self.to_pass(me, end, via).start()

        for t in range(LINE):

            @pl.when(self.plain(t))
            def _(t=t):
                self.direct(t).start()

    def forward(self):
        for me, end in ((1, 3), (2, 0)):

            @pl.when(self.r == me)
            def _(me=me, end=end):
                self.to_pass(me, end, end).wait_recv()
                rows = self.passed.shape[0]
                step = 64

                def add(i, unused):
                    at = pl.ds(pl.multiple_of(i * step, step), step)
                    self.passed[at, :] = (
                        self.parts[end, at, :].astype(jnp.float32)
                        + self.passed[at, :].astype(jnp.float32)
                    ).astype(jnp.bfloat16)
                    return unused

                lax.fori_loop(0, rows // step, add, 0)
                self.added(end).start()

    def finish(self, write):
        r = self.r
        for t in range(LINE):

            @pl.when(jnp.logical_not(unsent_to(r, t)))
            def _(t=t):
                send_to(
                    self.parts.at[t], self.landed.at[t], self.sent.at[t], self.arrived.at[t],
                    "row", t,
                ).wait_recv()

        def total_of(sources):
            step = 32

            def add(i, unused):
                at = pl.ds(pl.multiple_of(i * step, step), step)
                total = self.parts[r, at, :].astype(jnp.float32)
                for t in sources:
                    total = total + self.landed[t, at, :].astype(jnp.float32)
                write(at, total)
                return unused

            lax.fori_loop(0, self.passed.shape[0] // step, add, 0)

        at_end = (r == 0) | (r == 3)

        @pl.when(at_end)
        def _():
            total_of((1, 2))

        @pl.when(jnp.logical_not(at_end))
        def _():
            total_of((0, 3, 3 - r))

        for me, end, via in ((0, 3, 1), (3, 0, 2)):

            @pl.when(r == me)
            def _(me=me, end=end, via=via):
                self.to_pass(me, end, via).wait_send()

        for t in range(LINE):

            @pl.when(jnp.logical_not(unsent_to(r, t)))
            def _(t=t):
                self.direct(t).wait_send()


def unsent_to(r, t):
    return ((r == 0) & (t == 3)) | ((r == 3) & (t == 0)) | (r == t)


class PlaneGather:
    semaphores = (
        pltpu.SemaphoreType.DMA((PIECES, 7)),
        pltpu.SemaphoreType.DMA((PIECES, 7)),
        pltpu.SemaphoreType.DMA((1,)),
    )
    first = tuple(range(PIECES // 2))
    second = tuple(range(PIECES // 2, PIECES))

    def __init__(self, block, full, sent, arrived, other):
        h = lax.axis_index("head")
        self.h, self.side, self.x, self.y = h, sibling_of(h), across_of(h), along_of(h)
        self.far = across_of(self.y)
        self.block, self.full = block, full
        self.sent, self.arrived, self.other = sent, arrived, other
        self.rows = block.shape[0] // PIECES

    def piece(self, owner, c):
        return self.full.at[owner, pl.ds(c * self.rows, self.rows)]

    def own(self, c, lane, target):
        return send_to(
            self.block.at[pl.ds(c * self.rows, self.rows)], self.piece(self.h, c),
            self.sent.at[c, lane], self.arrived.at[c, lane], "head", target,
        )

    def hand(self, owner, c, lane, target):
        return send_to(
            self.piece(owner, c), self.piece(owner, c), self.sent.at[c, lane],
            self.arrived.at[c, lane], "head", target,
        )

    def local(self):
        return pltpu.make_async_copy(self.block, self.full.at[self.h], self.other.at[0])

    def start(self):
        for a, b in zip(self.first, self.second):
            self.own(a, 1, self.x).start()
            self.own(b, 2, self.y).start()
        for a, b in zip(self.first, self.second):
            self.own(b, 1, self.x).start()
            self.own(a, 2, self.y).start()
        for c in range(PIECES):
            self.own(c, 0, self.side).start()
        self.local().start()

    def relay(self, place):
        a, b = self.first[place], self.second[place]
        self.hand(self.x, a, 1, self.x).wait_recv()
        self.hand(self.x, a, 3, self.y).start()
        self.hand(self.x, a, 4, self.side).start()
        self.hand(self.y, b, 2, self.y).wait_recv()
        self.hand(self.y, b, 3, self.x).start()
        self.hand(self.y, b, 5, self.side).start()

    def rest(self):
        for a, b in zip(self.first, self.second):
            self.hand(self.x, b, 1, self.x).wait_recv()
            self.hand(self.x, b, 4, self.side).start()
            self.hand(self.y, a, 2, self.y).wait_recv()
            self.hand(self.y, a, 5, self.side).start()

    def end(self):
        for pair in zip(self.first, self.second):
            for c in pair:
                self.hand(self.far, c, 3, self.side).wait_recv()
                self.hand(self.far, c, 6, self.side).start()
        side = self.side
        for c in range(PIECES):
            for owner, lane in (
                (side, 0), (across_of(side), 4), (along_of(side), 5),
                (across_of(along_of(side)), 6),
            ):
                self.hand(owner, c, lane, side).wait_recv()
        for c in range(PIECES):
            for lane in range(7):
                self.own(c, lane, side).wait_send()
        self.local().wait()


class PlaneReduce:
    semaphores = (
        pltpu.SemaphoreType.DMA((4,)),
        pltpu.SemaphoreType.DMA((4,)),
        pltpu.SemaphoreType.DMA((4,)),
        pltpu.SemaphoreType.DMA((3,)),
    )

    @staticmethod
    def buffers(rows, width):
        return [
            pltpu.VMEM((4, rows, width), jnp.bfloat16),
            pltpu.VMEM((4, rows, width), jnp.bfloat16),
            pltpu.VMEM((4, rows, width), jnp.bfloat16),
            pltpu.VMEM((3, rows, width), jnp.bfloat16),
        ]

    def __init__(self, staged, beside, mine, landed, side_sent, side_arrived, sent, arrived):
        h = lax.axis_index("head")
        self.h, self.core, self.chip = h, lax.rem(h, 2), lax.div(h, 2)
        self.staged, self.beside, self.mine, self.landed = staged, beside, mine, landed
        self.side_sent, self.side_arrived = side_sent, side_arrived
        self.sent, self.arrived = sent, arrived

    def aside(self, chip):
        return send_to(
            self.staged.at[chip], self.beside.at[chip], self.side_sent.at[chip],
            self.side_arrived.at[chip], "head", sibling_of(self.h),
        )

    def place(self, chip):
        flip_x = lax.rem(chip + self.chip, 2)
        flip_y = lax.rem(lax.div(chip, 2) + lax.div(self.chip, 2), 2)
        return flip_x + 2 * flip_y - 1

    def across(self, chip):
        at = self.place(chip)
        return send_to(
            self.mine.at[chip], self.landed.at[at], self.sent.at[chip], self.arrived.at[at],
            "head", 2 * chip + self.core,
        )

    def put(self, block, value):
        chip, core = lax.div(block, 2), lax.rem(block, 2)

        @pl.when(core == self.core)
        def _():
            self.mine[chip] = value

        @pl.when(core != self.core)
        def _():
            self.staged[chip] = value
            self.aside(chip).start()

    def pass_on(self, block):
        chip, core = lax.div(block, 2), lax.rem(block, 2)

        @pl.when(core == self.core)
        def _():
            self.aside(chip).wait_recv()
            rows = self.mine.shape[1]
            step = 32

            def add(i, unused):
                at = pl.ds(pl.multiple_of(i * step, step), step)
                self.mine[chip, at, :] = (
                    self.mine[chip, at, :].astype(jnp.float32)
                    + self.beside[chip, at, :].astype(jnp.float32)
                ).astype(jnp.bfloat16)
                return unused

            lax.fori_loop(0, rows // step, add, 0)

            @pl.when(chip != self.chip)
            def _():
                self.across(chip).start()

    def arrive(self):
        for at in range(3):
            send_to(
                self.landed.at[at], self.landed.at[at], self.sent.at[0], self.arrived.at[at],
                "head", self.h,
            ).wait_recv()

    def total(self, at):
        value = self.mine[self.chip, at, :].astype(jnp.float32)
        for place in range(3):
            value = value + self.landed[place, at, :].astype(jnp.float32)
        return value

    def finish(self):
        for chip in range(4):
            self.aside(chip).wait_send()

            @pl.when(chip != self.chip)
            def _(chip=chip):
                self.across(chip).wait_send()


def norm_apply(rows, gain):
    return rows * lax.rsqrt(jnp.mean(rows * rows, axis=-1, keepdims=True) + EPSILON) * gain


def gather(values, axis_name, axis):
    return lax.all_gather(values, axis_name, axis=axis, tiled=True)


def scatter(values, axis_name, axis):
    return lax.psum_scatter(values, axis_name, scatter_dimension=axis, tiled=True)

def norm_rows(rows, gain):
    return rows * lax.rsqrt(jnp.mean(rows * rows, axis=-1, keepdims=True) + EPSILON) * gain


def open_body(
    x_ref, tile_ref, xs, ys, zs, full, xf, yf, zf, gains_ref,
    normed, column, spread, gain_sent, gain_arrived, wide_sent, wide_arrived, *semaphores,
):
    r, h = lax.axis_index("row"), lax.axis_index("head")
    lines = [
        LineGather(src, dst, *semaphores[3 * k : 3 * k + 3])
        for k, (src, dst) in enumerate(((xs, xf), (ys, yf), (zs, zf)))
    ]
    plane = PlaneGather(normed, full, *semaphores[9:12])
    meet(True, "all")

    def up_line(t):
        return send_to(
            column.at[r], column.at[r], gain_sent.at[t], gain_arrived.at[r], "row", t
        )

    def from_line(t):
        return send_to(
            column.at[t], column.at[t], gain_sent.at[t], gain_arrived.at[t], "row", t
        )

    def over_plane(step, owner):
        return send_to(
            column, spread.at[owner], wide_sent.at[step], wide_arrived.at[owner], "head",
            lax.rem(h + step, PLANE),
        )

    column[r] = tile_ref[...]
    for step in range(1, LINE):
        up_line(lax.rem(r + step, LINE)).start()
    for line in lines:
        line.start()
    for step in range(1, LINE):
        from_line(lax.rem(r + step, LINE)).wait_recv()
    for step in range(1, PLANE):
        over_plane(step, h).start()
    spread[h] = column[...]
    for step in range(1, PLANE):
        over_plane(step, lax.rem(h + step, PLANE)).wait_recv()

    share = tile_ref.shape[1] // 2
    low = lax.broadcasted_iota(jnp.int32, (1, 2 * share), 1) < share
    for line_place in range(LINE):
        for pair in range(PLANE // 2):
            even = spread[2 * pair, line_place][0:1, :]
            odd = spread[2 * pair + 1, line_place][0:1, :]
            at = (line_place * (PLANE // 2) + pair) * 2 * share
            gains_ref[0:1, at : at + 2 * share] = jnp.where(low, even, pltpu.roll(odd, share, 1))
            gains_ref[1:2, at : at + 2 * share] = jnp.where(low, pltpu.roll(even, share, 1), odd)

    def make(i, unused):
        at = pl.ds(pl.multiple_of(i * CHUNK, CHUNK), CHUNK)
        normed[at, :] = norm_rows(x_ref[at, :].astype(jnp.float32), gains_ref[0:1, :]).astype(
            jnp.bfloat16
        )
        return unused

    lax.fori_loop(0, x_ref.shape[0] // CHUNK, make, 0)
    plane.start()
    plane.relay(0)
    lines[0].forward()
    plane.relay(1)
    plane.rest()
    plane.end()
    for line in lines[1:]:
        line.forward()
    for line in lines:
        line.finish()
    for step in range(1, LINE):
        up_line(lax.rem(r + step, LINE)).wait_send()
    for step in range(1, PLANE):
        over_plane(step, h).wait_send()


def open_block(layer_in, tile, weights):
    rows, width = layer_in.shape
    return pl.pallas_call(
        open_body,
        in_specs=[IN_VMEM, IN_VMEM] + [ANYWHERE] * 3,
        out_specs=[ANYWHERE] * 4 + [IN_VMEM],
        out_shape=[jax.ShapeDtypeStruct((PLANE, rows, width), jnp.bfloat16)]
        + [jax.ShapeDtypeStruct((LINE,) + item.shape, item.dtype) for item in weights]
        + [jax.ShapeDtypeStruct((2, width), jnp.float32)],
        scratch_shapes=[
            pltpu.VMEM((rows, width), jnp.bfloat16),
            pltpu.VMEM((LINE,) + tile.shape, jnp.float32),
            pltpu.VMEM((PLANE, LINE) + tile.shape, jnp.float32),
            pltpu.SemaphoreType.DMA((LINE,)),
            pltpu.SemaphoreType.DMA((LINE,)),
            pltpu.SemaphoreType.DMA((PLANE,)),
            pltpu.SemaphoreType.DMA((PLANE,)),
            *(LineGather.semaphores * 3),
            *PlaneGather.semaphores,
        ],
        compiler_params=pltpu.CompilerParams(
            collective_id=0, has_side_effects=True, vmem_limit_bytes=24 * 2**20
        ),
        name="open_block",
    )(layer_in, tile, *weights)


def forward_linked_body(
    normed_ref, xw_ref, yw_ref, ow_ref, taps_ref, vec_ref, wr_ref, we_ref, keep_ref,
    x_ref, gain_ref, shard,
    u_ref, by_ref, before_ref, states_ref, mixed_ref, residual_ref, two_ref, gathered,
    window, conv, conv_low, rate, entry, carry, *links,
):
    step = pl.program_id(0)
    plane = PlaneReduce(*links[:8])
    line = LineGather(shard, gathered, *links[8:11])

    @pl.when(step == 0)
    def _():
        meet(True, "near")
        line.start()

    @pl.when(step > 0)
    def _():
        plane.pass_on(step - 1)

    value = forward_step(
        normed_ref, xw_ref, yw_ref, ow_ref, taps_ref, vec_ref, wr_ref, we_ref, keep_ref,
        u_ref, by_ref, before_ref, states_ref, mixed_ref,
        window, conv, conv_low, rate, entry, carry,
    )
    plane.put(step, value)

    @pl.when(step == 6)
    def _():
        line.forward()

    @pl.when(step == PLANE - 1)
    def _():
        plane.pass_on(step)
        plane.arrive()

        def make(i, unused):
            at = pl.ds(pl.multiple_of(i * CHUNK, CHUNK), CHUNK)
            residual = x_ref[at, :].astype(jnp.float32) + plane.total(at)
            residual_ref[at, :] = residual
            two_ref[at, :] = norm_rows(residual, gain_ref[...]).astype(jnp.bfloat16)
            return unused

        lax.fori_loop(0, x_ref.shape[0] // CHUNK, make, 0)
        plane.finish()
        line.finish()


def forward_linked(normed, xw, yw, ow, taps, vec, wr, we, keep, layer_in, gain, shard):
    length, width = normed.shape
    chans = xw.shape[1]
    rows = length // PLANE
    tile = lambda columns: pl.BlockSpec((rows, columns), lambda i: (i, 0))
    return pl.pallas_call(
        forward_linked_body,
        grid=(PLANE,),
        in_specs=[
            tile(width), whole(xw.shape), whole(yw.shape), whole(ow.shape), whole(taps.shape),
            whole(vec.shape), whole(wr.shape), whole(we.shape), tile(keep.shape[1]),
            whole(layer_in.shape), whole(gain.shape), ANYWHERE,
        ],
        out_specs=[tile(chans)] * 5 + [whole((rows, width))] * 2 + [ANYWHERE],
        out_shape=[
            jax.ShapeDtypeStruct((length, chans), jnp.bfloat16),
            jax.ShapeDtypeStruct((length, chans), jnp.float32),
            jax.ShapeDtypeStruct((length, chans), jnp.float32),
            jax.ShapeDtypeStruct((length, chans), jnp.bfloat16),
            jax.ShapeDtypeStruct((length, chans), jnp.bfloat16),
            jax.ShapeDtypeStruct((rows, width), jnp.float32),
            jax.ShapeDtypeStruct((rows, width), jnp.bfloat16),
            jax.ShapeDtypeStruct((LINE,) + shard.shape, shard.dtype),
        ],
        scratch_shapes=[
            pltpu.VMEM((rows + 8, chans), jnp.float32),
            pltpu.VMEM((rows, chans), jnp.float32),
            pltpu.VMEM((rows, chans), jnp.bfloat16),
            pltpu.VMEM((rows, chans), jnp.float32),
            pltpu.VMEM((rows, chans), jnp.float32),
            pltpu.VMEM((8, chans), jnp.float32),
            *PlaneReduce.buffers(rows, width),
            *PlaneReduce.semaphores,
            *LineGather.semaphores,
        ],
        compiler_params=pltpu.CompilerParams(
            collective_id=1, has_side_effects=True, vmem_limit_bytes=56 * 2**20
        ),
        name="mixer_forward_linked",
    )(normed, xw, yw, ow, taps, vec, wr, we, keep, layer_in, gain, shard)


def spread_body(block, shard, full, gathered, *semaphores):
    plane = PlaneGather(block, full, *semaphores[:3])
    line = LineGather(shard, gathered, *semaphores[3:6])
    meet(True, "near")
    line.start()
    plane.start()
    plane.relay(0)
    plane.relay(1)
    plane.rest()
    line.forward()
    plane.end()
    line.finish()


def spread(block, shard, place):
    return pl.pallas_call(
        spread_body,
        in_specs=[ANYWHERE] * 2,
        out_specs=[ANYWHERE] * 2,
        out_shape=[
            jax.ShapeDtypeStruct((PLANE,) + block.shape, block.dtype),
            jax.ShapeDtypeStruct((LINE,) + shard.shape, shard.dtype),
        ],
        scratch_shapes=[*PlaneGather.semaphores, *LineGather.semaphores],
        compiler_params=pltpu.CompilerParams(collective_id=place, has_side_effects=True),
        name="spread",
    )(block, shard)


def ffn_up_body(
    two_ref, gate_ref, up_ref, cot, shard,
    gates_ref, ups_ref, hidden_ref, full, gathered, *semaphores,
):
    step = pl.program_id(0)
    plane = PlaneGather(cot, full, *semaphores[:3])
    line = LineGather(shard, gathered, *semaphores[3:6])

    @pl.when(step == 0)
    def _():
        meet(True, "near")
        line.start()
        plane.start()

    @pl.when(step == 3)
    def _():
        plane.relay(0)

    @pl.when(step == 5)
    def _():
        plane.relay(1)

    gates = dot_plain(two_ref[...], gate_ref[...])
    ups = dot_plain(two_ref[...], up_ref[...])
    gates_ref[...] = gates
    ups_ref[...] = ups
    rows = gates_ref.shape[0]

    def make(i, unused):
        at = pl.ds(pl.multiple_of(i * CHUNK, CHUNK), CHUNK)
        hidden_ref[at, :] = (gelu_only(gates_ref[at, :]) * ups_ref[at, :]).astype(jnp.bfloat16)
        return unused

    lax.fori_loop(0, rows // CHUNK, make, 0)

    @pl.when(step == PLANE - 1)
    def _():
        plane.rest()
        line.forward()
        plane.end()
        line.finish()


def ffn_up(two, gate, up, cot, shard):
    length, width = two.shape
    units = gate.shape[1]
    rows = length // PLANE
    tile = lambda columns: pl.BlockSpec((rows, columns), lambda i: (i, 0))
    return pl.pallas_call(
        ffn_up_body,
        grid=(PLANE,),
        in_specs=[tile(width), whole(gate.shape), whole(up.shape), ANYWHERE, ANYWHERE],
        out_specs=[tile(units)] * 3 + [ANYWHERE] * 2,
        out_shape=[
            jax.ShapeDtypeStruct((length, units), jnp.float32),
            jax.ShapeDtypeStruct((length, units), jnp.float32),
            jax.ShapeDtypeStruct((length, units), jnp.bfloat16),
            jax.ShapeDtypeStruct((PLANE,) + cot.shape, cot.dtype),
            jax.ShapeDtypeStruct((LINE,) + shard.shape, shard.dtype),
        ],
        scratch_shapes=[*PlaneGather.semaphores, *LineGather.semaphores],
        compiler_params=pltpu.CompilerParams(
            collective_id=3, has_side_effects=True, vmem_limit_bytes=40 * 2**20
        ),
        name="ffn_up",
    )(two, gate, up, cot, shard)
def once(shape):
    return pl.BlockSpec(
        shape, lambda i: (0,) * len(shape), pipeline_mode=pl.Buffered(buffer_count=1)
    )


def norm_back(rows, gain, incoming):
    scale = lax.rsqrt(jnp.mean(rows * rows, axis=-1, keepdims=True) + EPSILON)
    scaled = incoming * gain
    inner = jnp.mean(scaled * rows, axis=-1, keepdims=True)
    return scale * scaled - rows * (scale * scale * scale * inner), incoming * rows * scale


def to_parts(total, parts):
    rows = parts.shape[1]
    step = 64

    def move(i, unused):
        at = pl.ds(pl.multiple_of(i * step, step), step)
        for t in range(LINE):
            here = pl.ds(pl.multiple_of(t * rows + i * step, step), step)
            parts[t, at, :] = total[here, :].astype(jnp.bfloat16)
        return unused

    lax.fori_loop(0, rows // step, move, 0)


def sum_eight(value):
    total = value[0:8, :]
    for k in range(1, value.shape[0] // 8):
        total = total + value[8 * k : 8 * k + 8, :]
    return total


def ffn_back_body(
    cot_ref, hidden_ref, two_ref, gates_ref, ups_ref, gate_ref, up_ref, down_ref,
    residual_ref, own_cot_ref, gain_ref,
    d_gates_ref, d_ups_ref, gate_parts, down_out, d_res_ref, d_low_ref, gain_out,
    total, parts, eight, *links,
):
    step = pl.program_id(0)
    line = LineReduce(parts, *links[:5])
    plane = PlaneReduce(*links[5:])

    @pl.when(step == 0)
    def _():
        total[...] = jnp.zeros_like(total)
        meet(True, "near")

    @pl.when(step < PLANE)
    def _():
        total[...] += contract_first(cot_ref[...], hidden_ref[...])

    @pl.when(step == PLANE - 1)
    def _():
        to_parts(total, parts)
        line.start()
        total[...] = jnp.zeros_like(total)

    @pl.when(step > PLANE)
    def _():
        plane.pass_on(step - PLANE - 1)

    @pl.when(step >= PLANE)
    def _():
        d_hidden = dot_plain(cot_ref[...], down_ref[...])
        gelu_gate, slope = gelu_both(gates_ref[...])
        d_gates_ref[...] = (d_hidden * ups_ref[...] * slope).astype(jnp.bfloat16)
        d_ups_ref[...] = (d_hidden * gelu_gate).astype(jnp.bfloat16)
        value = contract_last(d_gates_ref[...], gate_ref[...]) + contract_last(
            d_ups_ref[...], up_ref[...]
        )
        plane.put(step - PLANE, value.astype(jnp.bfloat16))
        total[...] += contract_first(two_ref[...], d_gates_ref[...])

    @pl.when(step == PLANE + 4)
    def _():
        line.forward()

    @pl.when(step == 2 * PLANE - 1)
    def _():
        plane.pass_on(step - PLANE)
        to_parts(total, gate_parts)
        plane.arrive()
        eight[...] = jnp.zeros_like(eight)

        def back(i, unused):
            at = pl.ds(pl.multiple_of(i * CHUNK, CHUNK), CHUNK)
            d_rows, d_gain = norm_back(residual_ref[at, :], gain_ref[...], plane.total(at))
            d_residual = own_cot_ref[at, :].astype(jnp.float32) + d_rows
            d_res_ref[at, :] = d_residual
            d_low_ref[at, :] = d_residual.astype(jnp.bfloat16)
            eight[...] += sum_eight(d_gain)
            return unused

        lax.fori_loop(0, residual_ref.shape[0] // CHUNK, back, 0)
        gain_out[...] = jnp.sum(eight[...], axis=0, keepdims=True)

        def write(at, value):
            down_out[at, :] = value

        line.finish(write)
        plane.finish()


def ffn_back(
    cot_group, hidden, two_group, gates, ups, gate, up, down, residual, own_cot, gain
):
    length, width = cot_group.shape
    units = gate.shape[1]
    rows, share = length // PLANE, width // LINE
    early = lambda columns: pl.BlockSpec((rows, columns), lambda i: (jnp.minimum(i, PLANE - 1), 0))
    late = lambda columns: pl.BlockSpec(
        (rows, columns), lambda i: (jnp.maximum(i - PLANE, 0), 0)
    )
    both = pl.BlockSpec((rows, width), lambda i: (lax.rem(i, PLANE), 0))
    return pl.pallas_call(
        ffn_back_body,
        grid=(2 * PLANE,),
        in_specs=[
            both, early(units), late(width), late(units), late(units), once(gate.shape),
            once(up.shape), once(down.shape), once(residual.shape), once(own_cot.shape),
            once(gain.shape),
        ],
        out_specs=[
            late(units), late(units), once((LINE, share, units)), once((share, units)),
            once((rows, width)), once((rows, width)), once((1, width)),
        ],
        out_shape=[
            jax.ShapeDtypeStruct((length, units), jnp.bfloat16),
            jax.ShapeDtypeStruct((length, units), jnp.bfloat16),
            jax.ShapeDtypeStruct((LINE, share, units), jnp.bfloat16),
            jax.ShapeDtypeStruct((share, units), jnp.float32),
            jax.ShapeDtypeStruct((rows, width), jnp.float32),
            jax.ShapeDtypeStruct((rows, width), jnp.bfloat16),
            jax.ShapeDtypeStruct((1, width), jnp.float32),
        ],
        scratch_shapes=[
            pltpu.VMEM((width, units), jnp.float32),
            pltpu.VMEM((LINE, share, units), jnp.bfloat16),
            pltpu.VMEM((8, width), jnp.float32),
            *LineReduce.buffers(share, units),
            *LineReduce.semaphores,
            *PlaneReduce.buffers(rows, width),
            *PlaneReduce.semaphores,
        ],
        compiler_params=pltpu.CompilerParams(
            collective_id=4, has_side_effects=True, vmem_limit_bytes=62 * 2**20
        ),
        name="ffn_back",
    )(cot_group, hidden, two_group, gates, ups, gate, up, down, residual, own_cot, gain)


def turn_body(
    two_ref, d_ups_ref, gate_parts, block, up_parts, gate_out, full, total, *links
):
    step = pl.program_id(0)
    line = LineReduce(gate_parts, *links[:5])
    plane = PlaneGather(block, full, *links[5:])

    @pl.when(step == 0)
    def _():
        meet(True, "near")
        line.start()
        plane.start()
        total[...] = jnp.zeros_like(total)

    total[...] += contract_first(two_ref[...], d_ups_ref[...])

    @pl.when(step == PLANE - 2)
    def _():
        plane.relay(0)

    @pl.when(step == PLANE - 1)
    def _():
        plane.relay(1)
        to_parts(total, up_parts)
        line.forward()
        plane.rest()
        plane.end()

        def write(at, value):
            gate_out[at, :] = value

        line.finish(write)


def turn(two_group, d_ups, gate_parts, block):
    length, width = two_group.shape
    units = d_ups.shape[1]
    rows, share = length // PLANE, width // LINE
    tile = lambda columns: pl.BlockSpec((rows, columns), lambda i: (i, 0))
    return pl.pallas_call(
        turn_body,
        grid=(PLANE,),
        in_specs=[tile(width), tile(units), once(gate_parts.shape), ANYWHERE],
        out_specs=[once(gate_parts.shape), once((share, units)), ANYWHERE],
        out_shape=[
            jax.ShapeDtypeStruct(gate_parts.shape, jnp.bfloat16),
            jax.ShapeDtypeStruct((share, units), jnp.float32),
            jax.ShapeDtypeStruct((PLANE, rows, width), jnp.bfloat16),
        ],
        scratch_shapes=[
            pltpu.VMEM((width, units), jnp.float32),
            *LineReduce.buffers(share, units),
            *LineReduce.semaphores,
            *PlaneGather.semaphores,
        ],
        compiler_params=pltpu.CompilerParams(
            collective_id=5, has_side_effects=True, vmem_limit_bytes=48 * 2**20
        ),
        name="turn",
    )(two_group, d_ups, gate_parts, block)


def backward_linked_body(
    d_res_ref, xw_ref, yw_ref, ow_ref, taps_ref, vec_ref, wr_ref, we_ref, keep_ref,
    u_ref, u_prev_ref, by_ref, before_ref, states_ref, normed_ref, mixed_ref, up_parts,
    x_ref, gain_ref, d_residual_ref,
    x_parts, y_parts, out_parts, up_out, in_grad, gain_out, taps_out, vec_out, wr_out, we_out,
    d_bx, d_by, x_total, y_total, out_total, eight, *rest,
):
    scratch, links = rest[:11], rest[11:]
    step = pl.program_id(0)
    block = PLANE - 1 - step
    line = LineReduce(up_parts, *links[:5])
    plane = PlaneReduce(*links[5:])

    @pl.when(step == 0)
    def _():
        meet(True, "near")
        line.start()
        x_total[...] = jnp.zeros_like(x_total)
        y_total[...] = jnp.zeros_like(y_total)
        out_total[...] = jnp.zeros_like(out_total)

    @pl.when(step > 0)
    def _():
        plane.pass_on(block + 1)

    value = backward_step(
        d_res_ref, xw_ref, yw_ref, ow_ref, taps_ref, vec_ref, wr_ref, we_ref, keep_ref,
        u_ref, u_prev_ref, by_ref, before_ref, states_ref, d_bx, d_by,
        taps_out, vec_out, wr_out, we_out, *scratch,
    )
    plane.put(block, value)
    x_total[...] += contract_first(normed_ref[...], d_bx[...])
    y_total[...] += contract_first(normed_ref[...], d_by[...])
    out_total[...] += contract_first(d_res_ref[...], mixed_ref[...])

    @pl.when(step == 4)
    def _():
        line.forward()

    @pl.when(step == PLANE - 1)
    def _():
        plane.pass_on(block)
        to_parts(x_total, x_parts)
        to_parts(y_total, y_parts)
        to_parts(out_total, out_parts)
        plane.arrive()
        eight[...] = jnp.zeros_like(eight)

        def back(i, unused):
            at = pl.ds(pl.multiple_of(i * CHUNK, CHUNK), CHUNK)
            d_rows, d_gain = norm_back(
                x_ref[at, :].astype(jnp.float32), gain_ref[...], plane.total(at)
            )
            in_grad[at, :] = (d_residual_ref[at, :] + d_rows).astype(jnp.bfloat16)
            eight[...] += sum_eight(d_gain)
            return unused

        lax.fori_loop(0, x_ref.shape[0] // CHUNK, back, 0)
        gain_out[...] = jnp.sum(eight[...], axis=0, keepdims=True)

        def write(at, value):
            up_out[at, :] = value

        line.finish(write)
        plane.finish()


def backward_linked(
    d_res, xw, yw, ow, taps, vec, wr, we, keep, u, by, before, states, normed, mixed, up_parts,
    layer_in, gain, d_residual,
):
    length, width = d_res.shape
    chans, units = xw.shape[1], up_parts.shape[2]
    rows, share = length // PLANE, width // LINE
    tile = lambda columns: pl.BlockSpec((rows, columns), lambda i: (PLANE - 1 - i, 0))
    ahead = pl.BlockSpec(
        (16, chans), lambda i: (jnp.maximum((PLANE - 1 - i) * (rows // 16) - 1, 0), 0)
    )
    weights = (LINE, share, chans)
    return pl.pallas_call(
        backward_linked_body,
        grid=(PLANE,),
        in_specs=[
            tile(width), once(xw.shape), once(yw.shape), once(ow.shape), once(taps.shape),
            once(vec.shape), once(wr.shape), once(we.shape), tile(keep.shape[1]),
            tile(chans), ahead, tile(chans), tile(chans), tile(chans), tile(width), tile(chans),
            once(up_parts.shape), once(layer_in.shape), once(gain.shape), once(d_residual.shape),
        ],
        out_specs=[
            once(weights), once(weights), once(weights), once((share, units)),
            once((rows, width)), once((1, width)), once(taps.shape), once(vec.shape),
            once(wr.shape), once(we.shape),
        ],
        out_shape=[
            jax.ShapeDtypeStruct(weights, jnp.bfloat16),
            jax.ShapeDtypeStruct(weights, jnp.bfloat16),
            jax.ShapeDtypeStruct(weights, jnp.bfloat16),
            jax.ShapeDtypeStruct((share, units), jnp.float32),
            jax.ShapeDtypeStruct((rows, width), jnp.bfloat16),
            jax.ShapeDtypeStruct((1, width), jnp.float32),
            jax.ShapeDtypeStruct(taps.shape, jnp.float32),
            jax.ShapeDtypeStruct(vec.shape, jnp.float32),
            jax.ShapeDtypeStruct(wr.shape, jnp.float32),
            jax.ShapeDtypeStruct(we.shape, jnp.float32),
        ],
        scratch_shapes=[
            pltpu.VMEM((rows, chans), jnp.bfloat16),
            pltpu.VMEM((rows, chans), jnp.bfloat16),
            pltpu.VMEM((width, chans), jnp.float32),
            pltpu.VMEM((width, chans), jnp.float32),
            pltpu.VMEM((width, chans), jnp.float32),
            pltpu.VMEM((8, width), jnp.float32),
            pltpu.VMEM((rows + 8, chans), jnp.float32),
            pltpu.VMEM((rows, chans), jnp.float32),
            pltpu.VMEM((rows, chans), jnp.bfloat16),
            pltpu.VMEM((rows, chans), jnp.float32),
            pltpu.VMEM((rows, chans), jnp.float32),
            pltpu.VMEM((rows, chans), jnp.float32),
            pltpu.VMEM((rows + 8, chans), jnp.float32),
            pltpu.VMEM((rows, chans), jnp.bfloat16),
            pltpu.VMEM((rows, chans), jnp.bfloat16),
            pltpu.VMEM((8, chans), jnp.float32),
            pltpu.VMEM((64, chans), jnp.float32),
            *LineReduce.buffers(share, units),
            *LineReduce.semaphores,
            *PlaneReduce.buffers(rows, width),
            *PlaneReduce.semaphores,
        ],
        compiler_params=pltpu.CompilerParams(
            collective_id=6, has_side_effects=True, vmem_limit_bytes=62 * 2**20
        ),
        name="mixer_backward_linked",
    )(
        d_res, xw, yw, ow, taps, vec, wr, we, keep, u, u, by, before, states, normed, mixed,
        up_parts, layer_in, gain, d_residual,
    )


def close_body(
    hidden_ref, down_ref, x_parts, y_parts, out_parts, residual_ref, gains_ref, small,
    layer_out, x_out, y_out, out_out, gains_out, small_out,
    gathered, line_gains, both_gains, plane_gains,
    gain_sent, gain_arrived, wide_sent, wide_arrived, *links,
):
    r, h = lax.axis_index("row"), lax.axis_index("head")
    step = pl.program_id(0)
    reduces = [
        LineReduce(parts, *links[5 * k : 5 * k + 5])
        for k, parts in enumerate((out_parts, x_parts, y_parts))
    ]
    outs = (out_out, x_out, y_out)
    line = LineGather(small, gathered, *links[15:18])
    plane = PlaneReduce(*links[18:26])

    def to_row(t, owner):
        return send_to(
            gains_ref.at[t], line_gains.at[owner], gain_sent.at[t], gain_arrived.at[owner],
            "row", t,
        )

    def over_plane(place, owner):
        return send_to(
            both_gains, plane_gains.at[owner], wide_sent.at[place], wide_arrived.at[owner],
            "head", lax.rem(h + place, PLANE),
        )

    @pl.when(step == 0)
    def _():
        meet(True, "all")
        for place in range(1, LINE):
            to_row(lax.rem(r + place, LINE), r).start()
        line.start()
        for item in reduces:
            item.start()

    @pl.when(step > 0)
    def _():
        plane.pass_on(step - 1)

    plane.put(step, contract_last(hidden_ref[...], down_ref[...]).astype(jnp.bfloat16))

    @pl.when(step == 2)
    def _():
        total = gains_ref[r]
        for place in range(1, LINE):
            t = lax.rem(r + place, LINE)
            to_row(t, t).wait_recv()
            total = total + line_gains[t]
        both_gains[...] = total
        for place in range(1, PLANE):
            over_plane(place, h).start()

    @pl.when(step == PLANE - 1)
    def _():
        plane.pass_on(step)
        reduces[0].forward()
        line.forward()
        total = both_gains[...]
        for place in range(1, PLANE):
            owner = lax.rem(h + place, PLANE)
            over_plane(place, owner).wait_recv()
            total = total + plane_gains[owner]
        mine = lax.broadcasted_iota(jnp.int32, total.shape, 0) == h
        gains_out[...] = jnp.sum(jnp.where(mine, total, 0.0), axis=0, keepdims=True)
        reduces[1].forward()
        plane.arrive()

        def make(i, unused):
            at = pl.ds(pl.multiple_of(i * CHUNK, CHUNK), CHUNK)
            layer_out[at, :] = (residual_ref[at, :] + plane.total(at)).astype(jnp.bfloat16)
            return unused

        lax.fori_loop(0, residual_ref.shape[0] // CHUNK, make, 0)
        reduces[2].forward()
        line.finish()
        total = gathered[0].astype(jnp.float32)
        for t in range(1, LINE):
            total = total + gathered[t].astype(jnp.float32)
        small_out[...] = total
        for item, out in zip(reduces, outs):

            def write(at, value, out=out):
                out[at, :] = value

            item.finish(write)
        plane.finish()
        for place in range(1, LINE):
            to_row(lax.rem(r + place, LINE), r).wait_send()
        for place in range(1, PLANE):
            over_plane(place, h).wait_send()


def close_block(hidden, down, x_parts, y_parts, out_parts, residual, gains, small):
    length, units = hidden.shape
    rows, width = residual.shape
    share, chans = x_parts.shape[1:]
    return pl.pallas_call(
        close_body,
        grid=(PLANE,),
        in_specs=[
            pl.BlockSpec((rows, units), lambda i: (i, 0)), once(down.shape),
            once(x_parts.shape), once(y_parts.shape), once(out_parts.shape),
            once(residual.shape), once(gains.shape), once(small.shape),
        ],
        out_specs=[
            once((rows, width)), once((share, chans)), once((share, chans)),
            once((share, chans)), once((1, gains.shape[2])), once(small.shape),
        ],
        out_shape=[
            jax.ShapeDtypeStruct((rows, width), jnp.bfloat16),
            jax.ShapeDtypeStruct((share, chans), jnp.float32),
            jax.ShapeDtypeStruct((share, chans), jnp.float32),
            jax.ShapeDtypeStruct((share, chans), jnp.float32),
            jax.ShapeDtypeStruct((1, gains.shape[2]), jnp.float32),
            jax.ShapeDtypeStruct(small.shape, jnp.float32),
        ],
        scratch_shapes=[
            pltpu.VMEM((LINE,) + small.shape, jnp.bfloat16),
            pltpu.VMEM(gains.shape, jnp.float32),
            pltpu.VMEM(gains.shape[1:], jnp.float32),
            pltpu.VMEM((PLANE,) + gains.shape[1:], jnp.float32),
            pltpu.SemaphoreType.DMA((LINE,)),
            pltpu.SemaphoreType.DMA((LINE,)),
            pltpu.SemaphoreType.DMA((PLANE,)),
            pltpu.SemaphoreType.DMA((PLANE,)),
            *LineReduce.buffers(share, chans), *LineReduce.semaphores,
            *LineReduce.buffers(share, chans), *LineReduce.semaphores,
            *LineReduce.buffers(share, chans), *LineReduce.semaphores,
            *LineGather.semaphores,
            *PlaneReduce.buffers(rows, width), *PlaneReduce.semaphores,
        ],
        compiler_params=pltpu.CompilerParams(
            collective_id=7, has_side_effects=True, vmem_limit_bytes=56 * 2**20
        ),
        name="close_block",
    )(hidden, down, x_parts, y_parts, out_parts, residual, gains, small)


def mixer_params(
    conv_weight, conv_bias, rate_weight, rate_bias, entry_weight, entry_bias, decay_param, chans
):
    used = conv_bias.shape[0]
    spare = (0, chans - used)
    decay_wide = jnp.pad(decay_param, spare, constant_values=2.0)
    blank = jnp.zeros((chans,), jnp.float32)
    vec = jnp.stack(
        [
            jnp.pad(conv_bias, spare),
            jnp.pad(rate_bias, spare),
            jnp.pad(entry_bias, spare),
            -8.0 * jax.nn.softplus(-decay_wide),
            blank,
            blank,
            blank,
            blank,
        ]
    )
    taps = jnp.pad(conv_weight, ((0, 0), spare))
    return taps, vec, block_diagonal(rate_weight, chans), block_diagonal(entry_weight, chans)


def shards(
    layer_in,
    cotangent,
    mix_gain,
    ffn_gain,
    x_weight,
    y_weight,
    out_weight,
    conv_weight,
    conv_bias,
    rate_weight,
    rate_bias,
    entry_weight,
    entry_bias,
    decay_param,
    gate_weight,
    up_weight,
    down_weight,
    resets,
):
    heads, head_width = rate_weight.shape[:2]
    used = conv_bias.shape[0]
    chans = -(-used // 128) * 128
    widen = lambda values: jnp.pad(values, ((0, 0), (0, chans - used)))
    mix_full = gather(mix_gain, ("row", "head"), 0)
    ffn_full = gather(ffn_gain, ("row", "head"), 0)
    x_rows = gather(widen(x_weight), "row", 0)
    y_rows = gather(widen(y_weight), "row", 0)
    out_rows = gather(widen(out_weight), "row", 0)
    gate_rows = gather(gate_weight, "row", 0)
    up_rows = gather(up_weight, "row", 0)
    down_rows = gather(down_weight, "row", 0)

    taps, vec, wr, we = mixer_params(
        conv_weight, conv_bias, rate_weight, rate_bias, entry_weight, entry_bias, decay_param, chans
    )
    keep = keep_columns(resets)

    inputs = layer_in.astype(jnp.float32)
    normed_f, norm_back_one = jax.vjp(norm_apply, inputs, mix_full.astype(jnp.float32))
    normed_group = gather(normed_f.astype(jnp.bfloat16), "head", 0)
    u, by, before, states, mixed, part = mixer_forward(
        normed_group, x_rows, y_rows, out_rows, taps, vec, wr, we, keep, ROWS
    )
    residual = inputs + scatter(part, "head", 0).astype(jnp.float32)
    normed_two_f, norm_back_two = jax.vjp(norm_apply, residual, ffn_full.astype(jnp.float32))
    cot_group = gather(cotangent, "head", 0)
    two_group = gather(normed_two_f.astype(jnp.bfloat16), "head", 0)
    gates = dot_plain(two_group, gate_rows)
    ups = dot_plain(two_group, up_rows)
    activated, slope = gelu_both(gates)
    hidden = (activated * ups).astype(jnp.bfloat16)
    ffn_part = contract_last(hidden, down_rows).astype(jnp.bfloat16)
    d_hidden = dot_plain(cot_group, down_rows)
    d_gates = (d_hidden * ups * slope).astype(jnp.bfloat16)
    d_ups = (d_hidden * activated).astype(jnp.bfloat16)
    d_two_part = (contract_last(d_gates, gate_rows) + contract_last(d_ups, up_rows)).astype(
        jnp.bfloat16
    )
    gate_grad = scatter(contract_first(two_group, d_gates).astype(jnp.bfloat16), "row", 0)
    up_grad = scatter(contract_first(two_group, d_ups).astype(jnp.bfloat16), "row", 0)
    down_grad = scatter(contract_first(cot_group, hidden).astype(jnp.bfloat16), "row", 0)
    layer_out = (residual + scatter(ffn_part, "head", 0).astype(jnp.float32)).astype(jnp.bfloat16)
    d_two = scatter(d_two_part, "head", 0).astype(jnp.float32)
    d_resid_norm, d_ffn_gain = norm_back_two(d_two)
    d_residual = cotangent.astype(jnp.float32) + d_resid_norm
    d_res_group = gather(d_residual.astype(jnp.bfloat16), "head", 0)
    d_bx, d_by, d_part, d_taps, d_vec, d_wr, d_we = mixer_backward(
        d_res_group, x_rows, y_rows, out_rows, taps, vec, wr, we, keep, u, by, before, states, ROWS
    )
    out_grad = scatter(contract_first(d_res_group, mixed).astype(jnp.bfloat16), "row", 0)
    x_grad = scatter(contract_first(normed_group, d_bx).astype(jnp.bfloat16), "row", 0)
    y_grad = scatter(contract_first(normed_group, d_by).astype(jnp.bfloat16), "row", 0)
    d_normed = scatter(d_part, "head", 0).astype(jnp.float32)
    d_inputs, d_mix_gain = norm_back_one(d_normed)
    layer_in_grad = (d_inputs + d_residual).astype(jnp.bfloat16)

    small = [
        d_taps[:, :used],
        d_vec[0, :used],
        diagonal_blocks(d_wr, heads, head_width),
        d_vec[1, :used],
        diagonal_blocks(d_we, heads, head_width),
        d_vec[2, :used],
        d_vec[3, :used] * (8.0 * jax.nn.sigmoid(-decay_param)),
    ]
    small = [lax.psum(item.astype(jnp.bfloat16), "row").astype(jnp.float32) for item in small]
    mix_part = scatter(d_mix_gain, ("row", "head"), 0)
    ffn_part_grad = scatter(d_ffn_gain, ("row", "head"), 0)
    wide = lambda values: values[:, :used].astype(jnp.float32)
    return (
        layer_out,
        layer_in_grad,
        mix_part,
        ffn_part_grad,
        wide(x_grad),
        wide(y_grad),
        wide(out_grad),
        *small,
        gate_grad.astype(jnp.float32),
        up_grad.astype(jnp.float32),
        down_grad.astype(jnp.float32),
    )

def shards_linked(
    layer_in,
    cotangent,
    mix_gain,
    ffn_gain,
    x_weight,
    y_weight,
    out_weight,
    conv_weight,
    conv_bias,
    rate_weight,
    rate_bias,
    entry_weight,
    entry_bias,
    decay_param,
    gate_weight,
    up_weight,
    down_weight,
    resets,
):
    heads, head_width = rate_weight.shape[:2]
    used = conv_bias.shape[0]
    chans = -(-used // 128) * 128
    widen = lambda values: jnp.pad(values, ((0, 0), (0, chans - used)))
    flat = lambda values: values.reshape((-1, values.shape[-1]))
    taps, vec, wr, we = mixer_params(
        conv_weight, conv_bias, rate_weight, rate_bias, entry_weight, entry_bias, decay_param, chans
    )
    keep = keep_columns(resets)
    own_gains = jnp.concatenate([mix_gain, ffn_gain]).astype(jnp.float32)
    tile = jnp.broadcast_to(own_gains, (8, own_gains.shape[0]))

    normed_group, x_rows, y_rows, out_rows, gains = open_block(
        layer_in, tile, (widen(x_weight), widen(y_weight), widen(out_weight))
    )
    normed_group, x_rows, y_rows, out_rows = map(flat, (normed_group, x_rows, y_rows, out_rows))
    u, by, before, states, mixed, residual, normed_two, gate_rows = forward_linked(
        normed_group, x_rows, y_rows, out_rows, taps, vec, wr, we, keep, layer_in, gains[1:2],
        gate_weight,
    )
    two_group, up_rows = spread(normed_two, up_weight, 2)
    gate_rows, two_group, up_rows = map(flat, (gate_rows, two_group, up_rows))
    gates, ups, hidden, cot_group, down_rows = ffn_up(
        two_group, gate_rows, up_rows, cotangent, down_weight
    )
    cot_group, down_rows = map(flat, (cot_group, down_rows))

    d_gates, d_ups, gate_parts, down_grad, d_residual, d_low, d_ffn_gain = ffn_back(
        cot_group, hidden, two_group, gates, ups, gate_rows, up_rows, down_rows, residual,
        cotangent, gains[1:2],
    )
    up_parts, gate_grad, d_res_group = turn(two_group, d_ups, gate_parts, d_low)
    (
        x_parts, y_parts, out_parts, up_grad, layer_in_grad, d_mix_gain, d_taps, d_vec, d_wr, d_we,
    ) = backward_linked(
        flat(d_res_group), x_rows, y_rows, out_rows, taps, vec, wr, we, keep, u, by, before,
        states, normed_group, mixed, up_parts, layer_in, gains[0:1], d_residual,
    )

    share = mix_gain.shape[0]
    split = lambda values: values.reshape(LINE, PLANE, share)
    gain_terms = jnp.concatenate([split(d_mix_gain), split(d_ffn_gain)], axis=2)
    blocks = [slice(h * head_width, (h + 1) * head_width) for h in range(heads)]
    packed = jnp.concatenate(
        [jnp.concatenate([d_wr[at, at], d_we[at, at]], axis=1) for at in blocks]
        + [
            d_taps[:, :used],
            d_vec[0:3, :used],
            d_vec[3:4, :used] * (8.0 * jax.nn.sigmoid(-decay_param)),
        ],
        axis=0,
    ).astype(jnp.bfloat16)
    packed = jnp.pad(packed, ((0, -packed.shape[0] % 16), (0, chans - used)))
    layer_out, x_grad, y_grad, out_grad, gain_grads, sums = close_block(
        hidden, down_rows, x_parts, y_parts, out_parts, residual, gain_terms, packed
    )
    gates_end = heads * head_width
    wide = lambda values: values[:, :used]
    return (
        layer_out,
        layer_in_grad,
        gain_grads[0, :share],
        gain_grads[0, share:],
        wide(x_grad),
        wide(y_grad),
        wide(out_grad),
        sums[gates_end : gates_end + 4, :used],
        sums[gates_end + 4, :used],
        sums[:gates_end, :head_width].reshape(heads, head_width, head_width),
        sums[gates_end + 5, :used],
        sums[:gates_end, head_width : 2 * head_width].reshape(heads, head_width, head_width),
        sums[gates_end + 6, :used],
        sums[gates_end + 7, :used],
        gate_grad,
        up_grad,
        down_grad,
    )


def solution(mesh):
    linked = mesh.shape["row"] == LINE and mesh.shape["head"] == PLANE
    return jax.shard_map(
        shards_linked if linked else shards,
        mesh=mesh,
        in_specs=(
            P(("row", "head"), None),
            P(("row", "head"), None),
            P(("row", "head")),
            P(("row", "head")),
            P("row", "head"),
            P("row", "head"),
            P("row", "head"),
            P(None, "head"),
            P("head"),
            P("head", None, None),
            P("head"),
            P("head", None, None),
            P("head"),
            P("head"),
            P("row", "head"),
            P("row", "head"),
            P("row", "head"),
            P("row", None),
        ),
        out_specs=(
            P(("row", "head"), None),
            P(("row", "head"), None),
            P(("row", "head")),
            P(("row", "head")),
            P("row", "head"),
            P("row", "head"),
            P("row", "head"),
            P(None, "head"),
            P("head"),
            P("head", None, None),
            P("head"),
            P("head", None, None),
            P("head"),
            P("head"),
            P("row", "head"),
            P("row", "head"),
            P("row", "head"),
        ),
        check_vma=False,
    )
```

```python
import jax
import jax.numpy as jnp
from jax import lax
from jax.experimental import pallas as pl
from jax.experimental.pallas import tpu as pltpu
from jax.sharding import PartitionSpec as P

EPSILON = 1e-06
ROWS = 256
GELU_A = 0.7978845608028654
GELU_B = 0.044715
CHUNK = 16
UNROLL = 4


def gelu_only(x):
    return 0.5 * x * (1.0 + jnp.tanh(GELU_A * (x + GELU_B * x * x * x)))


def gelu_both(x):
    square = x * x
    bent = jnp.tanh(GELU_A * x * (1.0 + GELU_B * square))
    half = 0.5 * (1.0 + bent)
    slope = half + 0.5 * x * (1.0 - bent * bent) * (GELU_A * (1.0 + 3.0 * GELU_B * square))
    return x * half, slope


def one_minus_exp(x, exp_x):
    return -jnp.tanh(0.5 * x) * (1.0 + exp_x)


def dot_plain(left, right):
    return jnp.dot(left, right, preferred_element_type=jnp.float32)


def contract_last(left, right):
    return lax.dot_general(
        left, right, (((1,), (1,)), ((), ())), preferred_element_type=jnp.float32
    )


def contract_first(left, right):
    return lax.dot_general(
        left, right, (((0,), (0,)), ((), ())), preferred_element_type=jnp.float32
    )


def sum_eight(value):
    total = value[0:8, :]
    for k in range(1, value.shape[0] // 8):
        total = total + value[8 * k : 8 * k + 8, :]
    return total


def conv_rows(window, keep, taps, shift):
    rows = window.shape[0] - 8
    total = taps[0:1] * window[8:] + shift
    for offset in range(1, 4):
        total = total + taps[offset : offset + 1] * (
            keep[:, offset : offset + 1] * window[8 - offset : 8 - offset + rows]
        )
    return total


def scan_down(decays, driven, carry):
    rows = decays.shape[0]
    place = lax.broadcasted_iota(jnp.int32, decays.shape, 0)
    step = 1
    while step < rows:
        inside = place >= step
        driven = jnp.where(inside, decays * pltpu.roll(driven, step, 0) + driven, driven)
        decays = jnp.where(inside, decays * pltpu.roll(decays, step, 0), decays)
        step *= 2
    return decays * carry + driven


def scan_up(decays, driven, carry):
    rows = decays.shape[0]
    place = lax.broadcasted_iota(jnp.int32, decays.shape, 0)
    step = 1
    while step < rows:
        inside = place < rows - step
        driven = jnp.where(inside, decays * pltpu.roll(driven, rows - step, 0) + driven, driven)
        decays = jnp.where(inside, decays * pltpu.roll(decays, rows - step, 0), decays)
        step *= 2
    return decays * carry + driven


def forward_step(
    normed_ref, xy_ref, ow_ref, taps_ref, vec_ref, wr_ref, we_ref, keep_ref,
    u_ref, by_ref, before_ref, states_ref, mixed_ref,
    window, conv, conv_low, rate, entry, carry,
):
    rows = normed_ref.shape[0]

    @pl.when(pl.program_id(0) == 0)
    def _():
        window[0:8, :] = jnp.zeros_like(window[0:8, :])
        carry[...] = jnp.zeros_like(carry)

    chans = u_ref.shape[1]
    branches = dot_plain(normed_ref[...], xy_ref[...])
    branch_x = branches[:, :chans].astype(jnp.bfloat16)
    u_ref[...] = branch_x
    window[pl.ds(8, rows), :] = branch_x.astype(jnp.float32)
    by_ref[...] = branches[:, chans:]

    def conv_step(j, unused):
        at = pl.multiple_of(j * CHUNK, CHUNK)
        made = conv_rows(
            window[pl.ds(at, CHUNK + 8), :], keep_ref[pl.ds(at, CHUNK), :],
            taps_ref[...], vec_ref[0:1, :],
        )
        conv[pl.ds(at, CHUNK), :] = made
        conv_low[pl.ds(at, CHUNK), :] = made.astype(jnp.bfloat16)
        return unused

    lax.fori_loop(0, rows // CHUNK, conv_step, 0, unroll=UNROLL)
    window[0:8, :] = window[pl.ds(rows, 8), :]
    rate[...] = dot_plain(conv_low[...], wr_ref[...]) + vec_ref[1:2, :]
    entry[...] = dot_plain(conv_low[...], we_ref[...]) + vec_ref[2:3, :]

    def scan_step(j, before):
        at = pl.multiple_of(j * CHUNK, CHUNK)
        here = pl.ds(at, CHUNK)
        carried = keep_ref[here, 0:1]
        log_decay = jax.nn.sigmoid(rate[here, :]) * vec_ref[3:4, :]
        exp_decay = jnp.exp(log_decay)
        lost = one_minus_exp(2.0 * log_decay, exp_decay * exp_decay)
        drop = lost * lax.rsqrt(jnp.maximum(lost, 1e-30))
        scaling = (1.0 - carried) + carried * drop
        driven = scaling * jax.nn.sigmoid(entry[here, :]) * conv[here, :]
        states = scan_down(exp_decay * carried, driven, before)
        first = lax.broadcasted_iota(jnp.int32, states.shape, 0) == 0
        before_ref[here, :] = jnp.where(first, before, pltpu.roll(states, 1, 0))
        states_low = states.astype(jnp.bfloat16)
        states_ref[here, :] = states_low
        mixed_ref[here, :] = (
            states_low.astype(jnp.float32) * gelu_only(by_ref[here, :])
        ).astype(jnp.bfloat16)
        return states[CHUNK - 1 : CHUNK, :]

    carry[0:1, :] = lax.fori_loop(0, rows // CHUNK, scan_step, carry[0:1, :], unroll=UNROLL)
    return contract_last(mixed_ref[...], ow_ref[...]).astype(jnp.bfloat16)


def forward_body(
    normed_ref, xy_ref, ow_ref, taps_ref, vec_ref, wr_ref, we_ref, keep_ref,
    u_ref, by_ref, before_ref, states_ref, mixed_ref, part_ref, *scratch,
):
    part_ref[...] = forward_step(
        normed_ref, xy_ref, ow_ref, taps_ref, vec_ref, wr_ref, we_ref, keep_ref,
        u_ref, by_ref, before_ref, states_ref, mixed_ref, *scratch,
    )


def backward_step(
    d_res_ref, xy_ref, ow_ref, taps_ref, vec_ref, wr_ref, we_ref, keep_ref,
    u_ref, u_prev_ref, by_ref, before_ref, states_ref,
    d_xy_ref, taps_out, vec_out, wr_out, we_out,
    window, conv, conv_low, rate, entry, d_mixed, d_conv, g_rate, g_entry, carry, sums,
):
    rows, chans = d_res_ref.shape[0], u_ref.shape[1]
    step_id = pl.program_id(0)

    @pl.when(step_id == 0)
    def _():
        d_conv[pl.ds(rows, 8), :] = jnp.zeros_like(d_conv[pl.ds(rows, 8), :])
        carry[...] = jnp.zeros_like(carry)
        sums[...] = jnp.zeros_like(sums)
        wr_out[...] = jnp.zeros_like(wr_out)
        we_out[...] = jnp.zeros_like(we_out)

    @pl.when(step_id > 0)
    def _():
        d_conv[pl.ds(rows, 8), :] = d_conv[0:8, :]

    d_mixed[...] = dot_plain(d_res_ref[...], ow_ref[...])
    window[0:8, :] = u_prev_ref[8:16, :].astype(jnp.float32)
    window[pl.ds(8, rows), :] = u_ref[...].astype(jnp.float32)

    def conv_step(j, unused):
        at = pl.multiple_of(j * CHUNK, CHUNK)
        made = conv_rows(
            window[pl.ds(at, CHUNK + 8), :], keep_ref[pl.ds(at, CHUNK), :],
            taps_ref[...], vec_ref[0:1, :],
        )
        conv[pl.ds(at, CHUNK), :] = made
        conv_low[pl.ds(at, CHUNK), :] = made.astype(jnp.bfloat16)
        return unused

    lax.fori_loop(0, rows // CHUNK, conv_step, 0, unroll=UNROLL)
    rate[...] = dot_plain(conv_low[...], wr_ref[...]) + vec_ref[1:2, :]
    entry[...] = dot_plain(conv_low[...], we_ref[...]) + vec_ref[2:3, :]

    def fold(value):
        return sum_eight(value)

    def scan_step(j, after):
        at = pl.multiple_of(rows - CHUNK - j * CHUNK, CHUNK)
        here = pl.ds(at, CHUNK)
        carried = keep_ref[here, 0:1]
        rate_gate = jax.nn.sigmoid(rate[here, :])
        entry_gate = jax.nn.sigmoid(entry[here, :])
        log_decay = rate_gate * vec_ref[3:4, :]
        exp_decay = jnp.exp(log_decay)
        exp_twice = exp_decay * exp_decay
        lost = one_minus_exp(2.0 * log_decay, exp_twice)
        inverse = lax.rsqrt(jnp.maximum(lost, 1e-30))
        drop = lost * inverse
        scaling = (1.0 - carried) + carried * drop
        decays = exp_decay * carried
        gelu_y, slope_y = gelu_both(by_ref[here, :])
        through = d_mixed[here, :]
        d_states = (through * gelu_y).astype(jnp.bfloat16).astype(jnp.float32)
        d_xy_ref[here, chans:] = (
            through * states_ref[here, :].astype(jnp.float32) * slope_y
        ).astype(jnp.bfloat16)
        passed = scan_up(decays, decays * d_states, after)
        last = lax.broadcasted_iota(jnp.int32, passed.shape, 0) == CHUNK - 1
        adjoint = d_states + jnp.where(last, after, pltpu.roll(passed, CHUNK - 1, 0))
        convolved = conv[here, :]
        gated = adjoint * entry_gate
        g_log = adjoint * before_ref[here, :] * decays - gated * convolved * (
            carried * (exp_twice * inverse)
        )
        g_pre_rate = g_log * vec_ref[3:4, :] * (rate_gate * (1.0 - rate_gate))
        direct = gated * scaling
        g_pre_entry = direct * convolved * (1.0 - entry_gate)
        d_conv[here, :] = direct
        g_rate[here, :] = g_pre_rate.astype(jnp.bfloat16)
        g_entry[here, :] = g_pre_entry.astype(jnp.bfloat16)
        sums[8:16, :] += fold(g_pre_rate)
        sums[16:24, :] += fold(g_pre_entry)
        sums[24:32, :] += fold(g_log * rate_gate)
        return passed[0:1, :]

    carry[0:1, :] = lax.fori_loop(0, rows // CHUNK, scan_step, carry[0:1, :], unroll=UNROLL)
    wr_out[...] += contract_first(conv_low[...], g_rate[...])
    we_out[...] += contract_first(conv_low[...], g_entry[...])
    d_conv[0:rows, :] += contract_last(g_rate[...], wr_ref[...]) + contract_last(
        g_entry[...], we_ref[...]
    )

    def back_step(j, unused):
        at = pl.multiple_of(j * CHUNK, CHUNK)
        here = pl.ds(at, CHUNK)
        keep = keep_ref[here, :]
        ahead = d_conv[pl.ds(at, CHUNK + 8), :]
        behind = window[pl.ds(at, CHUNK + 8), :]
        now = ahead[0:CHUNK]
        total = taps_ref[0:1, :] * now
        sums[0:8, :] += fold(now)
        sums[32:40, :] += fold(now * behind[8:])
        for offset in range(1, 4):
            total = total + taps_ref[offset : offset + 1, :] * (
                keep[:, 3 + offset : 4 + offset] * ahead[offset : offset + CHUNK]
            )
            base = 32 + 8 * offset
            sums[base : base + 8, :] += fold(
                now * (keep[:, offset : offset + 1] * behind[8 - offset : 8 - offset + CHUNK])
            )
        d_xy_ref[here, :chans] = total.astype(jnp.bfloat16)
        return unused

    lax.fori_loop(0, rows // CHUNK, back_step, 0, unroll=UNROLL)

    @pl.when(step_id == pl.num_programs(0) - 1)
    def _():
        vec_out[...] = jnp.zeros_like(vec_out)
        for place in range(4):
            vec_out[place : place + 1, :] = jnp.sum(
                sums[8 * place : 8 * place + 8, :], axis=0, keepdims=True
            )
            taps_out[place : place + 1, :] = jnp.sum(
                sums[32 + 8 * place : 40 + 8 * place, :], axis=0, keepdims=True
            )

    return contract_last(d_xy_ref[...], xy_ref[...]).astype(jnp.bfloat16)


def backward_body(
    d_res_ref, xy_ref, ow_ref, taps_ref, vec_ref, wr_ref, we_ref, keep_ref,
    u_ref, u_prev_ref, by_ref, before_ref, states_ref,
    d_xy_ref, part_ref, *rest,
):
    part_ref[...] = backward_step(
        d_res_ref, xy_ref, ow_ref, taps_ref, vec_ref, wr_ref, we_ref, keep_ref,
        u_ref, u_prev_ref, by_ref, before_ref, states_ref, d_xy_ref, *rest,
    )


def whole(shape):
    return pl.BlockSpec(shape, lambda i: (0,) * len(shape))


def mixer_forward(normed, xy, ow, taps, vec, wr, we, keep, rows):
    length, width = normed.shape
    chans = ow.shape[1]
    tile = lambda columns: pl.BlockSpec((rows, columns), lambda i: (i, 0))
    return pl.pallas_call(
        forward_body,
        grid=(length // rows,),
        in_specs=[
            tile(width), whole(xy.shape), whole(ow.shape), whole(taps.shape),
            whole(vec.shape), whole(wr.shape), whole(we.shape), tile(keep.shape[1]),
        ],
        out_specs=[tile(chans)] * 5 + [tile(width)],
        out_shape=[
            jax.ShapeDtypeStruct((length, chans), jnp.bfloat16),
            jax.ShapeDtypeStruct((length, chans), jnp.float32),
            jax.ShapeDtypeStruct((length, chans), jnp.float32),
            jax.ShapeDtypeStruct((length, chans), jnp.bfloat16),
            jax.ShapeDtypeStruct((length, chans), jnp.bfloat16),
            jax.ShapeDtypeStruct((length, width), jnp.bfloat16),
        ],
        scratch_shapes=[
            pltpu.VMEM((rows + 8, chans), jnp.float32),
            pltpu.VMEM((rows, chans), jnp.float32),
            pltpu.VMEM((rows, chans), jnp.bfloat16),
            pltpu.VMEM((rows, chans), jnp.float32),
            pltpu.VMEM((rows, chans), jnp.float32),
            pltpu.VMEM((8, chans), jnp.float32),
        ],
        compiler_params=pltpu.CompilerParams(vmem_limit_bytes=48 * 2**20),
        cost_estimate=pl.CostEstimate(
            flops=6 * length * width * chans,
            bytes_accessed=4 * length * width + 30 * length * chans,
            transcendentals=6 * length * chans,
        ),
        name="mixer_forward",
    )(normed, xy, ow, taps, vec, wr, we, keep)


def mixer_backward(d_res, xy, ow, taps, vec, wr, we, keep, u, by, before, states, rows):
    length, width = d_res.shape
    chans = ow.shape[1]
    blocks = length // rows
    tile = lambda columns: pl.BlockSpec((rows, columns), lambda i: (blocks - 1 - i, 0))
    ahead = pl.BlockSpec(
        (16, chans), lambda i: (jnp.maximum((blocks - 1 - i) * (rows // 16) - 1, 0), 0)
    )
    return pl.pallas_call(
        backward_body,
        grid=(blocks,),
        in_specs=[
            tile(width), whole(xy.shape), whole(ow.shape), whole(taps.shape),
            whole(vec.shape), whole(wr.shape), whole(we.shape), tile(keep.shape[1]),
            tile(chans), ahead, tile(chans), tile(chans), tile(chans),
        ],
        out_specs=[
            tile(2 * chans), tile(width), whole(taps.shape), whole(vec.shape),
            whole(wr.shape), whole(we.shape),
        ],
        out_shape=[
            jax.ShapeDtypeStruct((length, 2 * chans), jnp.bfloat16),
            jax.ShapeDtypeStruct((length, width), jnp.bfloat16),
            jax.ShapeDtypeStruct(taps.shape, jnp.float32),
            jax.ShapeDtypeStruct(vec.shape, jnp.float32),
            jax.ShapeDtypeStruct(wr.shape, jnp.float32),
            jax.ShapeDtypeStruct(we.shape, jnp.float32),
        ],
        scratch_shapes=[
            pltpu.VMEM((rows + 8, chans), jnp.float32),
            pltpu.VMEM((rows, chans), jnp.float32),
            pltpu.VMEM((rows, chans), jnp.bfloat16),
            pltpu.VMEM((rows, chans), jnp.float32),
            pltpu.VMEM((rows, chans), jnp.float32),
            pltpu.VMEM((rows, chans), jnp.float32),
            pltpu.VMEM((rows + 8, chans), jnp.float32),
            pltpu.VMEM((rows, chans), jnp.bfloat16),
            pltpu.VMEM((rows, chans), jnp.bfloat16),
            pltpu.VMEM((8, chans), jnp.float32),
            pltpu.VMEM((64, chans), jnp.float32),
        ],
        compiler_params=pltpu.CompilerParams(vmem_limit_bytes=48 * 2**20),
        cost_estimate=pl.CostEstimate(
            flops=6 * length * width * chans,
            bytes_accessed=4 * length * width + 30 * length * chans,
            transcendentals=6 * length * chans,
        ),
        name="mixer_backward",
    )(d_res, xy, ow, taps, vec, wr, we, keep, u, u, by, before, states)


def keep_columns(resets):
    length = resets.shape[1]
    position = lax.broadcasted_iota(jnp.int32, resets.shape, 1)
    starts = jnp.maximum(resets, (position == 0).astype(jnp.int32)).astype(jnp.float32)
    carried = (1.0 - starts).reshape(-1)
    seqs = resets.shape[0]

    def back(values, by):
        values = values.reshape(seqs, length)
        return jnp.pad(values, ((0, 0), (by, 0)))[:, :length].reshape(-1)

    def ahead(values, by):
        values = values.reshape(seqs, length)
        return jnp.pad(values, ((0, 0), (0, by)))[:, by:].reshape(-1)

    one = carried
    two = one * back(carried, 1)
    three = two * back(carried, 2)
    return jnp.stack(
        [carried, one, two, three, ahead(one, 1), ahead(two, 2), ahead(three, 3), carried], axis=1
    )


def block_diagonal(blocks, chans):
    heads, width, unused = blocks.shape
    rows = [
        jnp.pad(blocks[h], ((0, 0), (h * width, chans - (h + 1) * width))) for h in range(heads)
    ]
    full = jnp.concatenate(rows, axis=0)
    return jnp.pad(full, ((0, chans - heads * width), (0, 0)))


def diagonal_blocks(full, heads, width):
    return jnp.stack(
        [full[h * width : (h + 1) * width, h * width : (h + 1) * width] for h in range(heads)]
    )


MESH = pl.DeviceIdType.MESH
ANYWHERE = pl.BlockSpec(memory_space=pl.ANY)
IN_VMEM = pl.BlockSpec(memory_space=pltpu.VMEM)
LINE = 4
PLANE = 8
PIECES = 4


def send_to(src, dst, sent, arrived, axis, target):
    return pltpu.make_async_remote_copy(
        src_ref=src,
        dst_ref=dst,
        send_sem=sent,
        recv_sem=arrived,
        device_id={axis: target},
        device_id_type=MESH,
    )


def sibling_of(h):
    return h + 1 - 2 * lax.rem(h, 2)


def across_of(h):
    return h + 2 - 4 * lax.rem(lax.div(h, 2), 2)


def along_of(h):
    return lax.rem(h + 4, PLANE)


def meet(row_line, plane):
    r, h = lax.axis_index("row"), lax.axis_index("head")
    barrier = pltpu.get_barrier_semaphore()
    count = 0
    if row_line:
        for step in range(1, LINE):
            pl.semaphore_signal(
                barrier, inc=1, device_id={"row": lax.rem(r + step, LINE)}, device_id_type=MESH
            )
        count += LINE - 1
    if plane == "all":
        for step in range(1, PLANE):
            pl.semaphore_signal(
                barrier, inc=1, device_id={"head": lax.rem(h + step, PLANE)}, device_id_type=MESH
            )
        count += PLANE - 1
    if plane == "near":
        for target in (sibling_of(h), across_of(h), along_of(h)):
            pl.semaphore_signal(barrier, inc=1, device_id={"head": target}, device_id_type=MESH)
        count += 3
    pl.semaphore_wait(barrier, count)


class LineGather:
    semaphores = (
        pltpu.SemaphoreType.DMA((LINE,)),
        pltpu.SemaphoreType.DMA((LINE,)),
        pltpu.SemaphoreType.DMA((2,)),
    )

    def __init__(self, shard, full, sent, arrived, other):
        self.r = lax.axis_index("row")
        self.shard, self.full, self.sent, self.arrived, self.other = (
            shard, full, sent, arrived, other,
        )

    def near(self, t):
        gap = self.r - t
        return (gap != 0) & (gap < 3) & (gap > -3)

    def own(self, t):
        return send_to(
            self.shard, self.full.at[self.r], self.sent.at[t], self.arrived.at[self.r], "row", t
        )

    def handed(self, origin, target):
        return send_to(
            self.full.at[origin], self.full.at[origin], self.other.at[0], self.arrived.at[origin],
            "row", target,
        )

    def local(self):
        return pltpu.make_async_copy(self.shard, self.full.at[self.r], self.other.at[1])

    def start(self):
        for t in range(LINE):

            @pl.when(self.near(t))
            def _(t=t):
                self.own(t).start()

        self.local().start()

    def forward(self):
        for me, origin, target in ((2, 0, 3), (1, 3, 0)):

            @pl.when(self.r == me)
            def _(origin=origin, target=target):
                copy = self.handed(origin, target)
                copy.wait_recv()
                copy.start()

    def finish(self):
        r = self.r
        for t in range(LINE):
            known = (r == t) | ((r == 2) & (t == 0)) | ((r == 1) & (t == 3))

            @pl.when(jnp.logical_not(known))
            def _(t=t):
                self.handed(t, t).wait_recv()

            @pl.when(self.near(t))
            def _(t=t):
                self.own(t).wait_send()

        for me, origin, target in ((2, 0, 3), (1, 3, 0)):

            @pl.when(r == me)
            def _(origin=origin, target=target):
                self.handed(origin, target).wait_send()

        self.local().wait()


class LineReduce:
    semaphores = (
        pltpu.SemaphoreType.DMA((LINE,)),
        pltpu.SemaphoreType.DMA((LINE,)),
        pltpu.SemaphoreType.DMA((2,)),
    )

    @staticmethod
    def buffers(rows, width):
        return [
            pltpu.VMEM((LINE, rows, width), jnp.bfloat16),
            pltpu.VMEM((rows, width), jnp.bfloat16),
        ]

    def __init__(self, parts, landed, passed, sent, arrived, other):
        self.r = lax.axis_index("row")
        self.parts, self.landed, self.passed = parts, landed, passed
        self.sent, self.arrived, self.other = sent, arrived, other

    def to_pass(self, me, origin, via):
        return send_to(
            self.parts.at[origin], self.passed, self.sent.at[origin], self.other.at[0], "row", via
        )

    def direct(self, t):
        return send_to(
            self.parts.at[t], self.landed.at[self.r], self.sent.at[t], self.arrived.at[self.r],
            "row", t,
        )

    def added(self, t):
        return send_to(
            self.passed, self.landed.at[self.r], self.sent.at[t], self.arrived.at[self.r], "row", t
        )

    def plain(self, t):
        r = self.r
        ends = ((r == 0) & (t == 3)) | ((r == 3) & (t == 0))
        added = ((r == 1) & (t == 3)) | ((r == 2) & (t == 0))
        return jnp.logical_not(ends | added | (r == t))

    def start(self):
        for me, end, via in ((0, 3, 1), (3, 0, 2)):

            @pl.when(self.r == me)
            def _(me=me, end=end, via=via):
                self.to_pass(me, end, via).start()

        for t in range(LINE):

            @pl.when(self.plain(t))
            def _(t=t):
                self.direct(t).start()

    def forward(self):
        for me, end in ((1, 3), (2, 0)):

            @pl.when(self.r == me)
            def _(me=me, end=end):
                self.to_pass(me, end, end).wait_recv()
                rows = self.passed.shape[0]
                step = 64

                def add(i, unused):
                    at = pl.ds(pl.multiple_of(i * step, step), step)
                    self.passed[at, :] = (
                        self.parts[end, at, :].astype(jnp.float32)
                        + self.passed[at, :].astype(jnp.float32)
                    ).astype(jnp.bfloat16)
                    return unused

                lax.fori_loop(0, rows // step, add, 0)
                self.added(end).start()

    def finish(self, write):
        r = self.r
        for t in range(LINE):

            @pl.when(jnp.logical_not(unsent_to(r, t)))
            def _(t=t):
                send_to(
                    self.parts.at[t], self.landed.at[t], self.sent.at[t], self.arrived.at[t],
                    "row", t,
                ).wait_recv()

        def total_of(sources):
            step = 32

            def add(i, unused):
                at = pl.ds(pl.multiple_of(i * step, step), step)
                total = self.parts[r, at, :].astype(jnp.float32)
                for t in sources:
                    total = total + self.landed[t, at, :].astype(jnp.float32)
                write(at, total)
                return unused

            lax.fori_loop(0, self.passed.shape[0] // step, add, 0)

        at_end = (r == 0) | (r == 3)

        @pl.when(at_end)
        def _():
            total_of((1, 2))

        @pl.when(jnp.logical_not(at_end))
        def _():
            total_of((0, 3, 3 - r))

        for me, end, via in ((0, 3, 1), (3, 0, 2)):

            @pl.when(r == me)
            def _(me=me, end=end, via=via):
                self.to_pass(me, end, via).wait_send()

        for t in range(LINE):

            @pl.when(jnp.logical_not(unsent_to(r, t)))
            def _(t=t):
                self.direct(t).wait_send()


def unsent_to(r, t):
    return ((r == 0) & (t == 3)) | ((r == 3) & (t == 0)) | (r == t)


class PlaneGather:
    semaphores = (
        pltpu.SemaphoreType.DMA((PIECES, 7)),
        pltpu.SemaphoreType.DMA((PIECES, 7)),
        pltpu.SemaphoreType.DMA((1,)),
    )
    first = tuple(range(PIECES // 2))
    second = tuple(range(PIECES // 2, PIECES))

    def __init__(self, block, full, sent, arrived, other):
        h = lax.axis_index("head")
        self.h, self.side, self.x, self.y = h, sibling_of(h), across_of(h), along_of(h)
        self.far = across_of(self.y)
        self.block, self.full = block, full
        self.sent, self.arrived, self.other = sent, arrived, other
        self.rows = block.shape[0] // PIECES

    def piece(self, owner, c):
        return self.full.at[owner, pl.ds(c * self.rows, self.rows)]

    def own(self, c, lane, target):
        return send_to(
            self.block.at[pl.ds(c * self.rows, self.rows)], self.piece(self.h, c),
            self.sent.at[c, lane], self.arrived.at[c, lane], "head", target,
        )

    def hand(self, owner, c, lane, target):
        return send_to(
            self.piece(owner, c), self.piece(owner, c), self.sent.at[c, lane],
            self.arrived.at[c, lane], "head", target,
        )

    def local(self):
        return pltpu.make_async_copy(self.block, self.full.at[self.h], self.other.at[0])

    def start(self):
        for a, b in zip(self.first, self.second):
            self.own(a, 1, self.x).start()
            self.own(b, 2, self.y).start()
        for a, b in zip(self.first, self.second):
            self.own(b, 1, self.x).start()
            self.own(a, 2, self.y).start()
        for c in range(PIECES):
            self.own(c, 0, self.side).start()
        self.local().start()

    def relay(self, place):
        a, b = self.first[place], self.second[place]
        self.hand(self.x, a, 1, self.x).wait_recv()
        self.hand(self.x, a, 3, self.y).start()
        self.hand(self.x, a, 4, self.side).start()
        self.hand(self.y, b, 2, self.y).wait_recv()
        self.hand(self.y, b, 3, self.x).start()
        self.hand(self.y, b, 5, self.side).start()

    def rest(self):
        for a, b in zip(self.first, self.second):
            self.hand(self.x, b, 1, self.x).wait_recv()
            self.hand(self.x, b, 4, self.side).start()
            self.hand(self.y, a, 2, self.y).wait_recv()
            self.hand(self.y, a, 5, self.side).start()

    def end(self):
        for pair in zip(self.first, self.second):
            for c in pair:
                self.hand(self.far, c, 3, self.side).wait_recv()
                self.hand(self.far, c, 6, self.side).start()
        side = self.side
        for c in range(PIECES):
            for owner, lane in (
                (side, 0), (across_of(side), 4), (along_of(side), 5),
                (across_of(along_of(side)), 6),
            ):
                self.hand(owner, c, lane, side).wait_recv()
        for c in range(PIECES):
            for lane in range(7):
                self.own(c, lane, side).wait_send()
        self.local().wait()


class PlaneReduce:
    semaphores = (
        pltpu.SemaphoreType.DMA((4,)),
        pltpu.SemaphoreType.DMA((4,)),
        pltpu.SemaphoreType.DMA((4, 2)),
        pltpu.SemaphoreType.DMA((2, 2)),
        pltpu.SemaphoreType.DMA((2,)),
    )

    @staticmethod
    def buffers(rows, width):
        return [
            pltpu.VMEM((4, rows, width), jnp.bfloat16),
            pltpu.VMEM((4, rows, width), jnp.bfloat16),
            pltpu.VMEM((4, rows, width), jnp.bfloat16),
            pltpu.VMEM((2, rows // 2, width), jnp.bfloat16),
            pltpu.VMEM((2, rows, width), jnp.bfloat16),
        ]

    def __init__(
        self, staged, beside, mine, relayed, landed,
        side_sent, side_arrived, sent, arrived, relay_arrived,
    ):
        h = lax.axis_index("head")
        self.h, self.core, self.chip = h, lax.rem(h, 2), lax.div(h, 2)
        self.staged, self.beside, self.mine = staged, beside, mine
        self.relayed, self.landed = relayed, landed
        self.side_sent, self.side_arrived = side_sent, side_arrived
        self.sent, self.arrived, self.relay_arrived = sent, arrived, relay_arrived
        self.half = mine.shape[1] // 2

    def aside(self, chip):
        return send_to(
            self.staged.at[chip], self.beside.at[chip], self.side_sent.at[chip],
            self.side_arrived.at[chip], "head", sibling_of(self.h),
        )

    def relation(self, chip):
        flip_x = lax.rem(chip + self.chip, 2)
        flip_y = lax.rem(lax.div(chip, 2) + lax.div(self.chip, 2), 2)
        return flip_x + 2 * flip_y

    def part(self, half):
        return pl.ds(half * self.half, self.half)

    def home(self, chip, way, half):
        return send_to(
            self.mine.at[chip, self.part(half)], self.landed.at[way, self.part(half)],
            self.sent.at[chip, half], self.arrived.at[way, half], "head",
            (across_of, along_of)[way](self.h),
        )

    def opposite(self, chip, half):
        return send_to(
            self.mine.at[chip, self.part(half)], self.relayed.at[half], self.sent.at[chip, half],
            self.relay_arrived.at[half], "head", (along_of, across_of)[half](self.h),
        )

    def put(self, block, value):
        chip, core = lax.div(block, 2), lax.rem(block, 2)

        @pl.when(core == self.core)
        def _():
            self.mine[chip] = value

        @pl.when(core != self.core)
        def _():
            self.staged[chip] = value
            self.aside(chip).start()

    def pass_on(self, block):
        chip, core = lax.div(block, 2), lax.rem(block, 2)

        @pl.when(core == self.core)
        def _():
            self.aside(chip).wait_recv()
            step = 32

            def add(i, unused):
                at = pl.ds(pl.multiple_of(i * step, step), step)
                self.mine[chip, at, :] = (
                    self.mine[chip, at, :].astype(jnp.float32)
                    + self.beside[chip, at, :].astype(jnp.float32)
                ).astype(jnp.bfloat16)
                return unused

            lax.fori_loop(0, 2 * self.half // step, add, 0)
            relation = self.relation(chip)

            @pl.when(relation == 1)
            def _():
                self.home(chip, 0, 1).start()

            @pl.when(relation == 2)
            def _():
                self.home(chip, 1, 0).start()

            @pl.when(relation == 3)
            def _():
                self.opposite(chip, 0).start()
                self.opposite(chip, 1).start()

    def relay(self, block):
        chip, core = lax.div(block, 2), lax.rem(block, 2)
        for way in (0, 1):

            @pl.when((core == self.core) & (self.relation(chip) == way + 1))
            def _(way=way):
                self.opposite(chip, way).wait_recv()
                step = 32

                def add(i, unused):
                    at = pl.ds(pl.multiple_of(i * step, step), step)
                    here = pl.ds(pl.multiple_of(way * self.half + i * step, step), step)
                    self.mine[chip, here, :] = (
                        self.mine[chip, here, :].astype(jnp.float32)
                        + self.relayed[way, at, :].astype(jnp.float32)
                    ).astype(jnp.bfloat16)
                    return unused

                lax.fori_loop(0, self.half // step, add, 0)
                self.home(chip, way, way).start()

    def arrive(self):
        for way in (0, 1):
            for half in (0, 1):
                self.home(self.chip, way, half).wait_recv()

    def total(self, at):
        value = self.mine[self.chip, at, :].astype(jnp.float32)
        return (
            value
            + self.landed[0, at, :].astype(jnp.float32)
            + self.landed[1, at, :].astype(jnp.float32)
        )

    def finish(self):
        for chip in range(4):
            self.aside(chip).wait_send()

            @pl.when(chip != self.chip)
            def _(chip=chip):
                self.home(chip, 0, 0).wait_send()
                self.home(chip, 0, 1).wait_send()


def norm_apply(rows, gain):
    return rows * lax.rsqrt(jnp.mean(rows * rows, axis=-1, keepdims=True) + EPSILON) * gain


def gather(values, axis_name, axis):
    return lax.all_gather(values, axis_name, axis=axis, tiled=True)


def scatter(values, axis_name, axis):
    return lax.psum_scatter(values, axis_name, scatter_dimension=axis, tiled=True)

def norm_rows(rows, gain):
    return rows * lax.rsqrt(jnp.mean(rows * rows, axis=-1, keepdims=True) + EPSILON) * gain


def open_body(
    x_ref, tile_ref, xy_shard, out_shard, full, xy_full, out_full, gains_ref,
    normed, column, spread, gain_sent, gain_arrived, wide_sent, wide_arrived, *semaphores,
):
    r, h = lax.axis_index("row"), lax.axis_index("head")
    lines = [
        LineGather(src, dst, *semaphores[3 * k : 3 * k + 3])
        for k, (src, dst) in enumerate(((xy_shard, xy_full), (out_shard, out_full)))
    ]
    plane = PlaneGather(normed, full, *semaphores[6:9])
    meet(True, "all")

    def up_line(t):
        return send_to(
            column.at[r], column.at[r], gain_sent.at[t], gain_arrived.at[r], "row", t
        )

    def from_line(t):
        return send_to(
            column.at[t], column.at[t], gain_sent.at[t], gain_arrived.at[t], "row", t
        )

    def over_plane(step, owner):
        return send_to(
            column, spread.at[owner], wide_sent.at[step], wide_arrived.at[owner], "head",
            lax.rem(h + step, PLANE),
        )

    column[r] = tile_ref[...]
    for step in range(1, LINE):
        up_line(lax.rem(r + step, LINE)).start()
    for line in lines:
        line.start()
    for step in range(1, LINE):
        from_line(lax.rem(r + step, LINE)).wait_recv()
    for step in range(1, PLANE):
        over_plane(step, h).start()
    spread[h] = column[...]
    for step in range(1, PLANE):
        over_plane(step, lax.rem(h + step, PLANE)).wait_recv()

    share = tile_ref.shape[1] // 2
    low = lax.broadcasted_iota(jnp.int32, (1, 2 * share), 1) < share
    for line_place in range(LINE):
        for pair in range(PLANE // 2):
            even = spread[2 * pair, line_place][0:1, :]
            odd = spread[2 * pair + 1, line_place][0:1, :]
            at = (line_place * (PLANE // 2) + pair) * 2 * share
            gains_ref[0:1, at : at + 2 * share] = jnp.where(low, even, pltpu.roll(odd, share, 1))
            gains_ref[1:2, at : at + 2 * share] = jnp.where(low, pltpu.roll(even, share, 1), odd)

    def make(i, unused):
        at = pl.ds(pl.multiple_of(i * CHUNK, CHUNK), CHUNK)
        normed[at, :] = norm_rows(x_ref[at, :].astype(jnp.float32), gains_ref[0:1, :]).astype(
            jnp.bfloat16
        )
        return unused

    lax.fori_loop(0, x_ref.shape[0] // CHUNK, make, 0)
    plane.start()
    plane.relay(0)
    lines[0].forward()
    plane.relay(1)
    plane.rest()
    plane.end()
    for line in lines[1:]:
        line.forward()
    for line in lines:
        line.finish()
    for step in range(1, LINE):
        up_line(lax.rem(r + step, LINE)).wait_send()
    for step in range(1, PLANE):
        over_plane(step, h).wait_send()


def open_block(layer_in, tile, weights):
    rows, width = layer_in.shape
    return pl.pallas_call(
        open_body,
        in_specs=[IN_VMEM, IN_VMEM] + [ANYWHERE] * 2,
        out_specs=[ANYWHERE] * 3 + [IN_VMEM],
        out_shape=[jax.ShapeDtypeStruct((PLANE, rows, width), jnp.bfloat16)]
        + [jax.ShapeDtypeStruct((LINE,) + item.shape, item.dtype) for item in weights]
        + [jax.ShapeDtypeStruct((2, width), jnp.float32)],
        scratch_shapes=[
            pltpu.VMEM((rows, width), jnp.bfloat16),
            pltpu.VMEM((LINE,) + tile.shape, jnp.float32),
            pltpu.VMEM((PLANE, LINE) + tile.shape, jnp.float32),
            pltpu.SemaphoreType.DMA((LINE,)),
            pltpu.SemaphoreType.DMA((LINE,)),
            pltpu.SemaphoreType.DMA((PLANE,)),
            pltpu.SemaphoreType.DMA((PLANE,)),
            *(LineGather.semaphores * 2),
            *PlaneGather.semaphores,
        ],
        compiler_params=pltpu.CompilerParams(
            collective_id=0, has_side_effects=True, vmem_limit_bytes=24 * 2**20
        ),
        name="open_block",
    )(layer_in, tile, *weights)


def forward_linked_body(
    normed_ref, xy_ref, ow_ref, taps_ref, vec_ref, wr_ref, we_ref, keep_ref,
    x_ref, gain_ref, shard,
    u_ref, by_ref, before_ref, states_ref, mixed_ref, residual_ref, two_ref, gathered,
    window, conv, conv_low, rate, entry, carry, *links,
):
    step = pl.program_id(0)
    plane = PlaneReduce(*links[:10])
    line = LineGather(shard, gathered, *links[10:13])

    @pl.when(step == 0)
    def _():
        meet(True, "near")
        line.start()

    @pl.when(step > 0)
    def _():
        plane.pass_on(step - 1)

    @pl.when(step > 2)
    def _():
        plane.relay(step - 3)

    value = forward_step(
        normed_ref, xy_ref, ow_ref, taps_ref, vec_ref, wr_ref, we_ref, keep_ref,
        u_ref, by_ref, before_ref, states_ref, mixed_ref,
        window, conv, conv_low, rate, entry, carry,
    )
    plane.put(step, value)

    @pl.when(step == 6)
    def _():
        line.forward()

    @pl.when(step == PLANE - 1)
    def _():
        plane.relay(step - 2)
        plane.pass_on(step)
        plane.relay(step - 1)
        plane.relay(step)
        plane.arrive()

        def make(i, unused):
            at = pl.ds(pl.multiple_of(i * CHUNK, CHUNK), CHUNK)
            residual = x_ref[at, :].astype(jnp.float32) + plane.total(at)
            residual_ref[at, :] = residual
            two_ref[at, :] = norm_rows(residual, gain_ref[...]).astype(jnp.bfloat16)
            return unused

        lax.fori_loop(0, x_ref.shape[0] // CHUNK, make, 0)
        plane.finish()
        line.finish()


def forward_linked(normed, xy, ow, taps, vec, wr, we, keep, layer_in, gain, shard):
    length, width = normed.shape
    chans = ow.shape[1]
    rows = length // PLANE
    tile = lambda columns: pl.BlockSpec((rows, columns), lambda i: (i, 0))
    return pl.pallas_call(
        forward_linked_body,
        grid=(PLANE,),
        in_specs=[
            tile(width), whole(xy.shape), whole(ow.shape), whole(taps.shape),
            whole(vec.shape), whole(wr.shape), whole(we.shape), tile(keep.shape[1]),
            whole(layer_in.shape), whole(gain.shape), ANYWHERE,
        ],
        out_specs=[tile(chans)] * 5 + [whole((rows, width))] * 2 + [ANYWHERE],
        out_shape=[
            jax.ShapeDtypeStruct((length, chans), jnp.bfloat16),
            jax.ShapeDtypeStruct((length, chans), jnp.float32),
            jax.ShapeDtypeStruct((length, chans), jnp.float32),
            jax.ShapeDtypeStruct((length, chans), jnp.bfloat16),
            jax.ShapeDtypeStruct((length, chans), jnp.bfloat16),
            jax.ShapeDtypeStruct((rows, width), jnp.float32),
            jax.ShapeDtypeStruct((rows, width), jnp.bfloat16),
            jax.ShapeDtypeStruct((LINE,) + shard.shape, shard.dtype),
        ],
        scratch_shapes=[
            pltpu.VMEM((rows + 8, chans), jnp.float32),
            pltpu.VMEM((rows, chans), jnp.float32),
            pltpu.VMEM((rows, chans), jnp.bfloat16),
            pltpu.VMEM((rows, chans), jnp.float32),
            pltpu.VMEM((rows, chans), jnp.float32),
            pltpu.VMEM((8, chans), jnp.float32),
            *PlaneReduce.buffers(rows, width),
            *PlaneReduce.semaphores,
            *LineGather.semaphores,
        ],
        compiler_params=pltpu.CompilerParams(
            collective_id=1, has_side_effects=True, vmem_limit_bytes=56 * 2**20
        ),
        name="mixer_forward_linked",
    )(normed, xy, ow, taps, vec, wr, we, keep, layer_in, gain, shard)


def ffn_up_body(
    own_two, gate_ref, own_cot, up_shard, down_shard,
    two_out, cot_out, up_out, down_out, gates_out, ups_out, hidden_out, down_parts,
    two, cot, up, gates, ups, hidden, total, copied, *semaphores,
):
    h = lax.axis_index("head")
    rows = own_two.shape[0]
    units = gates.shape[1]
    up_line = LineGather(up_shard, up, *semaphores[0:3])
    down_line = LineGather(down_shard, down_out, *semaphores[3:6])
    two_plane = PlaneGather(own_two, two, *semaphores[6:9])
    cot_plane = PlaneGather(own_cot, cot, *semaphores[9:12])
    outward = [
        pltpu.make_async_copy(src, dst, copied.at[k])
        for k, (src, dst) in enumerate(
            (
                (two, two_out), (cot, cot_out), (up, up_out), (gates, gates_out),
                (ups, ups_out), (hidden, hidden_out),
            )
        )
    ]
    meet(True, "near")
    up_line.start()
    down_line.start()
    two_plane.start()

    def at_block(block):
        return pl.ds(pl.multiple_of(block * rows, rows), rows)

    def make_gates(k, unused):
        block = lax.rem(h + k, PLANE)
        gates[at_block(block), :] = dot_plain(two[block], gate_ref[...])
        return unused

    gates[at_block(h), :] = dot_plain(own_two[...], gate_ref[...])
    two_plane.relay(0)
    two_plane.relay(1)
    two_plane.rest()
    cot_plane.start()
    two_plane.end()
    outward[0].start()
    up_line.forward()
    lax.fori_loop(1, 3, make_gates, 0)
    cot_plane.relay(0)
    lax.fori_loop(3, 6, make_gates, 0)
    cot_plane.relay(1)
    lax.fori_loop(6, PLANE, make_gates, 0)
    outward[3].start()
    cot_plane.rest()
    up_line.finish()
    outward[2].start()

    def make_hidden(block, unused):
        at = at_block(block)
        value = jnp.zeros((rows, units), jnp.float32)
        share = up.shape[1]
        for t in range(LINE):
            value = value + dot_plain(two[block, :, t * share : (t + 1) * share], up[t])
        ups[at, :] = value

        def make(i, unused):
            here = pl.ds(pl.multiple_of(block * rows + i * CHUNK, CHUNK), CHUNK)
            hidden[here, :] = (gelu_only(gates[here, :]) * ups[here, :]).astype(jnp.bfloat16)
            return unused

        lax.fori_loop(0, rows // CHUNK, make, 0, unroll=UNROLL)
        return unused

    lax.fori_loop(0, PLANE, make_hidden, 0)
    outward[4].start()
    outward[5].start()
    cot_plane.end()
    outward[1].start()
    down_line.forward()
    total[...] = contract_first(cot[0], hidden[0:rows, :])

    def add_down(block, unused):
        total[...] += contract_first(cot[block], hidden[at_block(block), :])
        return unused

    lax.fori_loop(1, PLANE, add_down, 0)
    to_parts(total, down_parts)
    down_line.finish()
    for copy in outward:
        copy.wait()


def ffn_up(own_two, gate, own_cot, up_shard, down_shard):
    rows, width = own_two.shape
    share, units = up_shard.shape
    length = rows * PLANE
    group = jax.ShapeDtypeStruct((PLANE, rows, width), jnp.bfloat16)
    weight = jax.ShapeDtypeStruct((LINE, share, units), jnp.bfloat16)
    return pl.pallas_call(
        ffn_up_body,
        in_specs=[IN_VMEM, IN_VMEM, ANYWHERE, ANYWHERE, ANYWHERE],
        out_specs=[ANYWHERE] * 7 + [IN_VMEM],
        out_shape=[
            group,
            group,
            weight,
            weight,
            jax.ShapeDtypeStruct((length, units), jnp.float32),
            jax.ShapeDtypeStruct((length, units), jnp.float32),
            jax.ShapeDtypeStruct((length, units), jnp.bfloat16),
            weight,
        ],
        scratch_shapes=[
            pltpu.VMEM((PLANE, rows, width), jnp.bfloat16),
            pltpu.VMEM((PLANE, rows, width), jnp.bfloat16),
            pltpu.VMEM((LINE, share, units), jnp.bfloat16),
            pltpu.VMEM((length, units), jnp.float32),
            pltpu.VMEM((length, units), jnp.float32),
            pltpu.VMEM((length, units), jnp.bfloat16),
            pltpu.VMEM((width, units), jnp.float32),
            pltpu.SemaphoreType.DMA((6,)),
            *(LineGather.semaphores * 2),
            *(PlaneGather.semaphores * 2),
        ],
        compiler_params=pltpu.CompilerParams(
            collective_id=2, has_side_effects=True, vmem_limit_bytes=60 * 2**20
        ),
        name="ffn_up",
    )(own_two, gate, own_cot, up_shard, down_shard)
def once(shape):
    return pl.BlockSpec(
        shape, lambda i: (0,) * len(shape), pipeline_mode=pl.Buffered(buffer_count=1)
    )


def norm_back(rows, gain, incoming):
    scale = lax.rsqrt(jnp.mean(rows * rows, axis=-1, keepdims=True) + EPSILON)
    scaled = incoming * gain
    inner = jnp.mean(scaled * rows, axis=-1, keepdims=True)
    return scale * scaled - rows * (scale * scale * scale * inner), incoming * rows * scale


def to_parts(total, parts):
    rows = parts.shape[1]
    step = 64

    def move(i, unused):
        at = pl.ds(pl.multiple_of(i * step, step), step)
        for t in range(LINE):
            here = pl.ds(pl.multiple_of(t * rows + i * step, step), step)
            parts[t, at, :] = total[here, :].astype(jnp.bfloat16)
        return unused

    lax.fori_loop(0, rows // step, move, 0)


def ffn_back_body(
    cot_ref, two_ref, gates_ref, ups_ref, gate_ref, up_ref, down_ref, parts,
    residual_ref, own_cot_ref, gain_ref,
    d_ups_ref, gate_parts, down_out, d_res_ref, d_low_ref, gain_out,
    total, d_gates, d_hidden, eight, *links,
):
    step = pl.program_id(0)
    line = LineReduce(parts, *links[:5])
    plane = PlaneReduce(*links[5:])
    rows = cot_ref.shape[0]

    @pl.when(step == 0)
    def _():
        meet(True, "near")
        line.start()
        total[...] = jnp.zeros_like(total)

    @pl.when(step > 0)
    def _():
        plane.pass_on(step - 1)

    @pl.when(step > 2)
    def _():
        plane.relay(step - 3)

    d_hidden[...] = dot_plain(cot_ref[...], down_ref[...])

    def make(i, unused):
        at = pl.ds(pl.multiple_of(i * CHUNK, CHUNK), CHUNK)
        gelu_gate, slope = gelu_both(gates_ref[at, :])
        through = d_hidden[at, :]
        d_gates[at, :] = (through * ups_ref[at, :] * slope).astype(jnp.bfloat16)
        d_ups_ref[at, :] = (through * gelu_gate).astype(jnp.bfloat16)
        return unused

    lax.fori_loop(0, rows // CHUNK, make, 0, unroll=UNROLL)
    value = contract_last(d_gates[...], gate_ref[...]) + contract_last(d_ups_ref[...], up_ref[...])
    plane.put(step, value.astype(jnp.bfloat16))
    total[...] += contract_first(two_ref[...], d_gates[...])

    @pl.when(step == 4)
    def _():
        line.forward()

    @pl.when(step == PLANE - 1)
    def _():
        plane.relay(step - 2)
        plane.pass_on(step)
        plane.relay(step - 1)
        to_parts(total, gate_parts)
        plane.relay(step)
        plane.arrive()
        eight[...] = jnp.zeros_like(eight)

        def back(i, unused):
            at = pl.ds(pl.multiple_of(i * CHUNK, CHUNK), CHUNK)
            d_rows, d_gain = norm_back(residual_ref[at, :], gain_ref[...], plane.total(at))
            d_residual = own_cot_ref[at, :].astype(jnp.float32) + d_rows
            d_res_ref[at, :] = d_residual
            d_low_ref[at, :] = d_residual.astype(jnp.bfloat16)
            eight[...] += sum_eight(d_gain)
            return unused

        lax.fori_loop(0, rows // CHUNK, back, 0)
        gain_out[...] = jnp.sum(eight[...], axis=0, keepdims=True)

        def write(at, value):
            down_out[at, :] = value

        line.finish(write)
        plane.finish()


def ffn_back(
    cot_group, two_group, gates, ups, gate, up, down, parts, residual, own_cot, gain
):
    length, width = cot_group.shape
    units = gate.shape[1]
    rows, share = length // PLANE, width // LINE
    tile = lambda columns: pl.BlockSpec((rows, columns), lambda i: (i, 0))
    return pl.pallas_call(
        ffn_back_body,
        grid=(PLANE,),
        in_specs=[
            tile(width), tile(width), tile(units), tile(units), once(gate.shape),
            once(up.shape), once(down.shape), once(parts.shape), once(residual.shape),
            once(own_cot.shape), once(gain.shape),
        ],
        out_specs=[
            tile(units), once((LINE, share, units)), once((share, units)),
            once((rows, width)), once((rows, width)), once((1, width)),
        ],
        out_shape=[
            jax.ShapeDtypeStruct((length, units), jnp.bfloat16),
            jax.ShapeDtypeStruct((LINE, share, units), jnp.bfloat16),
            jax.ShapeDtypeStruct((share, units), jnp.float32),
            jax.ShapeDtypeStruct((rows, width), jnp.float32),
            jax.ShapeDtypeStruct((rows, width), jnp.bfloat16),
            jax.ShapeDtypeStruct((1, width), jnp.float32),
        ],
        scratch_shapes=[
            pltpu.VMEM((width, units), jnp.float32),
            pltpu.VMEM((rows, units), jnp.bfloat16),
            pltpu.VMEM((rows, units), jnp.float32),
            pltpu.VMEM((8, width), jnp.float32),
            *LineReduce.buffers(share, units),
            *LineReduce.semaphores,
            *PlaneReduce.buffers(rows, width),
            *PlaneReduce.semaphores,
        ],
        compiler_params=pltpu.CompilerParams(
            collective_id=4, has_side_effects=True, vmem_limit_bytes=60 * 2**20
        ),
        name="ffn_back",
    )(cot_group, two_group, gates, ups, gate, up, down, parts, residual, own_cot, gain)


def turn_body(
    two_ref, d_ups_ref, gate_parts, block, mixed_ref,
    up_parts, out_parts, gate_out, full_out,
    full, total, out_total, copied, *links,
):
    step = pl.program_id(0)
    line = LineReduce(gate_parts, *links[:5])
    plane = PlaneGather(block, full, *links[5:])
    rows = two_ref.shape[0]
    outward = pltpu.make_async_copy(full, full_out, copied)

    @pl.when(step == 0)
    def _():
        meet(True, "near")
        line.start()
        plane.start()
        total[...] = jnp.zeros_like(total)

    total[...] += contract_first(two_ref[...], d_ups_ref[...])

    @pl.when(step == PLANE - 3)
    def _():
        plane.relay(0)

    @pl.when(step == PLANE - 1)
    def _():
        plane.relay(1)
        to_parts(total, up_parts)
        plane.rest()
        line.forward()
        plane.end()
        outward.start()
        out_total[...] = contract_first(full[0], mixed_ref[0:rows, :])

        def add(b, unused):
            at = pl.ds(pl.multiple_of(b * rows, rows), rows)
            out_total[...] += contract_first(full[b], mixed_ref[at, :])
            return unused

        lax.fori_loop(1, PLANE, add, 0)
        to_parts(out_total, out_parts)

        def write(at, value):
            gate_out[at, :] = value

        line.finish(write)
        outward.wait()


def turn(two_group, d_ups, gate_parts, block, mixed):
    length, width = two_group.shape
    units, chans = d_ups.shape[1], mixed.shape[1]
    rows, share = length // PLANE, width // LINE
    tile = lambda columns: pl.BlockSpec((rows, columns), lambda i: (i, 0))
    return pl.pallas_call(
        turn_body,
        grid=(PLANE,),
        in_specs=[
            tile(width), tile(units), once(gate_parts.shape), ANYWHERE, once(mixed.shape)
        ],
        out_specs=[
            once(gate_parts.shape), once((LINE, share, chans)), once((share, units)), ANYWHERE
        ],
        out_shape=[
            jax.ShapeDtypeStruct(gate_parts.shape, jnp.bfloat16),
            jax.ShapeDtypeStruct((LINE, share, chans), jnp.bfloat16),
            jax.ShapeDtypeStruct((share, units), jnp.float32),
            jax.ShapeDtypeStruct((PLANE, rows, width), jnp.bfloat16),
        ],
        scratch_shapes=[
            pltpu.VMEM((PLANE, rows, width), jnp.bfloat16),
            pltpu.VMEM((width, units), jnp.float32),
            pltpu.VMEM((width, chans), jnp.float32),
            pltpu.SemaphoreType.DMA,
            *LineReduce.buffers(share, units),
            *LineReduce.semaphores,
            *PlaneGather.semaphores,
        ],
        compiler_params=pltpu.CompilerParams(
            collective_id=5, has_side_effects=True, vmem_limit_bytes=56 * 2**20
        ),
        name="turn",
    )(two_group, d_ups, gate_parts, block, mixed)


def backward_linked_body(
    d_res_ref, xy_ref, ow_ref, taps_ref, vec_ref, wr_ref, we_ref, keep_ref,
    u_ref, u_prev_ref, by_ref, before_ref, states_ref, normed_ref, up_parts, out_parts,
    x_ref, gain_ref, d_residual_ref,
    xy_parts, up_out, out_out, in_grad, gain_out, taps_out, vec_out, wr_out, we_out,
    d_xy, xy_total, eight, *rest,
):
    scratch, links = rest[:11], rest[11:]
    step = pl.program_id(0)
    block = PLANE - 1 - step
    line = LineReduce(up_parts, *links[:5])
    out_line = LineReduce(out_parts, *links[5:10])
    plane = PlaneReduce(*links[10:])

    @pl.when(step == 0)
    def _():
        meet(True, "near")
        line.start()
        out_line.start()
        xy_total[...] = jnp.zeros_like(xy_total)

    @pl.when(step > 0)
    def _():
        plane.pass_on(block + 1)

    @pl.when(step > 2)
    def _():
        plane.relay(block + 3)

    value = backward_step(
        d_res_ref, xy_ref, ow_ref, taps_ref, vec_ref, wr_ref, we_ref, keep_ref,
        u_ref, u_prev_ref, by_ref, before_ref, states_ref, d_xy,
        taps_out, vec_out, wr_out, we_out, *scratch,
    )
    plane.put(block, value)
    xy_total[...] += contract_first(normed_ref[...], d_xy[...])

    @pl.when(step == 4)
    def _():
        line.forward()

    @pl.when(step == PLANE - 1)
    def _():
        plane.relay(block + 2)
        plane.pass_on(block)
        plane.relay(block + 1)
        to_parts(xy_total, xy_parts)
        plane.relay(block)
        out_line.forward()
        plane.arrive()
        eight[...] = jnp.zeros_like(eight)

        def back(i, unused):
            at = pl.ds(pl.multiple_of(i * CHUNK, CHUNK), CHUNK)
            d_rows, d_gain = norm_back(
                x_ref[at, :].astype(jnp.float32), gain_ref[...], plane.total(at)
            )
            in_grad[at, :] = (d_residual_ref[at, :] + d_rows).astype(jnp.bfloat16)
            eight[...] += sum_eight(d_gain)
            return unused

        lax.fori_loop(0, x_ref.shape[0] // CHUNK, back, 0)
        gain_out[...] = jnp.sum(eight[...], axis=0, keepdims=True)

        def write(at, value):
            up_out[at, :] = value

        def write_out(at, value):
            out_out[at, :] = value

        line.finish(write)
        out_line.finish(write_out)
        plane.finish()


def backward_linked(
    d_res, xy, ow, taps, vec, wr, we, keep, u, by, before, states, normed, up_parts, out_parts,
    layer_in, gain, d_residual,
):
    length, width = d_res.shape
    chans, units = ow.shape[1], up_parts.shape[2]
    rows, share = length // PLANE, width // LINE
    tile = lambda columns: pl.BlockSpec((rows, columns), lambda i: (PLANE - 1 - i, 0))
    ahead = pl.BlockSpec(
        (16, chans), lambda i: (jnp.maximum((PLANE - 1 - i) * (rows // 16) - 1, 0), 0)
    )
    return pl.pallas_call(
        backward_linked_body,
        grid=(PLANE,),
        in_specs=[
            tile(width), once(xy.shape), once(ow.shape), once(taps.shape),
            once(vec.shape), once(wr.shape), once(we.shape), tile(keep.shape[1]),
            tile(chans), ahead, tile(chans), tile(chans), tile(chans), tile(width),
            once(up_parts.shape), once(out_parts.shape), once(layer_in.shape), once(gain.shape), once(d_residual.shape),
        ],
        out_specs=[
            once((LINE, share, 2 * chans)), once((share, units)), once((share, chans)),
            once((rows, width)), once((1, width)), once(taps.shape), once(vec.shape),
            once(wr.shape), once(we.shape),
        ],
        out_shape=[
            jax.ShapeDtypeStruct((LINE, share, 2 * chans), jnp.bfloat16),
            jax.ShapeDtypeStruct((share, units), jnp.float32),
            jax.ShapeDtypeStruct((share, chans), jnp.float32),
            jax.ShapeDtypeStruct((rows, width), jnp.bfloat16),
            jax.ShapeDtypeStruct((1, width), jnp.float32),
            jax.ShapeDtypeStruct(taps.shape, jnp.float32),
            jax.ShapeDtypeStruct(vec.shape, jnp.float32),
            jax.ShapeDtypeStruct(wr.shape, jnp.float32),
            jax.ShapeDtypeStruct(we.shape, jnp.float32),
        ],
        scratch_shapes=[
            pltpu.VMEM((rows, 2 * chans), jnp.bfloat16),
            pltpu.VMEM((width, 2 * chans), jnp.float32),
            pltpu.VMEM((8, width), jnp.float32),
            pltpu.VMEM((rows + 8, chans), jnp.float32),
            pltpu.VMEM((rows, chans), jnp.float32),
            pltpu.VMEM((rows, chans), jnp.bfloat16),
            pltpu.VMEM((rows, chans), jnp.float32),
            pltpu.VMEM((rows, chans), jnp.float32),
            pltpu.VMEM((rows, chans), jnp.float32),
            pltpu.VMEM((rows + 8, chans), jnp.float32),
            pltpu.VMEM((rows, chans), jnp.bfloat16),
            pltpu.VMEM((rows, chans), jnp.bfloat16),
            pltpu.VMEM((8, chans), jnp.float32),
            pltpu.VMEM((64, chans), jnp.float32),
            *LineReduce.buffers(share, units),
            *LineReduce.semaphores,
            *LineReduce.buffers(share, chans),
            *LineReduce.semaphores,
            *PlaneReduce.buffers(rows, width),
            *PlaneReduce.semaphores,
        ],
        compiler_params=pltpu.CompilerParams(
            collective_id=6, has_side_effects=True, vmem_limit_bytes=62 * 2**20
        ),
        name="mixer_backward_linked",
    )(
        d_res, xy, ow, taps, vec, wr, we, keep, u, u, by, before, states, normed,
        up_parts, out_parts, layer_in, gain, d_residual,
    )


def close_body(
    hidden_ref, down_ref, xy_parts, residual_ref, gains_ref, small,
    layer_out, xy_out, gains_out, small_out,
    gathered, line_gains, both_gains, plane_gains,
    gain_sent, gain_arrived, wide_sent, wide_arrived, *links,
):
    r, h = lax.axis_index("row"), lax.axis_index("head")
    step = pl.program_id(0)
    xy_line = LineReduce(xy_parts, *links[0:5])
    line = LineGather(small, gathered, *links[5:8])
    plane = PlaneReduce(*links[8:18])

    def to_row(t, owner):
        return send_to(
            gains_ref.at[t], line_gains.at[owner], gain_sent.at[t], gain_arrived.at[owner],
            "row", t,
        )

    def over_plane(place, owner):
        return send_to(
            both_gains, plane_gains.at[owner], wide_sent.at[place], wide_arrived.at[owner],
            "head", lax.rem(h + place, PLANE),
        )

    @pl.when(step == 0)
    def _():
        meet(True, "all")
        for place in range(1, LINE):
            to_row(lax.rem(r + place, LINE), r).start()
        line.start()
        xy_line.start()

    @pl.when(step > 0)
    def _():
        plane.pass_on(step - 1)

    @pl.when(step > 2)
    def _():
        plane.relay(step - 3)

    plane.put(step, contract_last(hidden_ref[...], down_ref[...]).astype(jnp.bfloat16))

    @pl.when(step == 2)
    def _():
        total = gains_ref[r]
        for place in range(1, LINE):
            t = lax.rem(r + place, LINE)
            to_row(t, t).wait_recv()
            total = total + line_gains[t]
        both_gains[...] = total
        for place in range(1, PLANE):
            over_plane(place, h).start()

    @pl.when(step == PLANE - 1)
    def _():
        plane.relay(step - 2)
        plane.pass_on(step)
        plane.relay(step - 1)
        plane.relay(step)
        line.forward()
        xy_line.forward()
        total = both_gains[...]
        for place in range(1, PLANE):
            owner = lax.rem(h + place, PLANE)
            over_plane(place, owner).wait_recv()
            total = total + plane_gains[owner]
        mine = lax.broadcasted_iota(jnp.int32, total.shape, 0) == h
        gains_out[...] = jnp.sum(jnp.where(mine, total, 0.0), axis=0, keepdims=True)
        plane.arrive()

        def make(i, unused):
            at = pl.ds(pl.multiple_of(i * CHUNK, CHUNK), CHUNK)
            layer_out[at, :] = (residual_ref[at, :] + plane.total(at)).astype(jnp.bfloat16)
            return unused

        lax.fori_loop(0, residual_ref.shape[0] // CHUNK, make, 0)
        line.finish()
        total = gathered[0].astype(jnp.float32)
        for t in range(1, LINE):
            total = total + gathered[t].astype(jnp.float32)
        small_out[...] = total

        def write(at, value):
            xy_out[at, :] = value

        xy_line.finish(write)
        plane.finish()
        for place in range(1, LINE):
            to_row(lax.rem(r + place, LINE), r).wait_send()
        for place in range(1, PLANE):
            over_plane(place, h).wait_send()


def close_block(hidden, down, xy_parts, residual, gains, small):
    length, units = hidden.shape
    rows, width = residual.shape
    share, columns = xy_parts.shape[1:]
    return pl.pallas_call(
        close_body,
        grid=(PLANE,),
        in_specs=[
            pl.BlockSpec((rows, units), lambda i: (i, 0)), once(down.shape),
            once(xy_parts.shape), once(residual.shape), once(gains.shape), once(small.shape),
        ],
        out_specs=[
            once((rows, width)), once((share, columns)), once((1, gains.shape[2])), once(small.shape),
        ],
        out_shape=[
            jax.ShapeDtypeStruct((rows, width), jnp.bfloat16),
            jax.ShapeDtypeStruct((share, columns), jnp.float32),
            jax.ShapeDtypeStruct((1, gains.shape[2]), jnp.float32),
            jax.ShapeDtypeStruct(small.shape, jnp.float32),
        ],
        scratch_shapes=[
            pltpu.VMEM((LINE,) + small.shape, jnp.bfloat16),
            pltpu.VMEM(gains.shape, jnp.float32),
            pltpu.VMEM(gains.shape[1:], jnp.float32),
            pltpu.VMEM((PLANE,) + gains.shape[1:], jnp.float32),
            pltpu.SemaphoreType.DMA((LINE,)),
            pltpu.SemaphoreType.DMA((LINE,)),
            pltpu.SemaphoreType.DMA((PLANE,)),
            pltpu.SemaphoreType.DMA((PLANE,)),
            *LineReduce.buffers(share, columns), *LineReduce.semaphores,
            *LineGather.semaphores,
            *PlaneReduce.buffers(rows, width), *PlaneReduce.semaphores,
        ],
        compiler_params=pltpu.CompilerParams(
            collective_id=7, has_side_effects=True, vmem_limit_bytes=56 * 2**20
        ),
        name="close_block",
    )(hidden, down, xy_parts, residual, gains, small)


def mixer_params(
    conv_weight, conv_bias, rate_weight, rate_bias, entry_weight, entry_bias, decay_param, chans
):
    used = conv_bias.shape[0]
    spare = (0, chans - used)
    decay_wide = jnp.pad(decay_param, spare, constant_values=2.0)
    blank = jnp.zeros((chans,), jnp.float32)
    vec = jnp.stack(
        [
            jnp.pad(conv_bias, spare),
            jnp.pad(rate_bias, spare),
            jnp.pad(entry_bias, spare),
            -8.0 * jax.nn.softplus(-decay_wide),
            blank,
            blank,
            blank,
            blank,
        ]
    )
    taps = jnp.pad(conv_weight, ((0, 0), spare))
    return taps, vec, block_diagonal(rate_weight, chans), block_diagonal(entry_weight, chans)


def shards(
    layer_in,
    cotangent,
    mix_gain,
    ffn_gain,
    x_weight,
    y_weight,
    out_weight,
    conv_weight,
    conv_bias,
    rate_weight,
    rate_bias,
    entry_weight,
    entry_bias,
    decay_param,
    gate_weight,
    up_weight,
    down_weight,
    resets,
):
    heads, head_width = rate_weight.shape[:2]
    used = conv_bias.shape[0]
    chans = -(-used // 128) * 128
    widen = lambda values: jnp.pad(values, ((0, 0), (0, chans - used)))
    mix_full = gather(mix_gain, ("row", "head"), 0)
    ffn_full = gather(ffn_gain, ("row", "head"), 0)
    xy_shard = jnp.concatenate([widen(x_weight), widen(y_weight)], axis=1)
    xy_rows = gather(xy_shard, "row", 0)
    out_rows = gather(widen(out_weight), "row", 0)
    gate_rows = gather(gate_weight, "row", 0)
    up_rows = gather(up_weight, "row", 0)
    down_rows = gather(down_weight, "row", 0)

    taps, vec, wr, we = mixer_params(
        conv_weight, conv_bias, rate_weight, rate_bias, entry_weight, entry_bias, decay_param, chans
    )
    keep = keep_columns(resets)

    inputs = layer_in.astype(jnp.float32)
    normed_f, norm_back_one = jax.vjp(norm_apply, inputs, mix_full.astype(jnp.float32))
    normed_group = gather(normed_f.astype(jnp.bfloat16), "head", 0)
    u, by, before, states, mixed, part = mixer_forward(
        normed_group, xy_rows, out_rows, taps, vec, wr, we, keep, ROWS
    )
    residual = inputs + scatter(part, "head", 0).astype(jnp.float32)
    normed_two_f, norm_back_two = jax.vjp(norm_apply, residual, ffn_full.astype(jnp.float32))
    cot_group = gather(cotangent, "head", 0)
    two_group = gather(normed_two_f.astype(jnp.bfloat16), "head", 0)
    gates = dot_plain(two_group, gate_rows)
    ups = dot_plain(two_group, up_rows)
    activated, slope = gelu_both(gates)
    hidden = (activated * ups).astype(jnp.bfloat16)
    ffn_part = contract_last(hidden, down_rows).astype(jnp.bfloat16)
    d_hidden = dot_plain(cot_group, down_rows)
    d_gates = (d_hidden * ups * slope).astype(jnp.bfloat16)
    d_ups = (d_hidden * activated).astype(jnp.bfloat16)
    d_two_part = (contract_last(d_gates, gate_rows) + contract_last(d_ups, up_rows)).astype(
        jnp.bfloat16
    )
    gate_grad = scatter(contract_first(two_group, d_gates).astype(jnp.bfloat16), "row", 0)
    up_grad = scatter(contract_first(two_group, d_ups).astype(jnp.bfloat16), "row", 0)
    down_grad = scatter(contract_first(cot_group, hidden).astype(jnp.bfloat16), "row", 0)
    layer_out = (residual + scatter(ffn_part, "head", 0).astype(jnp.float32)).astype(jnp.bfloat16)
    d_two = scatter(d_two_part, "head", 0).astype(jnp.float32)
    d_resid_norm, d_ffn_gain = norm_back_two(d_two)
    d_residual = cotangent.astype(jnp.float32) + d_resid_norm
    d_res_group = gather(d_residual.astype(jnp.bfloat16), "head", 0)
    d_xy, d_part, d_taps, d_vec, d_wr, d_we = mixer_backward(
        d_res_group, xy_rows, out_rows, taps, vec, wr, we, keep, u, by, before, states, ROWS
    )
    out_grad = scatter(contract_first(d_res_group, mixed).astype(jnp.bfloat16), "row", 0)
    xy_grad = scatter(contract_first(normed_group, d_xy).astype(jnp.bfloat16), "row", 0)
    d_normed = scatter(d_part, "head", 0).astype(jnp.float32)
    d_inputs, d_mix_gain = norm_back_one(d_normed)
    layer_in_grad = (d_inputs + d_residual).astype(jnp.bfloat16)

    small = [
        d_taps[:, :used],
        d_vec[0, :used],
        diagonal_blocks(d_wr, heads, head_width),
        d_vec[1, :used],
        diagonal_blocks(d_we, heads, head_width),
        d_vec[2, :used],
        d_vec[3, :used] * (8.0 * jax.nn.sigmoid(-decay_param)),
    ]
    small = [lax.psum(item.astype(jnp.bfloat16), "row").astype(jnp.float32) for item in small]
    mix_part = scatter(d_mix_gain, ("row", "head"), 0)
    ffn_part_grad = scatter(d_ffn_gain, ("row", "head"), 0)
    wide = lambda values: values[:, :used].astype(jnp.float32)
    return (
        layer_out,
        layer_in_grad,
        mix_part,
        ffn_part_grad,
        wide(xy_grad),
        wide(xy_grad[:, chans:]),
        wide(out_grad),
        *small,
        gate_grad.astype(jnp.float32),
        up_grad.astype(jnp.float32),
        down_grad.astype(jnp.float32),
    )

def shards_linked(
    layer_in,
    cotangent,
    mix_gain,
    ffn_gain,
    x_weight,
    y_weight,
    out_weight,
    conv_weight,
    conv_bias,
    rate_weight,
    rate_bias,
    entry_weight,
    entry_bias,
    decay_param,
    gate_weight,
    up_weight,
    down_weight,
    resets,
):
    heads, head_width = rate_weight.shape[:2]
    used = conv_bias.shape[0]
    chans = -(-used // 128) * 128
    widen = lambda values: jnp.pad(values, ((0, 0), (0, chans - used)))
    flat = lambda values: values.reshape((-1, values.shape[-1]))
    taps, vec, wr, we = mixer_params(
        conv_weight, conv_bias, rate_weight, rate_bias, entry_weight, entry_bias, decay_param, chans
    )
    keep = keep_columns(resets)
    own_gains = jnp.concatenate([mix_gain, ffn_gain]).astype(jnp.float32)
    tile = jnp.broadcast_to(own_gains, (8, own_gains.shape[0]))

    normed_group, xy_rows, out_rows, gains = open_block(
        layer_in,
        tile,
        (jnp.concatenate([widen(x_weight), widen(y_weight)], axis=1), widen(out_weight)),
    )
    normed_group, xy_rows, out_rows = map(flat, (normed_group, xy_rows, out_rows))
    u, by, before, states, mixed, residual, normed_two, gate_rows = forward_linked(
        normed_group, xy_rows, out_rows, taps, vec, wr, we, keep, layer_in, gains[1:2], gate_weight
    )
    gate_rows = flat(gate_rows)
    two_group, cot_group, up_rows, down_rows, gates, ups, hidden, down_parts = ffn_up(
        normed_two, gate_rows, cotangent, up_weight, down_weight
    )
    two_group, cot_group, up_rows, down_rows = map(
        flat, (two_group, cot_group, up_rows, down_rows)
    )
    d_ups, gate_parts, down_grad, d_residual, d_low, d_ffn_gain = ffn_back(
        cot_group, two_group, gates, ups, gate_rows, up_rows, down_rows, down_parts, residual,
        cotangent, gains[1:2],
    )
    up_parts, out_parts, gate_grad, d_res_group = turn(
        two_group, d_ups, gate_parts, d_low, mixed
    )
    (
        xy_parts, up_grad, out_grad, layer_in_grad, d_mix_gain, d_taps, d_vec, d_wr, d_we,
    ) = backward_linked(
        flat(d_res_group), xy_rows, out_rows, taps, vec, wr, we, keep, u, by, before, states,
        normed_group, up_parts, out_parts, layer_in, gains[0:1], d_residual,
    )

    share = mix_gain.shape[0]
    split = lambda values: values.reshape(LINE, PLANE, share)
    gain_terms = jnp.concatenate([split(d_mix_gain), split(d_ffn_gain)], axis=2)
    blocks = [slice(h * head_width, (h + 1) * head_width) for h in range(heads)]
    packed = jnp.concatenate(
        [jnp.concatenate([d_wr[at, at], d_we[at, at]], axis=1) for at in blocks]
        + [
            d_taps[:, :used],
            d_vec[0:3, :used],
            d_vec[3:4, :used] * (8.0 * jax.nn.sigmoid(-decay_param)),
        ],
        axis=0,
    ).astype(jnp.bfloat16)
    packed = jnp.pad(packed, ((0, -packed.shape[0] % 16), (0, chans - used)))
    layer_out, xy_grad, gain_grads, sums = close_block(
        hidden, down_rows, xy_parts, residual, gain_terms, packed
    )
    gates_end = heads * head_width
    wide = lambda values: values[:, :used]
    return (
        layer_out,
        layer_in_grad,
        gain_grads[0, :share],
        gain_grads[0, share:],
        wide(xy_grad),
        wide(xy_grad[:, chans:]),
        wide(out_grad),
        sums[gates_end : gates_end + 4, :used],
        sums[gates_end + 4, :used],
        sums[:gates_end, :head_width].reshape(heads, head_width, head_width),
        sums[gates_end + 5, :used],
        sums[:gates_end, head_width : 2 * head_width].reshape(heads, head_width, head_width),
        sums[gates_end + 6, :used],
        sums[gates_end + 7, :used],
        gate_grad,
        up_grad,
        down_grad,
    )


def solution(mesh):
    linked = mesh.shape["row"] == LINE and mesh.shape["head"] == PLANE
    return jax.shard_map(
        shards_linked if linked else shards,
        mesh=mesh,
        in_specs=(
            P(("row", "head"), None),
            P(("row", "head"), None),
            P(("row", "head")),
            P(("row", "head")),
            P("row", "head"),
            P("row", "head"),
            P("row", "head"),
            P(None, "head"),
            P("head"),
            P("head", None, None),
            P("head"),
            P("head", None, None),
            P("head"),
            P("head"),
            P("row", "head"),
            P("row", "head"),
            P("row", "head"),
            P("row", None),
        ),
        out_specs=(
            P(("row", "head"), None),
            P(("row", "head"), None),
            P(("row", "head")),
            P(("row", "head")),
            P("row", "head"),
            P("row", "head"),
            P("row", "head"),
            P(None, "head"),
            P("head"),
            P("head", None, None),
            P("head"),
            P("head", None, None),
            P("head"),
            P("head"),
            P("row", "head"),
            P("row", "head"),
            P("row", "head"),
        ),
        check_vma=False,
    )
```

```python
import functools

import jax
import jax.numpy as jnp
from jax import lax
from jax.experimental import pallas as pl
from jax.experimental.pallas import tpu as pltpu
from jax.sharding import PartitionSpec as P

EPSILON = 1e-06
ROWS = 256
GELU_A = 0.7978845608028654
GELU_B = 0.044715
CHUNK = 16
UNROLL = 4


def gelu_only(x):
    return 0.5 * x * (1.0 + jnp.tanh(GELU_A * (x + GELU_B * x * x * x)))


def gelu_both(x):
    square = x * x
    bent = jnp.tanh(GELU_A * x * (1.0 + GELU_B * square))
    half = 0.5 * (1.0 + bent)
    slope = half + 0.5 * x * (1.0 - bent * bent) * (GELU_A * (1.0 + 3.0 * GELU_B * square))
    return x * half, slope


def one_minus_exp(x, exp_x):
    return -jnp.tanh(0.5 * x) * (1.0 + exp_x)


def dot_plain(left, right):
    return jnp.dot(left, right, preferred_element_type=jnp.float32)


def contract_last(left, right):
    return lax.dot_general(
        left, right, (((1,), (1,)), ((), ())), preferred_element_type=jnp.float32
    )


def contract_first(left, right):
    return lax.dot_general(
        left, right, (((0,), (0,)), ((), ())), preferred_element_type=jnp.float32
    )


def sum_eight(value):
    total = value[0:8, :]
    for k in range(1, value.shape[0] // 8):
        total = total + value[8 * k : 8 * k + 8, :]
    return total


def conv_rows(window, keep, taps, shift):
    rows = window.shape[0] - 8
    total = taps[0:1] * window[8:] + shift
    for offset in range(1, 4):
        total = total + taps[offset : offset + 1] * (
            keep[:, offset : offset + 1] * window[8 - offset : 8 - offset + rows]
        )
    return total


def scan_down(decays, driven, carry):
    rows = decays.shape[0]
    place = lax.broadcasted_iota(jnp.int32, decays.shape, 0)
    step = 1
    while step < rows:
        inside = place >= step
        driven = jnp.where(inside, decays * pltpu.roll(driven, step, 0) + driven, driven)
        decays = jnp.where(inside, decays * pltpu.roll(decays, step, 0), decays)
        step *= 2
    return decays * carry + driven


def scan_up(decays, driven, carry):
    rows = decays.shape[0]
    place = lax.broadcasted_iota(jnp.int32, decays.shape, 0)
    step = 1
    while step < rows:
        inside = place < rows - step
        driven = jnp.where(inside, decays * pltpu.roll(driven, rows - step, 0) + driven, driven)
        decays = jnp.where(inside, decays * pltpu.roll(decays, rows - step, 0), decays)
        step *= 2
    return decays * carry + driven


def forward_step(
    normed_ref, xy_ref, taps_ref, vec_ref, wr_ref, we_ref, keep_ref,
    u_ref, by_ref, before_ref, states_ref, mixed_ref,
    window, conv, conv_low, rate, entry, carry,
):
    rows = normed_ref.shape[0]

    @pl.when(pl.program_id(0) == 0)
    def _():
        window[0:8, :] = jnp.zeros_like(window[0:8, :])
        carry[...] = jnp.zeros_like(carry)

    chans = u_ref.shape[1]
    branches = dot_plain(normed_ref[...], xy_ref[...])
    branch_x = branches[:, :chans].astype(jnp.bfloat16)
    u_ref[...] = branch_x
    window[pl.ds(8, rows), :] = branch_x.astype(jnp.float32)
    by_ref[...] = branches[:, chans:]

    def conv_step(j, unused):
        at = pl.multiple_of(j * CHUNK, CHUNK)
        made = conv_rows(
            window[pl.ds(at, CHUNK + 8), :], keep_ref[pl.ds(at, CHUNK), :],
            taps_ref[...], vec_ref[0:1, :],
        )
        conv[pl.ds(at, CHUNK), :] = made
        conv_low[pl.ds(at, CHUNK), :] = made.astype(jnp.bfloat16)
        return unused

    lax.fori_loop(0, rows // CHUNK, conv_step, 0, unroll=UNROLL)
    window[0:8, :] = window[pl.ds(rows, 8), :]
    rate[...] = dot_plain(conv_low[...], wr_ref[...]) + vec_ref[1:2, :]
    entry[...] = dot_plain(conv_low[...], we_ref[...]) + vec_ref[2:3, :]

    def scan_step(j, before):
        at = pl.multiple_of(j * CHUNK, CHUNK)
        here = pl.ds(at, CHUNK)
        carried = keep_ref[here, 0:1]
        log_decay = jax.nn.sigmoid(rate[here, :]) * vec_ref[3:4, :]
        exp_decay = jnp.exp(log_decay)
        lost = one_minus_exp(2.0 * log_decay, exp_decay * exp_decay)
        drop = lost * lax.rsqrt(jnp.maximum(lost, 1e-30))
        scaling = (1.0 - carried) + carried * drop
        driven = scaling * jax.nn.sigmoid(entry[here, :]) * conv[here, :]
        states = scan_down(exp_decay * carried, driven, before)
        first = lax.broadcasted_iota(jnp.int32, states.shape, 0) == 0
        before_ref[here, :] = jnp.where(first, before, pltpu.roll(states, 1, 0))
        states_low = states.astype(jnp.bfloat16)
        states_ref[here, :] = states_low
        mixed_ref[here, :] = (
            states_low.astype(jnp.float32) * gelu_only(by_ref[here, :])
        ).astype(jnp.bfloat16)
        return states[CHUNK - 1 : CHUNK, :]

    carry[0:1, :] = lax.fori_loop(0, rows // CHUNK, scan_step, carry[0:1, :], unroll=UNROLL)


def forward_body(
    normed_ref, xy_ref, ow_ref, taps_ref, vec_ref, wr_ref, we_ref, keep_ref,
    u_ref, by_ref, before_ref, states_ref, mixed_ref, part_ref, *scratch,
):
    forward_step(
        normed_ref, xy_ref, taps_ref, vec_ref, wr_ref, we_ref, keep_ref,
        u_ref, by_ref, before_ref, states_ref, mixed_ref, *scratch,
    )
    part_ref[...] = contract_last(mixed_ref[...], ow_ref[...]).astype(jnp.bfloat16)


def backward_step(
    d_res_ref, xy_ref, ow_ref, taps_ref, vec_ref, wr_ref, we_ref, keep_ref,
    u_ref, u_prev_ref, by_ref, before_ref, states_ref,
    d_xy_ref, taps_out, vec_out, wr_out, we_out,
    window, conv, conv_low, rate, entry, d_mixed, d_conv, g_rate, g_entry, carry, sums,
):
    rows, chans = d_res_ref.shape[0], u_ref.shape[1]
    step_id = pl.program_id(0)

    @pl.when(step_id == 0)
    def _():
        d_conv[pl.ds(rows, 8), :] = jnp.zeros_like(d_conv[pl.ds(rows, 8), :])
        carry[...] = jnp.zeros_like(carry)
        sums[...] = jnp.zeros_like(sums)
        wr_out[...] = jnp.zeros_like(wr_out)
        we_out[...] = jnp.zeros_like(we_out)

    @pl.when(step_id > 0)
    def _():
        d_conv[pl.ds(rows, 8), :] = d_conv[0:8, :]

    d_mixed[...] = dot_plain(d_res_ref[...], ow_ref[...])
    window[0:8, :] = u_prev_ref[8:16, :].astype(jnp.float32)
    window[pl.ds(8, rows), :] = u_ref[...].astype(jnp.float32)

    def conv_step(j, unused):
        at = pl.multiple_of(j * CHUNK, CHUNK)
        made = conv_rows(
            window[pl.ds(at, CHUNK + 8), :], keep_ref[pl.ds(at, CHUNK), :],
            taps_ref[...], vec_ref[0:1, :],
        )
        conv[pl.ds(at, CHUNK), :] = made
        conv_low[pl.ds(at, CHUNK), :] = made.astype(jnp.bfloat16)
        return unused

    lax.fori_loop(0, rows // CHUNK, conv_step, 0, unroll=UNROLL)
    rate[...] = dot_plain(conv_low[...], wr_ref[...]) + vec_ref[1:2, :]
    entry[...] = dot_plain(conv_low[...], we_ref[...]) + vec_ref[2:3, :]

    def fold(value):
        return sum_eight(value)

    def scan_step(j, after):
        at = pl.multiple_of(rows - CHUNK - j * CHUNK, CHUNK)
        here = pl.ds(at, CHUNK)
        carried = keep_ref[here, 0:1]
        rate_gate = jax.nn.sigmoid(rate[here, :])
        entry_gate = jax.nn.sigmoid(entry[here, :])
        log_decay = rate_gate * vec_ref[3:4, :]
        exp_decay = jnp.exp(log_decay)
        exp_twice = exp_decay * exp_decay
        lost = one_minus_exp(2.0 * log_decay, exp_twice)
        inverse = lax.rsqrt(jnp.maximum(lost, 1e-30))
        drop = lost * inverse
        scaling = (1.0 - carried) + carried * drop
        decays = exp_decay * carried
        gelu_y, slope_y = gelu_both(by_ref[here, :])
        through = d_mixed[here, :]
        d_states = (through * gelu_y).astype(jnp.bfloat16).astype(jnp.float32)
        d_xy_ref[here, chans:] = (
            through * states_ref[here, :].astype(jnp.float32) * slope_y
        ).astype(jnp.bfloat16)
        passed = scan_up(decays, decays * d_states, after)
        last = lax.broadcasted_iota(jnp.int32, passed.shape, 0) == CHUNK - 1
        adjoint = d_states + jnp.where(last, after, pltpu.roll(passed, CHUNK - 1, 0))
        convolved = conv[here, :]
        gated = adjoint * entry_gate
        g_log = adjoint * before_ref[here, :] * decays - gated * convolved * (
            carried * (exp_twice * inverse)
        )
        g_pre_rate = g_log * vec_ref[3:4, :] * (rate_gate * (1.0 - rate_gate))
        direct = gated * scaling
        g_pre_entry = direct * convolved * (1.0 - entry_gate)
        d_conv[here, :] = direct
        g_rate[here, :] = g_pre_rate.astype(jnp.bfloat16)
        g_entry[here, :] = g_pre_entry.astype(jnp.bfloat16)
        sums[8:16, :] += fold(g_pre_rate)
        sums[16:24, :] += fold(g_pre_entry)
        sums[24:32, :] += fold(g_log * rate_gate)
        return passed[0:1, :]

    carry[0:1, :] = lax.fori_loop(0, rows // CHUNK, scan_step, carry[0:1, :], unroll=UNROLL)
    wr_out[...] += contract_first(conv_low[...], g_rate[...])
    we_out[...] += contract_first(conv_low[...], g_entry[...])
    d_conv[0:rows, :] += contract_last(g_rate[...], wr_ref[...]) + contract_last(
        g_entry[...], we_ref[...]
    )

    def back_step(j, unused):
        at = pl.multiple_of(j * CHUNK, CHUNK)
        here = pl.ds(at, CHUNK)
        keep = keep_ref[here, :]
        ahead = d_conv[pl.ds(at, CHUNK + 8), :]
        behind = window[pl.ds(at, CHUNK + 8), :]
        now = ahead[0:CHUNK]
        total = taps_ref[0:1, :] * now
        sums[0:8, :] += fold(now)
        sums[32:40, :] += fold(now * behind[8:])
        for offset in range(1, 4):
            total = total + taps_ref[offset : offset + 1, :] * (
                keep[:, 3 + offset : 4 + offset] * ahead[offset : offset + CHUNK]
            )
            base = 32 + 8 * offset
            sums[base : base + 8, :] += fold(
                now * (keep[:, offset : offset + 1] * behind[8 - offset : 8 - offset + CHUNK])
            )
        d_xy_ref[here, :chans] = total.astype(jnp.bfloat16)
        return unused

    lax.fori_loop(0, rows // CHUNK, back_step, 0, unroll=UNROLL)

    @pl.when(step_id == pl.num_programs(0) - 1)
    def _():
        vec_out[...] = jnp.zeros_like(vec_out)
        for place in range(4):
            vec_out[place : place + 1, :] = jnp.sum(
                sums[8 * place : 8 * place + 8, :], axis=0, keepdims=True
            )
            taps_out[place : place + 1, :] = jnp.sum(
                sums[32 + 8 * place : 40 + 8 * place, :], axis=0, keepdims=True
            )

    return contract_last(d_xy_ref[...], xy_ref[...]).astype(jnp.bfloat16)


def backward_body(
    d_res_ref, xy_ref, ow_ref, taps_ref, vec_ref, wr_ref, we_ref, keep_ref,
    u_ref, u_prev_ref, by_ref, before_ref, states_ref,
    d_xy_ref, part_ref, *rest,
):
    part_ref[...] = backward_step(
        d_res_ref, xy_ref, ow_ref, taps_ref, vec_ref, wr_ref, we_ref, keep_ref,
        u_ref, u_prev_ref, by_ref, before_ref, states_ref, d_xy_ref, *rest,
    )


def whole(shape):
    return pl.BlockSpec(shape, lambda i: (0,) * len(shape))


def mixer_forward(normed, xy, ow, taps, vec, wr, we, keep, rows):
    length, width = normed.shape
    chans = ow.shape[1]
    tile = lambda columns: pl.BlockSpec((rows, columns), lambda i: (i, 0))
    return pl.pallas_call(
        forward_body,
        grid=(length // rows,),
        in_specs=[
            tile(width), whole(xy.shape), whole(ow.shape), whole(taps.shape),
            whole(vec.shape), whole(wr.shape), whole(we.shape), tile(keep.shape[1]),
        ],
        out_specs=[tile(chans)] * 5 + [tile(width)],
        out_shape=[
            jax.ShapeDtypeStruct((length, chans), jnp.bfloat16),
            jax.ShapeDtypeStruct((length, chans), jnp.float32),
            jax.ShapeDtypeStruct((length, chans), jnp.float32),
            jax.ShapeDtypeStruct((length, chans), jnp.bfloat16),
            jax.ShapeDtypeStruct((length, chans), jnp.bfloat16),
            jax.ShapeDtypeStruct((length, width), jnp.bfloat16),
        ],
        scratch_shapes=[
            pltpu.VMEM((rows + 8, chans), jnp.float32),
            pltpu.VMEM((rows, chans), jnp.float32),
            pltpu.VMEM((rows, chans), jnp.bfloat16),
            pltpu.VMEM((rows, chans), jnp.float32),
            pltpu.VMEM((rows, chans), jnp.float32),
            pltpu.VMEM((8, chans), jnp.float32),
        ],
        compiler_params=pltpu.CompilerParams(vmem_limit_bytes=48 * 2**20),
        cost_estimate=pl.CostEstimate(
            flops=6 * length * width * chans,
            bytes_accessed=4 * length * width + 30 * length * chans,
            transcendentals=6 * length * chans,
        ),
        name="mixer_forward",
    )(normed, xy, ow, taps, vec, wr, we, keep)


def mixer_backward(d_res, xy, ow, taps, vec, wr, we, keep, u, by, before, states, rows):
    length, width = d_res.shape
    chans = ow.shape[1]
    blocks = length // rows
    tile = lambda columns: pl.BlockSpec((rows, columns), lambda i: (blocks - 1 - i, 0))
    ahead = pl.BlockSpec(
        (16, chans), lambda i: (jnp.maximum((blocks - 1 - i) * (rows // 16) - 1, 0), 0)
    )
    return pl.pallas_call(
        backward_body,
        grid=(blocks,),
        in_specs=[
            tile(width), whole(xy.shape), whole(ow.shape), whole(taps.shape),
            whole(vec.shape), whole(wr.shape), whole(we.shape), tile(keep.shape[1]),
            tile(chans), ahead, tile(chans), tile(chans), tile(chans),
        ],
        out_specs=[
            tile(2 * chans), tile(width), whole(taps.shape), whole(vec.shape),
            whole(wr.shape), whole(we.shape),
        ],
        out_shape=[
            jax.ShapeDtypeStruct((length, 2 * chans), jnp.bfloat16),
            jax.ShapeDtypeStruct((length, width), jnp.bfloat16),
            jax.ShapeDtypeStruct(taps.shape, jnp.float32),
            jax.ShapeDtypeStruct(vec.shape, jnp.float32),
            jax.ShapeDtypeStruct(wr.shape, jnp.float32),
            jax.ShapeDtypeStruct(we.shape, jnp.float32),
        ],
        scratch_shapes=[
            pltpu.VMEM((rows + 8, chans), jnp.float32),
            pltpu.VMEM((rows, chans), jnp.float32),
            pltpu.VMEM((rows, chans), jnp.bfloat16),
            pltpu.VMEM((rows, chans), jnp.float32),
            pltpu.VMEM((rows, chans), jnp.float32),
            pltpu.VMEM((rows, chans), jnp.float32),
            pltpu.VMEM((rows + 8, chans), jnp.float32),
            pltpu.VMEM((rows, chans), jnp.bfloat16),
            pltpu.VMEM((rows, chans), jnp.bfloat16),
            pltpu.VMEM((8, chans), jnp.float32),
            pltpu.VMEM((64, chans), jnp.float32),
        ],
        compiler_params=pltpu.CompilerParams(vmem_limit_bytes=48 * 2**20),
        cost_estimate=pl.CostEstimate(
            flops=6 * length * width * chans,
            bytes_accessed=4 * length * width + 30 * length * chans,
            transcendentals=6 * length * chans,
        ),
        name="mixer_backward",
    )(d_res, xy, ow, taps, vec, wr, we, keep, u, u, by, before, states)


def keep_columns(resets):
    length = resets.shape[1]
    position = lax.broadcasted_iota(jnp.int32, resets.shape, 1)
    starts = jnp.maximum(resets, (position == 0).astype(jnp.int32)).astype(jnp.float32)
    carried = (1.0 - starts).reshape(-1)
    seqs = resets.shape[0]

    def back(values, by):
        values = values.reshape(seqs, length)
        return jnp.pad(values, ((0, 0), (by, 0)))[:, :length].reshape(-1)

    def ahead(values, by):
        values = values.reshape(seqs, length)
        return jnp.pad(values, ((0, 0), (0, by)))[:, by:].reshape(-1)

    one = carried
    two = one * back(carried, 1)
    three = two * back(carried, 2)
    return jnp.stack(
        [carried, one, two, three, ahead(one, 1), ahead(two, 2), ahead(three, 3), carried], axis=1
    )


def block_diagonal(blocks, chans):
    heads, width, unused = blocks.shape
    rows = [
        jnp.pad(blocks[h], ((0, 0), (h * width, chans - (h + 1) * width))) for h in range(heads)
    ]
    full = jnp.concatenate(rows, axis=0)
    return jnp.pad(full, ((0, chans - heads * width), (0, 0)))


def diagonal_blocks(full, heads, width):
    return jnp.stack(
        [full[h * width : (h + 1) * width, h * width : (h + 1) * width] for h in range(heads)]
    )


MESH = pl.DeviceIdType.MESH
ANYWHERE = pl.BlockSpec(memory_space=pl.ANY)
IN_VMEM = pl.BlockSpec(memory_space=pltpu.VMEM)
LINE = 4
PLANE = 8
PIECES = 4


def send_to(src, dst, sent, arrived, axis, target):
    return pltpu.make_async_remote_copy(
        src_ref=src,
        dst_ref=dst,
        send_sem=sent,
        recv_sem=arrived,
        device_id={axis: target},
        device_id_type=MESH,
    )


def sibling_of(h):
    return h + 1 - 2 * lax.rem(h, 2)


def across_of(h):
    return h + 2 - 4 * lax.rem(lax.div(h, 2), 2)


def along_of(h):
    return lax.rem(h + 4, PLANE)


def meet(row_line, plane):
    r, h = lax.axis_index("row"), lax.axis_index("head")
    barrier = pltpu.get_barrier_semaphore()
    count = 0
    if row_line:
        for step in range(1, LINE):
            pl.semaphore_signal(
                barrier, inc=1, device_id={"row": lax.rem(r + step, LINE)}, device_id_type=MESH
            )
        count += LINE - 1
    if plane == "all":
        for step in range(1, PLANE):
            pl.semaphore_signal(
                barrier, inc=1, device_id={"head": lax.rem(h + step, PLANE)}, device_id_type=MESH
            )
        count += PLANE - 1
    if plane == "near":
        for target in (sibling_of(h), across_of(h), along_of(h)):
            pl.semaphore_signal(barrier, inc=1, device_id={"head": target}, device_id_type=MESH)
        count += 3
    pl.semaphore_wait(barrier, count)


class LineGather:
    semaphores = (
        pltpu.SemaphoreType.DMA((LINE,)),
        pltpu.SemaphoreType.DMA((LINE,)),
        pltpu.SemaphoreType.DMA((2,)),
    )

    def __init__(self, shard, full, sent, arrived, other, source=None, target=None):
        self.r = lax.axis_index("row")
        self.shard, self.full = shard, full
        self.sent, self.arrived, self.other = sent, arrived, other
        self.source = shard if source is None else shard.at[source]
        self.target = target

    def slot(self, origin):
        return self.full.at[origin] if self.target is None else self.full.at[origin, self.target]

    def own(self, t):
        return send_to(
            self.source, self.slot(self.r), self.sent.at[t], self.arrived.at[self.r], "row", t
        )

    def handed(self, origin, target):
        return send_to(
            self.slot(origin), self.slot(origin), self.other.at[0], self.arrived.at[origin],
            "row", target,
        )

    def local(self):
        return pltpu.make_async_copy(self.source, self.slot(self.r), self.other.at[1])

    def start(self):
        for gap in (2, -2, 1, -1):
            t = self.r + gap

            @pl.when((t >= 0) & (t < LINE))
            def _(t=t):
                self.own(t).start()

        self.local().start()

    def forward(self):
        for me, origin, target in ((2, 0, 3), (1, 3, 0)):

            @pl.when(self.r == me)
            def _(origin=origin, target=target):
                copy = self.handed(origin, target)
                copy.wait_recv()
                copy.start()

    def finish(self):
        r = self.r
        for t in range(LINE):
            known = (r == t) | ((r == 2) & (t == 0)) | ((r == 1) & (t == 3))
            near = (r != t) & (r - t < 3) & (t - r < 3)

            @pl.when(jnp.logical_not(known))
            def _(t=t):
                self.handed(t, t).wait_recv()

            @pl.when(near)
            def _(t=t):
                self.own(t).wait_send()

        for me, origin, target in ((2, 0, 3), (1, 3, 0)):

            @pl.when(r == me)
            def _(origin=origin, target=target):
                self.handed(origin, target).wait_send()

        self.local().wait()


class LineReduce:
    semaphores = (
        pltpu.SemaphoreType.DMA((LINE,)),
        pltpu.SemaphoreType.DMA((LINE,)),
        pltpu.SemaphoreType.DMA((2,)),
    )

    @staticmethod
    def buffers(rows, width):
        return [
            pltpu.VMEM((LINE, rows, width), jnp.bfloat16),
            pltpu.VMEM((rows, width), jnp.bfloat16),
        ]

    def __init__(self, parts, landed, passed, sent, arrived, other):
        self.r = lax.axis_index("row")
        self.parts, self.landed, self.passed = parts, landed, passed
        self.sent, self.arrived, self.other = sent, arrived, other

    def to_pass(self, me, origin, via):
        return send_to(
            self.parts.at[origin], self.passed, self.sent.at[origin], self.other.at[0], "row", via
        )

    def direct(self, t):
        return send_to(
            self.parts.at[t], self.landed.at[self.r], self.sent.at[t], self.arrived.at[self.r],
            "row", t,
        )

    def added(self, t):
        return send_to(
            self.passed, self.landed.at[self.r], self.sent.at[t], self.arrived.at[self.r], "row", t
        )

    def plain(self, t):
        r = self.r
        ends = ((r == 0) & (t == 3)) | ((r == 3) & (t == 0))
        added = ((r == 1) & (t == 3)) | ((r == 2) & (t == 0))
        return jnp.logical_not(ends | added | (r == t))

    def start(self):
        for me, end, via in ((0, 3, 1), (3, 0, 2)):

            @pl.when(self.r == me)
            def _(me=me, end=end, via=via):
                self.to_pass(me, end, via).start()

        for t in range(LINE):

            @pl.when(self.plain(t))
            def _(t=t):
                self.direct(t).start()

    def forward(self):
        for me, end in ((1, 3), (2, 0)):

            @pl.when(self.r == me)
            def _(me=me, end=end):
                self.to_pass(me, end, end).wait_recv()
                rows = self.passed.shape[0]
                step = 64

                def add(i, unused):
                    at = pl.ds(pl.multiple_of(i * step, step), step)
                    self.passed[at, :] = (
                        self.parts[end, at, :].astype(jnp.float32)
                        + self.passed[at, :].astype(jnp.float32)
                    ).astype(jnp.bfloat16)
                    return unused

                lax.fori_loop(0, rows // step, add, 0)
                self.added(end).start()

    def finish(self, write):
        r = self.r
        for t in range(LINE):

            @pl.when(jnp.logical_not(unsent_to(r, t)))
            def _(t=t):
                send_to(
                    self.parts.at[t], self.landed.at[t], self.sent.at[t], self.arrived.at[t],
                    "row", t,
                ).wait_recv()

        def total_of(sources):
            step = 32

            def add(i, unused):
                at = pl.ds(pl.multiple_of(i * step, step), step)
                total = self.parts[r, at, :].astype(jnp.float32)
                for t in sources:
                    total = total + self.landed[t, at, :].astype(jnp.float32)
                write(at, total)
                return unused

            lax.fori_loop(0, self.passed.shape[0] // step, add, 0)

        at_end = (r == 0) | (r == 3)

        @pl.when(at_end)
        def _():
            total_of((1, 2))

        @pl.when(jnp.logical_not(at_end))
        def _():
            total_of((0, 3, 3 - r))

        for me, end, via in ((0, 3, 1), (3, 0, 2)):

            @pl.when(r == me)
            def _(me=me, end=end, via=via):
                self.to_pass(me, end, via).wait_send()

        for t in range(LINE):

            @pl.when(jnp.logical_not(unsent_to(r, t)))
            def _(t=t):
                self.direct(t).wait_send()


def unsent_to(r, t):
    return ((r == 0) & (t == 3)) | ((r == 3) & (t == 0)) | (r == t)


class PlaneGather:
    semaphores = (
        pltpu.SemaphoreType.DMA((PIECES, 7)),
        pltpu.SemaphoreType.DMA((PIECES, 7)),
        pltpu.SemaphoreType.DMA((PIECES,)),
    )
    first = tuple(range(PIECES // 2))
    second = tuple(range(PIECES // 2, PIECES))

    def __init__(self, block, full, sent, arrived, other, source=None, target=None):
        h = lax.axis_index("head")
        self.source, self.target = source, target
        self.h, self.side, self.x, self.y = h, sibling_of(h), across_of(h), along_of(h)
        self.far = across_of(self.y)
        self.block, self.full = block, full
        self.sent, self.arrived, self.other = sent, arrived, other
        self.rows = block.shape[0] // PIECES

    def piece(self, owner, c):
        rows = pl.ds(c * self.rows, self.rows)
        if self.target is None:
            return self.full.at[owner, rows]
        return self.full.at[owner, rows, self.target]

    def mine(self, c):
        rows = pl.ds(c * self.rows, self.rows)
        return self.block.at[rows] if self.source is None else self.block.at[rows, self.source]

    def own(self, c, lane, target):
        return send_to(
            self.mine(c), self.piece(self.h, c),
            self.sent.at[c, lane], self.arrived.at[c, lane], "head", target,
        )

    def hand(self, owner, c, lane, target):
        return send_to(
            self.piece(owner, c), self.piece(owner, c), self.sent.at[c, lane],
            self.arrived.at[c, lane], "head", target,
        )

    def local(self, c):
        return pltpu.make_async_copy(self.mine(c), self.piece(self.h, c), self.other.at[c])

    def start(self):
        for a, b in zip(self.first, self.second):
            self.own(a, 1, self.x).start()
            self.own(b, 2, self.y).start()
        for a, b in zip(self.first, self.second):
            self.own(b, 1, self.x).start()
            self.own(a, 2, self.y).start()
        for c in range(PIECES):
            self.own(c, 0, self.side).start()
            self.local(c).start()

    def relay(self, place):
        a, b = self.first[place], self.second[place]
        self.hand(self.x, a, 1, self.x).wait_recv()
        self.hand(self.x, a, 3, self.y).start()
        self.hand(self.x, a, 4, self.side).start()
        self.hand(self.y, b, 2, self.y).wait_recv()
        self.hand(self.y, b, 3, self.x).start()
        self.hand(self.y, b, 5, self.side).start()

    def rest(self):
        for a, b in zip(self.first, self.second):
            self.hand(self.x, b, 1, self.x).wait_recv()
            self.hand(self.x, b, 4, self.side).start()
            self.hand(self.y, a, 2, self.y).wait_recv()
            self.hand(self.y, a, 5, self.side).start()

    def end(self):
        for pair in zip(self.first, self.second):
            for c in pair:
                self.hand(self.far, c, 3, self.side).wait_recv()
                self.hand(self.far, c, 6, self.side).start()
        side = self.side
        for c in range(PIECES):
            for owner, lane in (
                (side, 0), (across_of(side), 4), (along_of(side), 5),
                (across_of(along_of(side)), 6),
            ):
                self.hand(owner, c, lane, side).wait_recv()
        for c in range(PIECES):
            for lane in range(7):
                self.own(c, lane, side).wait_send()
            self.local(c).wait()


class PlaneReduce:
    semaphores = (
        pltpu.SemaphoreType.DMA((4,)),
        pltpu.SemaphoreType.DMA((4,)),
        pltpu.SemaphoreType.DMA((4, 2)),
        pltpu.SemaphoreType.DMA((2, 2)),
        pltpu.SemaphoreType.DMA((2,)),
    )

    @staticmethod
    def buffers(rows, width):
        return [
            pltpu.VMEM((4, rows, width), jnp.bfloat16),
            pltpu.VMEM((4, rows, width), jnp.bfloat16),
            pltpu.VMEM((4, rows, width), jnp.bfloat16),
            pltpu.VMEM((2, rows // 2, width), jnp.bfloat16),
            pltpu.VMEM((2, rows, width), jnp.bfloat16),
        ]

    def __init__(
        self, staged, beside, mine, relayed, landed,
        side_sent, side_arrived, sent, arrived, relay_arrived,
    ):
        h = lax.axis_index("head")
        self.h, self.core, self.chip = h, lax.rem(h, 2), lax.div(h, 2)
        self.staged, self.beside, self.mine = staged, beside, mine
        self.relayed, self.landed = relayed, landed
        self.side_sent, self.side_arrived = side_sent, side_arrived
        self.sent, self.arrived, self.relay_arrived = sent, arrived, relay_arrived
        self.half = mine.shape[1] // 2

    def aside(self, chip):
        return send_to(
            self.staged.at[chip], self.beside.at[chip], self.side_sent.at[chip],
            self.side_arrived.at[chip], "head", sibling_of(self.h),
        )

    def relation(self, chip):
        flip_x = lax.rem(chip + self.chip, 2)
        flip_y = lax.rem(lax.div(chip, 2) + lax.div(self.chip, 2), 2)
        return flip_x + 2 * flip_y

    def part(self, half):
        return pl.ds(half * self.half, self.half)

    def home(self, chip, way, half):
        return send_to(
            self.mine.at[chip, self.part(half)], self.landed.at[way, self.part(half)],
            self.sent.at[chip, half], self.arrived.at[way, half], "head",
            (across_of, along_of)[way](self.h),
        )

    def opposite(self, chip, half):
        return send_to(
            self.mine.at[chip, self.part(half)], self.relayed.at[half], self.sent.at[chip, half],
            self.relay_arrived.at[half], "head", (along_of, across_of)[half](self.h),
        )

    def put(self, block, value):
        chip, core = lax.div(block, 2), lax.rem(block, 2)

        @pl.when(core == self.core)
        def _():
            self.mine[chip] = value

        @pl.when(core != self.core)
        def _():
            self.staged[chip] = value
            self.aside(chip).start()

    def pass_on(self, block):
        chip, core = lax.div(block, 2), lax.rem(block, 2)

        @pl.when(core == self.core)
        def _():
            self.aside(chip).wait_recv()
            step = 32

            def add(i, unused):
                at = pl.ds(pl.multiple_of(i * step, step), step)
                self.mine[chip, at, :] = (
                    self.mine[chip, at, :].astype(jnp.float32)
                    + self.beside[chip, at, :].astype(jnp.float32)
                ).astype(jnp.bfloat16)
                return unused

            lax.fori_loop(0, 2 * self.half // step, add, 0)
            relation = self.relation(chip)

            @pl.when(relation == 1)
            def _():
                self.home(chip, 0, 1).start()

            @pl.when(relation == 2)
            def _():
                self.home(chip, 1, 0).start()

            @pl.when(relation == 3)
            def _():
                self.opposite(chip, 0).start()
                self.opposite(chip, 1).start()

    def relay(self, block):
        chip, core = lax.div(block, 2), lax.rem(block, 2)
        for way in (0, 1):

            @pl.when((core == self.core) & (self.relation(chip) == way + 1))
            def _(way=way):
                self.opposite(chip, way).wait_recv()
                step = 32

                def add(i, unused):
                    at = pl.ds(pl.multiple_of(i * step, step), step)
                    here = pl.ds(pl.multiple_of(way * self.half + i * step, step), step)
                    self.mine[chip, here, :] = (
                        self.mine[chip, here, :].astype(jnp.float32)
                        + self.relayed[way, at, :].astype(jnp.float32)
                    ).astype(jnp.bfloat16)
                    return unused

                lax.fori_loop(0, self.half // step, add, 0)
                self.home(chip, way, way).start()

    def arrive(self):
        for way in (0, 1):
            for half in (0, 1):
                self.home(self.chip, way, half).wait_recv()

    def total(self, at):
        value = self.mine[self.chip, at, :].astype(jnp.float32)
        return (
            value
            + self.landed[0, at, :].astype(jnp.float32)
            + self.landed[1, at, :].astype(jnp.float32)
        )

    def finish(self):
        for chip in range(4):
            self.aside(chip).wait_send()

            @pl.when(chip != self.chip)
            def _(chip=chip):
                self.home(chip, 0, 0).wait_send()
                self.home(chip, 0, 1).wait_send()


def norm_apply(rows, gain):
    return rows * lax.rsqrt(jnp.mean(rows * rows, axis=-1, keepdims=True) + EPSILON) * gain


def gather(values, axis_name, axis):
    return lax.all_gather(values, axis_name, axis=axis, tiled=True)


def scatter(values, axis_name, axis):
    return lax.psum_scatter(values, axis_name, scatter_dimension=axis, tiled=True)

def once(shape):
    return pl.BlockSpec(
        shape, lambda i: (0,) * len(shape), pipeline_mode=pl.Buffered(buffer_count=1)
    )


def norm_rows(rows, gain):
    return rows * lax.rsqrt(jnp.mean(rows * rows, axis=-1, keepdims=True) + EPSILON) * gain


def open_body(
    x_ref, tile_ref, cot, xy_shard, out_shard, full, cot_out, xy_full, out_full, gains_ref,
    normed, column, spread, gain_sent, gain_arrived, wide_sent, wide_arrived, *semaphores,
):
    r, h = lax.axis_index("row"), lax.axis_index("head")
    xy_line = LineGather(xy_shard, xy_full, *semaphores[0:3])
    out_line = LineGather(out_shard, out_full, *semaphores[3:6])
    plane = PlaneGather(normed, full, *semaphores[6:9])
    cot_plane = PlaneGather(
        cot, cot_out, *semaphores[9:12], source=pl.ds(0, cot_out.shape[2])
    )
    meet(True, "all")

    def up_line(t):
        return send_to(
            column.at[r], column.at[r], gain_sent.at[t], gain_arrived.at[r], "row", t
        )

    def from_line(t):
        return send_to(
            column.at[t], column.at[t], gain_sent.at[t], gain_arrived.at[t], "row", t
        )

    def over_plane(step, owner):
        return send_to(
            column, spread.at[owner], wide_sent.at[step], wide_arrived.at[owner], "head",
            lax.rem(h + step, PLANE),
        )

    column[r] = tile_ref[...]
    for step in range(1, LINE):
        up_line(lax.rem(r + step, LINE)).start()
    xy_line.start()
    out_line.start()
    for step in range(1, LINE):
        from_line(lax.rem(r + step, LINE)).wait_recv()
    for step in range(1, PLANE):
        over_plane(step, h).start()
    cot_plane.start()
    spread[h] = column[...]
    for step in range(1, PLANE):
        over_plane(step, lax.rem(h + step, PLANE)).wait_recv()

    share = tile_ref.shape[1] // 2
    low = lax.broadcasted_iota(jnp.int32, (1, 2 * share), 1) < share
    for line_place in range(LINE):
        for pair in range(PLANE // 2):
            even = spread[2 * pair, line_place][0:1, :]
            odd = spread[2 * pair + 1, line_place][0:1, :]
            at = (line_place * (PLANE // 2) + pair) * 2 * share
            gains_ref[0:1, at : at + 2 * share] = jnp.where(low, even, pltpu.roll(odd, share, 1))
            gains_ref[1:2, at : at + 2 * share] = jnp.where(low, pltpu.roll(even, share, 1), odd)

    def make(i, unused):
        at = pl.ds(pl.multiple_of(i * CHUNK, CHUNK), CHUNK)
        normed[at, :] = norm_rows(x_ref[at, :].astype(jnp.float32), gains_ref[0:1, :]).astype(
            jnp.bfloat16
        )
        return unused

    lax.fori_loop(0, x_ref.shape[0] // CHUNK, make, 0)
    plane.start()
    cot_plane.relay(0)
    cot_plane.relay(1)
    cot_plane.rest()
    plane.relay(0)
    xy_line.forward()
    plane.relay(1)
    cot_plane.end()
    plane.rest()
    plane.end()
    out_line.forward()
    xy_line.finish()
    out_line.finish()
    for step in range(1, LINE):
        up_line(lax.rem(r + step, LINE)).wait_send()
    for step in range(1, PLANE):
        over_plane(step, h).wait_send()


def open_block(layer_in, tile, cot, xy_shard, out_shard):
    rows, width = layer_in.shape
    return pl.pallas_call(
        open_body,
        in_specs=[IN_VMEM, IN_VMEM, ANYWHERE, ANYWHERE, ANYWHERE],
        out_specs=[ANYWHERE] * 4 + [IN_VMEM],
        out_shape=[
            jax.ShapeDtypeStruct((PLANE, rows, width), jnp.bfloat16),
            jax.ShapeDtypeStruct((PLANE, rows, width // 2), jnp.bfloat16),
            jax.ShapeDtypeStruct((LINE,) + xy_shard.shape, jnp.bfloat16),
            jax.ShapeDtypeStruct((LINE,) + out_shard.shape, jnp.bfloat16),
            jax.ShapeDtypeStruct((2, width), jnp.float32),
        ],
        scratch_shapes=[
            pltpu.VMEM((rows, width), jnp.bfloat16),
            pltpu.VMEM((LINE,) + tile.shape, jnp.float32),
            pltpu.VMEM((PLANE, LINE) + tile.shape, jnp.float32),
            pltpu.SemaphoreType.DMA((LINE,)),
            pltpu.SemaphoreType.DMA((LINE,)),
            pltpu.SemaphoreType.DMA((PLANE,)),
            pltpu.SemaphoreType.DMA((PLANE,)),
            *(LineGather.semaphores * 2),
            *(PlaneGather.semaphores * 2),
        ],
        compiler_params=pltpu.CompilerParams(
            collective_id=0, has_side_effects=True, vmem_limit_bytes=61 * 2**20
        ),
        name="open_block",
    )(layer_in, tile, cot, xy_shard, out_shard)


def forward_linked_body(
    normed_ref, xy_ref, ow_ref, taps_ref, vec_ref, wr_ref, we_ref, keep_ref,
    x_ref, gain_ref, gate_shard, up_shard,
    u_ref, by_ref, before_ref, states_ref, mixed_ref, residual_ref, two_ref, gate_out, up_out,
    window, conv, conv_low, rate, entry, carry, *links,
):
    step = pl.program_id(0)
    plane = PlaneReduce(*links[:10])
    gate_line = LineGather(gate_shard, gate_out, *links[10:13])
    up_line = LineGather(up_shard, up_out, *links[13:16], source=pl.ds(0, up_out.shape[1]))

    @pl.when(step == 0)
    def _():
        meet(True, "near")
        gate_line.start()
        up_line.start()

    @pl.when(step > 0)
    def _():
        plane.pass_on(step - 1)

    @pl.when(step > 2)
    def _():
        plane.relay(step - 3)

    forward_step(
        normed_ref, xy_ref, taps_ref, vec_ref, wr_ref, we_ref, keep_ref,
        u_ref, by_ref, before_ref, states_ref, mixed_ref,
        window, conv, conv_low, rate, entry, carry,
    )
    plane.put(step, contract_last(mixed_ref[...], ow_ref[...]).astype(jnp.bfloat16))

    @pl.when(step == 6)
    def _():
        gate_line.forward()

    @pl.when(step == PLANE - 1)
    def _():
        plane.relay(step - 2)
        plane.pass_on(step)
        plane.relay(step - 1)
        plane.relay(step)
        up_line.forward()
        plane.arrive()

        def make(i, unused):
            at = pl.ds(pl.multiple_of(i * CHUNK, CHUNK), CHUNK)
            residual = x_ref[at, :].astype(jnp.float32) + plane.total(at)
            residual_ref[at, :] = residual
            two_ref[at, :] = norm_rows(residual, gain_ref[...]).astype(jnp.bfloat16)
            return unused

        lax.fori_loop(0, x_ref.shape[0] // CHUNK, make, 0)
        plane.finish()
        gate_line.finish()
        up_line.finish()


def forward_linked(normed, xy, ow, taps, vec, wr, we, keep, layer_in, gain, gate_shard, up_shard):
    length, width = normed.shape
    chans = ow.shape[1]
    rows = length // PLANE
    share, units = up_shard.shape
    tile = lambda columns: pl.BlockSpec((rows, columns), lambda i: (i, 0))
    return pl.pallas_call(
        forward_linked_body,
        grid=(PLANE,),
        in_specs=[
            tile(width), once(xy.shape), once(ow.shape), once(taps.shape),
            once(vec.shape), once(wr.shape), once(we.shape), tile(keep.shape[1]),
            once(layer_in.shape), once(gain.shape), ANYWHERE, ANYWHERE,
        ],
        out_specs=[tile(chans)] * 5 + [once((rows, width))] * 2 + [ANYWHERE] * 2,
        out_shape=[
            jax.ShapeDtypeStruct((length, chans), jnp.bfloat16),
            jax.ShapeDtypeStruct((length, chans), jnp.float32),
            jax.ShapeDtypeStruct((length, chans), jnp.float32),
            jax.ShapeDtypeStruct((length, chans), jnp.bfloat16),
            jax.ShapeDtypeStruct((length, chans), jnp.bfloat16),
            jax.ShapeDtypeStruct((rows, width), jnp.float32),
            jax.ShapeDtypeStruct((rows, width), jnp.bfloat16),
            jax.ShapeDtypeStruct((LINE,) + gate_shard.shape, jnp.bfloat16),
            jax.ShapeDtypeStruct((LINE, share // 2, units), jnp.bfloat16),
        ],
        scratch_shapes=[
            pltpu.VMEM((rows + 8, chans), jnp.float32),
            pltpu.VMEM((rows, chans), jnp.float32),
            pltpu.VMEM((rows, chans), jnp.bfloat16),
            pltpu.VMEM((rows, chans), jnp.float32),
            pltpu.VMEM((rows, chans), jnp.float32),
            pltpu.VMEM((8, chans), jnp.float32),
            *PlaneReduce.buffers(rows, width),
            *PlaneReduce.semaphores,
            *(LineGather.semaphores * 2),
        ],
        compiler_params=pltpu.CompilerParams(
            collective_id=1, has_side_effects=True, vmem_limit_bytes=61 * 2**20
        ),
        name="mixer_forward_linked",
    )(normed, xy, ow, taps, vec, wr, we, keep, layer_in, gain, gate_shard, up_shard)


def ffn_up_body(
    own_two, gate_ref, own_cot, cot_half, up_half, up_shard, down_shard,
    two_out, cot_out, up_out, down_out, gates_out, ups_out, hidden_out, down_parts,
    two, cot, up, gates, ups, hidden, total, copied, brought, *semaphores,
):
    h = lax.axis_index("head")
    rows = own_two.shape[0]
    units = gates.shape[1]
    width, share = own_two.shape[1], up.shape[1]
    late_rows, late_columns = pl.ds(share // 2, share // 2), pl.ds(width // 2, width // 2)
    up_line = LineGather(up_shard, up, *semaphores[0:3], source=late_rows, target=late_rows)
    down_line = LineGather(down_shard, down_out, *semaphores[3:6])
    two_plane = PlaneGather(own_two, two, *semaphores[6:9])
    cot_plane = PlaneGather(
        own_cot, cot, *semaphores[9:12], source=late_columns, target=late_columns
    )
    inward = [
        pltpu.make_async_copy(up_half, up.at[:, pl.ds(0, share // 2)], brought.at[0]),
        pltpu.make_async_copy(cot_half, cot.at[:, :, pl.ds(0, width // 2)], brought.at[1]),
    ]
    outward = [
        pltpu.make_async_copy(src, dst, copied.at[k])
        for k, (src, dst) in enumerate(
            (
                (two, two_out), (cot, cot_out), (up, up_out), (gates, gates_out),
                (ups, ups_out), (hidden, hidden_out),
            )
        )
    ]
    meet(True, "near")
    up_line.start()
    down_line.start()
    two_plane.start()
    for copy in inward:
        copy.start()

    def at_block(block):
        return pl.ds(pl.multiple_of(block * rows, rows), rows)

    def make_gates(k, unused):
        block = lax.rem(h + k, PLANE)
        gates[at_block(block), :] = dot_plain(two[block], gate_ref[...])
        return unused

    gates[at_block(h), :] = dot_plain(own_two[...], gate_ref[...])
    two_plane.relay(0)
    two_plane.relay(1)
    two_plane.rest()
    cot_plane.start()
    two_plane.end()
    outward[0].start()
    up_line.forward()
    lax.fori_loop(1, 3, make_gates, 0)
    cot_plane.relay(0)
    lax.fori_loop(3, 6, make_gates, 0)
    cot_plane.relay(1)
    lax.fori_loop(6, PLANE, make_gates, 0)
    outward[3].start()
    cot_plane.rest()
    up_line.finish()
    for copy in inward:
        copy.wait()
    outward[2].start()

    def make_hidden(block, unused):
        at = at_block(block)
        value = jnp.zeros((rows, units), jnp.float32)
        for t in range(LINE):
            value = value + dot_plain(two[block, :, t * share : (t + 1) * share], up[t])
        ups[at, :] = value

        def make(i, unused):
            here = pl.ds(pl.multiple_of(block * rows + i * CHUNK, CHUNK), CHUNK)
            hidden[here, :] = (gelu_only(gates[here, :]) * ups[here, :]).astype(jnp.bfloat16)
            return unused

        lax.fori_loop(0, rows // CHUNK, make, 0, unroll=UNROLL)
        return unused

    lax.fori_loop(0, PLANE, make_hidden, 0)
    outward[4].start()
    outward[5].start()
    cot_plane.end()
    outward[1].start()
    down_line.forward()
    total[...] = contract_first(cot[0], hidden[0:rows, :])

    def add_down(block, unused):
        total[...] += contract_first(cot[block], hidden[at_block(block), :])
        return unused

    lax.fori_loop(1, PLANE, add_down, 0)
    to_parts(total, down_parts)
    down_line.finish()
    for copy in outward:
        copy.wait()


def ffn_up(own_two, gate, own_cot, cot_half, up_half, up_shard, down_shard):
    rows, width = own_two.shape
    share, units = up_shard.shape
    length = rows * PLANE
    group = jax.ShapeDtypeStruct((PLANE, rows, width), jnp.bfloat16)
    weight = jax.ShapeDtypeStruct((LINE, share, units), jnp.bfloat16)
    return pl.pallas_call(
        ffn_up_body,
        in_specs=[IN_VMEM, IN_VMEM] + [ANYWHERE] * 5,
        out_specs=[ANYWHERE] * 7 + [IN_VMEM],
        out_shape=[
            group,
            group,
            weight,
            weight,
            jax.ShapeDtypeStruct((length, units), jnp.float32),
            jax.ShapeDtypeStruct((length, units), jnp.float32),
            jax.ShapeDtypeStruct((length, units), jnp.bfloat16),
            weight,
        ],
        scratch_shapes=[
            pltpu.VMEM((PLANE, rows, width), jnp.bfloat16),
            pltpu.VMEM((PLANE, rows, width), jnp.bfloat16),
            pltpu.VMEM((LINE, share, units), jnp.bfloat16),
            pltpu.VMEM((length, units), jnp.float32),
            pltpu.VMEM((length, units), jnp.float32),
            pltpu.VMEM((length, units), jnp.bfloat16),
            pltpu.VMEM((width, units), jnp.float32),
            pltpu.SemaphoreType.DMA((6,)),
            pltpu.SemaphoreType.DMA((2,)),
            *(LineGather.semaphores * 2),
            *(PlaneGather.semaphores * 2),
        ],
        compiler_params=pltpu.CompilerParams(
            collective_id=2, has_side_effects=True, vmem_limit_bytes=61 * 2**20
        ),
        name="ffn_up",
    )(own_two, gate, own_cot, cot_half, up_half, up_shard, down_shard)
def far_first(step):
    chip = lax.div(lax.axis_index("head"), 2)
    place = lax.div(step, 2)
    x = lax.rem(lax.rem(chip, 2) + 1 - lax.div(place, 2), 2)
    y = lax.rem(lax.div(chip, 2) + 1 + lax.rem(place, 2), 2)
    return 2 * (2 * y + x) + lax.rem(step, 2)


def norm_back(rows, gain, incoming):
    scale = lax.rsqrt(jnp.mean(rows * rows, axis=-1, keepdims=True) + EPSILON)
    scaled = incoming * gain
    inner = jnp.mean(scaled * rows, axis=-1, keepdims=True)
    return scale * scaled - rows * (scale * scale * scale * inner), incoming * rows * scale


def to_parts(total, parts):
    rows = parts.shape[1]
    step = 64

    def move(i, unused):
        at = pl.ds(pl.multiple_of(i * step, step), step)
        for t in range(LINE):
            here = pl.ds(pl.multiple_of(t * rows + i * step, step), step)
            parts[t, at, :] = total[here, :].astype(jnp.bfloat16)
        return unused

    lax.fori_loop(0, rows // step, move, 0)


def ffn_back_body(
    cot_ref, two_ref, gates_ref, ups_ref, gate_ref, up_ref, down_ref, parts,
    residual_ref, own_cot_ref, gain_ref,
    d_ups_ref, gate_parts, down_out, d_res_ref, d_low_ref, gain_out,
    total, d_gates, d_hidden, eight, *links,
):
    step = pl.program_id(0)
    line = LineReduce(parts, *links[:5])
    plane = PlaneReduce(*links[5:])
    rows = cot_ref.shape[0]

    @pl.when(step == 0)
    def _():
        meet(True, "near")
        line.start()
        total[...] = jnp.zeros_like(total)

    @pl.when(step > 0)
    def _():
        plane.pass_on(far_first(step - 1))

    @pl.when(step > 2)
    def _():
        plane.relay(far_first(step - 3))

    d_hidden[...] = dot_plain(cot_ref[...], down_ref[...])

    def make(i, unused):
        at = pl.ds(pl.multiple_of(i * CHUNK, CHUNK), CHUNK)
        gelu_gate, slope = gelu_both(gates_ref[at, :])
        through = d_hidden[at, :]
        d_gates[at, :] = (through * ups_ref[at, :] * slope).astype(jnp.bfloat16)
        d_ups_ref[at, :] = (through * gelu_gate).astype(jnp.bfloat16)
        return unused

    lax.fori_loop(0, rows // CHUNK, make, 0, unroll=UNROLL)
    value = contract_last(d_gates[...], gate_ref[...]) + contract_last(d_ups_ref[...], up_ref[...])
    plane.put(far_first(step), value.astype(jnp.bfloat16))
    total[...] += contract_first(two_ref[...], d_gates[...])

    @pl.when(step == 4)
    def _():
        line.forward()

    @pl.when(step == PLANE - 1)
    def _():
        plane.relay(far_first(step - 2))
        plane.pass_on(far_first(step))
        plane.relay(far_first(step - 1))
        to_parts(total, gate_parts)
        plane.relay(far_first(step))
        plane.arrive()
        eight[...] = jnp.zeros_like(eight)

        def back(i, unused):
            at = pl.ds(pl.multiple_of(i * CHUNK, CHUNK), CHUNK)
            d_rows, d_gain = norm_back(residual_ref[at, :], gain_ref[...], plane.total(at))
            d_residual = own_cot_ref[at, :].astype(jnp.float32) + d_rows
            d_res_ref[at, :] = d_residual
            d_low_ref[at, :] = d_residual.astype(jnp.bfloat16)
            eight[...] += sum_eight(d_gain)
            return unused

        lax.fori_loop(0, rows // CHUNK, back, 0)
        gain_out[...] = jnp.sum(eight[...], axis=0, keepdims=True)

        def write(at, value):
            down_out[at, :] = value

        line.finish(write)
        plane.finish()


def ffn_back(
    cot_group, two_group, gates, ups, gate, up, down, parts, residual, own_cot, gain
):
    length, width = cot_group.shape
    units = gate.shape[1]
    rows, share = length // PLANE, width // LINE
    tile = lambda columns: pl.BlockSpec((rows, columns), lambda i: (far_first(i), 0))
    return pl.pallas_call(
        ffn_back_body,
        grid=(PLANE,),
        in_specs=[
            tile(width), tile(width), tile(units), tile(units), once(gate.shape),
            once(up.shape), once(down.shape), once(parts.shape), once(residual.shape),
            once(own_cot.shape), once(gain.shape),
        ],
        out_specs=[
            tile(units), once((LINE, share, units)), once((share, units)),
            once((rows, width)), once((rows, width)), once((1, width)),
        ],
        out_shape=[
            jax.ShapeDtypeStruct((length, units), jnp.bfloat16),
            jax.ShapeDtypeStruct((LINE, share, units), jnp.bfloat16),
            jax.ShapeDtypeStruct((share, units), jnp.float32),
            jax.ShapeDtypeStruct((rows, width), jnp.float32),
            jax.ShapeDtypeStruct((rows, width), jnp.bfloat16),
            jax.ShapeDtypeStruct((1, width), jnp.float32),
        ],
        scratch_shapes=[
            pltpu.VMEM((width, units), jnp.float32),
            pltpu.VMEM((rows, units), jnp.bfloat16),
            pltpu.VMEM((rows, units), jnp.float32),
            pltpu.VMEM((8, width), jnp.float32),
            *LineReduce.buffers(share, units),
            *LineReduce.semaphores,
            *PlaneReduce.buffers(rows, width),
            *PlaneReduce.semaphores,
        ],
        compiler_params=pltpu.CompilerParams(
            collective_id=4, has_side_effects=True, vmem_limit_bytes=61 * 2**20
        ),
        name="ffn_back",
    )(cot_group, two_group, gates, ups, gate, up, down, parts, residual, own_cot, gain)


def turn_body(
    two_ref, d_ups_ref, gate_parts, block, mixed_ref,
    up_parts, out_parts, gate_out, full_out,
    full, total, out_total, copied, *links,
):
    step = pl.program_id(0)
    line = LineReduce(gate_parts, *links[:5])
    plane = PlaneGather(block, full, *links[5:])
    rows = two_ref.shape[0]
    outward = pltpu.make_async_copy(full, full_out, copied)

    @pl.when(step == 0)
    def _():
        meet(True, "near")
        line.start()
        plane.start()
        total[...] = jnp.zeros_like(total)

    total[...] += contract_first(two_ref[...], d_ups_ref[...])

    @pl.when(step == PLANE - 3)
    def _():
        plane.relay(0)
        line.forward()

    @pl.when(step == PLANE - 1)
    def _():
        plane.relay(1)
        to_parts(total, up_parts)
        plane.rest()
        plane.end()
        outward.start()
        out_total[...] = contract_first(full[0], mixed_ref[0:rows, :])

        def add(b, unused):
            at = pl.ds(pl.multiple_of(b * rows, rows), rows)
            out_total[...] += contract_first(full[b], mixed_ref[at, :])
            return unused

        lax.fori_loop(1, PLANE, add, 0)
        to_parts(out_total, out_parts)

        def write(at, value):
            gate_out[at, :] = value

        line.finish(write)
        outward.wait()


def turn(two_group, d_ups, gate_parts, block, mixed):
    length, width = two_group.shape
    units, chans = d_ups.shape[1], mixed.shape[1]
    rows, share = length // PLANE, width // LINE
    tile = lambda columns: pl.BlockSpec((rows, columns), lambda i: (i, 0))
    return pl.pallas_call(
        turn_body,
        grid=(PLANE,),
        in_specs=[
            tile(width), tile(units), once(gate_parts.shape), ANYWHERE, once(mixed.shape)
        ],
        out_specs=[
            once(gate_parts.shape), once((LINE, share, chans)), once((share, units)), ANYWHERE
        ],
        out_shape=[
            jax.ShapeDtypeStruct(gate_parts.shape, jnp.bfloat16),
            jax.ShapeDtypeStruct((LINE, share, chans), jnp.bfloat16),
            jax.ShapeDtypeStruct((share, units), jnp.float32),
            jax.ShapeDtypeStruct((PLANE, rows, width), jnp.bfloat16),
        ],
        scratch_shapes=[
            pltpu.VMEM((PLANE, rows, width), jnp.bfloat16),
            pltpu.VMEM((width, units), jnp.float32),
            pltpu.VMEM((width, chans), jnp.float32),
            pltpu.SemaphoreType.DMA,
            *LineReduce.buffers(share, units),
            *LineReduce.semaphores,
            *PlaneGather.semaphores,
        ],
        compiler_params=pltpu.CompilerParams(
            collective_id=5, has_side_effects=True, vmem_limit_bytes=61 * 2**20
        ),
        name="turn",
    )(two_group, d_ups, gate_parts, block, mixed)


def pack_small(head_width, taps, vec, params, wr, we, small):
    columns = small.shape[1]
    step = 16
    last = (2 * head_width + 7) // 8 * 8

    def move(i, unused):
        at = pl.ds(pl.multiple_of(i * step, step), step)
        shape = (step, columns)
        row = lax.broadcasted_iota(jnp.int32, shape, 0) + i * step
        left = lax.broadcasted_iota(jnp.int32, shape, 1) < head_width
        rate, entry = wr[at, :], we[at, :]
        first = jnp.where(left, rate, pltpu.roll(entry, head_width, 1))
        second = jnp.where(left, pltpu.roll(rate, columns - head_width, 1), entry)
        small[at, :] = jnp.where(row < head_width, first, second).astype(jnp.bfloat16)
        return unused

    lax.fori_loop(0, last // step, move, 0)
    scaled = vec[0:4, :] * jnp.concatenate(
        [jnp.ones((3, columns), jnp.float32), params[4:5, :]], axis=0
    )
    tail = jnp.concatenate([taps[...], scaled], axis=0).astype(jnp.bfloat16)
    here = last // step * step
    rate, entry = wr[here : here + 8, :], we[here : here + 8, :]
    left = lax.broadcasted_iota(jnp.int32, (8, columns), 1) < head_width
    rest = jnp.where(left, pltpu.roll(rate, columns - head_width, 1), entry).astype(jnp.bfloat16)
    small[here : here + 16, :] = jnp.concatenate([rest, tail], axis=0)


def split_gains(mix, ffn, out):
    share = out.shape[2] // 2
    low = lax.broadcasted_iota(jnp.int32, (1, 2 * share), 1) < share
    for r in range(LINE):
        lines = []
        for pair in range(PLANE // 2):
            at = (r * (PLANE // 2) + pair) * 2 * share
            one, two = mix[:, at : at + 2 * share], ffn[:, at : at + 2 * share]
            lines.append(jnp.where(low, one, pltpu.roll(two, share, 1)))
            lines.append(jnp.where(low, pltpu.roll(one, share, 1), two))
        out[r] = jnp.concatenate(lines, axis=0)


def backward_linked_body(
    head_width,
    d_res_ref, xy_ref, ow_ref, taps_ref, vec_ref, wr_ref, we_ref, keep_ref,
    u_ref, u_prev_ref, by_ref, before_ref, states_ref, normed_ref, up_parts, out_parts,
    x_ref, gain_ref, d_residual_ref, ffn_gain_ref,
    xy_parts, up_out, out_out, in_grad, gains_out, small_out,
    taps_sum, vec_sum, wr_sum, we_sum, small, gathered, d_xy, xy_total, eight, *rest,
):
    scratch, links = rest[:11], rest[11:]
    step = pl.program_id(0)
    block = PLANE - 1 - step
    line = LineReduce(up_parts, *links[:5])
    out_line = LineReduce(out_parts, *links[5:10])
    small_line = LineGather(small, gathered, *links[10:13])
    plane = PlaneReduce(*links[13:])

    @pl.when(step == 0)
    def _():
        meet(True, "near")
        line.start()
        out_line.start()
        xy_total[...] = jnp.zeros_like(xy_total)

    @pl.when(step > 0)
    def _():
        plane.pass_on(block + 1)

    @pl.when(step > 2)
    def _():
        plane.relay(block + 3)

    value = backward_step(
        d_res_ref, xy_ref, ow_ref, taps_ref, vec_ref, wr_ref, we_ref, keep_ref,
        u_ref, u_prev_ref, by_ref, before_ref, states_ref, d_xy,
        taps_sum, vec_sum, wr_sum, we_sum, *scratch,
    )
    plane.put(block, value)
    xy_total[...] += contract_first(normed_ref[...], d_xy[...])

    @pl.when(step == 4)
    def _():
        line.forward()

    @pl.when(step == PLANE - 1)
    def _():
        plane.relay(block + 2)
        plane.pass_on(block)
        pack_small(head_width, taps_sum, vec_sum, vec_ref, wr_sum, we_sum, small)
        small_line.start()
        plane.relay(block + 1)
        to_parts(xy_total, xy_parts)
        plane.relay(block)
        out_line.forward()
        small_line.forward()
        plane.arrive()
        eight[...] = jnp.zeros_like(eight)

        def back(i, unused):
            at = pl.ds(pl.multiple_of(i * CHUNK, CHUNK), CHUNK)
            d_rows, d_gain = norm_back(
                x_ref[at, :].astype(jnp.float32), gain_ref[...], plane.total(at)
            )
            in_grad[at, :] = (d_residual_ref[at, :] + d_rows).astype(jnp.bfloat16)
            eight[...] += sum_eight(d_gain)
            return unused

        lax.fori_loop(0, x_ref.shape[0] // CHUNK, back, 0)
        split_gains(jnp.sum(eight[...], axis=0, keepdims=True), ffn_gain_ref[...], gains_out)

        def write(at, value):
            up_out[at, :] = value

        def write_out(at, value):
            out_out[at, :] = value

        line.finish(write)
        out_line.finish(write_out)
        small_line.finish()

        def add_small(i, unused):
            at = pl.ds(pl.multiple_of(i * CHUNK, CHUNK), CHUNK)
            total = gathered[0, at, :].astype(jnp.float32)
            for t in range(1, LINE):
                total = total + gathered[t, at, :].astype(jnp.float32)
            small_out[at, :] = total
            return unused

        lax.fori_loop(0, small.shape[0] // CHUNK, add_small, 0)
        plane.finish()


def backward_linked(
    d_res, xy, ow, taps, vec, wr, we, keep, u, by, before, states, normed, up_parts, out_parts,
    layer_in, gain, d_residual, ffn_gain, head_width,
):
    length, width = d_res.shape
    chans, units = ow.shape[1], up_parts.shape[2]
    rows, share = length // PLANE, width // LINE
    tile = lambda columns: pl.BlockSpec((rows, columns), lambda i: (PLANE - 1 - i, 0))
    ahead = pl.BlockSpec(
        (16, chans), lambda i: (jnp.maximum((PLANE - 1 - i) * (rows // 16) - 1, 0), 0)
    )
    small = ((2 * head_width + 7) // 8 * 8 // 16 * 16 + 16, chans)
    gain_terms = (LINE, PLANE, width // (LINE * PLANE) * 2)
    return pl.pallas_call(
        functools.partial(backward_linked_body, head_width),
        grid=(PLANE,),
        in_specs=[
            tile(width), once(xy.shape), once(ow.shape), once(taps.shape),
            once(vec.shape), once(wr.shape), once(we.shape), tile(keep.shape[1]),
            tile(chans), ahead, tile(chans), tile(chans), tile(chans), tile(width),
            once(up_parts.shape), once(out_parts.shape), once(layer_in.shape), once(gain.shape), once(d_residual.shape), once(ffn_gain.shape),
        ],
        out_specs=[
            once((LINE, share, 2 * chans)), once((share, units)), once((share, chans)),
            once((rows, width)), once(gain_terms), once(small),
        ],
        out_shape=[
            jax.ShapeDtypeStruct((LINE, share, 2 * chans), jnp.bfloat16),
            jax.ShapeDtypeStruct((share, units), jnp.float32),
            jax.ShapeDtypeStruct((share, chans), jnp.float32),
            jax.ShapeDtypeStruct((rows, width), jnp.bfloat16),
            jax.ShapeDtypeStruct(gain_terms, jnp.float32),
            jax.ShapeDtypeStruct(small, jnp.float32),
        ],
        scratch_shapes=[
            pltpu.VMEM(taps.shape, jnp.float32),
            pltpu.VMEM(vec.shape, jnp.float32),
            pltpu.VMEM(wr.shape, jnp.float32),
            pltpu.VMEM(we.shape, jnp.float32),
            pltpu.VMEM(small, jnp.bfloat16),
            pltpu.VMEM((LINE,) + small, jnp.bfloat16),
            pltpu.VMEM((rows, 2 * chans), jnp.bfloat16),
            pltpu.VMEM((width, 2 * chans), jnp.float32),
            pltpu.VMEM((8, width), jnp.float32),
            pltpu.VMEM((rows + 8, chans), jnp.float32),
            pltpu.VMEM((rows, chans), jnp.float32),
            pltpu.VMEM((rows, chans), jnp.bfloat16),
            pltpu.VMEM((rows, chans), jnp.float32),
            pltpu.VMEM((rows, chans), jnp.float32),
            pltpu.VMEM((rows, chans), jnp.float32),
            pltpu.VMEM((rows + 8, chans), jnp.float32),
            pltpu.VMEM((rows, chans), jnp.bfloat16),
            pltpu.VMEM((rows, chans), jnp.bfloat16),
            pltpu.VMEM((8, chans), jnp.float32),
            pltpu.VMEM((64, chans), jnp.float32),
            *LineReduce.buffers(share, units),
            *LineReduce.semaphores,
            *LineReduce.buffers(share, chans),
            *LineReduce.semaphores,
            *LineGather.semaphores,
            *PlaneReduce.buffers(rows, width),
            *PlaneReduce.semaphores,
        ],
        compiler_params=pltpu.CompilerParams(
            collective_id=6, has_side_effects=True, vmem_limit_bytes=61 * 2**20
        ),
        name="mixer_backward_linked",
    )(
        d_res, xy, ow, taps, vec, wr, we, keep, u, u, by, before, states, normed,
        up_parts, out_parts, layer_in, gain, d_residual, ffn_gain,
    )


def close_body(
    hidden_ref, down_ref, xy_parts, residual_ref, gains_ref,
    layer_out, xy_out, gains_out,
    line_gains, both_gains, plane_gains,
    gain_sent, gain_arrived, wide_sent, wide_arrived, *links,
):
    r, h = lax.axis_index("row"), lax.axis_index("head")
    step = pl.program_id(0)
    xy_line = LineReduce(xy_parts, *links[0:5])
    plane = PlaneReduce(*links[5:])

    def to_row(t, owner):
        return send_to(
            gains_ref.at[t], line_gains.at[owner], gain_sent.at[t], gain_arrived.at[owner],
            "row", t,
        )

    def over_plane(place, owner):
        return send_to(
            both_gains, plane_gains.at[owner], wide_sent.at[place], wide_arrived.at[owner],
            "head", lax.rem(h + place, PLANE),
        )

    @pl.when(step == 0)
    def _():
        meet(True, "all")
        for place in range(1, LINE):
            to_row(lax.rem(r + place, LINE), r).start()
        xy_line.start()

    @pl.when(step > 0)
    def _():
        plane.pass_on(far_first(step - 1))

    @pl.when(step > 2)
    def _():
        plane.relay(far_first(step - 3))

    plane.put(far_first(step), contract_last(hidden_ref[...], down_ref[...]).astype(jnp.bfloat16))

    @pl.when(step == 2)
    def _():
        total = gains_ref[r]
        for place in range(1, LINE):
            t = lax.rem(r + place, LINE)
            to_row(t, t).wait_recv()
            total = total + line_gains[t]
        both_gains[...] = total
        for place in range(1, PLANE):
            over_plane(place, h).start()

    @pl.when(step == PLANE - 1)
    def _():
        plane.relay(far_first(step - 2))
        plane.pass_on(far_first(step))
        plane.relay(far_first(step - 1))
        plane.relay(far_first(step))
        xy_line.forward()
        total = both_gains[...]
        for place in range(1, PLANE):
            owner = lax.rem(h + place, PLANE)
            over_plane(place, owner).wait_recv()
            total = total + plane_gains[owner]
        mine = lax.broadcasted_iota(jnp.int32, total.shape, 0) == h
        gains_out[...] = jnp.sum(jnp.where(mine, total, 0.0), axis=0, keepdims=True)
        plane.arrive()

        def make(i, unused):
            at = pl.ds(pl.multiple_of(i * CHUNK, CHUNK), CHUNK)
            layer_out[at, :] = (residual_ref[at, :] + plane.total(at)).astype(jnp.bfloat16)
            return unused

        lax.fori_loop(0, residual_ref.shape[0] // CHUNK, make, 0)
        def write(at, value):
            xy_out[at, :] = value

        xy_line.finish(write)
        plane.finish()
        for place in range(1, LINE):
            to_row(lax.rem(r + place, LINE), r).wait_send()
        for place in range(1, PLANE):
            over_plane(place, h).wait_send()


def close_block(hidden, down, xy_parts, residual, gains):
    length, units = hidden.shape
    rows, width = residual.shape
    share, columns = xy_parts.shape[1:]
    return pl.pallas_call(
        close_body,
        grid=(PLANE,),
        in_specs=[
            pl.BlockSpec((rows, units), lambda i: (far_first(i), 0)), once(down.shape),
            once(xy_parts.shape), once(residual.shape), once(gains.shape),
        ],
        out_specs=[
            once((rows, width)), once((share, columns)), once((1, gains.shape[2])),
        ],
        out_shape=[
            jax.ShapeDtypeStruct((rows, width), jnp.bfloat16),
            jax.ShapeDtypeStruct((share, columns), jnp.float32),
            jax.ShapeDtypeStruct((1, gains.shape[2]), jnp.float32),
        ],
        scratch_shapes=[
            pltpu.VMEM(gains.shape, jnp.float32),
            pltpu.VMEM(gains.shape[1:], jnp.float32),
            pltpu.VMEM((PLANE,) + gains.shape[1:], jnp.float32),
            pltpu.SemaphoreType.DMA((LINE,)),
            pltpu.SemaphoreType.DMA((LINE,)),
            pltpu.SemaphoreType.DMA((PLANE,)),
            pltpu.SemaphoreType.DMA((PLANE,)),
            *LineReduce.buffers(share, columns), *LineReduce.semaphores,
            *PlaneReduce.buffers(rows, width), *PlaneReduce.semaphores,
        ],
        compiler_params=pltpu.CompilerParams(
            collective_id=7, has_side_effects=True, vmem_limit_bytes=61 * 2**20
        ),
        name="close_block",
    )(hidden, down, xy_parts, residual, gains)


def mixer_params(
    conv_weight, conv_bias, rate_weight, rate_bias, entry_weight, entry_bias, decay_param, chans
):
    used = conv_bias.shape[0]
    spare = (0, chans - used)
    decay_wide = jnp.pad(decay_param, spare, constant_values=2.0)
    blank = jnp.zeros((chans,), jnp.float32)
    vec = jnp.stack(
        [
            jnp.pad(conv_bias, spare),
            jnp.pad(rate_bias, spare),
            jnp.pad(entry_bias, spare),
            -8.0 * jax.nn.softplus(-decay_wide),
            8.0 * jax.nn.sigmoid(-decay_wide),
            blank,
            blank,
            blank,
        ]
    )
    taps = jnp.pad(conv_weight, ((0, 0), spare))
    return taps, vec, block_diagonal(rate_weight, chans), block_diagonal(entry_weight, chans)


def shards(
    layer_in,
    cotangent,
    mix_gain,
    ffn_gain,
    x_weight,
    y_weight,
    out_weight,
    conv_weight,
    conv_bias,
    rate_weight,
    rate_bias,
    entry_weight,
    entry_bias,
    decay_param,
    gate_weight,
    up_weight,
    down_weight,
    resets,
):
    heads, head_width = rate_weight.shape[:2]
    used = conv_bias.shape[0]
    chans = -(-used // 128) * 128
    widen = lambda values: jnp.pad(values, ((0, 0), (0, chans - used)))
    mix_full = gather(mix_gain, ("row", "head"), 0)
    ffn_full = gather(ffn_gain, ("row", "head"), 0)
    xy_shard = jnp.concatenate([widen(x_weight), widen(y_weight)], axis=1)
    xy_rows = gather(xy_shard, "row", 0)
    out_rows = gather(widen(out_weight), "row", 0)
    gate_rows = gather(gate_weight, "row", 0)
    up_rows = gather(up_weight, "row", 0)
    down_rows = gather(down_weight, "row", 0)

    taps, vec, wr, we = mixer_params(
        conv_weight, conv_bias, rate_weight, rate_bias, entry_weight, entry_bias, decay_param, chans
    )
    keep = keep_columns(resets)

    inputs = layer_in.astype(jnp.float32)
    normed_f, norm_back_one = jax.vjp(norm_apply, inputs, mix_full.astype(jnp.float32))
    normed_group = gather(normed_f.astype(jnp.bfloat16), "head", 0)
    u, by, before, states, mixed, part = mixer_forward(
        normed_group, xy_rows, out_rows, taps, vec, wr, we, keep, ROWS
    )
    residual = inputs + scatter(part, "head", 0).astype(jnp.float32)
    normed_two_f, norm_back_two = jax.vjp(norm_apply, residual, ffn_full.astype(jnp.float32))
    cot_group = gather(cotangent, "head", 0)
    two_group = gather(normed_two_f.astype(jnp.bfloat16), "head", 0)
    gates = dot_plain(two_group, gate_rows)
    ups = dot_plain(two_group, up_rows)
    activated, slope = gelu_both(gates)
    hidden = (activated * ups).astype(jnp.bfloat16)
    ffn_part = contract_last(hidden, down_rows).astype(jnp.bfloat16)
    d_hidden = dot_plain(cot_group, down_rows)
    d_gates = (d_hidden * ups * slope).astype(jnp.bfloat16)
    d_ups = (d_hidden * activated).astype(jnp.bfloat16)
    d_two_part = (contract_last(d_gates, gate_rows) + contract_last(d_ups, up_rows)).astype(
        jnp.bfloat16
    )
    gate_grad = scatter(contract_first(two_group, d_gates).astype(jnp.bfloat16), "row", 0)
    up_grad = scatter(contract_first(two_group, d_ups).astype(jnp.bfloat16), "row", 0)
    down_grad = scatter(contract_first(cot_group, hidden).astype(jnp.bfloat16), "row", 0)
    layer_out = (residual + scatter(ffn_part, "head", 0).astype(jnp.float32)).astype(jnp.bfloat16)
    d_two = scatter(d_two_part, "head", 0).astype(jnp.float32)
    d_resid_norm, d_ffn_gain = norm_back_two(d_two)
    d_residual = cotangent.astype(jnp.float32) + d_resid_norm
    d_res_group = gather(d_residual.astype(jnp.bfloat16), "head", 0)
    d_xy, d_part, d_taps, d_vec, d_wr, d_we = mixer_backward(
        d_res_group, xy_rows, out_rows, taps, vec, wr, we, keep, u, by, before, states, ROWS
    )
    out_grad = scatter(contract_first(d_res_group, mixed).astype(jnp.bfloat16), "row", 0)
    xy_grad = scatter(contract_first(normed_group, d_xy).astype(jnp.bfloat16), "row", 0)
    d_normed = scatter(d_part, "head", 0).astype(jnp.float32)
    d_inputs, d_mix_gain = norm_back_one(d_normed)
    layer_in_grad = (d_inputs + d_residual).astype(jnp.bfloat16)

    small = [
        d_taps[:, :used],
        d_vec[0, :used],
        diagonal_blocks(d_wr, heads, head_width),
        d_vec[1, :used],
        diagonal_blocks(d_we, heads, head_width),
        d_vec[2, :used],
        d_vec[3, :used] * (8.0 * jax.nn.sigmoid(-decay_param)),
    ]
    small = [lax.psum(item.astype(jnp.bfloat16), "row").astype(jnp.float32) for item in small]
    mix_part = scatter(d_mix_gain, ("row", "head"), 0)
    ffn_part_grad = scatter(d_ffn_gain, ("row", "head"), 0)
    wide = lambda values: values[:, :used].astype(jnp.float32)
    return (
        layer_out,
        layer_in_grad,
        mix_part,
        ffn_part_grad,
        wide(xy_grad),
        wide(xy_grad[:, chans:]),
        wide(out_grad),
        *small,
        gate_grad.astype(jnp.float32),
        up_grad.astype(jnp.float32),
        down_grad.astype(jnp.float32),
    )

def shards_linked(
    layer_in,
    cotangent,
    mix_gain,
    ffn_gain,
    x_weight,
    y_weight,
    out_weight,
    conv_weight,
    conv_bias,
    rate_weight,
    rate_bias,
    entry_weight,
    entry_bias,
    decay_param,
    gate_weight,
    up_weight,
    down_weight,
    resets,
):
    heads, head_width = rate_weight.shape[:2]
    used = conv_bias.shape[0]
    chans = -(-used // 128) * 128
    widen = lambda values: jnp.pad(values, ((0, 0), (0, chans - used)))
    flat = lambda values: values.reshape((-1, values.shape[-1]))
    taps, vec, wr, we = mixer_params(
        conv_weight, conv_bias, rate_weight, rate_bias, entry_weight, entry_bias, decay_param, chans
    )
    keep = keep_columns(resets)
    own_gains = jnp.concatenate([mix_gain, ffn_gain]).astype(jnp.float32)
    tile = jnp.broadcast_to(own_gains, (8, own_gains.shape[0]))

    normed_group, cot_half, xy_rows, out_rows, gains = open_block(
        layer_in,
        tile,
        cotangent,
        jnp.concatenate([widen(x_weight), widen(y_weight)], axis=1),
        widen(out_weight),
    )
    normed_group, xy_rows, out_rows = map(flat, (normed_group, xy_rows, out_rows))
    u, by, before, states, mixed, residual, normed_two, gate_rows, up_half = forward_linked(
        normed_group, xy_rows, out_rows, taps, vec, wr, we, keep, layer_in, gains[1:2],
        gate_weight, up_weight,
    )
    gate_rows = flat(gate_rows)
    two_group, cot_group, up_rows, down_rows, gates, ups, hidden, down_parts = ffn_up(
        normed_two, gate_rows, cotangent, cot_half, up_half, up_weight, down_weight
    )
    two_group, cot_group, up_rows, down_rows = map(
        flat, (two_group, cot_group, up_rows, down_rows)
    )
    d_ups, gate_parts, down_grad, d_residual, d_low, d_ffn_gain = ffn_back(
        cot_group, two_group, gates, ups, gate_rows, up_rows, down_rows, down_parts, residual,
        cotangent, gains[1:2],
    )
    up_parts, out_parts, gate_grad, d_res_group = turn(
        two_group, d_ups, gate_parts, d_low, mixed
    )
    xy_parts, up_grad, out_grad, layer_in_grad, gain_terms, sums = backward_linked(
        flat(d_res_group), xy_rows, out_rows, taps, vec, wr, we, keep, u, by, before, states,
        normed_group, up_parts, out_parts, layer_in, gains[0:1], d_residual, d_ffn_gain,
        head_width,
    )
    layer_out, xy_grad, gain_grads = close_block(
        hidden, down_rows, xy_parts, residual, gain_terms
    )
    share = mix_gain.shape[0]
    ends = -(-used // 8) * 8
    gates_end = heads * head_width
    wide = lambda values: values[:, :used]
    return (
        layer_out,
        layer_in_grad,
        gain_grads[0, :share],
        gain_grads[0, share:],
        wide(xy_grad),
        wide(xy_grad[:, chans:]),
        wide(out_grad),
        sums[ends : ends + 4, :used],
        sums[ends + 4, :used],
        sums[:gates_end, :head_width].reshape(heads, head_width, head_width),
        sums[ends + 5, :used],
        sums[:gates_end, head_width : 2 * head_width].reshape(heads, head_width, head_width),
        sums[ends + 6, :used],
        sums[ends + 7, :used],
        gate_grad,
        up_grad,
        down_grad,
    )


def solution(mesh):
    linked = mesh.shape["row"] == LINE and mesh.shape["head"] == PLANE
    return jax.shard_map(
        shards_linked if linked else shards,
        mesh=mesh,
        in_specs=(
            P(("row", "head"), None),
            P(("row", "head"), None),
            P(("row", "head")),
            P(("row", "head")),
            P("row", "head"),
            P("row", "head"),
            P("row", "head"),
            P(None, "head"),
            P("head"),
            P("head", None, None),
            P("head"),
            P("head", None, None),
            P("head"),
            P("head"),
            P("row", "head"),
            P("row", "head"),
            P("row", "head"),
            P("row", None),
        ),
        out_specs=(
            P(("row", "head"), None),
            P(("row", "head"), None),
            P(("row", "head")),
            P(("row", "head")),
            P("row", "head"),
            P("row", "head"),
            P("row", "head"),
            P(None, "head"),
            P("head"),
            P("head", None, None),
            P("head"),
            P("head", None, None),
            P("head"),
            P("head"),
            P("row", "head"),
            P("row", "head"),
            P("row", "head"),
        ),
        check_vma=False,
    )
```

```python
import functools

import jax
import jax.numpy as jnp
from jax import lax
from jax.experimental import pallas as pl
from jax.experimental.pallas import tpu as pltpu
from jax.sharding import PartitionSpec as P

EPSILON = 1e-06
ROWS = 256
GELU_A = 0.7978845608028654
GELU_B = 0.044715
CHUNK = 16
UNROLL = 4


def gelu_only(x):
    return 0.5 * x * (1.0 + jnp.tanh(GELU_A * (x + GELU_B * x * x * x)))


def gelu_both(x):
    square = x * x
    bent = jnp.tanh(GELU_A * x * (1.0 + GELU_B * square))
    half = 0.5 * (1.0 + bent)
    slope = half + 0.5 * x * (1.0 - bent * bent) * (GELU_A * (1.0 + 3.0 * GELU_B * square))
    return x * half, slope


def one_minus_exp(x, exp_x):
    return -jnp.tanh(0.5 * x) * (1.0 + exp_x)


def dot_plain(left, right):
    return jnp.dot(left, right, preferred_element_type=jnp.float32)


def contract_last(left, right):
    return lax.dot_general(
        left, right, (((1,), (1,)), ((), ())), preferred_element_type=jnp.float32
    )


def contract_first(left, right):
    return lax.dot_general(
        left, right, (((0,), (0,)), ((), ())), preferred_element_type=jnp.float32
    )


def sum_eight(value):
    total = value[0:8, :]
    for k in range(1, value.shape[0] // 8):
        total = total + value[8 * k : 8 * k + 8, :]
    return total


def conv_rows(window, keep, taps, shift):
    rows = window.shape[0] - 8
    total = taps[0:1] * window[8:] + shift
    for offset in range(1, 4):
        total = total + taps[offset : offset + 1] * (
            keep[:, offset : offset + 1] * window[8 - offset : 8 - offset + rows]
        )
    return total


def scan_down(decays, driven, carry):
    rows = decays.shape[0]
    place = lax.broadcasted_iota(jnp.int32, decays.shape, 0)
    step = 1
    while step < rows:
        inside = place >= step
        driven = jnp.where(inside, decays * pltpu.roll(driven, step, 0) + driven, driven)
        decays = jnp.where(inside, decays * pltpu.roll(decays, step, 0), decays)
        step *= 2
    return decays * carry + driven


def scan_up(decays, driven, carry):
    rows = decays.shape[0]
    place = lax.broadcasted_iota(jnp.int32, decays.shape, 0)
    step = 1
    while step < rows:
        inside = place < rows - step
        driven = jnp.where(inside, decays * pltpu.roll(driven, rows - step, 0) + driven, driven)
        decays = jnp.where(inside, decays * pltpu.roll(decays, rows - step, 0), decays)
        step *= 2
    return decays * carry + driven


def forward_step(
    normed_ref, xy_ref, taps_ref, vec_ref, wr_ref, we_ref, keep_ref,
    u_ref, by_ref, before_ref, states_ref, mixed_ref,
    window, conv, conv_low, rate, entry, carry,
):
    rows = normed_ref.shape[0]

    @pl.when(pl.program_id(0) == 0)
    def _():
        window[0:8, :] = jnp.zeros_like(window[0:8, :])
        carry[...] = jnp.zeros_like(carry)

    chans = u_ref.shape[1]
    branches = contract_last(normed_ref[...], xy_ref[...])
    branch_x = branches[:, :chans].astype(jnp.bfloat16)
    u_ref[...] = branch_x
    window[pl.ds(8, rows), :] = branch_x.astype(jnp.float32)
    by_ref[...] = branches[:, chans:]

    def conv_step(j, unused):
        at = pl.multiple_of(j * CHUNK, CHUNK)
        made = conv_rows(
            window[pl.ds(at, CHUNK + 8), :], keep_ref[pl.ds(at, CHUNK), :],
            taps_ref[...], vec_ref[0:1, :],
        )
        conv[pl.ds(at, CHUNK), :] = made
        conv_low[pl.ds(at, CHUNK), :] = made.astype(jnp.bfloat16)
        return unused

    lax.fori_loop(0, rows // CHUNK, conv_step, 0, unroll=UNROLL)
    window[0:8, :] = window[pl.ds(rows, 8), :]
    rate[...] = dot_plain(conv_low[...], wr_ref[...]) + vec_ref[1:2, :]
    entry[...] = dot_plain(conv_low[...], we_ref[...]) + vec_ref[2:3, :]

    def scan_step(j, before):
        at = pl.multiple_of(j * CHUNK, CHUNK)
        here = pl.ds(at, CHUNK)
        carried = keep_ref[here, 0:1]
        log_decay = jax.nn.sigmoid(rate[here, :]) * vec_ref[3:4, :]
        exp_decay = jnp.exp(log_decay)
        lost = one_minus_exp(2.0 * log_decay, exp_decay * exp_decay)
        drop = lost * lax.rsqrt(jnp.maximum(lost, 1e-30))
        scaling = (1.0 - carried) + carried * drop
        driven = scaling * jax.nn.sigmoid(entry[here, :]) * conv[here, :]
        states = scan_down(exp_decay * carried, driven, before)
        first = lax.broadcasted_iota(jnp.int32, states.shape, 0) == 0
        before_ref[here, :] = jnp.where(first, before, pltpu.roll(states, 1, 0))
        states_low = states.astype(jnp.bfloat16)
        states_ref[here, :] = states_low
        mixed_ref[here, :] = (
            states_low.astype(jnp.float32) * gelu_only(by_ref[here, :])
        ).astype(jnp.bfloat16)
        return states[CHUNK - 1 : CHUNK, :]

    carry[0:1, :] = lax.fori_loop(0, rows // CHUNK, scan_step, carry[0:1, :], unroll=UNROLL)


def forward_body(
    normed_ref, xy_ref, ow_ref, taps_ref, vec_ref, wr_ref, we_ref, keep_ref,
    u_ref, by_ref, before_ref, states_ref, mixed_ref, part_ref, *scratch,
):
    forward_step(
        normed_ref, xy_ref, taps_ref, vec_ref, wr_ref, we_ref, keep_ref,
        u_ref, by_ref, before_ref, states_ref, mixed_ref, *scratch,
    )
    part_ref[...] = dot_plain(mixed_ref[...], ow_ref[...]).astype(jnp.bfloat16)


def backward_step(
    first_step, last_step, d_mixed, taps_ref, vec_ref, wr_ref, we_ref, keep_ref,
    u_ref, u_prev_ref, by_ref, before_ref, states_ref,
    d_xy_ref, taps_out, vec_out, wr_out, we_out,
    window, conv, conv_low, rate, entry, d_conv, g_rate, g_entry, carry, sums,
):
    rows, chans = u_ref.shape

    @pl.when(first_step)
    def _():
        d_conv[pl.ds(rows, 8), :] = jnp.zeros_like(d_conv[pl.ds(rows, 8), :])
        carry[...] = jnp.zeros_like(carry)
        sums[...] = jnp.zeros_like(sums)
        wr_out[...] = jnp.zeros_like(wr_out)
        we_out[...] = jnp.zeros_like(we_out)

    @pl.when(jnp.logical_not(first_step))
    def _():
        d_conv[pl.ds(rows, 8), :] = d_conv[0:8, :]

    window[0:8, :] = u_prev_ref[8:16, :].astype(jnp.float32)
    window[pl.ds(8, rows), :] = u_ref[...].astype(jnp.float32)

    def conv_step(j, unused):
        at = pl.multiple_of(j * CHUNK, CHUNK)
        made = conv_rows(
            window[pl.ds(at, CHUNK + 8), :], keep_ref[pl.ds(at, CHUNK), :],
            taps_ref[...], vec_ref[0:1, :],
        )
        conv[pl.ds(at, CHUNK), :] = made
        conv_low[pl.ds(at, CHUNK), :] = made.astype(jnp.bfloat16)
        return unused

    lax.fori_loop(0, rows // CHUNK, conv_step, 0, unroll=UNROLL)
    rate[...] = dot_plain(conv_low[...], wr_ref[...]) + vec_ref[1:2, :]
    entry[...] = dot_plain(conv_low[...], we_ref[...]) + vec_ref[2:3, :]

    def fold(value):
        return sum_eight(value)

    def scan_step(j, after):
        at = pl.multiple_of(rows - CHUNK - j * CHUNK, CHUNK)
        here = pl.ds(at, CHUNK)
        carried = keep_ref[here, 0:1]
        rate_gate = jax.nn.sigmoid(rate[here, :])
        entry_gate = jax.nn.sigmoid(entry[here, :])
        log_decay = rate_gate * vec_ref[3:4, :]
        exp_decay = jnp.exp(log_decay)
        exp_twice = exp_decay * exp_decay
        lost = one_minus_exp(2.0 * log_decay, exp_twice)
        inverse = lax.rsqrt(jnp.maximum(lost, 1e-30))
        drop = lost * inverse
        scaling = (1.0 - carried) + carried * drop
        decays = exp_decay * carried
        gelu_y, slope_y = gelu_both(by_ref[here, :])
        through = d_mixed[here, :]
        d_states = (through * gelu_y).astype(jnp.bfloat16).astype(jnp.float32)
        d_xy_ref[here, chans:] = (
            through * states_ref[here, :].astype(jnp.float32) * slope_y
        ).astype(jnp.bfloat16)
        passed = scan_up(decays, decays * d_states, after)
        last = lax.broadcasted_iota(jnp.int32, passed.shape, 0) == CHUNK - 1
        adjoint = d_states + jnp.where(last, after, pltpu.roll(passed, CHUNK - 1, 0))
        convolved = conv[here, :]
        gated = adjoint * entry_gate
        g_log = adjoint * before_ref[here, :] * decays - gated * convolved * (
            carried * (exp_twice * inverse)
        )
        g_pre_rate = g_log * vec_ref[3:4, :] * (rate_gate * (1.0 - rate_gate))
        direct = gated * scaling
        g_pre_entry = direct * convolved * (1.0 - entry_gate)
        d_conv[here, :] = direct
        g_rate[here, :] = g_pre_rate.astype(jnp.bfloat16)
        g_entry[here, :] = g_pre_entry.astype(jnp.bfloat16)
        sums[8:16, :] += fold(g_pre_rate)
        sums[16:24, :] += fold(g_pre_entry)
        sums[24:32, :] += fold(g_log * rate_gate)
        return passed[0:1, :]

    carry[0:1, :] = lax.fori_loop(0, rows // CHUNK, scan_step, carry[0:1, :], unroll=UNROLL)
    wr_out[...] += contract_first(conv_low[...], g_rate[...])
    we_out[...] += contract_first(conv_low[...], g_entry[...])
    d_conv[0:rows, :] += contract_last(g_rate[...], wr_ref[...]) + contract_last(
        g_entry[...], we_ref[...]
    )

    def back_step(j, unused):
        at = pl.multiple_of(j * CHUNK, CHUNK)
        here = pl.ds(at, CHUNK)
        keep = keep_ref[here, :]
        ahead = d_conv[pl.ds(at, CHUNK + 8), :]
        behind = window[pl.ds(at, CHUNK + 8), :]
        now = ahead[0:CHUNK]
        total = taps_ref[0:1, :] * now
        sums[0:8, :] += fold(now)
        sums[32:40, :] += fold(now * behind[8:])
        for offset in range(1, 4):
            total = total + taps_ref[offset : offset + 1, :] * (
                keep[:, 3 + offset : 4 + offset] * ahead[offset : offset + CHUNK]
            )
            base = 32 + 8 * offset
            sums[base : base + 8, :] += fold(
                now * (keep[:, offset : offset + 1] * behind[8 - offset : 8 - offset + CHUNK])
            )
        d_xy_ref[here, :chans] = total.astype(jnp.bfloat16)
        return unused

    lax.fori_loop(0, rows // CHUNK, back_step, 0, unroll=UNROLL)

    @pl.when(last_step)
    def _():
        vec_out[...] = jnp.zeros_like(vec_out)
        for place in range(4):
            vec_out[place : place + 1, :] = jnp.sum(
                sums[8 * place : 8 * place + 8, :], axis=0, keepdims=True
            )
            taps_out[place : place + 1, :] = jnp.sum(
                sums[32 + 8 * place : 40 + 8 * place, :], axis=0, keepdims=True
            )


def backward_body(
    d_res_ref, xy_ref, ow_ref, taps_ref, vec_ref, wr_ref, we_ref, keep_ref,
    u_ref, u_prev_ref, by_ref, before_ref, states_ref,
    d_xy_ref, part_ref, taps_out, vec_out, wr_out, we_out, d_mixed, *scratch,
):
    step = pl.program_id(0)
    d_mixed[...] = contract_last(d_res_ref[...], ow_ref[...])
    backward_step(
        step == 0, step == pl.num_programs(0) - 1, d_mixed, taps_ref, vec_ref, wr_ref,
        we_ref, keep_ref, u_ref, u_prev_ref, by_ref, before_ref, states_ref, d_xy_ref,
        taps_out, vec_out, wr_out, we_out, *scratch,
    )
    part_ref[...] = dot_plain(d_xy_ref[...], xy_ref[...]).astype(jnp.bfloat16)


def whole(shape):
    return pl.BlockSpec(shape, lambda i: (0,) * len(shape))


def mixer_forward(normed, xy, ow, taps, vec, wr, we, keep, rows):
    length, width = normed.shape
    chans = ow.shape[0]
    tile = lambda columns: pl.BlockSpec((rows, columns), lambda i: (i, 0))
    return pl.pallas_call(
        forward_body,
        grid=(length // rows,),
        in_specs=[
            tile(width), whole(xy.shape), whole(ow.shape), whole(taps.shape),
            whole(vec.shape), whole(wr.shape), whole(we.shape), tile(keep.shape[1]),
        ],
        out_specs=[tile(chans)] * 5 + [tile(width)],
        out_shape=[
            jax.ShapeDtypeStruct((length, chans), jnp.bfloat16),
            jax.ShapeDtypeStruct((length, chans), jnp.float32),
            jax.ShapeDtypeStruct((length, chans), jnp.float32),
            jax.ShapeDtypeStruct((length, chans), jnp.bfloat16),
            jax.ShapeDtypeStruct((length, chans), jnp.bfloat16),
            jax.ShapeDtypeStruct((length, width), jnp.bfloat16),
        ],
        scratch_shapes=[
            pltpu.VMEM((rows + 8, chans), jnp.float32),
            pltpu.VMEM((rows, chans), jnp.float32),
            pltpu.VMEM((rows, chans), jnp.bfloat16),
            pltpu.VMEM((rows, chans), jnp.float32),
            pltpu.VMEM((rows, chans), jnp.float32),
            pltpu.VMEM((8, chans), jnp.float32),
        ],
        compiler_params=pltpu.CompilerParams(vmem_limit_bytes=48 * 2**20),
        cost_estimate=pl.CostEstimate(
            flops=6 * length * width * chans,
            bytes_accessed=4 * length * width + 30 * length * chans,
            transcendentals=6 * length * chans,
        ),
        name="mixer_forward",
    )(normed, xy, ow, taps, vec, wr, we, keep)


def mixer_backward(d_res, xy, ow, taps, vec, wr, we, keep, u, by, before, states, rows):
    length, width = d_res.shape
    chans = ow.shape[0]
    blocks = length // rows
    tile = lambda columns: pl.BlockSpec((rows, columns), lambda i: (blocks - 1 - i, 0))
    ahead = pl.BlockSpec(
        (16, chans), lambda i: (jnp.maximum((blocks - 1 - i) * (rows // 16) - 1, 0), 0)
    )
    return pl.pallas_call(
        backward_body,
        grid=(blocks,),
        in_specs=[
            tile(width), whole(xy.shape), whole(ow.shape), whole(taps.shape),
            whole(vec.shape), whole(wr.shape), whole(we.shape), tile(keep.shape[1]),
            tile(chans), ahead, tile(chans), tile(chans), tile(chans),
        ],
        out_specs=[
            tile(2 * chans), tile(width), whole(taps.shape), whole(vec.shape),
            whole(wr.shape), whole(we.shape),
        ],
        out_shape=[
            jax.ShapeDtypeStruct((length, 2 * chans), jnp.bfloat16),
            jax.ShapeDtypeStruct((length, width), jnp.bfloat16),
            jax.ShapeDtypeStruct(taps.shape, jnp.float32),
            jax.ShapeDtypeStruct(vec.shape, jnp.float32),
            jax.ShapeDtypeStruct(wr.shape, jnp.float32),
            jax.ShapeDtypeStruct(we.shape, jnp.float32),
        ],
        scratch_shapes=[
            pltpu.VMEM((rows, chans), jnp.float32),
            pltpu.VMEM((rows + 8, chans), jnp.float32),
            pltpu.VMEM((rows, chans), jnp.float32),
            pltpu.VMEM((rows, chans), jnp.bfloat16),
            pltpu.VMEM((rows, chans), jnp.float32),
            pltpu.VMEM((rows, chans), jnp.float32),
            pltpu.VMEM((rows + 8, chans), jnp.float32),
            pltpu.VMEM((rows, chans), jnp.bfloat16),
            pltpu.VMEM((rows, chans), jnp.bfloat16),
            pltpu.VMEM((8, chans), jnp.float32),
            pltpu.VMEM((64, chans), jnp.float32),
        ],
        compiler_params=pltpu.CompilerParams(vmem_limit_bytes=48 * 2**20),
        cost_estimate=pl.CostEstimate(
            flops=6 * length * width * chans,
            bytes_accessed=4 * length * width + 30 * length * chans,
            transcendentals=6 * length * chans,
        ),
        name="mixer_backward",
    )(d_res, xy, ow, taps, vec, wr, we, keep, u, u, by, before, states)


def keep_columns(resets):
    length = resets.shape[1]
    position = lax.broadcasted_iota(jnp.int32, resets.shape, 1)
    starts = jnp.maximum(resets, (position == 0).astype(jnp.int32)).astype(jnp.float32)
    carried = (1.0 - starts).reshape(-1)
    seqs = resets.shape[0]

    def back(values, by):
        values = values.reshape(seqs, length)
        return jnp.pad(values, ((0, 0), (by, 0)))[:, :length].reshape(-1)

    def ahead(values, by):
        values = values.reshape(seqs, length)
        return jnp.pad(values, ((0, 0), (0, by)))[:, by:].reshape(-1)

    one = carried
    two = one * back(carried, 1)
    three = two * back(carried, 2)
    return jnp.stack(
        [carried, one, two, three, ahead(one, 1), ahead(two, 2), ahead(three, 3), carried], axis=1
    )


def block_diagonal(blocks, chans):
    heads, width, unused = blocks.shape
    rows = [
        jnp.pad(blocks[h], ((0, 0), (h * width, chans - (h + 1) * width))) for h in range(heads)
    ]
    full = jnp.concatenate(rows, axis=0)
    return jnp.pad(full, ((0, chans - heads * width), (0, 0)))


def diagonal_blocks(full, heads, width):
    return jnp.stack(
        [full[h * width : (h + 1) * width, h * width : (h + 1) * width] for h in range(heads)]
    )


MESH = pl.DeviceIdType.MESH
ANYWHERE = pl.BlockSpec(memory_space=pl.ANY)
IN_VMEM = pl.BlockSpec(memory_space=pltpu.VMEM)
LINE = 4
PLANE = 8
PIECES = 4


def send_to(src, dst, sent, arrived, axis, target):
    return pltpu.make_async_remote_copy(
        src_ref=src,
        dst_ref=dst,
        send_sem=sent,
        recv_sem=arrived,
        device_id={axis: target},
        device_id_type=MESH,
    )


def sibling_of(h):
    return h + 1 - 2 * lax.rem(h, 2)


def across_of(h):
    return h + 2 - 4 * lax.rem(lax.div(h, 2), 2)


def along_of(h):
    return lax.rem(h + 4, PLANE)


def meet(row_line, plane):
    r, h = lax.axis_index("row"), lax.axis_index("head")
    barrier = pltpu.get_barrier_semaphore()
    count = 0
    if row_line:
        for step in range(1, LINE):
            pl.semaphore_signal(
                barrier, inc=1, device_id={"row": lax.rem(r + step, LINE)}, device_id_type=MESH
            )
        count += LINE - 1
    if plane == "all":
        for step in range(1, PLANE):
            pl.semaphore_signal(
                barrier, inc=1, device_id={"head": lax.rem(h + step, PLANE)}, device_id_type=MESH
            )
        count += PLANE - 1
    if plane == "near":
        for target in (sibling_of(h), across_of(h), along_of(h)):
            pl.semaphore_signal(barrier, inc=1, device_id={"head": target}, device_id_type=MESH)
        count += 3
    pl.semaphore_wait(barrier, count)


class Bring:
    def __init__(self, sources, places, semaphores):
        self.copies = [
            pltpu.make_async_copy(src, dst, semaphores.at[k])
            for k, (src, dst) in enumerate(zip(sources, places))
        ]

    def start(self):
        for copy in self.copies:
            copy.start()

    def wait(self, *which):
        for k in which:
            self.copies[k].wait()


def held(*arrays):
    return [pltpu.VMEM(item.shape, item.dtype) for item in arrays] + [
        pltpu.SemaphoreType.DMA((len(arrays),))
    ]


class LineGather:
    semaphores = (
        pltpu.SemaphoreType.DMA((LINE,)),
        pltpu.SemaphoreType.DMA((LINE,)),
        pltpu.SemaphoreType.DMA((2,)),
    )

    def __init__(self, source, slot, sent, arrived, other):
        self.r = lax.axis_index("row")
        self.source, self.slot = source, slot
        self.sent, self.arrived, self.other = sent, arrived, other

    def own(self, t):
        return send_to(
            self.source, self.slot(self.r), self.sent.at[t], self.arrived.at[self.r], "row", t
        )

    def handed(self, origin, target):
        return send_to(
            self.slot(origin), self.slot(origin), self.other.at[0], self.arrived.at[origin],
            "row", target,
        )

    def local(self):
        return pltpu.make_async_copy(self.source, self.slot(self.r), self.other.at[1])

    def start(self):
        for gap in (2, -2, 1, -1):
            t = self.r + gap

            @pl.when((t >= 0) & (t < LINE))
            def _(t=t):
                self.own(t).start()

        self.local().start()

    def forward(self):
        for me, origin, target in ((2, 0, 3), (1, 3, 0)):

            @pl.when(self.r == me)
            def _(origin=origin, target=target):
                copy = self.handed(origin, target)
                copy.wait_recv()
                copy.start()

    def finish(self):
        r = self.r
        for t in range(LINE):
            known = (r == t) | ((r == 2) & (t == 0)) | ((r == 1) & (t == 3))
            near = (r != t) & (r - t < 3) & (t - r < 3)

            @pl.when(jnp.logical_not(known))
            def _(t=t):
                self.handed(t, t).wait_recv()

            @pl.when(near)
            def _(t=t):
                self.own(t).wait_send()

        for me, origin, target in ((2, 0, 3), (1, 3, 0)):

            @pl.when(r == me)
            def _(origin=origin, target=target):
                self.handed(origin, target).wait_send()

        self.local().wait()


class LineReduce:
    semaphores = (
        pltpu.SemaphoreType.DMA((LINE,)),
        pltpu.SemaphoreType.DMA((LINE,)),
        pltpu.SemaphoreType.DMA((2,)),
    )

    @staticmethod
    def buffers(rows, width):
        return [
            pltpu.VMEM((LINE, rows, width), jnp.bfloat16),
            pltpu.VMEM((rows, width), jnp.bfloat16),
        ]

    def __init__(self, source, parts, landed, passed, sent, arrived, other):
        self.r = lax.axis_index("row")
        self.source, self.parts, self.landed, self.passed = source, parts, landed, passed
        self.sent, self.arrived, self.other = sent, arrived, other

    def to_pass(self, me, origin, via):
        return send_to(
            self.source.at[origin], self.passed, self.sent.at[origin], self.other.at[0], "row", via
        )

    def direct(self, t):
        return send_to(
            self.source.at[t], self.landed.at[self.r], self.sent.at[t], self.arrived.at[self.r],
            "row", t,
        )

    def added(self, t):
        return send_to(
            self.passed, self.landed.at[self.r], self.sent.at[t], self.arrived.at[self.r], "row", t
        )

    def plain(self, t):
        r = self.r
        ends = ((r == 0) & (t == 3)) | ((r == 3) & (t == 0))
        added = ((r == 1) & (t == 3)) | ((r == 2) & (t == 0))
        return jnp.logical_not(ends | added | (r == t))

    def start(self):
        for me, end, via in ((0, 3, 1), (3, 0, 2)):

            @pl.when(self.r == me)
            def _(me=me, end=end, via=via):
                self.to_pass(me, end, via).start()

        for t in range(LINE):

            @pl.when(self.plain(t))
            def _(t=t):
                self.direct(t).start()

    def forward(self):
        for me, end in ((1, 3), (2, 0)):

            @pl.when(self.r == me)
            def _(me=me, end=end):
                self.to_pass(me, end, end).wait_recv()
                rows = self.passed.shape[0]
                step = 32

                def add(i, unused):
                    at = pl.ds(pl.multiple_of(i * step, step), step)
                    self.passed[at, :] = (
                        self.parts[end, at, :].astype(jnp.float32)
                        + self.passed[at, :].astype(jnp.float32)
                    ).astype(jnp.bfloat16)
                    return unused

                lax.fori_loop(0, rows // step, add, 0)
                self.added(end).start()

    def finish(self, write):
        r = self.r
        for t in range(LINE):

            @pl.when(jnp.logical_not(unsent_to(r, t)))
            def _(t=t):
                send_to(
                    self.source.at[t], self.landed.at[t], self.sent.at[t], self.arrived.at[t],
                    "row", t,
                ).wait_recv()

        def total_of(sources):
            step = 32

            def add(i, unused):
                at = pl.ds(pl.multiple_of(i * step, step), step)
                total = self.parts[r, at, :].astype(jnp.float32)
                for t in sources:
                    total = total + self.landed[t, at, :].astype(jnp.float32)
                write(at, total)
                return unused

            lax.fori_loop(0, self.passed.shape[0] // step, add, 0)

        at_end = (r == 0) | (r == 3)

        @pl.when(at_end)
        def _():
            total_of((1, 2))

        @pl.when(jnp.logical_not(at_end))
        def _():
            total_of((0, 3, 3 - r))

        for me, end, via in ((0, 3, 1), (3, 0, 2)):

            @pl.when(r == me)
            def _(me=me, end=end, via=via):
                self.to_pass(me, end, via).wait_send()

        for t in range(LINE):

            @pl.when(jnp.logical_not(unsent_to(r, t)))
            def _(t=t):
                self.direct(t).wait_send()


def unsent_to(r, t):
    return ((r == 0) & (t == 3)) | ((r == 3) & (t == 0)) | (r == t)


class PlaneGather:
    semaphores = (
        pltpu.SemaphoreType.DMA((PIECES, 7)),
        pltpu.SemaphoreType.DMA((PIECES, 7)),
        pltpu.SemaphoreType.DMA((PIECES,)),
    )
    first = tuple(range(PIECES // 2))
    second = tuple(range(PIECES // 2, PIECES))

    def __init__(self, block, full, sent, arrived, other, source=None, target=None):
        h = lax.axis_index("head")
        self.source, self.target = source, target
        self.h, self.side, self.x, self.y = h, sibling_of(h), across_of(h), along_of(h)
        self.far = across_of(self.y)
        self.block, self.full = block, full
        self.sent, self.arrived, self.other = sent, arrived, other
        self.rows = block.shape[0] // PIECES

    def piece(self, owner, c):
        rows = pl.ds(c * self.rows, self.rows)
        if self.target is None:
            return self.full.at[owner, rows]
        return self.full.at[owner, rows, self.target]

    def mine(self, c):
        rows = pl.ds(c * self.rows, self.rows)
        return self.block.at[rows] if self.source is None else self.block.at[rows, self.source]

    def own(self, c, lane, target):
        return send_to(
            self.mine(c), self.piece(self.h, c),
            self.sent.at[c, lane], self.arrived.at[c, lane], "head", target,
        )

    def hand(self, owner, c, lane, target):
        return send_to(
            self.piece(owner, c), self.piece(owner, c), self.sent.at[c, lane],
            self.arrived.at[c, lane], "head", target,
        )

    def local(self, c):
        return pltpu.make_async_copy(self.mine(c), self.piece(self.h, c), self.other.at[c])

    def start(self):
        for a, b in zip(self.first, self.second):
            self.own(a, 1, self.x).start()
            self.own(b, 2, self.y).start()
        for a, b in zip(self.first, self.second):
            self.own(b, 1, self.x).start()
            self.own(a, 2, self.y).start()
        for c in range(PIECES):
            self.own(c, 0, self.side).start()
            self.local(c).start()

    def relay(self, place):
        a, b = self.first[place], self.second[place]
        self.hand(self.x, a, 1, self.x).wait_recv()
        self.hand(self.x, a, 3, self.y).start()
        self.hand(self.x, a, 4, self.side).start()
        self.hand(self.y, b, 2, self.y).wait_recv()
        self.hand(self.y, b, 3, self.x).start()
        self.hand(self.y, b, 5, self.side).start()

    def rest(self):
        for a, b in zip(self.first, self.second):
            self.hand(self.x, b, 1, self.x).wait_recv()
            self.hand(self.x, b, 4, self.side).start()
            self.hand(self.y, a, 2, self.y).wait_recv()
            self.hand(self.y, a, 5, self.side).start()

    def beside(self):
        for c in range(PIECES):
            self.hand(self.side, c, 0, self.side).wait_recv()

    def far_side(self):
        for pair in zip(self.first, self.second):
            for c in pair:
                self.hand(self.far, c, 3, self.side).wait_recv()
                self.hand(self.far, c, 6, self.side).start()

    def end(self, beside=True):
        side = self.side
        if beside:
            self.beside()
        for c in range(PIECES):
            for owner, lane in (
                (across_of(side), 4), (along_of(side), 5), (across_of(along_of(side)), 6)
            ):
                self.hand(owner, c, lane, side).wait_recv()
        for c in range(PIECES):
            for lane in range(7):
                self.own(c, lane, side).wait_send()
            self.local(c).wait()


class PlaneReduce:
    semaphores = (
        pltpu.SemaphoreType.DMA((4,)),
        pltpu.SemaphoreType.DMA((4,)),
        pltpu.SemaphoreType.DMA((4, 2)),
        pltpu.SemaphoreType.DMA((2, 2)),
        pltpu.SemaphoreType.DMA((2,)),
    )

    @staticmethod
    def buffers(rows, width):
        return [
            pltpu.VMEM((4, rows, width), jnp.bfloat16),
            pltpu.VMEM((4, rows, width), jnp.bfloat16),
            pltpu.VMEM((4, rows, width), jnp.bfloat16),
            pltpu.VMEM((2, rows // 2, width), jnp.bfloat16),
            pltpu.VMEM((2, rows, width), jnp.bfloat16),
        ]

    def __init__(
        self, staged, beside, mine, relayed, landed,
        side_sent, side_arrived, sent, arrived, relay_arrived,
    ):
        h = lax.axis_index("head")
        self.h, self.core, self.chip = h, lax.rem(h, 2), lax.div(h, 2)
        self.staged, self.beside, self.mine = staged, beside, mine
        self.relayed, self.landed = relayed, landed
        self.side_sent, self.side_arrived = side_sent, side_arrived
        self.sent, self.arrived, self.relay_arrived = sent, arrived, relay_arrived
        self.half = mine.shape[1] // 2

    def aside(self, chip):
        return send_to(
            self.staged.at[chip], self.beside.at[chip], self.side_sent.at[chip],
            self.side_arrived.at[chip], "head", sibling_of(self.h),
        )

    def relation(self, chip):
        flip_x = lax.rem(chip + self.chip, 2)
        flip_y = lax.rem(lax.div(chip, 2) + lax.div(self.chip, 2), 2)
        return flip_x + 2 * flip_y

    def part(self, half):
        return pl.ds(half * self.half, self.half)

    def home(self, chip, way, half):
        return send_to(
            self.mine.at[chip, self.part(half)], self.landed.at[way, self.part(half)],
            self.sent.at[chip, half], self.arrived.at[way, half], "head",
            (across_of, along_of)[way](self.h),
        )

    def opposite(self, chip, half):
        return send_to(
            self.mine.at[chip, self.part(half)], self.relayed.at[half], self.sent.at[chip, half],
            self.relay_arrived.at[half], "head", (along_of, across_of)[half](self.h),
        )

    def put(self, block, value):
        chip, core = lax.div(block, 2), lax.rem(block, 2)

        @pl.when(core == self.core)
        def _():
            self.mine[chip] = value

        @pl.when(core != self.core)
        def _():
            self.staged[chip] = value
            self.aside(chip).start()

    def pass_on(self, block):
        chip, core = lax.div(block, 2), lax.rem(block, 2)

        @pl.when(core == self.core)
        def _():
            self.aside(chip).wait_recv()
            step = 32

            def add(i, unused):
                at = pl.ds(pl.multiple_of(i * step, step), step)
                self.mine[chip, at, :] = (
                    self.mine[chip, at, :].astype(jnp.float32)
                    + self.beside[chip, at, :].astype(jnp.float32)
                ).astype(jnp.bfloat16)
                return unused

            lax.fori_loop(0, 2 * self.half // step, add, 0)
            relation = self.relation(chip)

            @pl.when(relation == 1)
            def _():
                self.home(chip, 0, 1).start()

            @pl.when(relation == 2)
            def _():
                self.home(chip, 1, 0).start()

            @pl.when(relation == 3)
            def _():
                self.opposite(chip, 0).start()
                self.opposite(chip, 1).start()

    def relay(self, block):
        chip, core = lax.div(block, 2), lax.rem(block, 2)
        for way in (0, 1):

            @pl.when((core == self.core) & (self.relation(chip) == way + 1))
            def _(way=way):
                self.opposite(chip, way).wait_recv()
                step = 32

                def add(i, unused):
                    at = pl.ds(pl.multiple_of(i * step, step), step)
                    here = pl.ds(pl.multiple_of(way * self.half + i * step, step), step)
                    self.mine[chip, here, :] = (
                        self.mine[chip, here, :].astype(jnp.float32)
                        + self.relayed[way, at, :].astype(jnp.float32)
                    ).astype(jnp.bfloat16)
                    return unused

                lax.fori_loop(0, self.half // step, add, 0)
                self.home(chip, way, way).start()

    def arrive(self):
        for way in (0, 1):
            for half in (0, 1):
                self.home(self.chip, way, half).wait_recv()

    def total(self, at):
        value = self.mine[self.chip, at, :].astype(jnp.float32)
        return (
            value
            + self.landed[0, at, :].astype(jnp.float32)
            + self.landed[1, at, :].astype(jnp.float32)
        )

    def finish(self):
        for chip in range(4):
            self.aside(chip).wait_send()

            @pl.when(chip != self.chip)
            def _(chip=chip):
                self.home(chip, 0, 0).wait_send()
                self.home(chip, 0, 1).wait_send()


def norm_apply(rows, gain):
    return rows * lax.rsqrt(jnp.mean(rows * rows, axis=-1, keepdims=True) + EPSILON) * gain


def gather(values, axis_name, axis):
    return lax.all_gather(values, axis_name, axis=axis, tiled=True)


def scatter(values, axis_name, axis):
    return lax.psum_scatter(values, axis_name, scatter_dimension=axis, tiled=True)

def once(shape):
    return pl.BlockSpec(
        shape, lambda i: (0,) * len(shape), pipeline_mode=pl.Buffered(buffer_count=1)
    )


def norm_rows(rows, gain):
    return rows * lax.rsqrt(jnp.mean(rows * rows, axis=-1, keepdims=True) + EPSILON) * gain


def lay_out_params(
    taps_ref, biases, decay_ref, rate_ref, entry_ref, resets_ref,
    taps_out, vec_out, wr_out, we_out, keep_out, square, moved,
):
    used, width = decay_ref.shape[1], rate_ref.shape[1]
    columns = vec_out.shape[1]
    taps_out[...] = jnp.zeros_like(taps_out)
    taps_out[:, 0:used] = taps_ref[...]
    vec_out[...] = jnp.zeros_like(vec_out)
    for k, bias in enumerate(biases):
        vec_out[k : k + 1, 0:used] = bias[...]
    vec_out[3:4, :] = jnp.full((1, columns), 2.0, jnp.float32)
    vec_out[3:4, 0:used] = decay_ref[...]
    decay = vec_out[3:4, :]
    vec_out[3:4, :] = -8.0 * jnp.log1p(jnp.exp(-decay))
    vec_out[4:5, :] = 8.0 * jax.nn.sigmoid(-decay)
    for source, out in ((rate_ref, wr_out), (entry_ref, we_out)):
        square[...] = jnp.zeros_like(square)
        square[0:width, 0:width] = source[1].astype(jnp.float32)
        moved[...] = pltpu.roll(pltpu.roll(square[...], width, 0), width, 1)
        square[...] = jnp.zeros_like(square)
        square[0:width, 0:width] = source[0].astype(jnp.float32)
        out[...] = (square[...] + moved[...]).astype(jnp.bfloat16)
    resets = resets_ref[...]
    first = lax.broadcasted_iota(jnp.int32, resets.shape, 1) == 0
    one = jnp.where(first | (resets > 0), 0.0, 1.0)
    length = resets.shape[1]
    two = one * pltpu.roll(one, 1, 1)
    three = two * pltpu.roll(one, 2, 1)
    ahead = [pltpu.roll(item, length - k, 1) for k, item in ((1, one), (2, two), (3, three))]
    rows = jnp.concatenate(
        [one, one, two, three, *ahead, one, jnp.zeros((120, length), jnp.float32)], axis=0
    )
    for k in range(length // 128):
        turned = rows[:, k * 128 : (k + 1) * 128].T
        keep_out[k * 128 : (k + 1) * 128, :] = turned[:, 0:8]


def open_body(
    x_ref, mix_ref, ffn_ref, cot, xt_ref, yt_ref, ot_ref,
    taps_ref, conv_bias, rate_bias, entry_bias, decay_ref, rate_ref, entry_ref, resets_ref,
    full, cot_out, xy_full, out_full, gains_ref, taps_out, vec_out, wr_out, we_out, keep_out,
    shards, blank, square, moved,
    normed, column, spread, gain_sent, gain_arrived, wide_sent, wide_arrived, wiped, *semaphores,
):
    r, h = lax.axis_index("row"), lax.axis_index("head")
    held_rows, share = shards.shape[1:]
    used, chans = xt_ref.shape[0], out_full.shape[0]

    def slot(full, first):
        def at(origin):
            lanes = pl.ds(pl.multiple_of(origin * share, share), share)
            return full.at[pl.ds(first, held_rows), lanes]

        return at

    lines = [
        LineGather(shards.at[k], slot(dst, first), *semaphores[3 * k : 3 * k + 3])
        for k, (dst, first) in enumerate(((xy_full, 0), (xy_full, chans), (out_full, 0)))
    ]
    wipes = [
        pltpu.make_async_copy(
            blank, dst.at[pl.ds(first + held_rows, chans - held_rows)], wiped.at[k]
        )
        for k, (dst, first) in enumerate(((xy_full, 0), (xy_full, chans), (out_full, 0)))
    ]
    plane = PlaneGather(normed, full, *semaphores[9:12])
    cot_plane = PlaneGather(
        cot, cot_out, *semaphores[12:15], source=pl.ds(0, cot_out.shape[2])
    )
    for k, source in enumerate((xt_ref, yt_ref, ot_ref)):
        shards[k, held_rows - 16 :, :] = jnp.zeros((16, share), jnp.bfloat16)
        shards[k, 0:used, :] = source[...]
    gain_share = mix_ref.shape[1]
    low = lax.broadcasted_iota(jnp.int32, (8, 2 * gain_share), 1) < gain_share
    column[r] = jnp.zeros_like(column[r])
    column[r, 0:1, 0:gain_share] = mix_ref[...].astype(jnp.float32)
    column[r, 1:2, 0:gain_share] = ffn_ref[...].astype(jnp.float32)
    rows = column[r]
    column[r] = jnp.where(low, rows, pltpu.roll(pltpu.roll(rows, gain_share, 1), 7, 0))
    meet(True, "all")

    def up_line(t):
        return send_to(
            column.at[r], column.at[r], gain_sent.at[t], gain_arrived.at[r], "row", t
        )

    def from_line(t):
        return send_to(
            column.at[t], column.at[t], gain_sent.at[t], gain_arrived.at[t], "row", t
        )

    def over_plane(step, owner):
        return send_to(
            column, spread.at[owner], wide_sent.at[step], wide_arrived.at[owner], "head",
            lax.rem(h + step, PLANE),
        )

    for step in range(1, LINE):
        up_line(lax.rem(r + step, LINE)).start()
    for line in lines:
        line.start()
    blank[...] = jnp.zeros_like(blank)
    for wipe in wipes:
        wipe.start()
    for step in range(1, LINE):
        from_line(lax.rem(r + step, LINE)).wait_recv()
    for step in range(1, PLANE):
        over_plane(step, h).start()
    cot_plane.start()
    spread[h] = column[...]
    for step in range(1, PLANE):
        over_plane(step, lax.rem(h + step, PLANE)).wait_recv()

    low = lax.broadcasted_iota(jnp.int32, (1, 2 * gain_share), 1) < gain_share
    for line_place in range(LINE):
        for pair in range(PLANE // 2):
            even = spread[2 * pair, line_place][0:1, :]
            odd = spread[2 * pair + 1, line_place][0:1, :]
            at = (line_place * (PLANE // 2) + pair) * 2 * gain_share
            end = at + 2 * gain_share
            gains_ref[0:1, at:end] = jnp.where(low, even, pltpu.roll(odd, gain_share, 1))
            gains_ref[1:2, at:end] = jnp.where(low, pltpu.roll(even, gain_share, 1), odd)

    def make(i, unused):
        at = pl.ds(pl.multiple_of(i * CHUNK, CHUNK), CHUNK)
        normed[at, :] = norm_rows(x_ref[at, :].astype(jnp.float32), gains_ref[0:1, :]).astype(
            jnp.bfloat16
        )
        return unused

    lax.fori_loop(0, x_ref.shape[0] // CHUNK, make, 0)
    plane.start()
    lay_out_params(
        taps_ref, (conv_bias, rate_bias, entry_bias), decay_ref, rate_ref, entry_ref, resets_ref,
        taps_out, vec_out, wr_out, we_out, keep_out, square, moved,
    )
    cot_plane.relay(0)
    cot_plane.relay(1)
    lines[0].forward()
    cot_plane.rest()
    plane.relay(0)
    plane.relay(1)
    lines[1].forward()
    cot_plane.far_side()
    cot_plane.end()
    plane.rest()
    plane.far_side()
    plane.end()
    lines[2].forward()
    for line in lines:
        line.finish()
    for wipe in wipes:
        wipe.wait()
    for step in range(1, LINE):
        up_line(lax.rem(r + step, LINE)).wait_send()
    for step in range(1, PLANE):
        over_plane(step, h).wait_send()


def open_block(layer_in, gains, cot, weights, params):
    rows, width = layer_in.shape
    used, share = weights[0].shape
    chans, held_rows = -(-used // 128) * 128, -(-used // 16) * 16
    length = params[-1].shape[1]
    tile = (8, 2 * gains[0].shape[1])
    return pl.pallas_call(
        open_body,
        in_specs=[IN_VMEM, IN_VMEM, IN_VMEM, ANYWHERE] + [IN_VMEM] * 11,
        out_specs=[ANYWHERE] * 4 + [IN_VMEM] * 6,
        out_shape=[
            jax.ShapeDtypeStruct((PLANE, rows, width), jnp.bfloat16),
            jax.ShapeDtypeStruct((PLANE, rows, width // 2), jnp.bfloat16),
            jax.ShapeDtypeStruct((2 * chans, width), jnp.bfloat16),
            jax.ShapeDtypeStruct((chans, width), jnp.bfloat16),
            jax.ShapeDtypeStruct((2, width), jnp.float32),
            jax.ShapeDtypeStruct((4, chans), jnp.float32),
            jax.ShapeDtypeStruct((8, chans), jnp.float32),
            jax.ShapeDtypeStruct((chans, chans), jnp.bfloat16),
            jax.ShapeDtypeStruct((chans, chans), jnp.bfloat16),
            jax.ShapeDtypeStruct((length, 8), jnp.float32),
        ],
        scratch_shapes=[
            pltpu.VMEM((3, held_rows, share), jnp.bfloat16),
            pltpu.VMEM((chans - held_rows, width), jnp.bfloat16),
            pltpu.VMEM((chans, chans), jnp.float32),
            pltpu.VMEM((chans, chans), jnp.float32),
            pltpu.VMEM((rows, width), jnp.bfloat16),
            pltpu.VMEM((LINE,) + tile, jnp.float32),
            pltpu.VMEM((PLANE, LINE) + tile, jnp.float32),
            pltpu.SemaphoreType.DMA((LINE,)),
            pltpu.SemaphoreType.DMA((LINE,)),
            pltpu.SemaphoreType.DMA((PLANE,)),
            pltpu.SemaphoreType.DMA((PLANE,)),
            pltpu.SemaphoreType.DMA((3,)),
            *(LineGather.semaphores * 3),
            *(PlaneGather.semaphores * 2),
        ],
        compiler_params=pltpu.CompilerParams(
            collective_id=0, has_side_effects=True, vmem_limit_bytes=61 * 2**20
        ),
        name="open_block",
    )(layer_in, *gains, cot, *weights, *params)


def forward_linked_body(
    normed_ref, xy_hbm, ow_hbm, taps_ref, vec_ref, wr_ref, we_ref, keep_ref,
    x_hbm, gain_ref, gate_shard, up_shard,
    u_ref, by_ref, before_ref, states_ref, mixed_ref, residual_ref, two_ref, gate_out, up_out,
    xy_ref, ow_ref, x_ref, brought,
    window, conv, conv_low, rate, entry, carry, *links,
):
    step = pl.program_id(0)
    plane = PlaneReduce(*links[:10])
    gate_line = LineGather(gate_shard, lambda t: gate_out.at[t], *links[10:13])
    first_rows = up_shard.at[pl.ds(0, up_out.shape[1])]
    up_line = LineGather(first_rows, lambda t: up_out.at[t], *links[13:16])

    bring = Bring((xy_hbm, ow_hbm, x_hbm), (xy_ref, ow_ref, x_ref), brought)

    @pl.when(step == 0)
    def _():
        bring.start()
        meet(True, "near")
        gate_line.start()
        up_line.start()
        bring.wait(0, 1, 2)

    @pl.when(step > 0)
    def _():
        plane.pass_on(step - 1)

    @pl.when(step > 2)
    def _():
        plane.relay(step - 3)

    forward_step(
        normed_ref, xy_ref, taps_ref, vec_ref, wr_ref, we_ref, keep_ref,
        u_ref, by_ref, before_ref, states_ref, mixed_ref,
        window, conv, conv_low, rate, entry, carry,
    )
    plane.put(step, dot_plain(mixed_ref[...], ow_ref[...]).astype(jnp.bfloat16))

    @pl.when(step == 6)
    def _():
        gate_line.forward()

    @pl.when(step == PLANE - 1)
    def _():
        plane.relay(step - 2)
        plane.pass_on(step)
        plane.relay(step - 1)
        plane.relay(step)
        up_line.forward()
        plane.arrive()

        def make(i, unused):
            at = pl.ds(pl.multiple_of(i * CHUNK, CHUNK), CHUNK)
            residual = x_ref[at, :].astype(jnp.float32) + plane.total(at)
            residual_ref[at, :] = residual
            two_ref[at, :] = norm_rows(residual, gain_ref[...]).astype(jnp.bfloat16)
            return unused

        lax.fori_loop(0, x_ref.shape[0] // CHUNK, make, 0)
        plane.finish()
        gate_line.finish()
        up_line.finish()


def forward_linked(normed, xy, ow, taps, vec, wr, we, keep, layer_in, gain, gate_shard, up_shard):
    length, width = normed.shape
    chans = ow.shape[0]
    rows = length // PLANE
    share, units = up_shard.shape
    tile = lambda columns: pl.BlockSpec((rows, columns), lambda i: (i, 0))
    return pl.pallas_call(
        forward_linked_body,
        grid=(PLANE,),
        in_specs=[
            tile(width), ANYWHERE, ANYWHERE, once(taps.shape),
            once(vec.shape), once(wr.shape), once(we.shape), tile(keep.shape[1]),
            ANYWHERE, once(gain.shape), ANYWHERE, ANYWHERE,
        ],
        out_specs=[tile(chans)] * 5 + [once((rows, width))] * 2 + [ANYWHERE] * 2,
        out_shape=[
            jax.ShapeDtypeStruct((length, chans), jnp.bfloat16),
            jax.ShapeDtypeStruct((length, chans), jnp.float32),
            jax.ShapeDtypeStruct((length, chans), jnp.float32),
            jax.ShapeDtypeStruct((length, chans), jnp.bfloat16),
            jax.ShapeDtypeStruct((length, chans), jnp.bfloat16),
            jax.ShapeDtypeStruct((rows, width), jnp.float32),
            jax.ShapeDtypeStruct((rows, width), jnp.bfloat16),
            jax.ShapeDtypeStruct((LINE,) + gate_shard.shape, jnp.bfloat16),
            jax.ShapeDtypeStruct((LINE, share // 2, units), jnp.bfloat16),
        ],
        scratch_shapes=[
            *held(xy, ow, layer_in),
            pltpu.VMEM((rows + 8, chans), jnp.float32),
            pltpu.VMEM((rows, chans), jnp.float32),
            pltpu.VMEM((rows, chans), jnp.bfloat16),
            pltpu.VMEM((rows, chans), jnp.float32),
            pltpu.VMEM((rows, chans), jnp.float32),
            pltpu.VMEM((8, chans), jnp.float32),
            *PlaneReduce.buffers(rows, width),
            *PlaneReduce.semaphores,
            *(LineGather.semaphores * 2),
        ],
        compiler_params=pltpu.CompilerParams(
            collective_id=1, has_side_effects=True, vmem_limit_bytes=61 * 2**20
        ),
        name="mixer_forward_linked",
    )(normed, xy, ow, taps, vec, wr, we, keep, layer_in, gain, gate_shard, up_shard)


def ffn_up_body(
    own_two, gate_ref, own_cot, cot_half, up_half, up_shard, down_shard,
    two_out, cot_out, up_out, down_out, gates_out, ups_out, hidden_out, down_parts,
    two, cot, up, gates, ups, hidden, total, copied, brought, *semaphores,
):
    h = lax.axis_index("head")
    rows = own_two.shape[0]
    units = gates.shape[1]
    width, share = own_two.shape[1], up_shard.shape[0]
    half = share // 2
    late_columns = pl.ds(width // 2, width // 2)
    up_line = LineGather(
        up_shard.at[pl.ds(half, half)],
        lambda t: up.at[pl.ds(pl.multiple_of(t * share + half, half), half)],
        *semaphores[0:3],
    )
    down_line = LineGather(down_shard, lambda t: down_out.at[t], *semaphores[3:6])
    two_plane = PlaneGather(own_two, two, *semaphores[6:9])
    cot_plane = PlaneGather(
        own_cot, cot, *semaphores[9:12], source=late_columns, target=late_columns
    )
    inward = [
        pltpu.make_async_copy(up_half.at[t], up.at[pl.ds(t * share, half)], brought.at[t])
        for t in range(LINE)
    ]
    inward.append(
        pltpu.make_async_copy(cot_half, cot.at[:, :, pl.ds(0, width // 2)], brought.at[LINE])
    )
    outward = [
        pltpu.make_async_copy(src, dst, copied.at[k])
        for k, (src, dst) in enumerate(
            (
                (two, two_out), (cot, cot_out), (up, up_out), (gates, gates_out),
                (ups, ups_out), (hidden, hidden_out),
            )
        )
    ]
    meet(True, "near")
    up_line.start()
    down_line.start()
    two_plane.start()
    for copy in inward:
        copy.start()

    def at_block(block):
        return pl.ds(pl.multiple_of(block * rows, rows), rows)

    def make_gates(block):
        gates[at_block(block), :] = dot_plain(two[block], gate_ref[...])

    gates[at_block(h), :] = dot_plain(own_two[...], gate_ref[...])
    two_plane.relay(0)
    two_plane.beside()
    make_gates(two_plane.side)
    two_plane.relay(1)
    cot_plane.start()
    two_plane.rest()
    make_gates(two_plane.x)
    make_gates(two_plane.y)
    up_line.forward()
    two_plane.far_side()
    make_gates(two_plane.far)
    two_plane.end(beside=False)
    outward[0].start()
    cot_plane.relay(0)
    make_gates(across_of(two_plane.side))
    make_gates(along_of(two_plane.side))
    cot_plane.relay(1)
    make_gates(across_of(along_of(two_plane.side)))
    outward[3].start()
    up_line.finish()
    for copy in inward:
        copy.wait()
    outward[2].start()

    def make_hidden(block, unused):
        at = at_block(block)
        ups[at, :] = dot_plain(two[block], up[...])

        def make(i, unused):
            here = pl.ds(pl.multiple_of(block * rows + i * CHUNK, CHUNK), CHUNK)
            hidden[here, :] = (gelu_only(gates[here, :]) * ups[here, :]).astype(jnp.bfloat16)
            return unused

        lax.fori_loop(0, rows // CHUNK, make, 0, unroll=UNROLL)
        return unused

    lax.fori_loop(0, 2, make_hidden, 0)
    cot_plane.rest()
    lax.fori_loop(2, 5, make_hidden, 0)
    cot_plane.far_side()
    down_line.forward()
    lax.fori_loop(5, PLANE, make_hidden, 0)
    outward[4].start()
    outward[5].start()
    cot_plane.end()
    outward[1].start()
    total[...] = contract_first(cot[0], hidden[0:rows, :])

    def add_down(block, unused):
        total[...] += contract_first(cot[block], hidden[at_block(block), :])
        return unused

    lax.fori_loop(1, PLANE, add_down, 0)
    to_parts(total, down_parts)
    down_line.finish()
    for copy in outward:
        copy.wait()


def ffn_up(own_two, gate, own_cot, cot_half, up_half, up_shard, down_shard):
    rows, width = own_two.shape
    share, units = up_shard.shape
    length = rows * PLANE
    group = jax.ShapeDtypeStruct((PLANE, rows, width), jnp.bfloat16)
    weight = jax.ShapeDtypeStruct((LINE, share, units), jnp.bfloat16)
    return pl.pallas_call(
        ffn_up_body,
        in_specs=[IN_VMEM, IN_VMEM] + [ANYWHERE] * 5,
        out_specs=[ANYWHERE] * 7 + [IN_VMEM],
        out_shape=[
            group,
            group,
            jax.ShapeDtypeStruct((width, units), jnp.bfloat16),
            weight,
            jax.ShapeDtypeStruct((length, units), jnp.float32),
            jax.ShapeDtypeStruct((length, units), jnp.float32),
            jax.ShapeDtypeStruct((length, units), jnp.bfloat16),
            weight,
        ],
        scratch_shapes=[
            pltpu.VMEM((PLANE, rows, width), jnp.bfloat16),
            pltpu.VMEM((PLANE, rows, width), jnp.bfloat16),
            pltpu.VMEM((width, units), jnp.bfloat16),
            pltpu.VMEM((length, units), jnp.float32),
            pltpu.VMEM((length, units), jnp.float32),
            pltpu.VMEM((length, units), jnp.bfloat16),
            pltpu.VMEM((width, units), jnp.float32),
            pltpu.SemaphoreType.DMA((6,)),
            pltpu.SemaphoreType.DMA((LINE + 1,)),
            *(LineGather.semaphores * 2),
            *(PlaneGather.semaphores * 2),
        ],
        compiler_params=pltpu.CompilerParams(
            collective_id=2, has_side_effects=True, vmem_limit_bytes=61 * 2**20
        ),
        name="ffn_up",
    )(own_two, gate, own_cot, cot_half, up_half, up_shard, down_shard)
def far_first(step):
    chip = lax.div(lax.axis_index("head"), 2)
    place = lax.div(step, 2)
    x = lax.rem(lax.rem(chip, 2) + 1 - lax.div(place, 2), 2)
    y = lax.rem(lax.div(chip, 2) + 1 + lax.rem(place, 2), 2)
    return 2 * (2 * y + x) + lax.rem(step, 2)


def norm_back(rows, gain, incoming):
    scale = lax.rsqrt(jnp.mean(rows * rows, axis=-1, keepdims=True) + EPSILON)
    scaled = incoming * gain
    inner = jnp.mean(scaled * rows, axis=-1, keepdims=True)
    return scale * scaled - rows * (scale * scale * scale * inner), incoming * rows * scale


def to_parts(total, parts):
    rows = parts.shape[1]
    step = 64

    def move(i, unused):
        at = pl.ds(pl.multiple_of(i * step, step), step)
        for t in range(LINE):
            here = pl.ds(pl.multiple_of(t * rows + i * step, step), step)
            parts[t, at, :] = total[here, :].astype(jnp.bfloat16)
        return unused

    lax.fori_loop(0, rows // step, move, 0)


def to_turned_parts(total, parts, places):
    share = parts.shape[2]
    step = 32
    for first, target, count in places:

        def move(i, unused, first=first, target=target):
            here = pl.ds(pl.multiple_of(first + i * step, step), step)
            at = pl.ds(pl.multiple_of(target + i * step, step), step)
            for t in range(LINE):
                parts[t, at, :] = total[here, t * share : (t + 1) * share].astype(jnp.bfloat16)
            return unused

        lax.fori_loop(0, count // step, move, 0)


def ffn_back_body(
    cot_ref, two_ref, gates_ref, ups_ref, gate_hbm, up_hbm, down_hbm, parts_hbm,
    residual_hbm, own_cot_hbm, gain_ref,
    d_ups_ref, gate_parts, down_out, d_res_ref, d_low_ref, gain_out,
    gate_ref, up_ref, down_ref, parts, brought, late,
    total, d_gates, d_hidden, eight, *links,
):
    step = pl.program_id(0)
    line = LineReduce(parts_hbm, parts, *links[:5])
    plane = PlaneReduce(*links[5:])
    rows = cot_ref.shape[0]

    bring = Bring(
        (down_hbm, gate_hbm, up_hbm, parts_hbm), (down_ref, gate_ref, up_ref, parts), brought
    )
    into_outputs = Bring((residual_hbm, own_cot_hbm), (d_res_ref, d_low_ref), late)

    @pl.when(step == 0)
    def _():
        bring.start()
        meet(True, "near")
        line.start()
        into_outputs.start()
        bring.wait(0, 1, 2, 3)

    @pl.when((step > 2) & (step <= PLANE + 2))
    def _():
        plane.relay(far_first(step - 3))

    @pl.when(step < PLANE)
    def _():
        d_hidden[...] = dot_plain(cot_ref[...], down_ref[...])

        def make(i, unused):
            at = pl.ds(pl.multiple_of(i * CHUNK, CHUNK), CHUNK)
            gelu_gate, slope = gelu_both(gates_ref[at, :])
            through = d_hidden[at, :]
            d_gates[step, at, :] = (through * ups_ref[at, :] * slope).astype(jnp.bfloat16)
            d_ups_ref[at, :] = (through * gelu_gate).astype(jnp.bfloat16)
            return unused

        lax.fori_loop(0, rows // CHUNK, make, 0, unroll=UNROLL)

        @pl.when(step > 0)
        def _():
            plane.pass_on(far_first(step - 1))

        value = contract_last(d_gates[step], gate_ref[...]) + contract_last(
            d_ups_ref[...], up_ref[...]
        )
        plane.put(far_first(step), value.astype(jnp.bfloat16))

    @pl.when(step == PLANE)
    def _():
        total[...] = contract_first(two_ref[...], d_gates[0])

    @pl.when(step > PLANE)
    def _():
        total[...] += contract_first(two_ref[...], d_gates[step - PLANE])

    @pl.when(step == PLANE)
    def _():
        plane.pass_on(far_first(step - 1))

    @pl.when(step == 5)
    def _():
        line.forward()

    @pl.when(step == 2 * PLANE - 1)
    def _():
        to_parts(total, gate_parts)
        plane.arrive()
        into_outputs.wait(0, 1)
        eight[...] = jnp.zeros_like(eight)

        def back(i, unused):
            at = pl.ds(pl.multiple_of(i * CHUNK, CHUNK), CHUNK)
            d_rows, d_gain = norm_back(d_res_ref[at, :], gain_ref[...], plane.total(at))
            d_residual = d_low_ref[at, :].astype(jnp.float32) + d_rows
            d_res_ref[at, :] = d_residual
            d_low_ref[at, :] = d_residual.astype(jnp.bfloat16)
            eight[...] += sum_eight(d_gain)
            return unused

        lax.fori_loop(0, rows // CHUNK, back, 0)
        gain_out[...] = jnp.sum(eight[...], axis=0, keepdims=True)

        def write(at, value):
            down_out[at, :] = value

        line.finish(write)
        plane.finish()


def ffn_back(
    cot_group, two_group, gates, ups, gate, up, down, parts, residual, own_cot, gain
):
    length, width = cot_group.shape
    units = gate.shape[1]
    rows, share = length // PLANE, width // LINE
    tile = lambda columns: pl.BlockSpec(
        (rows, columns), lambda i: (far_first(jnp.minimum(i, PLANE - 1)), 0)
    )
    later = lambda columns: pl.BlockSpec(
        (rows, columns), lambda i: (far_first(jnp.maximum(i - PLANE, 0)), 0)
    )
    return pl.pallas_call(
        ffn_back_body,
        grid=(2 * PLANE,),
        in_specs=[
            tile(width), later(width), tile(units), tile(units),
            *([ANYWHERE] * 6), once(gain.shape),
        ],
        out_specs=[
            tile(units), once((LINE, share, units)), once((share, units)),
            once((rows, width)), once((rows, width)), once((1, width)),
        ],
        out_shape=[
            jax.ShapeDtypeStruct((length, units), jnp.bfloat16),
            jax.ShapeDtypeStruct((LINE, share, units), jnp.bfloat16),
            jax.ShapeDtypeStruct((share, units), jnp.float32),
            jax.ShapeDtypeStruct((rows, width), jnp.float32),
            jax.ShapeDtypeStruct((rows, width), jnp.bfloat16),
            jax.ShapeDtypeStruct((1, width), jnp.float32),
        ],
        scratch_shapes=[
            *held(gate, up, down, parts),
            pltpu.SemaphoreType.DMA((2,)),
            pltpu.VMEM((width, units), jnp.float32),
            pltpu.VMEM((PLANE, rows, units), jnp.bfloat16),
            pltpu.VMEM((rows, units), jnp.float32),
            pltpu.VMEM((8, width), jnp.float32),
            *LineReduce.buffers(share, units),
            *LineReduce.semaphores,
            *PlaneReduce.buffers(rows, width),
            *PlaneReduce.semaphores,
        ],
        compiler_params=pltpu.CompilerParams(
            collective_id=4, has_side_effects=True, vmem_limit_bytes=63 * 2**20
        ),
        name="ffn_back",
    )(cot_group, two_group, gates, ups, gate, up, down, parts, residual, own_cot, gain)


def turn_body(
    two_ref, d_ups_ref, parts_hbm, block, mixed_hbm, ow_hbm,
    up_parts, out_parts, gate_out, d_mixed_out,
    gate_parts, mixed_ref, ow_ref, brought,
    full, total, out_total, *links,
):
    step = pl.program_id(0)
    line = LineReduce(parts_hbm, gate_parts, *links[:5])
    plane = PlaneGather(block, full, *links[5:])
    rows = two_ref.shape[0]

    bring = Bring(
        (parts_hbm, mixed_hbm, ow_hbm), (gate_parts, mixed_ref, ow_ref), brought
    )

    @pl.when(step == 0)
    def _():
        bring.start()
        meet(True, "near")
        line.start()
        plane.start()
        total[...] = contract_first(two_ref[...], d_ups_ref[...])

    @pl.when(step > 0)
    def _():
        total[...] += contract_first(two_ref[...], d_ups_ref[...])

    @pl.when(step == 3)
    def _():
        plane.relay(0)

    @pl.when(step == PLANE - 2)
    def _():
        plane.relay(1)

    @pl.when(step == PLANE - 1)
    def _():
        bring.wait(0, 1, 2)
        line.forward()

        def add(owner, start=False):
            at = pl.ds(pl.multiple_of(owner * rows, rows), rows)
            d_mixed_out[at, :] = contract_last(full[owner], ow_ref[...])
            value = contract_first(mixed_ref[at, :], full[owner])
            out_total[...] = value if start else out_total[...] + value

        plane.beside()
        add(plane.side, start=True)
        to_parts(total, up_parts)
        plane.rest()
        add(plane.x)
        add(plane.y)
        plane.far_side()
        add(plane.far)
        plane.end(beside=False)
        add(plane.h)
        add(across_of(plane.side))
        add(along_of(plane.side))
        add(across_of(along_of(plane.side)))
        kept = out_parts.shape[1]
        to_turned_parts(out_total, out_parts, ((0, 0, kept),))

        def write(at, value):
            gate_out[at, :] = value

        line.finish(write)


def turn(two_group, d_ups, gate_parts, block, mixed, ow, kept):
    length, width = two_group.shape
    units, chans = d_ups.shape[1], mixed.shape[1]
    rows, share = length // PLANE, width // LINE
    tile = lambda columns: pl.BlockSpec((rows, columns), lambda i: (i, 0))
    return pl.pallas_call(
        turn_body,
        grid=(PLANE,),
        in_specs=[
            tile(width), tile(units), ANYWHERE, ANYWHERE, ANYWHERE, ANYWHERE,
        ],
        out_specs=[
            once(gate_parts.shape), once((LINE, kept, share)), once((share, units)),
            once((length, chans)),
        ],
        out_shape=[
            jax.ShapeDtypeStruct(gate_parts.shape, jnp.bfloat16),
            jax.ShapeDtypeStruct((LINE, kept, share), jnp.bfloat16),
            jax.ShapeDtypeStruct((share, units), jnp.float32),
            jax.ShapeDtypeStruct((length, chans), jnp.float32),
        ],
        scratch_shapes=[
            *held(gate_parts, mixed, ow),
            pltpu.VMEM((PLANE, rows, width), jnp.bfloat16),
            pltpu.VMEM((width, units), jnp.float32),
            pltpu.VMEM((chans, width), jnp.float32),
            *LineReduce.buffers(share, units),
            *LineReduce.semaphores,
            *PlaneGather.semaphores,
        ],
        compiler_params=pltpu.CompilerParams(
            collective_id=5, has_side_effects=True, vmem_limit_bytes=61 * 2**20
        ),
        name="turn",
    )(two_group, d_ups, gate_parts, block, mixed, ow)


def pack_small(head_width, taps, vec, params, wr, we, small):
    columns = small.shape[1]
    step = 16
    last = (2 * head_width + 7) // 8 * 8

    def move(i, unused):
        at = pl.ds(pl.multiple_of(i * step, step), step)
        shape = (step, columns)
        row = lax.broadcasted_iota(jnp.int32, shape, 0) + i * step
        left = lax.broadcasted_iota(jnp.int32, shape, 1) < head_width
        rate, entry = wr[at, :], we[at, :]
        first = jnp.where(left, rate, pltpu.roll(entry, head_width, 1))
        second = jnp.where(left, pltpu.roll(rate, columns - head_width, 1), entry)
        small[at, :] = jnp.where(row < head_width, first, second).astype(jnp.bfloat16)
        return unused

    lax.fori_loop(0, last // step, move, 0)
    scaled = vec[0:4, :] * jnp.concatenate(
        [jnp.ones((3, columns), jnp.float32), params[4:5, :]], axis=0
    )
    tail = jnp.concatenate([taps[...], scaled], axis=0).astype(jnp.bfloat16)
    here = last // step * step
    rate, entry = wr[here : here + 8, :], we[here : here + 8, :]
    left = lax.broadcasted_iota(jnp.int32, (8, columns), 1) < head_width
    rest = jnp.where(left, pltpu.roll(rate, columns - head_width, 1), entry).astype(jnp.bfloat16)
    small[here : here + 16, :] = jnp.concatenate([rest, tail], axis=0)
    if small.shape[0] > here + 16:
        small[here + 16 :, :] = jnp.zeros_like(small[here + 16 :, :])


def split_gains(mix, ffn, out):
    share = out.shape[2] // 2
    low = lax.broadcasted_iota(jnp.int32, (1, 2 * share), 1) < share
    for r in range(LINE):
        lines = []
        for pair in range(PLANE // 2):
            at = (r * (PLANE // 2) + pair) * 2 * share
            one, two = mix[:, at : at + 2 * share], ffn[:, at : at + 2 * share]
            lines.append(jnp.where(low, one, pltpu.roll(two, share, 1)))
            lines.append(jnp.where(low, pltpu.roll(one, share, 1), two))
        out[r] = jnp.concatenate(lines, axis=0)


def backward_linked_body(
    head_width,
    d_mixed_ref, xy_hbm, taps_ref, vec_ref, wr_ref, we_ref, keep_ref,
    u_ref, u_prev_ref, by_ref, before_ref, states_ref, normed_ref, up_hbm, out_hbm,
    x_hbm, gain_ref, d_residual_hbm, ffn_gain_ref,
    xy_parts, up_out, out_out, in_grad, gains_out, small_out,
    xy_ref, up_parts, out_parts, brought, late,
    out_sum, taps_sum, vec_sum, wr_sum, we_sum, small, small_parts, d_xy, d_all, xy_total, eight, *rest,
):
    scratch, links = rest[:10], rest[10:]
    step = pl.program_id(0)
    block = PLANE - 1 - step
    line = LineReduce(up_hbm, up_parts, *links[:5])
    out_line = LineReduce(out_hbm, out_parts, *links[5:10])
    small_line = LineReduce(small_parts, small_parts, *links[10:15])
    plane = PlaneReduce(*links[15:])

    bring = Bring(
        (xy_hbm, up_hbm, out_hbm), (xy_ref, up_parts, out_parts), brought
    )
    d_residual_ref = xy_total.at[0 : x_hbm.shape[0]]
    bring_late = Bring((x_hbm, d_residual_hbm), (in_grad, d_residual_ref), late)

    @pl.when(step == 0)
    def _():
        bring.start()
        meet(True, "near")
        line.start()
        out_line.start()
        bring.wait(0, 1, 2)

    @pl.when((step > 2) & (step <= PLANE))
    def _():
        plane.relay(block + 3)

    @pl.when(step == 4)
    def _():
        line.forward()

    @pl.when(step < PLANE)
    def _():
        backward_step(
            step == 0, step == PLANE - 1, d_mixed_ref, taps_ref, vec_ref, wr_ref, we_ref,
            keep_ref, u_ref, u_prev_ref, by_ref, before_ref, states_ref, d_xy,
            taps_sum, vec_sum, wr_sum, we_sum, *scratch,
        )
        d_all[step] = d_xy[...]

        @pl.when(step > 0)
        def _():
            plane.pass_on(block + 1)

        plane.put(block, dot_plain(d_xy[...], xy_ref[...]).astype(jnp.bfloat16))

    @pl.when(step == PLANE)
    def _():
        pack_small(head_width, taps_sum, vec_sum, vec_ref, wr_sum, we_sum, small)
        share = small_parts.shape[1]
        for t in range(LINE):
            small_parts[t] = small[t * share : (t + 1) * share, :]
        small_line.start()
        xy_total[...] = contract_first(d_all[0], normed_ref[...])

    @pl.when(step == PLANE)
    def _():
        plane.pass_on(0)

    @pl.when(step > PLANE)
    def _():
        xy_total[...] += contract_first(d_all[step - PLANE], normed_ref[...])

    @pl.when(step == PLANE + 2)
    def _():
        plane.relay(1)

    @pl.when(step == PLANE + 4)
    def _():
        out_line.forward()

    @pl.when(step == PLANE + 5)
    def _():
        plane.relay(0)

    @pl.when(step == 2 * PLANE - 1)
    def _():
        small_line.forward()
        kept, chans = out_parts.shape[1], d_xy.shape[1] // 2
        to_turned_parts(xy_total, xy_parts, ((0, 0, kept), (chans, kept, kept)))
        bring_late.start()
        plane.arrive()
        bring_late.wait(0, 1)
        eight[...] = jnp.zeros_like(eight)

        def back(i, unused):
            at = pl.ds(pl.multiple_of(i * CHUNK, CHUNK), CHUNK)
            d_rows, d_gain = norm_back(
                in_grad[at, :].astype(jnp.float32), gain_ref[...], plane.total(at)
            )
            in_grad[at, :] = (xy_total[at, :] + d_rows).astype(jnp.bfloat16)
            eight[...] += sum_eight(d_gain)
            return unused

        lax.fori_loop(0, in_grad.shape[0] // CHUNK, back, 0)
        split_gains(jnp.sum(eight[...], axis=0, keepdims=True), ffn_gain_ref[...], gains_out)

        def write(at, value):
            up_out[at, :] = value

        def write_out(at, value):
            out_sum[at, :] = value

        def write_small(at, value):
            small_out[at, :] = value.astype(jnp.bfloat16)

        line.finish(write)
        out_line.finish(write_out)
        out_out[...] = out_sum[0 : out_out.shape[0], :]
        small_line.finish(write_small)
        plane.finish()


def backward_linked(
    d_mixed, xy, taps, vec, wr, we, keep, u, by, before, states, normed, up_parts, out_parts,
    layer_in, gain, d_residual, ffn_gain, head_width, used,
):
    length, width = normed.shape
    chans, units = d_mixed.shape[1], up_parts.shape[2]
    rows, share = length // PLANE, width // LINE
    kept = out_parts.shape[1]
    place = lambda i: PLANE - 1 - jnp.minimum(i, PLANE - 1)
    tile = lambda columns: pl.BlockSpec((rows, columns), lambda i: (place(i), 0))
    later = lambda columns: pl.BlockSpec(
        (rows, columns), lambda i: (PLANE - 1 - jnp.maximum(i - PLANE, 0), 0)
    )
    ahead = pl.BlockSpec((16, chans), lambda i: (jnp.maximum(place(i) * (rows // 16) - 1, 0), 0))
    small_share = -(-((2 * head_width + 7) // 8 * 8 + 8) // (LINE * 32)) * 32
    gain_terms = (LINE, PLANE, width // (LINE * PLANE) * 2)
    return pl.pallas_call(
        functools.partial(backward_linked_body, head_width),
        grid=(2 * PLANE,),
        in_specs=[
            tile(chans), ANYWHERE, once(taps.shape), once(vec.shape), once(wr.shape),
            once(we.shape), tile(keep.shape[1]), tile(chans), ahead, tile(chans), tile(chans),
            tile(chans), later(width), ANYWHERE, ANYWHERE,
            ANYWHERE, once(gain.shape), ANYWHERE, once(ffn_gain.shape),
        ],
        out_specs=[
            once((LINE, 2 * kept, share)), once((share, units)), once((used, share)),
            once((rows, width)), once(gain_terms), once((small_share, chans)),
        ],
        out_shape=[
            jax.ShapeDtypeStruct((LINE, 2 * kept, share), jnp.bfloat16),
            jax.ShapeDtypeStruct((share, units), jnp.float32),
            jax.ShapeDtypeStruct((used, share), jnp.float32),
            jax.ShapeDtypeStruct((rows, width), jnp.bfloat16),
            jax.ShapeDtypeStruct(gain_terms, jnp.float32),
            jax.ShapeDtypeStruct((small_share, chans), jnp.bfloat16),
        ],
        scratch_shapes=[
            *held(xy, up_parts, out_parts),
            pltpu.SemaphoreType.DMA((2,)),
            pltpu.VMEM((kept, share), jnp.float32),
            pltpu.VMEM(taps.shape, jnp.float32),
            pltpu.VMEM(vec.shape, jnp.float32),
            pltpu.VMEM(wr.shape, jnp.float32),
            pltpu.VMEM(we.shape, jnp.float32),
            pltpu.VMEM((LINE * small_share, chans), jnp.bfloat16),
            pltpu.VMEM((LINE, small_share, chans), jnp.bfloat16),
            pltpu.VMEM((rows, 2 * chans), jnp.bfloat16),
            pltpu.VMEM((PLANE, rows, 2 * chans), jnp.bfloat16),
            pltpu.VMEM((2 * chans, width), jnp.float32),
            pltpu.VMEM((8, width), jnp.float32),
            pltpu.VMEM((rows + 8, chans), jnp.float32),
            pltpu.VMEM((rows, chans), jnp.float32),
            pltpu.VMEM((rows, chans), jnp.bfloat16),
            pltpu.VMEM((rows, chans), jnp.float32),
            pltpu.VMEM((rows, chans), jnp.float32),
            pltpu.VMEM((rows + 8, chans), jnp.float32),
            pltpu.VMEM((rows, chans), jnp.bfloat16),
            pltpu.VMEM((rows, chans), jnp.bfloat16),
            pltpu.VMEM((8, chans), jnp.float32),
            pltpu.VMEM((64, chans), jnp.float32),
            *LineReduce.buffers(share, units),
            *LineReduce.semaphores,
            *LineReduce.buffers(kept, share),
            *LineReduce.semaphores,
            *LineReduce.buffers(small_share, chans),
            *LineReduce.semaphores,
            *PlaneReduce.buffers(rows, width),
            *PlaneReduce.semaphores,
        ],
        compiler_params=pltpu.CompilerParams(
            collective_id=6, has_side_effects=True, vmem_limit_bytes=61 * 2**20
        ),
        name="mixer_backward_linked",
    )(
        d_mixed, xy, taps, vec, wr, we, keep, u, u, by, before, states, normed,
        up_parts, out_parts, layer_in, gain, d_residual, ffn_gain,
    )


def close_body(
    hidden_ref, down_hbm, xy_hbm, residual_hbm, gains_ref, small,
    layer_out, x_out, y_out, gains_out, small_out,
    down_ref, xy_parts, residual_ref, brought, xy_sum,
    gathered, line_gains, both_gains, plane_gains,
    gain_sent, gain_arrived, wide_sent, wide_arrived, *links,
):
    r, h = lax.axis_index("row"), lax.axis_index("head")
    step = pl.program_id(0)
    xy_line = LineReduce(xy_hbm, xy_parts, *links[0:5])
    small_line = LineGather(small, lambda t: gathered.at[t], *links[5:8])
    plane = PlaneReduce(*links[8:])

    def to_row(t, owner):
        return send_to(
            gains_ref.at[t], line_gains.at[owner], gain_sent.at[t], gain_arrived.at[owner],
            "row", t,
        )

    def over_plane(place, owner):
        return send_to(
            both_gains, plane_gains.at[owner], wide_sent.at[place], wide_arrived.at[owner],
            "head", lax.rem(h + place, PLANE),
        )

    bring = Bring(
        (down_hbm, xy_hbm, residual_hbm), (down_ref, xy_parts, residual_ref), brought
    )

    @pl.when(step == 0)
    def _():
        bring.start()
        meet(True, "all")
        for place in range(1, LINE):
            to_row(lax.rem(r + place, LINE), r).start()
        small_line.start()
        xy_line.start()
        bring.wait(0, 1, 2)

    @pl.when(step > 0)
    def _():
        plane.pass_on(far_first(step - 1))

    @pl.when(step > 2)
    def _():
        plane.relay(far_first(step - 3))

    plane.put(far_first(step), contract_last(hidden_ref[...], down_ref[...]).astype(jnp.bfloat16))

    @pl.when(step == 2)
    def _():
        total = gains_ref[r]
        for place in range(1, LINE):
            t = lax.rem(r + place, LINE)
            to_row(t, t).wait_recv()
            total = total + line_gains[t]
        both_gains[...] = total
        for place in range(1, PLANE):
            over_plane(place, h).start()

    @pl.when(step == PLANE - 1)
    def _():
        small_line.forward()
        xy_line.forward()
        plane.relay(far_first(step - 2))
        plane.pass_on(far_first(step))
        plane.relay(far_first(step - 1))
        plane.relay(far_first(step))
        total = both_gains[...]
        for place in range(1, PLANE):
            owner = lax.rem(h + place, PLANE)
            over_plane(place, owner).wait_recv()
            total = total + plane_gains[owner]
        mine = lax.broadcasted_iota(jnp.int32, total.shape, 0) == h
        gains_out[...] = jnp.sum(jnp.where(mine, total, 0.0), axis=0, keepdims=True)
        plane.arrive()

        def make(i, unused):
            at = pl.ds(pl.multiple_of(i * CHUNK, CHUNK), CHUNK)
            layer_out[at, :] = (residual_ref[at, :] + plane.total(at)).astype(jnp.bfloat16)
            return unused

        lax.fori_loop(0, residual_ref.shape[0] // CHUNK, make, 0)
        def write(at, value):
            xy_sum[at, :] = value

        xy_line.finish(write)
        used, kept = x_out.shape[0], xy_sum.shape[0] // 2
        x_out[...] = xy_sum[0:used, :]
        y_out[...] = xy_sum[kept : kept + used, :]
        small_line.finish()
        small_out[...] = gathered[...].astype(jnp.float32)
        plane.finish()
        for place in range(1, LINE):
            to_row(lax.rem(r + place, LINE), r).wait_send()
        for place in range(1, PLANE):
            over_plane(place, h).wait_send()


def close_block(hidden, down, xy_parts, residual, gains, small, used):
    length, units = hidden.shape
    rows, width = residual.shape
    both, share = xy_parts.shape[1:]
    return pl.pallas_call(
        close_body,
        grid=(PLANE,),
        in_specs=[
            pl.BlockSpec((rows, units), lambda i: (far_first(i), 0)), ANYWHERE,
            ANYWHERE, ANYWHERE, once(gains.shape), once(small.shape),
        ],
        out_specs=[
            once((rows, width)), once((used, share)), once((used, share)), once((1, gains.shape[2])),
            once((LINE,) + small.shape),
        ],
        out_shape=[
            jax.ShapeDtypeStruct((rows, width), jnp.bfloat16),
            jax.ShapeDtypeStruct((used, share), jnp.float32),
            jax.ShapeDtypeStruct((used, share), jnp.float32),
            jax.ShapeDtypeStruct((1, gains.shape[2]), jnp.float32),
            jax.ShapeDtypeStruct((LINE,) + small.shape, jnp.float32),
        ],
        scratch_shapes=[
            *held(down, xy_parts, residual),
            pltpu.VMEM((both, share), jnp.float32),
            pltpu.VMEM((LINE,) + small.shape, jnp.bfloat16),
            pltpu.VMEM(gains.shape, jnp.float32),
            pltpu.VMEM(gains.shape[1:], jnp.float32),
            pltpu.VMEM((PLANE,) + gains.shape[1:], jnp.float32),
            pltpu.SemaphoreType.DMA((LINE,)),
            pltpu.SemaphoreType.DMA((LINE,)),
            pltpu.SemaphoreType.DMA((PLANE,)),
            pltpu.SemaphoreType.DMA((PLANE,)),
            *LineReduce.buffers(both, share), *LineReduce.semaphores,
            *LineGather.semaphores,
            *PlaneReduce.buffers(rows, width), *PlaneReduce.semaphores,
        ],
        compiler_params=pltpu.CompilerParams(
            collective_id=7, has_side_effects=True, vmem_limit_bytes=61 * 2**20
        ),
        name="close_block",
    )(hidden, down, xy_parts, residual, gains, small)


def mixer_params(
    conv_weight, conv_bias, rate_weight, rate_bias, entry_weight, entry_bias, decay_param, chans
):
    used = conv_bias.shape[0]
    spare = (0, chans - used)
    decay_wide = jnp.pad(decay_param, spare, constant_values=2.0)
    blank = jnp.zeros((chans,), jnp.float32)
    vec = jnp.stack(
        [
            jnp.pad(conv_bias, spare),
            jnp.pad(rate_bias, spare),
            jnp.pad(entry_bias, spare),
            -8.0 * jax.nn.softplus(-decay_wide),
            8.0 * jax.nn.sigmoid(-decay_wide),
            blank,
            blank,
            blank,
        ]
    )
    taps = jnp.pad(conv_weight, ((0, 0), spare))
    return taps, vec, block_diagonal(rate_weight, chans), block_diagonal(entry_weight, chans)


def shards(
    layer_in,
    cotangent,
    mix_gain,
    ffn_gain,
    x_weight,
    y_weight,
    out_weight,
    conv_weight,
    conv_bias,
    rate_weight,
    rate_bias,
    entry_weight,
    entry_bias,
    decay_param,
    gate_weight,
    up_weight,
    down_weight,
    resets,
):
    heads, head_width = rate_weight.shape[:2]
    used = conv_bias.shape[0]
    chans = -(-used // 128) * 128
    widen = lambda values: jnp.pad(values, ((0, 0), (0, chans - used)))
    mix_full = gather(mix_gain, ("row", "head"), 0)
    ffn_full = gather(ffn_gain, ("row", "head"), 0)
    xy_shard = jnp.concatenate([widen(x_weight), widen(y_weight)], axis=1)
    xy_rows = gather(xy_shard, "row", 0).T
    out_rows = gather(widen(out_weight), "row", 0).T
    gate_rows = gather(gate_weight, "row", 0)
    up_rows = gather(up_weight, "row", 0)
    down_rows = gather(down_weight, "row", 0)

    taps, vec, wr, we = mixer_params(
        conv_weight, conv_bias, rate_weight, rate_bias, entry_weight, entry_bias, decay_param, chans
    )
    keep = keep_columns(resets)

    inputs = layer_in.astype(jnp.float32)
    normed_f, norm_back_one = jax.vjp(norm_apply, inputs, mix_full.astype(jnp.float32))
    normed_group = gather(normed_f.astype(jnp.bfloat16), "head", 0)
    u, by, before, states, mixed, part = mixer_forward(
        normed_group, xy_rows, out_rows, taps, vec, wr, we, keep, ROWS
    )
    residual = inputs + scatter(part, "head", 0).astype(jnp.float32)
    normed_two_f, norm_back_two = jax.vjp(norm_apply, residual, ffn_full.astype(jnp.float32))
    cot_group = gather(cotangent, "head", 0)
    two_group = gather(normed_two_f.astype(jnp.bfloat16), "head", 0)
    gates = dot_plain(two_group, gate_rows)
    ups = dot_plain(two_group, up_rows)
    activated, slope = gelu_both(gates)
    hidden = (activated * ups).astype(jnp.bfloat16)
    ffn_part = contract_last(hidden, down_rows).astype(jnp.bfloat16)
    d_hidden = dot_plain(cot_group, down_rows)
    d_gates = (d_hidden * ups * slope).astype(jnp.bfloat16)
    d_ups = (d_hidden * activated).astype(jnp.bfloat16)
    d_two_part = (contract_last(d_gates, gate_rows) + contract_last(d_ups, up_rows)).astype(
        jnp.bfloat16
    )
    gate_grad = scatter(contract_first(two_group, d_gates).astype(jnp.bfloat16), "row", 0)
    up_grad = scatter(contract_first(two_group, d_ups).astype(jnp.bfloat16), "row", 0)
    down_grad = scatter(contract_first(cot_group, hidden).astype(jnp.bfloat16), "row", 0)
    layer_out = (residual + scatter(ffn_part, "head", 0).astype(jnp.float32)).astype(jnp.bfloat16)
    d_two = scatter(d_two_part, "head", 0).astype(jnp.float32)
    d_resid_norm, d_ffn_gain = norm_back_two(d_two)
    d_residual = cotangent.astype(jnp.float32) + d_resid_norm
    d_res_group = gather(d_residual.astype(jnp.bfloat16), "head", 0)
    d_xy, d_part, d_taps, d_vec, d_wr, d_we = mixer_backward(
        d_res_group, xy_rows, out_rows, taps, vec, wr, we, keep, u, by, before, states, ROWS
    )
    out_grad = scatter(contract_first(d_res_group, mixed).astype(jnp.bfloat16), "row", 0)
    xy_grad = scatter(contract_first(normed_group, d_xy).astype(jnp.bfloat16), "row", 0)
    d_normed = scatter(d_part, "head", 0).astype(jnp.float32)
    d_inputs, d_mix_gain = norm_back_one(d_normed)
    layer_in_grad = (d_inputs + d_residual).astype(jnp.bfloat16)

    small = [
        d_taps[:, :used],
        d_vec[0, :used],
        diagonal_blocks(d_wr, heads, head_width),
        d_vec[1, :used],
        diagonal_blocks(d_we, heads, head_width),
        d_vec[2, :used],
        d_vec[3, :used] * (8.0 * jax.nn.sigmoid(-decay_param)),
    ]
    small = [lax.psum(item.astype(jnp.bfloat16), "row").astype(jnp.float32) for item in small]
    mix_part = scatter(d_mix_gain, ("row", "head"), 0)
    ffn_part_grad = scatter(d_ffn_gain, ("row", "head"), 0)
    wide = lambda values: values[:, :used].astype(jnp.float32)
    return (
        layer_out,
        layer_in_grad,
        mix_part,
        ffn_part_grad,
        wide(xy_grad),
        wide(xy_grad[:, chans:]),
        wide(out_grad),
        *small,
        gate_grad.astype(jnp.float32),
        up_grad.astype(jnp.float32),
        down_grad.astype(jnp.float32),
    )

def shards_linked(
    layer_in,
    cotangent,
    mix_gain,
    ffn_gain,
    x_weight,
    y_weight,
    out_weight,
    conv_weight,
    conv_bias,
    rate_weight,
    rate_bias,
    entry_weight,
    entry_bias,
    decay_param,
    gate_weight,
    up_weight,
    down_weight,
    resets,
):
    heads, head_width = rate_weight.shape[:2]
    used = conv_bias.shape[0]
    kept = -(-used // 16) * 16
    flat = lambda values: values.reshape((-1, values.shape[-1]))
    line = lambda values: values.reshape(1, -1)
    normed_group, cot_half, xy_rows, out_rows, gains, taps, vec, wr, we, keep = open_block(
        layer_in,
        (line(mix_gain), line(ffn_gain)),
        cotangent,
        (x_weight.T, y_weight.T, out_weight.T),
        (
            conv_weight,
            line(conv_bias),
            line(rate_bias),
            line(entry_bias),
            line(decay_param),
            rate_weight,
            entry_weight,
            resets,
        ),
    )
    normed_group = flat(normed_group)
    u, by, before, states, mixed, residual, normed_two, gate_rows, up_half = forward_linked(
        normed_group, xy_rows, out_rows, taps, vec, wr, we, keep, layer_in, gains[1:2],
        gate_weight, up_weight,
    )
    gate_rows = flat(gate_rows)
    two_group, cot_group, up_rows, down_rows, gates, ups, hidden, down_parts = ffn_up(
        normed_two, gate_rows, cotangent, cot_half, up_half, up_weight, down_weight
    )
    two_group, cot_group, down_rows = map(flat, (two_group, cot_group, down_rows))
    d_ups, gate_parts, down_grad, d_residual, d_low, d_ffn_gain = ffn_back(
        cot_group, two_group, gates, ups, gate_rows, up_rows, down_rows, down_parts, residual,
        cotangent, gains[1:2],
    )
    up_parts, out_parts, gate_grad, d_mixed = turn(
        two_group, d_ups, gate_parts, d_low, mixed, out_rows, kept
    )
    xy_parts, up_grad, out_grad, layer_in_grad, gain_terms, small = backward_linked(
        d_mixed, xy_rows, taps, vec, wr, we, keep, u, by, before, states,
        normed_group, up_parts, out_parts, layer_in, gains[0:1], d_residual, d_ffn_gain,
        head_width, used,
    )
    layer_out, x_grad, y_grad, gain_grads, sums = close_block(
        hidden, down_rows, xy_parts, residual, gain_terms, small, used
    )
    sums = flat(sums)
    share = mix_gain.shape[0]
    ends = -(-used // 8) * 8
    gates_end = heads * head_width
    return (
        layer_out,
        layer_in_grad,
        gain_grads[0, :share],
        gain_grads[0, share:],
        x_grad.T,
        y_grad.T,
        out_grad.T,
        sums[ends : ends + 4, :used],
        sums[ends + 4, :used],
        sums[:gates_end, :head_width].reshape(heads, head_width, head_width),
        sums[ends + 5, :used],
        sums[:gates_end, head_width : 2 * head_width].reshape(heads, head_width, head_width),
        sums[ends + 6, :used],
        sums[ends + 7, :used],
        gate_grad,
        up_grad,
        down_grad,
    )


def solution(mesh):
    linked = mesh.shape["row"] == LINE and mesh.shape["head"] == PLANE
    return jax.shard_map(
        shards_linked if linked else shards,
        mesh=mesh,
        in_specs=(
            P(("row", "head"), None),
            P(("row", "head"), None),
            P(("row", "head")),
            P(("row", "head")),
            P("row", "head"),
            P("row", "head"),
            P("row", "head"),
            P(None, "head"),
            P("head"),
            P("head", None, None),
            P("head"),
            P("head", None, None),
            P("head"),
            P("head"),
            P("row", "head"),
            P("row", "head"),
            P("row", "head"),
            P("row", None),
        ),
        out_specs=(
            P(("row", "head"), None),
            P(("row", "head"), None),
            P(("row", "head")),
            P(("row", "head")),
            P("row", "head"),
            P("row", "head"),
            P("row", "head"),
            P(None, "head"),
            P("head"),
            P("head", None, None),
            P("head"),
            P("head", None, None),
            P("head"),
            P("head"),
            P("row", "head"),
            P("row", "head"),
            P("row", "head"),
        ),
        check_vma=False,
    )
```

```python
import functools

import jax
import jax.numpy as jnp
from jax import lax
from jax.experimental import pallas as pl
from jax.experimental.pallas import tpu as pltpu
from jax.sharding import PartitionSpec as P

EPSILON = 1e-06
ROWS = 256
GELU_A = 0.7978845608028654
GELU_B = 0.044715
CHUNK = 16
UNROLL = 4


def gelu_only(x):
    return 0.5 * x * (1.0 + jnp.tanh(GELU_A * (x + GELU_B * x * x * x)))


def gelu_both(x):
    square = x * x
    bent = jnp.tanh(GELU_A * x * (1.0 + GELU_B * square))
    half = 0.5 * (1.0 + bent)
    slope = half + 0.5 * x * (1.0 - bent * bent) * (GELU_A * (1.0 + 3.0 * GELU_B * square))
    return x * half, slope


def one_minus_exp(x, exp_x):
    return -jnp.tanh(0.5 * x) * (1.0 + exp_x)


def dot_plain(left, right):
    return jnp.dot(left, right, preferred_element_type=jnp.float32)


def contract_last(left, right):
    return lax.dot_general(
        left, right, (((1,), (1,)), ((), ())), preferred_element_type=jnp.float32
    )


def contract_first(left, right):
    return lax.dot_general(
        left, right, (((0,), (0,)), ((), ())), preferred_element_type=jnp.float32
    )


def sum_eight(value):
    total = value[0:8, :]
    for k in range(1, value.shape[0] // 8):
        total = total + value[8 * k : 8 * k + 8, :]
    return total


def conv_rows(window, keep, taps, shift):
    rows = window.shape[0] - 8
    total = taps[0:1] * window[8:] + shift
    for offset in range(1, 4):
        total = total + taps[offset : offset + 1] * (
            keep[:, offset : offset + 1] * window[8 - offset : 8 - offset + rows]
        )
    return total


def scan_down(decays, driven, carry):
    rows = decays.shape[0]
    place = lax.broadcasted_iota(jnp.int32, decays.shape, 0)
    step = 1
    while step < rows:
        inside = place >= step
        driven = jnp.where(inside, decays * pltpu.roll(driven, step, 0) + driven, driven)
        decays = jnp.where(inside, decays * pltpu.roll(decays, step, 0), decays)
        step *= 2
    return decays * carry + driven


def scan_up(decays, driven, carry):
    rows = decays.shape[0]
    place = lax.broadcasted_iota(jnp.int32, decays.shape, 0)
    step = 1
    while step < rows:
        inside = place < rows - step
        driven = jnp.where(inside, decays * pltpu.roll(driven, rows - step, 0) + driven, driven)
        decays = jnp.where(inside, decays * pltpu.roll(decays, rows - step, 0), decays)
        step *= 2
    return decays * carry + driven


def forward_step(
    normed_ref, xy_ref, taps_ref, vec_ref, wr_ref, we_ref, keep_ref,
    u_ref, by_ref, before_ref, states_ref, mixed_ref,
    window, conv, conv_low, rate, entry, carry,
):
    rows = normed_ref.shape[0]

    @pl.when(pl.program_id(0) == 0)
    def _():
        window[0:8, :] = jnp.zeros_like(window[0:8, :])
        carry[...] = jnp.zeros_like(carry)

    chans = u_ref.shape[1]
    branches = contract_last(normed_ref[...], xy_ref[...])
    branch_x = branches[:, :chans].astype(jnp.bfloat16)
    u_ref[...] = branch_x
    window[pl.ds(8, rows), :] = branch_x.astype(jnp.float32)
    by_ref[...] = branches[:, chans:]

    def conv_step(j, unused):
        at = pl.multiple_of(j * CHUNK, CHUNK)
        made = conv_rows(
            window[pl.ds(at, CHUNK + 8), :], keep_ref[pl.ds(at, CHUNK), :],
            taps_ref[...], vec_ref[0:1, :],
        )
        conv[pl.ds(at, CHUNK), :] = made
        conv_low[pl.ds(at, CHUNK), :] = made.astype(jnp.bfloat16)
        return unused

    lax.fori_loop(0, rows // CHUNK, conv_step, 0, unroll=UNROLL)
    window[0:8, :] = window[pl.ds(rows, 8), :]
    rate[...] = dot_plain(conv_low[...], wr_ref[...]) + vec_ref[1:2, :]
    entry[...] = dot_plain(conv_low[...], we_ref[...]) + vec_ref[2:3, :]

    def scan_step(j, before):
        at = pl.multiple_of(j * CHUNK, CHUNK)
        here = pl.ds(at, CHUNK)
        carried = keep_ref[here, 0:1]
        log_decay = jax.nn.sigmoid(rate[here, :]) * vec_ref[3:4, :]
        exp_decay = jnp.exp(log_decay)
        lost = one_minus_exp(2.0 * log_decay, exp_decay * exp_decay)
        drop = lost * lax.rsqrt(jnp.maximum(lost, 1e-30))
        scaling = (1.0 - carried) + carried * drop
        driven = scaling * jax.nn.sigmoid(entry[here, :]) * conv[here, :]
        states = scan_down(exp_decay * carried, driven, before)
        first = lax.broadcasted_iota(jnp.int32, states.shape, 0) == 0
        before_ref[here, :] = jnp.where(first, before, pltpu.roll(states, 1, 0))
        states_low = states.astype(jnp.bfloat16)
        states_ref[here, :] = states_low
        mixed_ref[here, :] = (
            states_low.astype(jnp.float32) * gelu_only(by_ref[here, :])
        ).astype(jnp.bfloat16)
        return states[CHUNK - 1 : CHUNK, :]

    carry[0:1, :] = lax.fori_loop(0, rows // CHUNK, scan_step, carry[0:1, :], unroll=UNROLL)


def forward_body(
    normed_ref, xy_ref, ow_ref, taps_ref, vec_ref, wr_ref, we_ref, keep_ref,
    u_ref, by_ref, before_ref, states_ref, mixed_ref, part_ref, *scratch,
):
    forward_step(
        normed_ref, xy_ref, taps_ref, vec_ref, wr_ref, we_ref, keep_ref,
        u_ref, by_ref, before_ref, states_ref, mixed_ref, *scratch,
    )
    part_ref[...] = dot_plain(mixed_ref[...], ow_ref[...]).astype(jnp.bfloat16)


def backward_step(
    first_step, last_step, d_mixed, taps_ref, vec_ref, wr_ref, we_ref, keep_ref,
    u_ref, u_prev_ref, by_ref, before_ref, states_ref,
    d_xy_ref, taps_out, vec_out, wr_out, we_out,
    window, conv, conv_low, rate, entry, d_conv, g_rate, g_entry, carry, sums,
):
    rows, chans = u_ref.shape

    @pl.when(first_step)
    def _():
        d_conv[pl.ds(rows, 8), :] = jnp.zeros_like(d_conv[pl.ds(rows, 8), :])
        carry[...] = jnp.zeros_like(carry)
        sums[...] = jnp.zeros_like(sums)
        wr_out[...] = jnp.zeros_like(wr_out)
        we_out[...] = jnp.zeros_like(we_out)

    @pl.when(jnp.logical_not(first_step))
    def _():
        d_conv[pl.ds(rows, 8), :] = d_conv[0:8, :]

    window[0:8, :] = u_prev_ref[8:16, :].astype(jnp.float32)
    window[pl.ds(8, rows), :] = u_ref[...].astype(jnp.float32)

    def conv_step(j, unused):
        at = pl.multiple_of(j * CHUNK, CHUNK)
        made = conv_rows(
            window[pl.ds(at, CHUNK + 8), :], keep_ref[pl.ds(at, CHUNK), :],
            taps_ref[...], vec_ref[0:1, :],
        )
        conv[pl.ds(at, CHUNK), :] = made
        conv_low[pl.ds(at, CHUNK), :] = made.astype(jnp.bfloat16)
        return unused

    lax.fori_loop(0, rows // CHUNK, conv_step, 0, unroll=UNROLL)
    rate[...] = dot_plain(conv_low[...], wr_ref[...]) + vec_ref[1:2, :]
    entry[...] = dot_plain(conv_low[...], we_ref[...]) + vec_ref[2:3, :]

    def fold(value):
        return sum_eight(value)

    def scan_step(j, after):
        at = pl.multiple_of(rows - CHUNK - j * CHUNK, CHUNK)
        here = pl.ds(at, CHUNK)
        carried = keep_ref[here, 0:1]
        rate_gate = jax.nn.sigmoid(rate[here, :])
        entry_gate = jax.nn.sigmoid(entry[here, :])
        log_decay = rate_gate * vec_ref[3:4, :]
        exp_decay = jnp.exp(log_decay)
        exp_twice = exp_decay * exp_decay
        lost = one_minus_exp(2.0 * log_decay, exp_twice)
        inverse = lax.rsqrt(jnp.maximum(lost, 1e-30))
        drop = lost * inverse
        scaling = (1.0 - carried) + carried * drop
        decays = exp_decay * carried
        gelu_y, slope_y = gelu_both(by_ref[here, :])
        through = d_mixed[here, :]
        d_states = (through * gelu_y).astype(jnp.bfloat16).astype(jnp.float32)
        d_xy_ref[here, chans:] = (
            through * states_ref[here, :].astype(jnp.float32) * slope_y
        ).astype(jnp.bfloat16)
        passed = scan_up(decays, decays * d_states, after)
        last = lax.broadcasted_iota(jnp.int32, passed.shape, 0) == CHUNK - 1
        adjoint = d_states + jnp.where(last, after, pltpu.roll(passed, CHUNK - 1, 0))
        convolved = conv[here, :]
        gated = adjoint * entry_gate
        g_log = adjoint * before_ref[here, :] * decays - gated * convolved * (
            carried * (exp_twice * inverse)
        )
        g_pre_rate = g_log * vec_ref[3:4, :] * (rate_gate * (1.0 - rate_gate))
        direct = gated * scaling
        g_pre_entry = direct * convolved * (1.0 - entry_gate)
        d_conv[here, :] = direct
        g_rate[here, :] = g_pre_rate.astype(jnp.bfloat16)
        g_entry[here, :] = g_pre_entry.astype(jnp.bfloat16)
        sums[8:16, :] += fold(g_pre_rate)
        sums[16:24, :] += fold(g_pre_entry)
        sums[24:32, :] += fold(g_log * rate_gate)
        return passed[0:1, :]

    carry[0:1, :] = lax.fori_loop(0, rows // CHUNK, scan_step, carry[0:1, :], unroll=UNROLL)
    wr_out[...] += contract_first(conv_low[...], g_rate[...])
    we_out[...] += contract_first(conv_low[...], g_entry[...])
    d_conv[0:rows, :] += contract_last(g_rate[...], wr_ref[...]) + contract_last(
        g_entry[...], we_ref[...]
    )

    def back_step(j, unused):
        at = pl.multiple_of(j * CHUNK, CHUNK)
        here = pl.ds(at, CHUNK)
        keep = keep_ref[here, :]
        ahead = d_conv[pl.ds(at, CHUNK + 8), :]
        behind = window[pl.ds(at, CHUNK + 8), :]
        now = ahead[0:CHUNK]
        total = taps_ref[0:1, :] * now
        sums[0:8, :] += fold(now)
        sums[32:40, :] += fold(now * behind[8:])
        for offset in range(1, 4):
            total = total + taps_ref[offset : offset + 1, :] * (
                keep[:, 3 + offset : 4 + offset] * ahead[offset : offset + CHUNK]
            )
            base = 32 + 8 * offset
            sums[base : base + 8, :] += fold(
                now * (keep[:, offset : offset + 1] * behind[8 - offset : 8 - offset + CHUNK])
            )
        d_xy_ref[here, :chans] = total.astype(jnp.bfloat16)
        return unused

    lax.fori_loop(0, rows // CHUNK, back_step, 0, unroll=UNROLL)

    @pl.when(last_step)
    def _():
        vec_out[...] = jnp.zeros_like(vec_out)
        for place in range(4):
            vec_out[place : place + 1, :] = jnp.sum(
                sums[8 * place : 8 * place + 8, :], axis=0, keepdims=True
            )
            taps_out[place : place + 1, :] = jnp.sum(
                sums[32 + 8 * place : 40 + 8 * place, :], axis=0, keepdims=True
            )


def backward_body(
    d_res_ref, xy_ref, ow_ref, taps_ref, vec_ref, wr_ref, we_ref, keep_ref,
    u_ref, u_prev_ref, by_ref, before_ref, states_ref,
    d_xy_ref, part_ref, taps_out, vec_out, wr_out, we_out, d_mixed, *scratch,
):
    step = pl.program_id(0)
    d_mixed[...] = contract_last(d_res_ref[...], ow_ref[...])
    backward_step(
        step == 0, step == pl.num_programs(0) - 1, d_mixed, taps_ref, vec_ref, wr_ref,
        we_ref, keep_ref, u_ref, u_prev_ref, by_ref, before_ref, states_ref, d_xy_ref,
        taps_out, vec_out, wr_out, we_out, *scratch,
    )
    part_ref[...] = dot_plain(d_xy_ref[...], xy_ref[...]).astype(jnp.bfloat16)


def whole(shape):
    return pl.BlockSpec(shape, lambda i: (0,) * len(shape))


def mixer_forward(normed, xy, ow, taps, vec, wr, we, keep, rows):
    length, width = normed.shape
    chans = ow.shape[0]
    tile = lambda columns: pl.BlockSpec((rows, columns), lambda i: (i, 0))
    return pl.pallas_call(
        forward_body,
        grid=(length // rows,),
        in_specs=[
            tile(width), whole(xy.shape), whole(ow.shape), whole(taps.shape),
            whole(vec.shape), whole(wr.shape), whole(we.shape), tile(keep.shape[1]),
        ],
        out_specs=[tile(chans)] * 5 + [tile(width)],
        out_shape=[
            jax.ShapeDtypeStruct((length, chans), jnp.bfloat16),
            jax.ShapeDtypeStruct((length, chans), jnp.float32),
            jax.ShapeDtypeStruct((length, chans), jnp.float32),
            jax.ShapeDtypeStruct((length, chans), jnp.bfloat16),
            jax.ShapeDtypeStruct((length, chans), jnp.bfloat16),
            jax.ShapeDtypeStruct((length, width), jnp.bfloat16),
        ],
        scratch_shapes=[
            pltpu.VMEM((rows + 8, chans), jnp.float32),
            pltpu.VMEM((rows, chans), jnp.float32),
            pltpu.VMEM((rows, chans), jnp.bfloat16),
            pltpu.VMEM((rows, chans), jnp.float32),
            pltpu.VMEM((rows, chans), jnp.float32),
            pltpu.VMEM((8, chans), jnp.float32),
        ],
        compiler_params=pltpu.CompilerParams(vmem_limit_bytes=48 * 2**20),
        cost_estimate=pl.CostEstimate(
            flops=6 * length * width * chans,
            bytes_accessed=4 * length * width + 30 * length * chans,
            transcendentals=6 * length * chans,
        ),
        name="mixer_forward",
    )(normed, xy, ow, taps, vec, wr, we, keep)


def mixer_backward(d_res, xy, ow, taps, vec, wr, we, keep, u, by, before, states, rows):
    length, width = d_res.shape
    chans = ow.shape[0]
    blocks = length // rows
    tile = lambda columns: pl.BlockSpec((rows, columns), lambda i: (blocks - 1 - i, 0))
    ahead = pl.BlockSpec(
        (16, chans), lambda i: (jnp.maximum((blocks - 1 - i) * (rows // 16) - 1, 0), 0)
    )
    return pl.pallas_call(
        backward_body,
        grid=(blocks,),
        in_specs=[
            tile(width), whole(xy.shape), whole(ow.shape), whole(taps.shape),
            whole(vec.shape), whole(wr.shape), whole(we.shape), tile(keep.shape[1]),
            tile(chans), ahead, tile(chans), tile(chans), tile(chans),
        ],
        out_specs=[
            tile(2 * chans), tile(width), whole(taps.shape), whole(vec.shape),
            whole(wr.shape), whole(we.shape),
        ],
        out_shape=[
            jax.ShapeDtypeStruct((length, 2 * chans), jnp.bfloat16),
            jax.ShapeDtypeStruct((length, width), jnp.bfloat16),
            jax.ShapeDtypeStruct(taps.shape, jnp.float32),
            jax.ShapeDtypeStruct(vec.shape, jnp.float32),
            jax.ShapeDtypeStruct(wr.shape, jnp.float32),
            jax.ShapeDtypeStruct(we.shape, jnp.float32),
        ],
        scratch_shapes=[
            pltpu.VMEM((rows, chans), jnp.float32),
            pltpu.VMEM((rows + 8, chans), jnp.float32),
            pltpu.VMEM((rows, chans), jnp.float32),
            pltpu.VMEM((rows, chans), jnp.bfloat16),
            pltpu.VMEM((rows, chans), jnp.float32),
            pltpu.VMEM((rows, chans), jnp.float32),
            pltpu.VMEM((rows + 8, chans), jnp.float32),
            pltpu.VMEM((rows, chans), jnp.bfloat16),
            pltpu.VMEM((rows, chans), jnp.bfloat16),
            pltpu.VMEM((8, chans), jnp.float32),
            pltpu.VMEM((64, chans), jnp.float32),
        ],
        compiler_params=pltpu.CompilerParams(vmem_limit_bytes=48 * 2**20),
        cost_estimate=pl.CostEstimate(
            flops=6 * length * width * chans,
            bytes_accessed=4 * length * width + 30 * length * chans,
            transcendentals=6 * length * chans,
        ),
        name="mixer_backward",
    )(d_res, xy, ow, taps, vec, wr, we, keep, u, u, by, before, states)


def keep_columns(resets):
    length = resets.shape[1]
    position = lax.broadcasted_iota(jnp.int32, resets.shape, 1)
    starts = jnp.maximum(resets, (position == 0).astype(jnp.int32)).astype(jnp.float32)
    carried = (1.0 - starts).reshape(-1)
    seqs = resets.shape[0]

    def back(values, by):
        values = values.reshape(seqs, length)
        return jnp.pad(values, ((0, 0), (by, 0)))[:, :length].reshape(-1)

    def ahead(values, by):
        values = values.reshape(seqs, length)
        return jnp.pad(values, ((0, 0), (0, by)))[:, by:].reshape(-1)

    one = carried
    two = one * back(carried, 1)
    three = two * back(carried, 2)
    return jnp.stack(
        [carried, one, two, three, ahead(one, 1), ahead(two, 2), ahead(three, 3), carried], axis=1
    )


def block_diagonal(blocks, chans):
    heads, width, unused = blocks.shape
    rows = [
        jnp.pad(blocks[h], ((0, 0), (h * width, chans - (h + 1) * width))) for h in range(heads)
    ]
    full = jnp.concatenate(rows, axis=0)
    return jnp.pad(full, ((0, chans - heads * width), (0, 0)))


def diagonal_blocks(full, heads, width):
    return jnp.stack(
        [full[h * width : (h + 1) * width, h * width : (h + 1) * width] for h in range(heads)]
    )


MESH = pl.DeviceIdType.MESH
ANYWHERE = pl.BlockSpec(memory_space=pl.ANY)
IN_VMEM = pl.BlockSpec(memory_space=pltpu.VMEM)
LINE = 4
PLANE = 8
PIECES = 4


def send_to(src, dst, sent, arrived, axis, target):
    return pltpu.make_async_remote_copy(
        src_ref=src,
        dst_ref=dst,
        send_sem=sent,
        recv_sem=arrived,
        device_id={axis: target},
        device_id_type=MESH,
    )


def sibling_of(h):
    return h + 1 - 2 * lax.rem(h, 2)


def across_of(h):
    return h + 2 - 4 * lax.rem(lax.div(h, 2), 2)


def along_of(h):
    return lax.rem(h + 4, PLANE)


def meet(row_line, plane):
    r, h = lax.axis_index("row"), lax.axis_index("head")
    barrier = pltpu.get_barrier_semaphore()
    count = 0
    if row_line:
        for step in range(1, LINE):
            pl.semaphore_signal(
                barrier, inc=1, device_id={"row": lax.rem(r + step, LINE)}, device_id_type=MESH
            )
        count += LINE - 1
    if plane == "all":
        for step in range(1, PLANE):
            pl.semaphore_signal(
                barrier, inc=1, device_id={"head": lax.rem(h + step, PLANE)}, device_id_type=MESH
            )
        count += PLANE - 1
    if plane == "near":
        for target in (sibling_of(h), across_of(h), along_of(h)):
            pl.semaphore_signal(barrier, inc=1, device_id={"head": target}, device_id_type=MESH)
        count += 3
    pl.semaphore_wait(barrier, count)


class Bring:
    def __init__(self, sources, places, semaphores):
        self.copies = [
            pltpu.make_async_copy(src, dst, semaphores.at[k])
            for k, (src, dst) in enumerate(zip(sources, places))
        ]

    def start(self):
        for copy in self.copies:
            copy.start()

    def wait(self, *which):
        for k in which:
            self.copies[k].wait()


def held(*arrays):
    return [pltpu.VMEM(item.shape, item.dtype) for item in arrays] + [
        pltpu.SemaphoreType.DMA((len(arrays),))
    ]


class LineGather:
    semaphores = (
        pltpu.SemaphoreType.DMA((LINE,)),
        pltpu.SemaphoreType.DMA((LINE,)),
        pltpu.SemaphoreType.DMA((2,)),
    )

    def __init__(self, source, slot, sent, arrived, other):
        self.r = lax.axis_index("row")
        self.source, self.slot = source, slot
        self.sent, self.arrived, self.other = sent, arrived, other

    def own(self, t):
        return send_to(
            self.source, self.slot(self.r), self.sent.at[t], self.arrived.at[self.r], "row", t
        )

    def handed(self, origin, target):
        return send_to(
            self.slot(origin), self.slot(origin), self.other.at[0], self.arrived.at[origin],
            "row", target,
        )

    def local(self):
        return pltpu.make_async_copy(self.source, self.slot(self.r), self.other.at[1])

    def start(self):
        for gap in (2, -2, 1, -1):
            t = self.r + gap

            @pl.when((t >= 0) & (t < LINE))
            def _(t=t):
                self.own(t).start()

        self.local().start()

    def forward(self):
        for me, origin, target in ((2, 0, 3), (1, 3, 0)):

            @pl.when(self.r == me)
            def _(origin=origin, target=target):
                copy = self.handed(origin, target)
                copy.wait_recv()
                copy.start()

    def finish(self):
        r = self.r
        for t in range(LINE):
            known = (r == t) | ((r == 2) & (t == 0)) | ((r == 1) & (t == 3))
            near = (r != t) & (r - t < 3) & (t - r < 3)

            @pl.when(jnp.logical_not(known))
            def _(t=t):
                self.handed(t, t).wait_recv()

            @pl.when(near)
            def _(t=t):
                self.own(t).wait_send()

        for me, origin, target in ((2, 0, 3), (1, 3, 0)):

            @pl.when(r == me)
            def _(origin=origin, target=target):
                self.handed(origin, target).wait_send()

        self.local().wait()


class LineReduce:
    semaphores = (
        pltpu.SemaphoreType.DMA((LINE,)),
        pltpu.SemaphoreType.DMA((LINE,)),
        pltpu.SemaphoreType.DMA((2,)),
    )

    @staticmethod
    def buffers(rows, width):
        return [
            pltpu.VMEM((LINE, rows, width), jnp.bfloat16),
            pltpu.VMEM((rows, width), jnp.bfloat16),
        ]

    def __init__(self, source, parts, landed, passed, sent, arrived, other):
        self.r = lax.axis_index("row")
        self.source, self.parts, self.landed, self.passed = source, parts, landed, passed
        self.sent, self.arrived, self.other = sent, arrived, other

    def to_pass(self, me, origin, via):
        return send_to(
            self.source.at[origin], self.passed, self.sent.at[origin], self.other.at[0], "row", via
        )

    def direct(self, t):
        return send_to(
            self.source.at[t], self.landed.at[self.r], self.sent.at[t], self.arrived.at[self.r],
            "row", t,
        )

    def added(self, t):
        return send_to(
            self.passed, self.landed.at[self.r], self.sent.at[t], self.arrived.at[self.r], "row", t
        )

    def plain(self, t):
        r = self.r
        ends = ((r == 0) & (t == 3)) | ((r == 3) & (t == 0))
        added = ((r == 1) & (t == 3)) | ((r == 2) & (t == 0))
        return jnp.logical_not(ends | added | (r == t))

    def start(self):
        for me, end, via in ((0, 3, 1), (3, 0, 2)):

            @pl.when(self.r == me)
            def _(me=me, end=end, via=via):
                self.to_pass(me, end, via).start()

        for t in range(LINE):

            @pl.when(self.plain(t))
            def _(t=t):
                self.direct(t).start()

    def forward(self):
        for me, end in ((1, 3), (2, 0)):

            @pl.when(self.r == me)
            def _(me=me, end=end):
                self.to_pass(me, end, end).wait_recv()
                rows = self.passed.shape[0]
                step = 32

                def add(i, unused):
                    at = pl.ds(pl.multiple_of(i * step, step), step)
                    self.passed[at, :] = (
                        self.parts[end, at, :].astype(jnp.float32)
                        + self.passed[at, :].astype(jnp.float32)
                    ).astype(jnp.bfloat16)
                    return unused

                lax.fori_loop(0, rows // step, add, 0)
                self.added(end).start()

    def finish(self, write):
        r = self.r
        for t in range(LINE):

            @pl.when(jnp.logical_not(unsent_to(r, t)))
            def _(t=t):
                send_to(
                    self.source.at[t], self.landed.at[t], self.sent.at[t], self.arrived.at[t],
                    "row", t,
                ).wait_recv()

        def total_of(sources):
            step = 32

            def add(i, unused):
                at = pl.ds(pl.multiple_of(i * step, step), step)
                total = self.parts[r, at, :].astype(jnp.float32)
                for t in sources:
                    total = total + self.landed[t, at, :].astype(jnp.float32)
                write(at, total)
                return unused

            lax.fori_loop(0, self.passed.shape[0] // step, add, 0)

        at_end = (r == 0) | (r == 3)

        @pl.when(at_end)
        def _():
            total_of((1, 2))

        @pl.when(jnp.logical_not(at_end))
        def _():
            total_of((0, 3, 3 - r))

        for me, end, via in ((0, 3, 1), (3, 0, 2)):

            @pl.when(r == me)
            def _(me=me, end=end, via=via):
                self.to_pass(me, end, via).wait_send()

        for t in range(LINE):

            @pl.when(jnp.logical_not(unsent_to(r, t)))
            def _(t=t):
                self.direct(t).wait_send()


def unsent_to(r, t):
    return ((r == 0) & (t == 3)) | ((r == 3) & (t == 0)) | (r == t)


class PlaneGather:
    semaphores = (
        pltpu.SemaphoreType.DMA((PIECES, 7)),
        pltpu.SemaphoreType.DMA((PIECES, 7)),
        pltpu.SemaphoreType.DMA((PIECES,)),
    )
    first = tuple(range(PIECES // 2))
    second = tuple(range(PIECES // 2, PIECES))

    def __init__(self, block, full, sent, arrived, other, source=None, target=None):
        h = lax.axis_index("head")
        self.source, self.target = source, target
        self.h, self.side, self.x, self.y = h, sibling_of(h), across_of(h), along_of(h)
        self.far = across_of(self.y)
        self.block, self.full = block, full
        self.sent, self.arrived, self.other = sent, arrived, other
        self.rows = block.shape[0] // PIECES

    def piece(self, owner, c):
        rows = pl.ds(c * self.rows, self.rows)
        if self.target is None:
            return self.full.at[owner, rows]
        return self.full.at[owner, rows, self.target]

    def mine(self, c):
        rows = pl.ds(c * self.rows, self.rows)
        return self.block.at[rows] if self.source is None else self.block.at[rows, self.source]

    def own(self, c, lane, target):
        return send_to(
            self.mine(c), self.piece(self.h, c),
            self.sent.at[c, lane], self.arrived.at[c, lane], "head", target,
        )

    def hand(self, owner, c, lane, target):
        return send_to(
            self.piece(owner, c), self.piece(owner, c), self.sent.at[c, lane],
            self.arrived.at[c, lane], "head", target,
        )

    def local(self, c):
        return pltpu.make_async_copy(self.mine(c), self.piece(self.h, c), self.other.at[c])

    def start(self):
        for a, b in zip(self.first, self.second):
            self.own(a, 1, self.x).start()
            self.own(b, 2, self.y).start()
        for a, b in zip(self.first, self.second):
            self.own(b, 1, self.x).start()
            self.own(a, 2, self.y).start()
        for c in range(PIECES):
            self.own(c, 0, self.side).start()
            self.local(c).start()

    def relay(self, place):
        a, b = self.first[place], self.second[place]
        self.hand(self.x, a, 1, self.x).wait_recv()
        self.hand(self.x, a, 3, self.y).start()
        self.hand(self.x, a, 4, self.side).start()
        self.hand(self.y, b, 2, self.y).wait_recv()
        self.hand(self.y, b, 3, self.x).start()
        self.hand(self.y, b, 5, self.side).start()

    def rest(self):
        for a, b in zip(self.first, self.second):
            self.hand(self.x, b, 1, self.x).wait_recv()
            self.hand(self.x, b, 4, self.side).start()
            self.hand(self.y, a, 2, self.y).wait_recv()
            self.hand(self.y, a, 5, self.side).start()

    def beside(self):
        for c in range(PIECES):
            self.hand(self.side, c, 0, self.side).wait_recv()

    def far_side(self):
        for pair in zip(self.first, self.second):
            for c in pair:
                self.hand(self.far, c, 3, self.side).wait_recv()
                self.hand(self.far, c, 6, self.side).start()

    def end(self, beside=True):
        side = self.side
        if beside:
            self.beside()
        for c in range(PIECES):
            for owner, lane in (
                (across_of(side), 4), (along_of(side), 5), (across_of(along_of(side)), 6)
            ):
                self.hand(owner, c, lane, side).wait_recv()
        for c in range(PIECES):
            for lane in range(7):
                self.own(c, lane, side).wait_send()
            self.local(c).wait()


class PlaneReduce:
    semaphores = (
        pltpu.SemaphoreType.DMA((4,)),
        pltpu.SemaphoreType.DMA((4,)),
        pltpu.SemaphoreType.DMA((4, 2)),
        pltpu.SemaphoreType.DMA((2, 2)),
        pltpu.SemaphoreType.DMA((2,)),
    )

    @staticmethod
    def buffers(rows, width):
        return [
            pltpu.VMEM((4, rows, width), jnp.bfloat16),
            pltpu.VMEM((4, rows, width), jnp.bfloat16),
            pltpu.VMEM((4, rows, width), jnp.bfloat16),
            pltpu.VMEM((2, rows // 2, width), jnp.bfloat16),
            pltpu.VMEM((2, rows, width), jnp.bfloat16),
        ]

    def __init__(
        self, staged, beside, mine, relayed, landed,
        side_sent, side_arrived, sent, arrived, relay_arrived,
    ):
        h = lax.axis_index("head")
        self.h, self.core, self.chip = h, lax.rem(h, 2), lax.div(h, 2)
        self.staged, self.beside, self.mine = staged, beside, mine
        self.relayed, self.landed = relayed, landed
        self.side_sent, self.side_arrived = side_sent, side_arrived
        self.sent, self.arrived, self.relay_arrived = sent, arrived, relay_arrived
        self.half = mine.shape[1] // 2

    def aside(self, chip):
        return send_to(
            self.staged.at[chip], self.beside.at[chip], self.side_sent.at[chip],
            self.side_arrived.at[chip], "head", sibling_of(self.h),
        )

    def relation(self, chip):
        flip_x = lax.rem(chip + self.chip, 2)
        flip_y = lax.rem(lax.div(chip, 2) + lax.div(self.chip, 2), 2)
        return flip_x + 2 * flip_y

    def part(self, half):
        return pl.ds(half * self.half, self.half)

    def home(self, chip, way, half):
        return send_to(
            self.mine.at[chip, self.part(half)], self.landed.at[way, self.part(half)],
            self.sent.at[chip, half], self.arrived.at[way, half], "head",
            (across_of, along_of)[way](self.h),
        )

    def opposite(self, chip, half):
        return send_to(
            self.mine.at[chip, self.part(half)], self.relayed.at[half], self.sent.at[chip, half],
            self.relay_arrived.at[half], "head", (along_of, across_of)[half](self.h),
        )

    def put(self, block, value):
        chip, core = lax.div(block, 2), lax.rem(block, 2)

        @pl.when(core == self.core)
        def _():
            self.mine[chip] = value

        @pl.when(core != self.core)
        def _():
            self.staged[chip] = value
            self.aside(chip).start()

    def pass_on(self, block):
        chip, core = lax.div(block, 2), lax.rem(block, 2)

        @pl.when(core == self.core)
        def _():
            self.aside(chip).wait_recv()
            step = 32

            def add(i, unused):
                at = pl.ds(pl.multiple_of(i * step, step), step)
                self.mine[chip, at, :] = (
                    self.mine[chip, at, :].astype(jnp.float32)
                    + self.beside[chip, at, :].astype(jnp.float32)
                ).astype(jnp.bfloat16)
                return unused

            lax.fori_loop(0, 2 * self.half // step, add, 0)
            relation = self.relation(chip)

            @pl.when(relation == 1)
            def _():
                self.home(chip, 0, 1).start()

            @pl.when(relation == 2)
            def _():
                self.home(chip, 1, 0).start()

            @pl.when(relation == 3)
            def _():
                self.opposite(chip, 0).start()
                self.opposite(chip, 1).start()

    def relay(self, block):
        chip, core = lax.div(block, 2), lax.rem(block, 2)
        for way in (0, 1):

            @pl.when((core == self.core) & (self.relation(chip) == way + 1))
            def _(way=way):
                self.opposite(chip, way).wait_recv()
                step = 32

                def add(i, unused):
                    at = pl.ds(pl.multiple_of(i * step, step), step)
                    here = pl.ds(pl.multiple_of(way * self.half + i * step, step), step)
                    self.mine[chip, here, :] = (
                        self.mine[chip, here, :].astype(jnp.float32)
                        + self.relayed[way, at, :].astype(jnp.float32)
                    ).astype(jnp.bfloat16)
                    return unused

                lax.fori_loop(0, self.half // step, add, 0)
                self.home(chip, way, way).start()

    def arrive(self):
        for way in (0, 1):
            for half in (0, 1):
                self.home(self.chip, way, half).wait_recv()

    def total(self, at):
        value = self.mine[self.chip, at, :].astype(jnp.float32)
        return (
            value
            + self.landed[0, at, :].astype(jnp.float32)
            + self.landed[1, at, :].astype(jnp.float32)
        )

    def finish(self):
        for chip in range(4):
            self.aside(chip).wait_send()

            @pl.when(chip != self.chip)
            def _(chip=chip):
                self.home(chip, 0, 0).wait_send()
                self.home(chip, 0, 1).wait_send()


def norm_apply(rows, gain):
    return rows * lax.rsqrt(jnp.mean(rows * rows, axis=-1, keepdims=True) + EPSILON) * gain


def gather(values, axis_name, axis):
    return lax.all_gather(values, axis_name, axis=axis, tiled=True)


def scatter(values, axis_name, axis):
    return lax.psum_scatter(values, axis_name, scatter_dimension=axis, tiled=True)

def once(shape):
    return pl.BlockSpec(
        shape, lambda i: (0,) * len(shape), pipeline_mode=pl.Buffered(buffer_count=1)
    )


def norm_rows(rows, gain):
    return rows * lax.rsqrt(jnp.mean(rows * rows, axis=-1, keepdims=True) + EPSILON) * gain


def lay_out_params(
    taps_ref, rows_ref, gates_ref, resets_ref,
    taps_out, vec_out, wr_out, we_out, keep_out, square, moved,
):
    used, width = rows_ref.shape[1], gates_ref.shape[2]
    columns = vec_out.shape[1]
    taps_out[...] = jnp.zeros_like(taps_out)
    taps_out[:, 0:used] = taps_ref[...]
    vec_out[...] = jnp.zeros_like(vec_out)
    vec_out[3:4, :] = jnp.full((1, columns), 2.0, jnp.float32)
    vec_out[0:4, 0:used] = rows_ref[...]
    decay = vec_out[3:4, :]
    vec_out[3:4, :] = -8.0 * jnp.log1p(jnp.exp(-decay))
    vec_out[4:5, :] = 8.0 * jax.nn.sigmoid(-decay)
    for k, out in enumerate((wr_out, we_out)):
        square[...] = jnp.zeros_like(square)
        square[0:width, 0:width] = gates_ref[k, 1].astype(jnp.float32)
        moved[...] = pltpu.roll(pltpu.roll(square[...], width, 0), width, 1)
        square[...] = jnp.zeros_like(square)
        square[0:width, 0:width] = gates_ref[k, 0].astype(jnp.float32)
        out[...] = (square[...] + moved[...]).astype(jnp.bfloat16)
    resets = resets_ref[...]
    first = lax.broadcasted_iota(jnp.int32, resets.shape, 1) == 0
    one = jnp.where(first | (resets > 0), 0.0, 1.0)
    length = resets.shape[1]
    two = one * pltpu.roll(one, 1, 1)
    three = two * pltpu.roll(one, 2, 1)
    ahead = [pltpu.roll(item, length - k, 1) for k, item in ((1, one), (2, two), (3, three))]
    rows = jnp.concatenate(
        [one, one, two, three, *ahead, one, jnp.zeros((120, length), jnp.float32)], axis=0
    )
    for k in range(length // 128):
        turned = rows[:, k * 128 : (k + 1) * 128].T
        keep_out[k * 128 : (k + 1) * 128, :] = turned[:, 0:8]


def open_body(
    x_ref, mix_ref, ffn_ref, cot, xt_ref, yt_ref, ot_ref,
    taps_ref, rows_ref, gates_ref, resets_ref,
    full, cot_out, xy_full, out_full, gains_ref, taps_out, vec_out, wr_out, we_out, keep_out,
    shards, blank, square, moved,
    normed, column, spread, gain_sent, gain_arrived, wide_sent, wide_arrived, wiped, *semaphores,
):
    r, h = lax.axis_index("row"), lax.axis_index("head")
    held_rows, share = shards.shape[1:]
    used, chans = xt_ref.shape[0], out_full.shape[0]

    def slot(full, first):
        def at(origin):
            lanes = pl.ds(pl.multiple_of(origin * share, share), share)
            return full.at[pl.ds(first, held_rows), lanes]

        return at

    lines = [
        LineGather(shards.at[k], slot(dst, first), *semaphores[3 * k : 3 * k + 3])
        for k, (dst, first) in enumerate(((xy_full, 0), (xy_full, chans), (out_full, 0)))
    ]
    wipes = [
        pltpu.make_async_copy(
            blank, dst.at[pl.ds(first + held_rows, chans - held_rows)], wiped.at[k]
        )
        for k, (dst, first) in enumerate(((xy_full, 0), (xy_full, chans), (out_full, 0)))
    ]
    plane = PlaneGather(normed, full, *semaphores[9:12])
    cot_plane = PlaneGather(
        cot, cot_out, *semaphores[12:15], source=pl.ds(0, cot_out.shape[2])
    )
    for k, source in enumerate((xt_ref, yt_ref, ot_ref)):
        shards[k, held_rows - 16 :, :] = jnp.zeros((16, share), jnp.bfloat16)
        shards[k, 0:used, :] = source[...]
    gain_share = mix_ref.shape[1]
    low = lax.broadcasted_iota(jnp.int32, (8, 2 * gain_share), 1) < gain_share
    column[r] = jnp.zeros_like(column[r])
    column[r, 0:1, 0:gain_share] = mix_ref[...].astype(jnp.float32)
    column[r, 1:2, 0:gain_share] = ffn_ref[...].astype(jnp.float32)
    rows = column[r]
    column[r] = jnp.where(low, rows, pltpu.roll(pltpu.roll(rows, gain_share, 1), 7, 0))
    meet(True, "all")

    def up_line(t):
        return send_to(
            column.at[r], column.at[r], gain_sent.at[t], gain_arrived.at[r], "row", t
        )

    def from_line(t):
        return send_to(
            column.at[t], column.at[t], gain_sent.at[t], gain_arrived.at[t], "row", t
        )

    def over_plane(step, owner):
        return send_to(
            column, spread.at[owner], wide_sent.at[step], wide_arrived.at[owner], "head",
            lax.rem(h + step, PLANE),
        )

    for step in range(1, LINE):
        up_line(lax.rem(r + step, LINE)).start()
    for line in lines:
        line.start()
    blank[...] = jnp.zeros_like(blank)
    for wipe in wipes:
        wipe.start()
    for step in range(1, LINE):
        from_line(lax.rem(r + step, LINE)).wait_recv()
    for step in range(1, PLANE):
        over_plane(step, h).start()
    cot_plane.start()
    spread[h] = column[...]
    for step in range(1, PLANE):
        over_plane(step, lax.rem(h + step, PLANE)).wait_recv()

    low = lax.broadcasted_iota(jnp.int32, (1, 2 * gain_share), 1) < gain_share
    for line_place in range(LINE):
        for pair in range(PLANE // 2):
            even = spread[2 * pair, line_place][0:1, :]
            odd = spread[2 * pair + 1, line_place][0:1, :]
            at = (line_place * (PLANE // 2) + pair) * 2 * gain_share
            end = at + 2 * gain_share
            gains_ref[0:1, at:end] = jnp.where(low, even, pltpu.roll(odd, gain_share, 1))
            gains_ref[1:2, at:end] = jnp.where(low, pltpu.roll(even, gain_share, 1), odd)

    def make(i, unused):
        at = pl.ds(pl.multiple_of(i * CHUNK, CHUNK), CHUNK)
        normed[at, :] = norm_rows(x_ref[at, :].astype(jnp.float32), gains_ref[0:1, :]).astype(
            jnp.bfloat16
        )
        return unused

    lax.fori_loop(0, x_ref.shape[0] // CHUNK, make, 0)
    plane.start()
    lay_out_params(
        taps_ref, rows_ref, gates_ref, resets_ref,
        taps_out, vec_out, wr_out, we_out, keep_out, square, moved,
    )
    cot_plane.relay(0)
    cot_plane.relay(1)
    lines[0].forward()
    cot_plane.rest()
    plane.relay(0)
    plane.relay(1)
    lines[1].forward()
    cot_plane.far_side()
    cot_plane.end()
    plane.rest()
    plane.far_side()
    plane.end()
    lines[2].forward()
    for line in lines:
        line.finish()
    for wipe in wipes:
        wipe.wait()
    for step in range(1, LINE):
        up_line(lax.rem(r + step, LINE)).wait_send()
    for step in range(1, PLANE):
        over_plane(step, h).wait_send()


def open_block(layer_in, gains, cot, weights, params):
    rows, width = layer_in.shape
    used, share = weights[0].shape
    chans, held_rows = -(-used // 128) * 128, -(-used // 16) * 16
    length = params[-1].shape[1]
    tile = (8, 2 * gains[0].shape[1])
    return pl.pallas_call(
        open_body,
        in_specs=[IN_VMEM, IN_VMEM, IN_VMEM, ANYWHERE] + [IN_VMEM] * 7,
        out_specs=[ANYWHERE] * 4 + [IN_VMEM] * 6,
        out_shape=[
            jax.ShapeDtypeStruct((PLANE, rows, width), jnp.bfloat16),
            jax.ShapeDtypeStruct((PLANE, rows, width // 2), jnp.bfloat16),
            jax.ShapeDtypeStruct((2 * chans, width), jnp.bfloat16),
            jax.ShapeDtypeStruct((chans, width), jnp.bfloat16),
            jax.ShapeDtypeStruct((2, width), jnp.float32),
            jax.ShapeDtypeStruct((4, chans), jnp.float32),
            jax.ShapeDtypeStruct((8, chans), jnp.float32),
            jax.ShapeDtypeStruct((chans, chans), jnp.bfloat16),
            jax.ShapeDtypeStruct((chans, chans), jnp.bfloat16),
            jax.ShapeDtypeStruct((length, 8), jnp.float32),
        ],
        scratch_shapes=[
            pltpu.VMEM((3, held_rows, share), jnp.bfloat16),
            pltpu.VMEM((chans - held_rows, width), jnp.bfloat16),
            pltpu.VMEM((chans, chans), jnp.float32),
            pltpu.VMEM((chans, chans), jnp.float32),
            pltpu.VMEM((rows, width), jnp.bfloat16),
            pltpu.VMEM((LINE,) + tile, jnp.float32),
            pltpu.VMEM((PLANE, LINE) + tile, jnp.float32),
            pltpu.SemaphoreType.DMA((LINE,)),
            pltpu.SemaphoreType.DMA((LINE,)),
            pltpu.SemaphoreType.DMA((PLANE,)),
            pltpu.SemaphoreType.DMA((PLANE,)),
            pltpu.SemaphoreType.DMA((3,)),
            *(LineGather.semaphores * 3),
            *(PlaneGather.semaphores * 2),
        ],
        compiler_params=pltpu.CompilerParams(
            collective_id=0, has_side_effects=True, vmem_limit_bytes=61 * 2**20
        ),
        name="open_block",
    )(layer_in, *gains, cot, *weights, *params)


def forward_linked_body(
    normed_ref, xy_hbm, ow_hbm, taps_ref, vec_ref, wr_ref, we_ref, keep_ref,
    x_hbm, gain_ref, gate_shard, up_shard,
    u_ref, by_ref, before_ref, states_ref, mixed_ref, residual_ref, two_ref, gate_out, up_out,
    xy_ref, ow_ref, x_ref, brought,
    window, conv, conv_low, rate, entry, carry, *links,
):
    step = pl.program_id(0)
    plane = PlaneReduce(*links[:10])
    gate_line = LineGather(gate_shard, lambda t: gate_out.at[t], *links[10:13])
    first_rows = up_shard.at[pl.ds(0, up_out.shape[1])]
    up_line = LineGather(first_rows, lambda t: up_out.at[t], *links[13:16])

    bring = Bring((xy_hbm, ow_hbm, x_hbm), (xy_ref, ow_ref, x_ref), brought)

    @pl.when(step == 0)
    def _():
        bring.start()
        meet(True, "near")
        gate_line.start()
        up_line.start()
        bring.wait(0, 1, 2)

    @pl.when(step > 0)
    def _():
        plane.pass_on(step - 1)

    @pl.when(step > 2)
    def _():
        plane.relay(step - 3)

    forward_step(
        normed_ref, xy_ref, taps_ref, vec_ref, wr_ref, we_ref, keep_ref,
        u_ref, by_ref, before_ref, states_ref, mixed_ref,
        window, conv, conv_low, rate, entry, carry,
    )
    plane.put(step, dot_plain(mixed_ref[...], ow_ref[...]).astype(jnp.bfloat16))

    @pl.when(step == 6)
    def _():
        gate_line.forward()

    @pl.when(step == PLANE - 1)
    def _():
        plane.relay(step - 2)
        plane.pass_on(step)
        plane.relay(step - 1)
        plane.relay(step)
        up_line.forward()
        plane.arrive()

        def make(i, unused):
            at = pl.ds(pl.multiple_of(i * CHUNK, CHUNK), CHUNK)
            residual = x_ref[at, :].astype(jnp.float32) + plane.total(at)
            residual_ref[at, :] = residual
            two_ref[at, :] = norm_rows(residual, gain_ref[...]).astype(jnp.bfloat16)
            return unused

        lax.fori_loop(0, x_ref.shape[0] // CHUNK, make, 0)
        plane.finish()
        gate_line.finish()
        up_line.finish()


def forward_linked(normed, xy, ow, taps, vec, wr, we, keep, layer_in, gain, gate_shard, up_shard):
    length, width = normed.shape
    chans = ow.shape[0]
    rows = length // PLANE
    share, units = up_shard.shape
    tile = lambda columns: pl.BlockSpec((rows, columns), lambda i: (i, 0))
    return pl.pallas_call(
        forward_linked_body,
        grid=(PLANE,),
        in_specs=[
            tile(width), ANYWHERE, ANYWHERE, once(taps.shape),
            once(vec.shape), once(wr.shape), once(we.shape), tile(keep.shape[1]),
            ANYWHERE, once(gain.shape), ANYWHERE, ANYWHERE,
        ],
        out_specs=[tile(chans)] * 5 + [once((rows, width))] * 2 + [ANYWHERE] * 2,
        out_shape=[
            jax.ShapeDtypeStruct((length, chans), jnp.bfloat16),
            jax.ShapeDtypeStruct((length, chans), jnp.float32),
            jax.ShapeDtypeStruct((length, chans), jnp.float32),
            jax.ShapeDtypeStruct((length, chans), jnp.bfloat16),
            jax.ShapeDtypeStruct((length, chans), jnp.bfloat16),
            jax.ShapeDtypeStruct((rows, width), jnp.float32),
            jax.ShapeDtypeStruct((rows, width), jnp.bfloat16),
            jax.ShapeDtypeStruct((LINE,) + gate_shard.shape, jnp.bfloat16),
            jax.ShapeDtypeStruct((LINE, share // 2, units), jnp.bfloat16),
        ],
        scratch_shapes=[
            *held(xy, ow, layer_in),
            pltpu.VMEM((rows + 8, chans), jnp.float32),
            pltpu.VMEM((rows, chans), jnp.float32),
            pltpu.VMEM((rows, chans), jnp.bfloat16),
            pltpu.VMEM((rows, chans), jnp.float32),
            pltpu.VMEM((rows, chans), jnp.float32),
            pltpu.VMEM((8, chans), jnp.float32),
            *PlaneReduce.buffers(rows, width),
            *PlaneReduce.semaphores,
            *(LineGather.semaphores * 2),
        ],
        compiler_params=pltpu.CompilerParams(
            collective_id=1, has_side_effects=True, vmem_limit_bytes=61 * 2**20
        ),
        name="mixer_forward_linked",
    )(normed, xy, ow, taps, vec, wr, we, keep, layer_in, gain, gate_shard, up_shard)


def ffn_up_body(
    own_two, gate_ref, own_cot, cot_half, up_half, up_shard, down_shard,
    two_out, cot_out, up_out, down_out, gates_out, ups_out, hidden_out, down_parts,
    two, cot, up, gates, ups, hidden, total, copied, brought, *semaphores,
):
    h = lax.axis_index("head")
    rows = own_two.shape[0]
    units = gates.shape[1]
    width, share = own_two.shape[1], up_shard.shape[0]
    half = share // 2
    late_columns = pl.ds(width // 2, width // 2)
    up_line = LineGather(
        up_shard.at[pl.ds(half, half)],
        lambda t: up.at[pl.ds(pl.multiple_of(t * share + half, half), half)],
        *semaphores[0:3],
    )
    down_line = LineGather(down_shard, lambda t: down_out.at[t], *semaphores[3:6])
    two_plane = PlaneGather(own_two, two, *semaphores[6:9])
    cot_plane = PlaneGather(
        own_cot, cot, *semaphores[9:12], source=late_columns, target=late_columns
    )
    inward = [
        pltpu.make_async_copy(up_half.at[t], up.at[pl.ds(t * share, half)], brought.at[t])
        for t in range(LINE)
    ]
    inward.append(
        pltpu.make_async_copy(cot_half, cot.at[:, :, pl.ds(0, width // 2)], brought.at[LINE])
    )
    outward = [
        pltpu.make_async_copy(src, dst, copied.at[k])
        for k, (src, dst) in enumerate(
            (
                (two, two_out), (cot, cot_out), (up, up_out), (gates, gates_out),
                (ups, ups_out), (hidden, hidden_out),
            )
        )
    ]
    meet(True, "near")
    up_line.start()
    down_line.start()
    two_plane.start()
    for copy in inward:
        copy.start()

    def at_block(block):
        return pl.ds(pl.multiple_of(block * rows, rows), rows)

    def make_gates(block):
        gates[at_block(block), :] = dot_plain(two[block], gate_ref[...])

    gates[at_block(h), :] = dot_plain(own_two[...], gate_ref[...])
    two_plane.relay(0)
    two_plane.beside()
    make_gates(two_plane.side)
    two_plane.relay(1)
    cot_plane.start()
    two_plane.rest()
    make_gates(two_plane.x)
    make_gates(two_plane.y)
    up_line.forward()
    two_plane.far_side()
    make_gates(two_plane.far)
    two_plane.end(beside=False)
    outward[0].start()
    cot_plane.relay(0)
    make_gates(across_of(two_plane.side))
    make_gates(along_of(two_plane.side))
    cot_plane.relay(1)
    make_gates(across_of(along_of(two_plane.side)))
    outward[3].start()
    up_line.finish()
    for copy in inward:
        copy.wait()
    outward[2].start()

    def make_hidden(block, unused):
        at = at_block(block)
        ups[at, :] = dot_plain(two[block], up[...])

        def make(i, unused):
            here = pl.ds(pl.multiple_of(block * rows + i * CHUNK, CHUNK), CHUNK)
            hidden[here, :] = (gelu_only(gates[here, :]) * ups[here, :]).astype(jnp.bfloat16)
            return unused

        lax.fori_loop(0, rows // CHUNK, make, 0, unroll=UNROLL)
        return unused

    lax.fori_loop(0, 2, make_hidden, 0)
    cot_plane.rest()
    lax.fori_loop(2, 5, make_hidden, 0)
    cot_plane.far_side()
    down_line.forward()
    lax.fori_loop(5, PLANE, make_hidden, 0)
    outward[4].start()
    outward[5].start()
    cot_plane.end()
    outward[1].start()
    total[...] = contract_first(cot[0], hidden[0:rows, :])

    def add_down(block, unused):
        total[...] += contract_first(cot[block], hidden[at_block(block), :])
        return unused

    lax.fori_loop(1, PLANE, add_down, 0)
    to_parts(total, down_parts)
    down_line.finish()
    for copy in outward:
        copy.wait()


def ffn_up(own_two, gate, own_cot, cot_half, up_half, up_shard, down_shard):
    rows, width = own_two.shape
    share, units = up_shard.shape
    length = rows * PLANE
    group = jax.ShapeDtypeStruct((PLANE, rows, width), jnp.bfloat16)
    weight = jax.ShapeDtypeStruct((LINE, share, units), jnp.bfloat16)
    return pl.pallas_call(
        ffn_up_body,
        in_specs=[IN_VMEM, IN_VMEM] + [ANYWHERE] * 5,
        out_specs=[ANYWHERE] * 7 + [IN_VMEM],
        out_shape=[
            group,
            group,
            jax.ShapeDtypeStruct((width, units), jnp.bfloat16),
            weight,
            jax.ShapeDtypeStruct((length, units), jnp.float32),
            jax.ShapeDtypeStruct((length, units), jnp.float32),
            jax.ShapeDtypeStruct((length, units), jnp.bfloat16),
            weight,
        ],
        scratch_shapes=[
            pltpu.VMEM((PLANE, rows, width), jnp.bfloat16),
            pltpu.VMEM((PLANE, rows, width), jnp.bfloat16),
            pltpu.VMEM((width, units), jnp.bfloat16),
            pltpu.VMEM((length, units), jnp.float32),
            pltpu.VMEM((length, units), jnp.float32),
            pltpu.VMEM((length, units), jnp.bfloat16),
            pltpu.VMEM((width, units), jnp.float32),
            pltpu.SemaphoreType.DMA((6,)),
            pltpu.SemaphoreType.DMA((LINE + 1,)),
            *(LineGather.semaphores * 2),
            *(PlaneGather.semaphores * 2),
        ],
        compiler_params=pltpu.CompilerParams(
            collective_id=2, has_side_effects=True, vmem_limit_bytes=61 * 2**20
        ),
        name="ffn_up",
    )(own_two, gate, own_cot, cot_half, up_half, up_shard, down_shard)
def far_first(step):
    chip = lax.div(lax.axis_index("head"), 2)
    place = lax.div(step, 2)
    x = lax.rem(lax.rem(chip, 2) + 1 - lax.div(place, 2), 2)
    y = lax.rem(lax.div(chip, 2) + 1 + lax.rem(place, 2), 2)
    return 2 * (2 * y + x) + lax.rem(step, 2)


def norm_back(rows, gain, incoming):
    scale = lax.rsqrt(jnp.mean(rows * rows, axis=-1, keepdims=True) + EPSILON)
    scaled = incoming * gain
    inner = jnp.mean(scaled * rows, axis=-1, keepdims=True)
    return scale * scaled - rows * (scale * scale * scale * inner), incoming * rows * scale


def to_parts(total, parts):
    rows = parts.shape[1]
    step = 64

    def move(i, unused):
        at = pl.ds(pl.multiple_of(i * step, step), step)
        for t in range(LINE):
            here = pl.ds(pl.multiple_of(t * rows + i * step, step), step)
            parts[t, at, :] = total[here, :].astype(jnp.bfloat16)
        return unused

    lax.fori_loop(0, rows // step, move, 0)


def to_turned_parts(total, parts, places):
    share = parts.shape[2]
    step = 32
    for first, target, count in places:

        def move(i, unused, first=first, target=target):
            here = pl.ds(pl.multiple_of(first + i * step, step), step)
            at = pl.ds(pl.multiple_of(target + i * step, step), step)
            for t in range(LINE):
                parts[t, at, :] = total[here, t * share : (t + 1) * share].astype(jnp.bfloat16)
            return unused

        lax.fori_loop(0, count // step, move, 0)


def ffn_back_body(
    cot_ref, two_ref, gates_ref, ups_ref, gate_hbm, up_hbm, down_hbm, parts_hbm,
    residual_hbm, own_cot_hbm, gain_ref,
    d_ups_ref, gate_parts, down_out, d_res_ref, d_low_ref, gain_out,
    gate_ref, up_ref, down_ref, parts, brought, late,
    total, d_gates, d_hidden, eight, *links,
):
    step = pl.program_id(0)
    line = LineReduce(parts_hbm, parts, *links[:5])
    plane = PlaneReduce(*links[5:])
    rows = cot_ref.shape[0]

    bring = Bring(
        (down_hbm, gate_hbm, up_hbm, parts_hbm), (down_ref, gate_ref, up_ref, parts), brought
    )
    into_outputs = Bring((residual_hbm, own_cot_hbm), (d_res_ref, d_low_ref), late)

    @pl.when(step == 0)
    def _():
        bring.start()
        meet(True, "near")
        line.start()
        into_outputs.start()
        bring.wait(0, 1, 2, 3)

    @pl.when((step > 2) & (step <= PLANE + 2))
    def _():
        plane.relay(far_first(step - 3))

    @pl.when(step < PLANE)
    def _():
        d_hidden[...] = dot_plain(cot_ref[...], down_ref[...])

        def make(i, unused):
            at = pl.ds(pl.multiple_of(i * CHUNK, CHUNK), CHUNK)
            gelu_gate, slope = gelu_both(gates_ref[at, :])
            through = d_hidden[at, :]
            d_gates[step, at, :] = (through * ups_ref[at, :] * slope).astype(jnp.bfloat16)
            d_ups_ref[at, :] = (through * gelu_gate).astype(jnp.bfloat16)
            return unused

        lax.fori_loop(0, rows // CHUNK, make, 0, unroll=UNROLL)

        @pl.when(step > 0)
        def _():
            plane.pass_on(far_first(step - 1))

        value = contract_last(d_gates[step], gate_ref[...]) + contract_last(
            d_ups_ref[...], up_ref[...]
        )
        plane.put(far_first(step), value.astype(jnp.bfloat16))

    @pl.when(step == PLANE)
    def _():
        total[...] = contract_first(two_ref[...], d_gates[0])

    @pl.when(step > PLANE)
    def _():
        total[...] += contract_first(two_ref[...], d_gates[step - PLANE])

    @pl.when(step == PLANE)
    def _():
        plane.pass_on(far_first(step - 1))

    @pl.when(step == 5)
    def _():
        line.forward()

    @pl.when(step == 2 * PLANE - 1)
    def _():
        to_parts(total, gate_parts)
        plane.arrive()
        into_outputs.wait(0, 1)
        eight[...] = jnp.zeros_like(eight)

        def back(i, unused):
            at = pl.ds(pl.multiple_of(i * CHUNK, CHUNK), CHUNK)
            d_rows, d_gain = norm_back(d_res_ref[at, :], gain_ref[...], plane.total(at))
            d_residual = d_low_ref[at, :].astype(jnp.float32) + d_rows
            d_res_ref[at, :] = d_residual
            d_low_ref[at, :] = d_residual.astype(jnp.bfloat16)
            eight[...] += sum_eight(d_gain)
            return unused

        lax.fori_loop(0, rows // CHUNK, back, 0)
        gain_out[...] = jnp.sum(eight[...], axis=0, keepdims=True)

        def write(at, value):
            down_out[at, :] = value

        line.finish(write)
        plane.finish()


def ffn_back(
    cot_group, two_group, gates, ups, gate, up, down, parts, residual, own_cot, gain
):
    length, width = cot_group.shape
    units = gate.shape[1]
    rows, share = length // PLANE, width // LINE
    tile = lambda columns: pl.BlockSpec(
        (rows, columns), lambda i: (far_first(jnp.minimum(i, PLANE - 1)), 0)
    )
    later = lambda columns: pl.BlockSpec(
        (rows, columns), lambda i: (far_first(jnp.maximum(i - PLANE, 0)), 0)
    )
    return pl.pallas_call(
        ffn_back_body,
        grid=(2 * PLANE,),
        in_specs=[
            tile(width), later(width), tile(units), tile(units),
            *([ANYWHERE] * 6), once(gain.shape),
        ],
        out_specs=[
            tile(units), once((LINE, share, units)), once((share, units)),
            once((rows, width)), once((rows, width)), once((1, width)),
        ],
        out_shape=[
            jax.ShapeDtypeStruct((length, units), jnp.bfloat16),
            jax.ShapeDtypeStruct((LINE, share, units), jnp.bfloat16),
            jax.ShapeDtypeStruct((share, units), jnp.float32),
            jax.ShapeDtypeStruct((rows, width), jnp.float32),
            jax.ShapeDtypeStruct((rows, width), jnp.bfloat16),
            jax.ShapeDtypeStruct((1, width), jnp.float32),
        ],
        scratch_shapes=[
            *held(gate, up, down, parts),
            pltpu.SemaphoreType.DMA((2,)),
            pltpu.VMEM((width, units), jnp.float32),
            pltpu.VMEM((PLANE, rows, units), jnp.bfloat16),
            pltpu.VMEM((rows, units), jnp.float32),
            pltpu.VMEM((8, width), jnp.float32),
            *LineReduce.buffers(share, units),
            *LineReduce.semaphores,
            *PlaneReduce.buffers(rows, width),
            *PlaneReduce.semaphores,
        ],
        compiler_params=pltpu.CompilerParams(
            collective_id=4, has_side_effects=True, vmem_limit_bytes=63 * 2**20
        ),
        name="ffn_back",
    )(cot_group, two_group, gates, ups, gate, up, down, parts, residual, own_cot, gain)


def turn_body(
    two_ref, d_ups_ref, parts_hbm, block, mixed_hbm, ow_hbm,
    up_parts, out_parts, gate_out, d_mixed_out,
    gate_parts, mixed_ref, ow_ref, brought,
    full, total, out_total, *links,
):
    step = pl.program_id(0)
    line = LineReduce(parts_hbm, gate_parts, *links[:5])
    plane = PlaneGather(block, full, *links[5:])
    rows = two_ref.shape[0]

    bring = Bring(
        (parts_hbm, mixed_hbm, ow_hbm), (gate_parts, mixed_ref, ow_ref), brought
    )

    @pl.when(step == 0)
    def _():
        bring.start()
        meet(True, "near")
        line.start()
        plane.start()
        total[...] = contract_first(two_ref[...], d_ups_ref[...])

    @pl.when(step > 0)
    def _():
        total[...] += contract_first(two_ref[...], d_ups_ref[...])

    @pl.when(step == 3)
    def _():
        plane.relay(0)

    @pl.when(step == PLANE - 2)
    def _():
        plane.relay(1)

    @pl.when(step == PLANE - 1)
    def _():
        bring.wait(0, 1, 2)
        line.forward()

        def add(owner, start=False):
            at = pl.ds(pl.multiple_of(owner * rows, rows), rows)
            d_mixed_out[at, :] = contract_last(full[owner], ow_ref[...])
            value = contract_first(mixed_ref[at, :], full[owner])
            out_total[...] = value if start else out_total[...] + value

        plane.beside()
        add(plane.side, start=True)
        to_parts(total, up_parts)
        plane.rest()
        add(plane.x)
        add(plane.y)
        plane.far_side()
        add(plane.far)
        plane.end(beside=False)
        add(plane.h)
        add(across_of(plane.side))
        add(along_of(plane.side))
        add(across_of(along_of(plane.side)))
        kept = out_parts.shape[1]
        to_turned_parts(out_total, out_parts, ((0, 0, kept),))

        def write(at, value):
            gate_out[at, :] = value

        line.finish(write)


def turn(two_group, d_ups, gate_parts, block, mixed, ow, kept):
    length, width = two_group.shape
    units, chans = d_ups.shape[1], mixed.shape[1]
    rows, share = length // PLANE, width // LINE
    tile = lambda columns: pl.BlockSpec((rows, columns), lambda i: (i, 0))
    return pl.pallas_call(
        turn_body,
        grid=(PLANE,),
        in_specs=[
            tile(width), tile(units), ANYWHERE, ANYWHERE, ANYWHERE, ANYWHERE,
        ],
        out_specs=[
            once(gate_parts.shape), once((LINE, kept, share)), once((share, units)),
            once((length, chans)),
        ],
        out_shape=[
            jax.ShapeDtypeStruct(gate_parts.shape, jnp.bfloat16),
            jax.ShapeDtypeStruct((LINE, kept, share), jnp.bfloat16),
            jax.ShapeDtypeStruct((share, units), jnp.float32),
            jax.ShapeDtypeStruct((length, chans), jnp.float32),
        ],
        scratch_shapes=[
            *held(gate_parts, mixed, ow),
            pltpu.VMEM((PLANE, rows, width), jnp.bfloat16),
            pltpu.VMEM((width, units), jnp.float32),
            pltpu.VMEM((chans, width), jnp.float32),
            *LineReduce.buffers(share, units),
            *LineReduce.semaphores,
            *PlaneGather.semaphores,
        ],
        compiler_params=pltpu.CompilerParams(
            collective_id=5, has_side_effects=True, vmem_limit_bytes=61 * 2**20
        ),
        name="turn",
    )(two_group, d_ups, gate_parts, block, mixed, ow)


def pack_small(head_width, taps, vec, params, wr, we, small):
    columns = small.shape[1]
    step = 16
    last = (2 * head_width + 7) // 8 * 8

    def move(i, unused):
        at = pl.ds(pl.multiple_of(i * step, step), step)
        shape = (step, columns)
        row = lax.broadcasted_iota(jnp.int32, shape, 0) + i * step
        left = lax.broadcasted_iota(jnp.int32, shape, 1) < head_width
        rate, entry = wr[at, :], we[at, :]
        first = jnp.where(left, rate, pltpu.roll(entry, head_width, 1))
        second = jnp.where(left, pltpu.roll(rate, columns - head_width, 1), entry)
        small[at, :] = jnp.where(row < head_width, first, second).astype(jnp.bfloat16)
        return unused

    lax.fori_loop(0, last // step, move, 0)
    scaled = vec[0:4, :] * jnp.concatenate(
        [jnp.ones((3, columns), jnp.float32), params[4:5, :]], axis=0
    )
    tail = jnp.concatenate([taps[...], scaled], axis=0).astype(jnp.bfloat16)
    here = last // step * step
    rate, entry = wr[here : here + 8, :], we[here : here + 8, :]
    left = lax.broadcasted_iota(jnp.int32, (8, columns), 1) < head_width
    rest = jnp.where(left, pltpu.roll(rate, columns - head_width, 1), entry).astype(jnp.bfloat16)
    small[here : here + 16, :] = jnp.concatenate([rest, tail], axis=0)
    if small.shape[0] > here + 16:
        small[here + 16 :, :] = jnp.zeros_like(small[here + 16 :, :])


def split_gains(mix, ffn, out):
    share = out.shape[2] // 2
    low = lax.broadcasted_iota(jnp.int32, (1, 2 * share), 1) < share
    for r in range(LINE):
        lines = []
        for pair in range(PLANE // 2):
            at = (r * (PLANE // 2) + pair) * 2 * share
            one, two = mix[:, at : at + 2 * share], ffn[:, at : at + 2 * share]
            lines.append(jnp.where(low, one, pltpu.roll(two, share, 1)))
            lines.append(jnp.where(low, pltpu.roll(one, share, 1), two))
        out[r] = jnp.concatenate(lines, axis=0)


def backward_linked_body(
    head_width,
    d_mixed_ref, xy_hbm, taps_ref, vec_ref, wr_ref, we_ref, keep_ref,
    u_ref, u_prev_ref, by_ref, before_ref, states_ref, normed_ref, up_hbm, out_hbm,
    x_hbm, gain_ref, d_residual_hbm, ffn_gain_ref,
    xy_parts, up_out, out_out, in_grad, gains_out, small_out,
    xy_ref, up_parts, out_parts, brought, late,
    out_sum, taps_sum, vec_sum, wr_sum, we_sum, small, small_parts, d_xy, d_all, xy_total, eight, *rest,
):
    scratch, links = rest[:10], rest[10:]
    step = pl.program_id(0)
    block = PLANE - 1 - step
    line = LineReduce(up_hbm, up_parts, *links[:5])
    out_line = LineReduce(out_hbm, out_parts, *links[5:10])
    small_line = LineReduce(small_parts, small_parts, *links[10:15])
    plane = PlaneReduce(*links[15:])

    bring = Bring(
        (xy_hbm, up_hbm, out_hbm), (xy_ref, up_parts, out_parts), brought
    )
    d_residual_ref = xy_total.at[0 : x_hbm.shape[0]]
    bring_late = Bring((x_hbm, d_residual_hbm), (in_grad, d_residual_ref), late)

    @pl.when(step == 0)
    def _():
        bring.start()
        meet(True, "near")
        line.start()
        out_line.start()
        bring.wait(0, 1, 2)

    @pl.when((step > 0) & (step <= PLANE))
    def _():
        plane.pass_on(block + 1)

    @pl.when((step > 2) & (step <= PLANE))
    def _():
        plane.relay(block + 3)

    @pl.when(step == 4)
    def _():
        line.forward()

    @pl.when(step < PLANE)
    def _():
        backward_step(
            step == 0, step == PLANE - 1, d_mixed_ref, taps_ref, vec_ref, wr_ref, we_ref,
            keep_ref, u_ref, u_prev_ref, by_ref, before_ref, states_ref, d_xy,
            taps_sum, vec_sum, wr_sum, we_sum, *scratch,
        )
        d_all[step] = d_xy[...]
        plane.put(block, dot_plain(d_xy[...], xy_ref[...]).astype(jnp.bfloat16))

    @pl.when(step == PLANE)
    def _():
        pack_small(head_width, taps_sum, vec_sum, vec_ref, wr_sum, we_sum, small)
        share = small_parts.shape[1]
        for t in range(LINE):
            small_parts[t] = small[t * share : (t + 1) * share, :]
        small_line.start()
        xy_total[...] = contract_first(d_all[0], normed_ref[...])

    @pl.when(step > PLANE)
    def _():
        xy_total[...] += contract_first(d_all[step - PLANE], normed_ref[...])

    @pl.when(step == PLANE + 2)
    def _():
        plane.relay(1)

    @pl.when(step == PLANE + 4)
    def _():
        out_line.forward()

    @pl.when(step == PLANE + 5)
    def _():
        plane.relay(0)

    @pl.when(step == 2 * PLANE - 1)
    def _():
        small_line.forward()
        kept, chans = out_parts.shape[1], d_xy.shape[1] // 2
        to_turned_parts(xy_total, xy_parts, ((0, 0, kept), (chans, kept, kept)))
        bring_late.start()
        plane.arrive()
        bring_late.wait(0, 1)
        eight[...] = jnp.zeros_like(eight)

        def back(i, unused):
            at = pl.ds(pl.multiple_of(i * CHUNK, CHUNK), CHUNK)
            d_rows, d_gain = norm_back(
                in_grad[at, :].astype(jnp.float32), gain_ref[...], plane.total(at)
            )
            in_grad[at, :] = (xy_total[at, :] + d_rows).astype(jnp.bfloat16)
            eight[...] += sum_eight(d_gain)
            return unused

        lax.fori_loop(0, in_grad.shape[0] // CHUNK, back, 0)
        split_gains(jnp.sum(eight[...], axis=0, keepdims=True), ffn_gain_ref[...], gains_out)

        def write(at, value):
            up_out[at, :] = value

        def write_out(at, value):
            out_sum[at, :] = value

        def write_small(at, value):
            small_out[at, :] = value.astype(jnp.bfloat16)

        line.finish(write)
        out_line.finish(write_out)
        out_out[...] = out_sum[0 : out_out.shape[0], :]
        small_line.finish(write_small)
        plane.finish()


def backward_linked(
    d_mixed, xy, taps, vec, wr, we, keep, u, by, before, states, normed, up_parts, out_parts,
    layer_in, gain, d_residual, ffn_gain, head_width, used,
):
    length, width = normed.shape
    chans, units = d_mixed.shape[1], up_parts.shape[2]
    rows, share = length // PLANE, width // LINE
    kept = out_parts.shape[1]
    place = lambda i: PLANE - 1 - jnp.minimum(i, PLANE - 1)
    tile = lambda columns: pl.BlockSpec((rows, columns), lambda i: (place(i), 0))
    later = lambda columns: pl.BlockSpec(
        (rows, columns), lambda i: (PLANE - 1 - jnp.maximum(i - PLANE, 0), 0)
    )
    ahead = pl.BlockSpec((16, chans), lambda i: (jnp.maximum(place(i) * (rows // 16) - 1, 0), 0))
    small_share = -(-((2 * head_width + 7) // 8 * 8 + 8) // (LINE * 32)) * 32
    gain_terms = (LINE, PLANE, width // (LINE * PLANE) * 2)
    return pl.pallas_call(
        functools.partial(backward_linked_body, head_width),
        grid=(2 * PLANE,),
        in_specs=[
            tile(chans), ANYWHERE, once(taps.shape), once(vec.shape), once(wr.shape),
            once(we.shape), tile(keep.shape[1]), tile(chans), ahead, tile(chans), tile(chans),
            tile(chans), later(width), ANYWHERE, ANYWHERE,
            ANYWHERE, once(gain.shape), ANYWHERE, once(ffn_gain.shape),
        ],
        out_specs=[
            once((LINE, 2 * kept, share)), once((share, units)), once((used, share)),
            once((rows, width)), once(gain_terms), once((small_share, chans)),
        ],
        out_shape=[
            jax.ShapeDtypeStruct((LINE, 2 * kept, share), jnp.bfloat16),
            jax.ShapeDtypeStruct((share, units), jnp.float32),
            jax.ShapeDtypeStruct((used, share), jnp.float32),
            jax.ShapeDtypeStruct((rows, width), jnp.bfloat16),
            jax.ShapeDtypeStruct(gain_terms, jnp.float32),
            jax.ShapeDtypeStruct((small_share, chans), jnp.bfloat16),
        ],
        scratch_shapes=[
            *held(xy, up_parts, out_parts),
            pltpu.SemaphoreType.DMA((2,)),
            pltpu.VMEM((kept, share), jnp.float32),
            pltpu.VMEM(taps.shape, jnp.float32),
            pltpu.VMEM(vec.shape, jnp.float32),
            pltpu.VMEM(wr.shape, jnp.float32),
            pltpu.VMEM(we.shape, jnp.float32),
            pltpu.VMEM((LINE * small_share, chans), jnp.bfloat16),
            pltpu.VMEM((LINE, small_share, chans), jnp.bfloat16),
            pltpu.VMEM((rows, 2 * chans), jnp.bfloat16),
            pltpu.VMEM((PLANE, rows, 2 * chans), jnp.bfloat16),
            pltpu.VMEM((2 * chans, width), jnp.float32),
            pltpu.VMEM((8, width), jnp.float32),
            pltpu.VMEM((rows + 8, chans), jnp.float32),
            pltpu.VMEM((rows, chans), jnp.float32),
            pltpu.VMEM((rows, chans), jnp.bfloat16),
            pltpu.VMEM((rows, chans), jnp.float32),
            pltpu.VMEM((rows, chans), jnp.float32),
            pltpu.VMEM((rows + 8, chans), jnp.float32),
            pltpu.VMEM((rows, chans), jnp.bfloat16),
            pltpu.VMEM((rows, chans), jnp.bfloat16),
            pltpu.VMEM((8, chans), jnp.float32),
            pltpu.VMEM((64, chans), jnp.float32),
            *LineReduce.buffers(share, units),
            *LineReduce.semaphores,
            *LineReduce.buffers(kept, share),
            *LineReduce.semaphores,
            *LineReduce.buffers(small_share, chans),
            *LineReduce.semaphores,
            *PlaneReduce.buffers(rows, width),
            *PlaneReduce.semaphores,
        ],
        compiler_params=pltpu.CompilerParams(
            collective_id=6, has_side_effects=True, vmem_limit_bytes=61 * 2**20
        ),
        name="mixer_backward_linked",
    )(
        d_mixed, xy, taps, vec, wr, we, keep, u, u, by, before, states, normed,
        up_parts, out_parts, layer_in, gain, d_residual, ffn_gain,
    )


def close_body(
    hidden_ref, down_hbm, xy_hbm, residual_hbm, gains_ref, small,
    layer_out, x_out, y_out, gains_out, small_out,
    down_ref, xy_parts, residual_ref, brought, xy_sum,
    gathered, line_gains, both_gains, plane_gains,
    gain_sent, gain_arrived, wide_sent, wide_arrived, *links,
):
    r, h = lax.axis_index("row"), lax.axis_index("head")
    step = pl.program_id(0)
    xy_line = LineReduce(xy_hbm, xy_parts, *links[0:5])
    small_line = LineGather(small, lambda t: gathered.at[t], *links[5:8])
    plane = PlaneReduce(*links[8:])

    def to_row(t, owner):
        return send_to(
            gains_ref.at[t], line_gains.at[owner], gain_sent.at[t], gain_arrived.at[owner],
            "row", t,
        )

    def over_plane(place, owner):
        return send_to(
            both_gains, plane_gains.at[owner], wide_sent.at[place], wide_arrived.at[owner],
            "head", lax.rem(h + place, PLANE),
        )

    bring = Bring(
        (down_hbm, xy_hbm, residual_hbm), (down_ref, xy_parts, residual_ref), brought
    )

    @pl.when(step == 0)
    def _():
        bring.start()
        meet(True, "all")
        for place in range(1, LINE):
            to_row(lax.rem(r + place, LINE), r).start()
        small_line.start()
        xy_line.start()
        bring.wait(0, 1, 2)

    @pl.when(step > 0)
    def _():
        plane.pass_on(far_first(step - 1))

    @pl.when(step > 2)
    def _():
        plane.relay(far_first(step - 3))

    plane.put(far_first(step), contract_last(hidden_ref[...], down_ref[...]).astype(jnp.bfloat16))

    @pl.when(step == 2)
    def _():
        total = gains_ref[r]
        for place in range(1, LINE):
            t = lax.rem(r + place, LINE)
            to_row(t, t).wait_recv()
            total = total + line_gains[t]
        both_gains[...] = total
        for place in range(1, PLANE):
            over_plane(place, h).start()

    @pl.when(step == PLANE - 1)
    def _():
        small_line.forward()
        xy_line.forward()
        plane.relay(far_first(step - 2))
        plane.pass_on(far_first(step))
        plane.relay(far_first(step - 1))
        plane.relay(far_first(step))
        total = both_gains[...]
        for place in range(1, PLANE):
            owner = lax.rem(h + place, PLANE)
            over_plane(place, owner).wait_recv()
            total = total + plane_gains[owner]
        mine = lax.broadcasted_iota(jnp.int32, total.shape, 0) == h
        gains_out[...] = jnp.sum(jnp.where(mine, total, 0.0), axis=0, keepdims=True)
        plane.arrive()

        def make(i, unused):
            at = pl.ds(pl.multiple_of(i * CHUNK, CHUNK), CHUNK)
            layer_out[at, :] = (residual_ref[at, :] + plane.total(at)).astype(jnp.bfloat16)
            return unused

        lax.fori_loop(0, residual_ref.shape[0] // CHUNK, make, 0)
        def write(at, value):
            xy_sum[at, :] = value

        xy_line.finish(write)
        used, kept = x_out.shape[0], xy_sum.shape[0] // 2
        x_out[...] = xy_sum[0:used, :]
        y_out[...] = xy_sum[kept : kept + used, :]
        small_line.finish()
        small_out[...] = gathered[...].astype(jnp.float32)
        plane.finish()
        for place in range(1, LINE):
            to_row(lax.rem(r + place, LINE), r).wait_send()
        for place in range(1, PLANE):
            over_plane(place, h).wait_send()


def close_block(hidden, down, xy_parts, residual, gains, small, used):
    length, units = hidden.shape
    rows, width = residual.shape
    both, share = xy_parts.shape[1:]
    return pl.pallas_call(
        close_body,
        grid=(PLANE,),
        in_specs=[
            pl.BlockSpec((rows, units), lambda i: (far_first(i), 0)), ANYWHERE,
            ANYWHERE, ANYWHERE, once(gains.shape), once(small.shape),
        ],
        out_specs=[
            once((rows, width)), once((used, share)), once((used, share)), once((1, gains.shape[2])),
            once((LINE,) + small.shape),
        ],
        out_shape=[
            jax.ShapeDtypeStruct((rows, width), jnp.bfloat16),
            jax.ShapeDtypeStruct((used, share), jnp.float32),
            jax.ShapeDtypeStruct((used, share), jnp.float32),
            jax.ShapeDtypeStruct((1, gains.shape[2]), jnp.float32),
            jax.ShapeDtypeStruct((LINE,) + small.shape, jnp.float32),
        ],
        scratch_shapes=[
            *held(down, xy_parts, residual),
            pltpu.VMEM((both, share), jnp.float32),
            pltpu.VMEM((LINE,) + small.shape, jnp.bfloat16),
            pltpu.VMEM(gains.shape, jnp.float32),
            pltpu.VMEM(gains.shape[1:], jnp.float32),
            pltpu.VMEM((PLANE,) + gains.shape[1:], jnp.float32),
            pltpu.SemaphoreType.DMA((LINE,)),
            pltpu.SemaphoreType.DMA((LINE,)),
            pltpu.SemaphoreType.DMA((PLANE,)),
            pltpu.SemaphoreType.DMA((PLANE,)),
            *LineReduce.buffers(both, share), *LineReduce.semaphores,
            *LineGather.semaphores,
            *PlaneReduce.buffers(rows, width), *PlaneReduce.semaphores,
        ],
        compiler_params=pltpu.CompilerParams(
            collective_id=7, has_side_effects=True, vmem_limit_bytes=61 * 2**20
        ),
        name="close_block",
    )(hidden, down, xy_parts, residual, gains, small)


def hand_over_body(*refs):
    count = (len(refs) - 2) // 3
    sources, targets, held = refs[:count], refs[count : 2 * count], refs[2 * count : 3 * count]
    inward, outward = (
        [
            pltpu.make_async_copy(src, dst, done.at[k])
            for k, (src, dst) in enumerate(zip(starts, ends))
        ]
        for starts, ends, done in ((sources, held, refs[-2]), (held, targets, refs[-1]))
    )
    for copy in inward:
        copy.start()
    for first, second in zip(inward, outward):
        first.wait()
        second.start()
    for copy in outward:
        copy.wait()


def hand_over(*arrays):
    return pl.pallas_call(
        hand_over_body,
        in_specs=[ANYWHERE] * len(arrays),
        out_specs=[ANYWHERE] * len(arrays),
        out_shape=[jax.ShapeDtypeStruct(item.shape, item.dtype) for item in arrays],
        scratch_shapes=[pltpu.VMEM(item.shape, item.dtype) for item in arrays]
        + [pltpu.SemaphoreType.DMA((len(arrays),))] * 2,
        compiler_params=pltpu.CompilerParams(vmem_limit_bytes=61 * 2**20),
        name="hand_over",
    )(*arrays)


def mixer_params(
    conv_weight, conv_bias, rate_weight, rate_bias, entry_weight, entry_bias, decay_param, chans
):
    used = conv_bias.shape[0]
    spare = (0, chans - used)
    decay_wide = jnp.pad(decay_param, spare, constant_values=2.0)
    blank = jnp.zeros((chans,), jnp.float32)
    vec = jnp.stack(
        [
            jnp.pad(conv_bias, spare),
            jnp.pad(rate_bias, spare),
            jnp.pad(entry_bias, spare),
            -8.0 * jax.nn.softplus(-decay_wide),
            8.0 * jax.nn.sigmoid(-decay_wide),
            blank,
            blank,
            blank,
        ]
    )
    taps = jnp.pad(conv_weight, ((0, 0), spare))
    return taps, vec, block_diagonal(rate_weight, chans), block_diagonal(entry_weight, chans)


def shards(
    layer_in,
    cotangent,
    mix_gain,
    ffn_gain,
    x_weight,
    y_weight,
    out_weight,
    conv_weight,
    conv_bias,
    rate_weight,
    rate_bias,
    entry_weight,
    entry_bias,
    decay_param,
    gate_weight,
    up_weight,
    down_weight,
    resets,
):
    heads, head_width = rate_weight.shape[:2]
    used = conv_bias.shape[0]
    chans = -(-used // 128) * 128
    widen = lambda values: jnp.pad(values, ((0, 0), (0, chans - used)))
    mix_full = gather(mix_gain, ("row", "head"), 0)
    ffn_full = gather(ffn_gain, ("row", "head"), 0)
    xy_shard = jnp.concatenate([widen(x_weight), widen(y_weight)], axis=1)
    xy_rows = gather(xy_shard, "row", 0).T
    out_rows = gather(widen(out_weight), "row", 0).T
    gate_rows = gather(gate_weight, "row", 0)
    up_rows = gather(up_weight, "row", 0)
    down_rows = gather(down_weight, "row", 0)

    taps, vec, wr, we = mixer_params(
        conv_weight, conv_bias, rate_weight, rate_bias, entry_weight, entry_bias, decay_param, chans
    )
    keep = keep_columns(resets)

    inputs = layer_in.astype(jnp.float32)
    normed_f, norm_back_one = jax.vjp(norm_apply, inputs, mix_full.astype(jnp.float32))
    normed_group = gather(normed_f.astype(jnp.bfloat16), "head", 0)
    u, by, before, states, mixed, part = mixer_forward(
        normed_group, xy_rows, out_rows, taps, vec, wr, we, keep, ROWS
    )
    residual = inputs + scatter(part, "head", 0).astype(jnp.float32)
    normed_two_f, norm_back_two = jax.vjp(norm_apply, residual, ffn_full.astype(jnp.float32))
    cot_group = gather(cotangent, "head", 0)
    two_group = gather(normed_two_f.astype(jnp.bfloat16), "head", 0)
    gates = dot_plain(two_group, gate_rows)
    ups = dot_plain(two_group, up_rows)
    activated, slope = gelu_both(gates)
    hidden = (activated * ups).astype(jnp.bfloat16)
    ffn_part = contract_last(hidden, down_rows).astype(jnp.bfloat16)
    d_hidden = dot_plain(cot_group, down_rows)
    d_gates = (d_hidden * ups * slope).astype(jnp.bfloat16)
    d_ups = (d_hidden * activated).astype(jnp.bfloat16)
    d_two_part = (contract_last(d_gates, gate_rows) + contract_last(d_ups, up_rows)).astype(
        jnp.bfloat16
    )
    gate_grad = scatter(contract_first(two_group, d_gates).astype(jnp.bfloat16), "row", 0)
    up_grad = scatter(contract_first(two_group, d_ups).astype(jnp.bfloat16), "row", 0)
    down_grad = scatter(contract_first(cot_group, hidden).astype(jnp.bfloat16), "row", 0)
    layer_out = (residual + scatter(ffn_part, "head", 0).astype(jnp.float32)).astype(jnp.bfloat16)
    d_two = scatter(d_two_part, "head", 0).astype(jnp.float32)
    d_resid_norm, d_ffn_gain = norm_back_two(d_two)
    d_residual = cotangent.astype(jnp.float32) + d_resid_norm
    d_res_group = gather(d_residual.astype(jnp.bfloat16), "head", 0)
    d_xy, d_part, d_taps, d_vec, d_wr, d_we = mixer_backward(
        d_res_group, xy_rows, out_rows, taps, vec, wr, we, keep, u, by, before, states, ROWS
    )
    out_grad = scatter(contract_first(d_res_group, mixed).astype(jnp.bfloat16), "row", 0)
    xy_grad = scatter(contract_first(normed_group, d_xy).astype(jnp.bfloat16), "row", 0)
    d_normed = scatter(d_part, "head", 0).astype(jnp.float32)
    d_inputs, d_mix_gain = norm_back_one(d_normed)
    layer_in_grad = (d_inputs + d_residual).astype(jnp.bfloat16)

    small = [
        d_taps[:, :used],
        d_vec[0, :used],
        diagonal_blocks(d_wr, heads, head_width),
        d_vec[1, :used],
        diagonal_blocks(d_we, heads, head_width),
        d_vec[2, :used],
        d_vec[3, :used] * (8.0 * jax.nn.sigmoid(-decay_param)),
    ]
    small = [lax.psum(item.astype(jnp.bfloat16), "row").astype(jnp.float32) for item in small]
    mix_part = scatter(d_mix_gain, ("row", "head"), 0)
    ffn_part_grad = scatter(d_ffn_gain, ("row", "head"), 0)
    wide = lambda values: values[:, :used].astype(jnp.float32)
    return (
        layer_out,
        layer_in_grad,
        mix_part,
        ffn_part_grad,
        wide(xy_grad),
        wide(xy_grad[:, chans:]),
        wide(out_grad),
        *small,
        gate_grad.astype(jnp.float32),
        up_grad.astype(jnp.float32),
        down_grad.astype(jnp.float32),
    )

def shards_linked(
    layer_in,
    cotangent,
    mix_gain,
    ffn_gain,
    x_weight,
    y_weight,
    out_weight,
    conv_weight,
    conv_bias,
    rate_weight,
    rate_bias,
    entry_weight,
    entry_bias,
    decay_param,
    gate_weight,
    up_weight,
    down_weight,
    resets,
):
    heads, head_width = rate_weight.shape[:2]
    used = conv_bias.shape[0]
    kept = -(-used // 16) * 16
    flat = lambda values: values.reshape((-1, values.shape[-1]))
    line = lambda values: values.reshape(1, -1)
    normed_group, cot_half, xy_rows, out_rows, gains, taps, vec, wr, we, keep = open_block(
        layer_in,
        (line(mix_gain), line(ffn_gain)),
        cotangent,
        (x_weight.T, y_weight.T, out_weight.T),
        (
            conv_weight,
            jnp.stack([conv_bias, rate_bias, entry_bias, decay_param]),
            jnp.stack([rate_weight, entry_weight]),
            resets,
        ),
    )
    normed_group = flat(normed_group)
    u, by, before, states, mixed, residual, normed_two, gate_rows, up_half = forward_linked(
        normed_group, xy_rows, out_rows, taps, vec, wr, we, keep, layer_in, gains[1:2],
        gate_weight, up_weight,
    )
    gate_rows = flat(gate_rows)
    two_group, cot_group, up_rows, down_rows, gates, ups, hidden, down_parts = ffn_up(
        normed_two, gate_rows, cotangent, cot_half, up_half, up_weight, down_weight
    )
    two_group, cot_group, down_rows = map(flat, (two_group, cot_group, down_rows))
    d_ups, gate_parts, down_grad, d_residual, d_low, d_ffn_gain = ffn_back(
        cot_group, two_group, gates, ups, gate_rows, up_rows, down_rows, down_parts, residual,
        cotangent, gains[1:2],
    )
    up_parts, out_parts, gate_grad, d_mixed = turn(
        two_group, d_ups, gate_parts, d_low, mixed, out_rows, kept
    )
    xy_parts, up_grad, out_grad, layer_in_grad, gain_terms, small = backward_linked(
        d_mixed, xy_rows, taps, vec, wr, we, keep, u, by, before, states,
        normed_group, up_parts, out_parts, layer_in, gains[0:1], d_residual, d_ffn_gain,
        head_width, used,
    )
    layer_out, x_grad, y_grad, gain_grads, sums = close_block(
        hidden, down_rows, xy_parts, residual, gain_terms, small, used
    )
    sums = flat(sums)
    share = mix_gain.shape[0]
    ends = -(-used // 8) * 8
    (
        layer_out, layer_in_grad, x_grad, y_grad, out_grad, gate_grad, up_grad, down_grad,
    ) = hand_over(
        layer_out, layer_in_grad, x_grad, y_grad, out_grad, gate_grad, up_grad, down_grad
    )
    gates_end = heads * head_width
    return (
        layer_out,
        layer_in_grad,
        gain_grads[0, :share],
        gain_grads[0, share:],
        x_grad.T,
        y_grad.T,
        out_grad.T,
        sums[ends : ends + 4, :used],
        sums[ends + 4, :used],
        sums[:gates_end, :head_width].reshape(heads, head_width, head_width),
        sums[ends + 5, :used],
        sums[:gates_end, head_width : 2 * head_width].reshape(heads, head_width, head_width),
        sums[ends + 6, :used],
        sums[ends + 7, :used],
        gate_grad,
        up_grad,
        down_grad,
    )


def solution(mesh):
    linked = mesh.shape["row"] == LINE and mesh.shape["head"] == PLANE
    return jax.shard_map(
        shards_linked if linked else shards,
        mesh=mesh,
        in_specs=(
            P(("row", "head"), None),
            P(("row", "head"), None),
            P(("row", "head")),
            P(("row", "head")),
            P("row", "head"),
            P("row", "head"),
            P("row", "head"),
            P(None, "head"),
            P("head"),
            P("head", None, None),
            P("head"),
            P("head", None, None),
            P("head"),
            P("head"),
            P("row", "head"),
            P("row", "head"),
            P("row", "head"),
            P("row", None),
        ),
        out_specs=(
            P(("row", "head"), None),
            P(("row", "head"), None),
            P(("row", "head")),
            P(("row", "head")),
            P("row", "head"),
            P("row", "head"),
            P("row", "head"),
            P(None, "head"),
            P("head"),
            P("head", None, None),
            P("head"),
            P("head", None, None),
            P("head"),
            P("head"),
            P("row", "head"),
            P("row", "head"),
            P("row", "head"),
        ),
        check_vma=False,
    )
```

```python
import functools

import jax
import jax.numpy as jnp
from jax import lax
from jax.experimental import pallas as pl
from jax.experimental.pallas import tpu as pltpu
from jax.sharding import PartitionSpec as P

EPSILON = 1e-06
ROWS = 256
GELU_A = 0.7978845608028654
GELU_B = 0.044715
CHUNK = 16
UNROLL = 4


def gelu_only(x):
    return 0.5 * x * (1.0 + jnp.tanh(GELU_A * (x + GELU_B * x * x * x)))


def gelu_both(x):
    square = x * x
    bent = jnp.tanh(GELU_A * x * (1.0 + GELU_B * square))
    half = 0.5 * (1.0 + bent)
    slope = half + 0.5 * x * (1.0 - bent * bent) * (GELU_A * (1.0 + 3.0 * GELU_B * square))
    return x * half, slope


def one_minus_exp(x, exp_x):
    return -jnp.tanh(0.5 * x) * (1.0 + exp_x)


def dot_plain(left, right):
    return jnp.dot(left, right, preferred_element_type=jnp.float32)


def contract_last(left, right):
    return lax.dot_general(
        left, right, (((1,), (1,)), ((), ())), preferred_element_type=jnp.float32
    )


def contract_first(left, right):
    return lax.dot_general(
        left, right, (((0,), (0,)), ((), ())), preferred_element_type=jnp.float32
    )


def sum_eight(value):
    total = value[0:8, :]
    for k in range(1, value.shape[0] // 8):
        total = total + value[8 * k : 8 * k + 8, :]
    return total


def conv_rows(window, keep, taps, shift):
    rows = window.shape[0] - 8
    total = taps[0:1] * window[8:] + shift
    for offset in range(1, 4):
        total = total + taps[offset : offset + 1] * (
            keep[:, offset : offset + 1] * window[8 - offset : 8 - offset + rows]
        )
    return total


def scan_down(decays, driven, carry):
    rows = decays.shape[0]
    place = lax.broadcasted_iota(jnp.int32, decays.shape, 0)
    step = 1
    while step < rows:
        inside = place >= step
        driven = jnp.where(inside, decays * pltpu.roll(driven, step, 0) + driven, driven)
        decays = jnp.where(inside, decays * pltpu.roll(decays, step, 0), decays)
        step *= 2
    return decays * carry + driven


def scan_up(decays, driven, carry):
    rows = decays.shape[0]
    place = lax.broadcasted_iota(jnp.int32, decays.shape, 0)
    step = 1
    while step < rows:
        inside = place < rows - step
        driven = jnp.where(inside, decays * pltpu.roll(driven, rows - step, 0) + driven, driven)
        decays = jnp.where(inside, decays * pltpu.roll(decays, rows - step, 0), decays)
        step *= 2
    return decays * carry + driven


def forward_step(
    normed_ref, xy_ref, taps_ref, vec_ref, wr_ref, we_ref, keep_ref,
    u_ref, by_ref, before_ref, states_ref, mixed_ref,
    window, conv, conv_low, rate, entry, carry,
):
    rows = normed_ref.shape[0]

    @pl.when(pl.program_id(0) == 0)
    def _():
        window[0:8, :] = jnp.zeros_like(window[0:8, :])
        carry[...] = jnp.zeros_like(carry)

    chans = u_ref.shape[1]
    branches = contract_last(normed_ref[...], xy_ref[...])
    branch_x = branches[:, :chans].astype(jnp.bfloat16)
    u_ref[...] = branch_x
    window[pl.ds(8, rows), :] = branch_x.astype(jnp.float32)
    by_ref[...] = branches[:, chans:]

    def conv_step(j, unused):
        at = pl.multiple_of(j * CHUNK, CHUNK)
        made = conv_rows(
            window[pl.ds(at, CHUNK + 8), :], keep_ref[pl.ds(at, CHUNK), :],
            taps_ref[...], vec_ref[0:1, :],
        )
        conv[pl.ds(at, CHUNK), :] = made
        conv_low[pl.ds(at, CHUNK), :] = made.astype(jnp.bfloat16)
        return unused

    lax.fori_loop(0, rows // CHUNK, conv_step, 0, unroll=2 * UNROLL)
    window[0:8, :] = window[pl.ds(rows, 8), :]
    rate[...] = dot_plain(conv_low[...], wr_ref[...]) + vec_ref[1:2, :]
    entry[...] = dot_plain(conv_low[...], we_ref[...]) + vec_ref[2:3, :]

    def scan_step(j, before):
        at = pl.multiple_of(j * CHUNK, CHUNK)
        here = pl.ds(at, CHUNK)
        carried = keep_ref[here, 0:1]
        log_decay = jax.nn.sigmoid(rate[here, :]) * vec_ref[3:4, :]
        exp_decay = jnp.exp(log_decay)
        lost = one_minus_exp(2.0 * log_decay, exp_decay * exp_decay)
        drop = lost * lax.rsqrt(jnp.maximum(lost, 1e-30))
        scaling = (1.0 - carried) + carried * drop
        driven = scaling * jax.nn.sigmoid(entry[here, :]) * conv[here, :]
        states = scan_down(exp_decay * carried, driven, before)
        first = lax.broadcasted_iota(jnp.int32, states.shape, 0) == 0
        before_ref[here, :] = jnp.where(first, before, pltpu.roll(states, 1, 0))
        states_low = states.astype(jnp.bfloat16)
        states_ref[here, :] = states_low
        mixed_ref[here, :] = (
            states_low.astype(jnp.float32) * gelu_only(by_ref[here, :])
        ).astype(jnp.bfloat16)
        return states[CHUNK - 1 : CHUNK, :]

    carry[0:1, :] = lax.fori_loop(0, rows // CHUNK, scan_step, carry[0:1, :], unroll=2 * UNROLL)


def forward_body(
    normed_ref, xy_ref, ow_ref, taps_ref, vec_ref, wr_ref, we_ref, keep_ref,
    u_ref, by_ref, before_ref, states_ref, mixed_ref, part_ref, *scratch,
):
    forward_step(
        normed_ref, xy_ref, taps_ref, vec_ref, wr_ref, we_ref, keep_ref,
        u_ref, by_ref, before_ref, states_ref, mixed_ref, *scratch,
    )
    part_ref[...] = dot_plain(mixed_ref[...], ow_ref[...]).astype(jnp.bfloat16)


def backward_step(
    first_step, last_step, d_mixed, taps_ref, vec_ref, wr_ref, we_ref, keep_ref,
    u_ref, u_prev_ref, by_ref, before_ref, states_ref,
    d_xy_ref, taps_out, vec_out, wr_out, we_out,
    window, conv, conv_low, rate, entry, d_conv, g_rate, g_entry, carry, sums,
):
    rows, chans = u_ref.shape

    @pl.when(first_step)
    def _():
        d_conv[pl.ds(rows, 8), :] = jnp.zeros_like(d_conv[pl.ds(rows, 8), :])
        carry[...] = jnp.zeros_like(carry)
        sums[...] = jnp.zeros_like(sums)
        wr_out[...] = jnp.zeros_like(wr_out)
        we_out[...] = jnp.zeros_like(we_out)

    @pl.when(jnp.logical_not(first_step))
    def _():
        d_conv[pl.ds(rows, 8), :] = d_conv[0:8, :]

    window[0:8, :] = u_prev_ref[8:16, :].astype(jnp.float32)
    window[pl.ds(8, rows), :] = u_ref[...].astype(jnp.float32)

    def conv_step(j, unused):
        at = pl.multiple_of(j * CHUNK, CHUNK)
        made = conv_rows(
            window[pl.ds(at, CHUNK + 8), :], keep_ref[pl.ds(at, CHUNK), :],
            taps_ref[...], vec_ref[0:1, :],
        )
        conv[pl.ds(at, CHUNK), :] = made
        conv_low[pl.ds(at, CHUNK), :] = made.astype(jnp.bfloat16)
        return unused

    lax.fori_loop(0, rows // CHUNK, conv_step, 0, unroll=2 * UNROLL)
    rate[...] = dot_plain(conv_low[...], wr_ref[...]) + vec_ref[1:2, :]
    entry[...] = dot_plain(conv_low[...], we_ref[...]) + vec_ref[2:3, :]

    def fold(value):
        return sum_eight(value)

    def scan_step(j, after):
        at = pl.multiple_of(rows - CHUNK - j * CHUNK, CHUNK)
        here = pl.ds(at, CHUNK)
        carried = keep_ref[here, 0:1]
        rate_gate = jax.nn.sigmoid(rate[here, :])
        entry_gate = jax.nn.sigmoid(entry[here, :])
        log_decay = rate_gate * vec_ref[3:4, :]
        exp_decay = jnp.exp(log_decay)
        exp_twice = exp_decay * exp_decay
        lost = one_minus_exp(2.0 * log_decay, exp_twice)
        inverse = lax.rsqrt(jnp.maximum(lost, 1e-30))
        drop = lost * inverse
        scaling = (1.0 - carried) + carried * drop
        decays = exp_decay * carried
        gelu_y, slope_y = gelu_both(by_ref[here, :])
        through = d_mixed[here, :]
        d_states = (through * gelu_y).astype(jnp.bfloat16).astype(jnp.float32)
        d_xy_ref[here, chans:] = (
            through * states_ref[here, :].astype(jnp.float32) * slope_y
        ).astype(jnp.bfloat16)
        passed = scan_up(decays, decays * d_states, after)
        last = lax.broadcasted_iota(jnp.int32, passed.shape, 0) == CHUNK - 1
        adjoint = d_states + jnp.where(last, after, pltpu.roll(passed, CHUNK - 1, 0))
        convolved = conv[here, :]
        gated = adjoint * entry_gate
        g_log = adjoint * before_ref[here, :] * decays - gated * convolved * (
            carried * (exp_twice * inverse)
        )
        g_pre_rate = g_log * vec_ref[3:4, :] * (rate_gate * (1.0 - rate_gate))
        direct = gated * scaling
        g_pre_entry = direct * convolved * (1.0 - entry_gate)
        d_conv[here, :] = direct
        g_rate[here, :] = g_pre_rate.astype(jnp.bfloat16)
        g_entry[here, :] = g_pre_entry.astype(jnp.bfloat16)
        sums[8:16, :] += fold(g_pre_rate)
        sums[16:24, :] += fold(g_pre_entry)
        sums[24:32, :] += fold(g_log * rate_gate)
        return passed[0:1, :]

    carry[0:1, :] = lax.fori_loop(0, rows // CHUNK, scan_step, carry[0:1, :], unroll=2 * UNROLL)
    wr_out[...] += contract_first(conv_low[...], g_rate[...])
    we_out[...] += contract_first(conv_low[...], g_entry[...])
    d_conv[0:rows, :] += contract_last(g_rate[...], wr_ref[...]) + contract_last(
        g_entry[...], we_ref[...]
    )

    def back_step(j, unused):
        at = pl.multiple_of(j * CHUNK, CHUNK)
        here = pl.ds(at, CHUNK)
        keep = keep_ref[here, :]
        ahead = d_conv[pl.ds(at, CHUNK + 8), :]
        behind = window[pl.ds(at, CHUNK + 8), :]
        now = ahead[0:CHUNK]
        total = taps_ref[0:1, :] * now
        sums[0:8, :] += fold(now)
        sums[32:40, :] += fold(now * behind[8:])
        for offset in range(1, 4):
            total = total + taps_ref[offset : offset + 1, :] * (
                keep[:, 3 + offset : 4 + offset] * ahead[offset : offset + CHUNK]
            )
            base = 32 + 8 * offset
            sums[base : base + 8, :] += fold(
                now * (keep[:, offset : offset + 1] * behind[8 - offset : 8 - offset + CHUNK])
            )
        d_xy_ref[here, :chans] = total.astype(jnp.bfloat16)
        return unused

    lax.fori_loop(0, rows // CHUNK, back_step, 0, unroll=2 * UNROLL)

    @pl.when(last_step)
    def _():
        vec_out[...] = jnp.zeros_like(vec_out)
        for place in range(4):
            vec_out[place : place + 1, :] = jnp.sum(
                sums[8 * place : 8 * place + 8, :], axis=0, keepdims=True
            )
            taps_out[place : place + 1, :] = jnp.sum(
                sums[32 + 8 * place : 40 + 8 * place, :], axis=0, keepdims=True
            )


def backward_body(
    d_res_ref, xy_ref, ow_ref, taps_ref, vec_ref, wr_ref, we_ref, keep_ref,
    u_ref, u_prev_ref, by_ref, before_ref, states_ref,
    d_xy_ref, part_ref, taps_out, vec_out, wr_out, we_out, d_mixed, *scratch,
):
    step = pl.program_id(0)
    d_mixed[...] = contract_last(d_res_ref[...], ow_ref[...])
    backward_step(
        step == 0, step == pl.num_programs(0) - 1, d_mixed, taps_ref, vec_ref, wr_ref,
        we_ref, keep_ref, u_ref, u_prev_ref, by_ref, before_ref, states_ref, d_xy_ref,
        taps_out, vec_out, wr_out, we_out, *scratch,
    )
    part_ref[...] = dot_plain(d_xy_ref[...], xy_ref[...]).astype(jnp.bfloat16)


def whole(shape):
    return pl.BlockSpec(shape, lambda i: (0,) * len(shape))


def mixer_forward(normed, xy, ow, taps, vec, wr, we, keep, rows):
    length, width = normed.shape
    chans = ow.shape[0]
    tile = lambda columns: pl.BlockSpec((rows, columns), lambda i: (i, 0))
    return pl.pallas_call(
        forward_body,
        grid=(length // rows,),
        in_specs=[
            tile(width), whole(xy.shape), whole(ow.shape), whole(taps.shape),
            whole(vec.shape), whole(wr.shape), whole(we.shape), tile(keep.shape[1]),
        ],
        out_specs=[tile(chans)] * 5 + [tile(width)],
        out_shape=[
            jax.ShapeDtypeStruct((length, chans), jnp.bfloat16),
            jax.ShapeDtypeStruct((length, chans), jnp.float32),
            jax.ShapeDtypeStruct((length, chans), jnp.float32),
            jax.ShapeDtypeStruct((length, chans), jnp.bfloat16),
            jax.ShapeDtypeStruct((length, chans), jnp.bfloat16),
            jax.ShapeDtypeStruct((length, width), jnp.bfloat16),
        ],
        scratch_shapes=[
            pltpu.VMEM((rows + 8, chans), jnp.float32),
            pltpu.VMEM((rows, chans), jnp.float32),
            pltpu.VMEM((rows, chans), jnp.bfloat16),
            pltpu.VMEM((rows, chans), jnp.float32),
            pltpu.VMEM((rows, chans), jnp.float32),
            pltpu.VMEM((8, chans), jnp.float32),
        ],
        compiler_params=pltpu.CompilerParams(vmem_limit_bytes=48 * 2**20),
        cost_estimate=pl.CostEstimate(
            flops=6 * length * width * chans,
            bytes_accessed=4 * length * width + 30 * length * chans,
            transcendentals=6 * length * chans,
        ),
        name="mixer_forward",
    )(normed, xy, ow, taps, vec, wr, we, keep)


def mixer_backward(d_res, xy, ow, taps, vec, wr, we, keep, u, by, before, states, rows):
    length, width = d_res.shape
    chans = ow.shape[0]
    blocks = length // rows
    tile = lambda columns: pl.BlockSpec((rows, columns), lambda i: (blocks - 1 - i, 0))
    ahead = pl.BlockSpec(
        (16, chans), lambda i: (jnp.maximum((blocks - 1 - i) * (rows // 16) - 1, 0), 0)
    )
    return pl.pallas_call(
        backward_body,
        grid=(blocks,),
        in_specs=[
            tile(width), whole(xy.shape), whole(ow.shape), whole(taps.shape),
            whole(vec.shape), whole(wr.shape), whole(we.shape), tile(keep.shape[1]),
            tile(chans), ahead, tile(chans), tile(chans), tile(chans),
        ],
        out_specs=[
            tile(2 * chans), tile(width), whole(taps.shape), whole(vec.shape),
            whole(wr.shape), whole(we.shape),
        ],
        out_shape=[
            jax.ShapeDtypeStruct((length, 2 * chans), jnp.bfloat16),
            jax.ShapeDtypeStruct((length, width), jnp.bfloat16),
            jax.ShapeDtypeStruct(taps.shape, jnp.float32),
            jax.ShapeDtypeStruct(vec.shape, jnp.float32),
            jax.ShapeDtypeStruct(wr.shape, jnp.float32),
            jax.ShapeDtypeStruct(we.shape, jnp.float32),
        ],
        scratch_shapes=[
            pltpu.VMEM((rows, chans), jnp.float32),
            pltpu.VMEM((rows + 8, chans), jnp.float32),
            pltpu.VMEM((rows, chans), jnp.float32),
            pltpu.VMEM((rows, chans), jnp.bfloat16),
            pltpu.VMEM((rows, chans), jnp.float32),
            pltpu.VMEM((rows, chans), jnp.float32),
            pltpu.VMEM((rows + 8, chans), jnp.float32),
            pltpu.VMEM((rows, chans), jnp.bfloat16),
            pltpu.VMEM((rows, chans), jnp.bfloat16),
            pltpu.VMEM((8, chans), jnp.float32),
            pltpu.VMEM((64, chans), jnp.float32),
        ],
        compiler_params=pltpu.CompilerParams(vmem_limit_bytes=48 * 2**20),
        cost_estimate=pl.CostEstimate(
            flops=6 * length * width * chans,
            bytes_accessed=4 * length * width + 30 * length * chans,
            transcendentals=6 * length * chans,
        ),
        name="mixer_backward",
    )(d_res, xy, ow, taps, vec, wr, we, keep, u, u, by, before, states)


def keep_columns(resets):
    length = resets.shape[1]
    position = lax.broadcasted_iota(jnp.int32, resets.shape, 1)
    starts = jnp.maximum(resets, (position == 0).astype(jnp.int32)).astype(jnp.float32)
    carried = (1.0 - starts).reshape(-1)
    seqs = resets.shape[0]

    def back(values, by):
        values = values.reshape(seqs, length)
        return jnp.pad(values, ((0, 0), (by, 0)))[:, :length].reshape(-1)

    def ahead(values, by):
        values = values.reshape(seqs, length)
        return jnp.pad(values, ((0, 0), (0, by)))[:, by:].reshape(-1)

    one = carried
    two = one * back(carried, 1)
    three = two * back(carried, 2)
    return jnp.stack(
        [carried, one, two, three, ahead(one, 1), ahead(two, 2), ahead(three, 3), carried], axis=1
    )


def block_diagonal(blocks, chans):
    heads, width, unused = blocks.shape
    rows = [
        jnp.pad(blocks[h], ((0, 0), (h * width, chans - (h + 1) * width))) for h in range(heads)
    ]
    full = jnp.concatenate(rows, axis=0)
    return jnp.pad(full, ((0, chans - heads * width), (0, 0)))


def diagonal_blocks(full, heads, width):
    return jnp.stack(
        [full[h * width : (h + 1) * width, h * width : (h + 1) * width] for h in range(heads)]
    )


MESH = pl.DeviceIdType.MESH
ANYWHERE = pl.BlockSpec(memory_space=pl.ANY)
IN_VMEM = pl.BlockSpec(memory_space=pltpu.VMEM)
LINE = 4
PLANE = 8
PIECES = 4


def send_to(src, dst, sent, arrived, axis, target):
    return pltpu.make_async_remote_copy(
        src_ref=src,
        dst_ref=dst,
        send_sem=sent,
        recv_sem=arrived,
        device_id={axis: target},
        device_id_type=MESH,
    )


def sibling_of(h):
    return h + 1 - 2 * lax.rem(h, 2)


def across_of(h):
    return h + 2 - 4 * lax.rem(lax.div(h, 2), 2)


def along_of(h):
    return lax.rem(h + 4, PLANE)


def meet(row_line, plane):
    r, h = lax.axis_index("row"), lax.axis_index("head")
    barrier = pltpu.get_barrier_semaphore()
    count = 0
    if row_line:
        for step in range(1, LINE):
            pl.semaphore_signal(
                barrier, inc=1, device_id={"row": lax.rem(r + step, LINE)}, device_id_type=MESH
            )
        count += LINE - 1
    if plane == "all":
        for step in range(1, PLANE):
            pl.semaphore_signal(
                barrier, inc=1, device_id={"head": lax.rem(h + step, PLANE)}, device_id_type=MESH
            )
        count += PLANE - 1
    if plane == "near":
        for target in (sibling_of(h), across_of(h), along_of(h)):
            pl.semaphore_signal(barrier, inc=1, device_id={"head": target}, device_id_type=MESH)
        count += 3
    pl.semaphore_wait(barrier, count)


class Bring:
    def __init__(self, sources, places, semaphores):
        self.copies = [
            pltpu.make_async_copy(src, dst, semaphores.at[k])
            for k, (src, dst) in enumerate(zip(sources, places))
        ]

    def start(self):
        for copy in self.copies:
            copy.start()

    def wait(self, *which):
        for k in which:
            self.copies[k].wait()


def held(*arrays):
    return [pltpu.VMEM(item.shape, item.dtype) for item in arrays] + [
        pltpu.SemaphoreType.DMA((len(arrays),))
    ]


class LineGather:
    semaphores = (
        pltpu.SemaphoreType.DMA((LINE,)),
        pltpu.SemaphoreType.DMA((LINE,)),
        pltpu.SemaphoreType.DMA((2,)),
    )

    def __init__(self, source, slot, sent, arrived, other):
        self.r = lax.axis_index("row")
        self.source, self.slot = source, slot
        self.sent, self.arrived, self.other = sent, arrived, other

    def own(self, t):
        return send_to(
            self.source, self.slot(self.r), self.sent.at[t], self.arrived.at[self.r], "row", t
        )

    def handed(self, origin, target):
        return send_to(
            self.slot(origin), self.slot(origin), self.other.at[0], self.arrived.at[origin],
            "row", target,
        )

    def local(self):
        return pltpu.make_async_copy(self.source, self.slot(self.r), self.other.at[1])

    def start(self):
        for gap in (2, -2, 1, -1):
            t = self.r + gap

            @pl.when((t >= 0) & (t < LINE))
            def _(t=t):
                self.own(t).start()

        self.local().start()

    def forward(self):
        for me, origin, target in ((2, 0, 3), (1, 3, 0)):

            @pl.when(self.r == me)
            def _(origin=origin, target=target):
                copy = self.handed(origin, target)
                copy.wait_recv()
                copy.start()

    def finish(self):
        r = self.r
        for t in range(LINE):
            known = (r == t) | ((r == 2) & (t == 0)) | ((r == 1) & (t == 3))
            near = (r != t) & (r - t < 3) & (t - r < 3)

            @pl.when(jnp.logical_not(known))
            def _(t=t):
                self.handed(t, t).wait_recv()

            @pl.when(near)
            def _(t=t):
                self.own(t).wait_send()

        for me, origin, target in ((2, 0, 3), (1, 3, 0)):

            @pl.when(r == me)
            def _(origin=origin, target=target):
                self.handed(origin, target).wait_send()

        self.local().wait()


class LineReduce:
    semaphores = (
        pltpu.SemaphoreType.DMA((LINE,)),
        pltpu.SemaphoreType.DMA((LINE,)),
        pltpu.SemaphoreType.DMA((2,)),
    )

    @staticmethod
    def buffers(rows, width):
        return [
            pltpu.VMEM((LINE, rows, width), jnp.bfloat16),
            pltpu.VMEM((rows, width), jnp.bfloat16),
        ]

    def __init__(self, source, parts, landed, passed, sent, arrived, other):
        self.r = lax.axis_index("row")
        self.source, self.parts, self.landed, self.passed = source, parts, landed, passed
        self.sent, self.arrived, self.other = sent, arrived, other

    def to_pass(self, me, origin, via):
        return send_to(
            self.source.at[origin], self.passed, self.sent.at[origin], self.other.at[0], "row", via
        )

    def direct(self, t):
        return send_to(
            self.source.at[t], self.landed.at[self.r], self.sent.at[t], self.arrived.at[self.r],
            "row", t,
        )

    def added(self, t):
        return send_to(
            self.passed, self.landed.at[self.r], self.sent.at[t], self.arrived.at[self.r], "row", t
        )

    def plain(self, t):
        r = self.r
        ends = ((r == 0) & (t == 3)) | ((r == 3) & (t == 0))
        added = ((r == 1) & (t == 3)) | ((r == 2) & (t == 0))
        return jnp.logical_not(ends | added | (r == t))

    def start(self):
        for me, end, via in ((0, 3, 1), (3, 0, 2)):

            @pl.when(self.r == me)
            def _(me=me, end=end, via=via):
                self.to_pass(me, end, via).start()

        for gap in (2, -2, 1, -1):
            t = self.r + gap

            @pl.when((t >= 0) & (t < LINE) & self.plain(t))
            def _(t=t):
                self.direct(t).start()

    def forward(self):
        for me, end in ((1, 3), (2, 0)):

            @pl.when(self.r == me)
            def _(me=me, end=end):
                self.to_pass(me, end, end).wait_recv()
                rows = self.passed.shape[0]
                step = 32

                def add(i, unused):
                    at = pl.ds(pl.multiple_of(i * step, step), step)
                    self.passed[at, :] = (
                        self.parts[end, at, :].astype(jnp.float32)
                        + self.passed[at, :].astype(jnp.float32)
                    ).astype(jnp.bfloat16)
                    return unused

                lax.fori_loop(0, rows // step, add, 0)
                self.added(end).start()

    def finish(self, write):
        r = self.r
        for t in range(LINE):

            @pl.when(jnp.logical_not(unsent_to(r, t)))
            def _(t=t):
                send_to(
                    self.source.at[t], self.landed.at[t], self.sent.at[t], self.arrived.at[t],
                    "row", t,
                ).wait_recv()

        def total_of(sources):
            step = 32

            def add(i, unused):
                at = pl.ds(pl.multiple_of(i * step, step), step)
                total = self.parts[r, at, :].astype(jnp.float32)
                for t in sources:
                    total = total + self.landed[t, at, :].astype(jnp.float32)
                write(at, total)
                return unused

            lax.fori_loop(0, self.passed.shape[0] // step, add, 0)

        at_end = (r == 0) | (r == 3)

        @pl.when(at_end)
        def _():
            total_of((1, 2))

        @pl.when(jnp.logical_not(at_end))
        def _():
            total_of((0, 3, 3 - r))

        for me, end, via in ((0, 3, 1), (3, 0, 2)):

            @pl.when(r == me)
            def _(me=me, end=end, via=via):
                self.to_pass(me, end, via).wait_send()

        for t in range(LINE):

            @pl.when(jnp.logical_not(unsent_to(r, t)))
            def _(t=t):
                self.direct(t).wait_send()


def unsent_to(r, t):
    return ((r == 0) & (t == 3)) | ((r == 3) & (t == 0)) | (r == t)


class PlaneGather:
    semaphores = (
        pltpu.SemaphoreType.DMA((PIECES, 7)),
        pltpu.SemaphoreType.DMA((PIECES, 7)),
        pltpu.SemaphoreType.DMA((PIECES,)),
    )
    first = tuple(range(PIECES // 2))
    second = tuple(range(PIECES // 2, PIECES))

    def __init__(self, block, full, sent, arrived, other, source=None, target=None):
        h = lax.axis_index("head")
        self.source, self.target = source, target
        self.h, self.side, self.x, self.y = h, sibling_of(h), across_of(h), along_of(h)
        self.far = across_of(self.y)
        self.block, self.full = block, full
        self.sent, self.arrived, self.other = sent, arrived, other
        self.rows = block.shape[0] // PIECES

    def piece(self, owner, c):
        rows = pl.ds(c * self.rows, self.rows)
        if self.target is None:
            return self.full.at[owner, rows]
        return self.full.at[owner, rows, self.target]

    def mine(self, c):
        rows = pl.ds(c * self.rows, self.rows)
        return self.block.at[rows] if self.source is None else self.block.at[rows, self.source]

    def own(self, c, lane, target):
        return send_to(
            self.mine(c), self.piece(self.h, c),
            self.sent.at[c, lane], self.arrived.at[c, lane], "head", target,
        )

    def hand(self, owner, c, lane, target):
        return send_to(
            self.piece(owner, c), self.piece(owner, c), self.sent.at[c, lane],
            self.arrived.at[c, lane], "head", target,
        )

    def local(self, c):
        return pltpu.make_async_copy(self.mine(c), self.piece(self.h, c), self.other.at[c])

    def start(self):
        for a, b in zip(self.first, self.second):
            self.own(a, 1, self.x).start()
            self.own(b, 2, self.y).start()
        for a, b in zip(self.first, self.second):
            self.own(b, 1, self.x).start()
            self.own(a, 2, self.y).start()
        for c in range(PIECES):
            self.own(c, 0, self.side).start()
            self.local(c).start()

    def relay(self, place):
        a, b = self.first[place], self.second[place]
        self.hand(self.x, a, 1, self.x).wait_recv()
        self.hand(self.x, a, 3, self.y).start()
        self.hand(self.x, a, 4, self.side).start()
        self.hand(self.y, b, 2, self.y).wait_recv()
        self.hand(self.y, b, 3, self.x).start()
        self.hand(self.y, b, 5, self.side).start()

    def rest(self):
        for a, b in zip(self.first, self.second):
            self.hand(self.x, b, 1, self.x).wait_recv()
            self.hand(self.x, b, 4, self.side).start()
            self.hand(self.y, a, 2, self.y).wait_recv()
            self.hand(self.y, a, 5, self.side).start()

    def beside(self):
        for c in range(PIECES):
            self.hand(self.side, c, 0, self.side).wait_recv()

    def far_side(self):
        for pair in zip(self.first, self.second):
            for c in pair:
                self.hand(self.far, c, 3, self.side).wait_recv()
                self.hand(self.far, c, 6, self.side).start()

    def end(self, beside=True):
        side = self.side
        if beside:
            self.beside()
        for c in range(PIECES):
            for owner, lane in (
                (across_of(side), 4), (along_of(side), 5), (across_of(along_of(side)), 6)
            ):
                self.hand(owner, c, lane, side).wait_recv()
        for c in range(PIECES):
            for lane in range(7):
                self.own(c, lane, side).wait_send()
            self.local(c).wait()


class PlaneReduce:
    semaphores = (
        pltpu.SemaphoreType.DMA((4,)),
        pltpu.SemaphoreType.DMA((4,)),
        pltpu.SemaphoreType.DMA((4, 2)),
        pltpu.SemaphoreType.DMA((2, 2)),
        pltpu.SemaphoreType.DMA((2,)),
    )

    @staticmethod
    def buffers(rows, width):
        return [
            pltpu.VMEM((4, rows, width), jnp.bfloat16),
            pltpu.VMEM((4, rows, width), jnp.bfloat16),
            pltpu.VMEM((4, rows, width), jnp.bfloat16),
            pltpu.VMEM((2, rows // 2, width), jnp.bfloat16),
            pltpu.VMEM((2, rows, width), jnp.bfloat16),
        ]

    def __init__(
        self, staged, beside, mine, relayed, landed,
        side_sent, side_arrived, sent, arrived, relay_arrived,
    ):
        h = lax.axis_index("head")
        self.h, self.core, self.chip = h, lax.rem(h, 2), lax.div(h, 2)
        self.staged, self.beside, self.mine = staged, beside, mine
        self.relayed, self.landed = relayed, landed
        self.side_sent, self.side_arrived = side_sent, side_arrived
        self.sent, self.arrived, self.relay_arrived = sent, arrived, relay_arrived
        self.half = mine.shape[1] // 2

    def aside(self, chip):
        return send_to(
            self.staged.at[chip], self.beside.at[chip], self.side_sent.at[chip],
            self.side_arrived.at[chip], "head", sibling_of(self.h),
        )

    def relation(self, chip):
        flip_x = lax.rem(chip + self.chip, 2)
        flip_y = lax.rem(lax.div(chip, 2) + lax.div(self.chip, 2), 2)
        return flip_x + 2 * flip_y

    def part(self, half):
        return pl.ds(half * self.half, self.half)

    def home(self, chip, way, half):
        return send_to(
            self.mine.at[chip, self.part(half)], self.landed.at[way, self.part(half)],
            self.sent.at[chip, half], self.arrived.at[way, half], "head",
            (across_of, along_of)[way](self.h),
        )

    def opposite(self, chip, half):
        return send_to(
            self.mine.at[chip, self.part(half)], self.relayed.at[half], self.sent.at[chip, half],
            self.relay_arrived.at[half], "head", (along_of, across_of)[half](self.h),
        )

    def put(self, block, value):
        chip, core = lax.div(block, 2), lax.rem(block, 2)

        @pl.when(core == self.core)
        def _():
            self.mine[chip] = value

        @pl.when(core != self.core)
        def _():
            self.staged[chip] = value
            self.aside(chip).start()

    def pass_on(self, block):
        chip, core = lax.div(block, 2), lax.rem(block, 2)

        @pl.when(core == self.core)
        def _():
            self.aside(chip).wait_recv()
            step = 32

            def add(i, unused):
                at = pl.ds(pl.multiple_of(i * step, step), step)
                self.mine[chip, at, :] = (
                    self.mine[chip, at, :].astype(jnp.float32)
                    + self.beside[chip, at, :].astype(jnp.float32)
                ).astype(jnp.bfloat16)
                return unused

            lax.fori_loop(0, 2 * self.half // step, add, 0)
            relation = self.relation(chip)

            @pl.when(relation == 1)
            def _():
                self.home(chip, 0, 1).start()

            @pl.when(relation == 2)
            def _():
                self.home(chip, 1, 0).start()

            @pl.when(relation == 3)
            def _():
                self.opposite(chip, 0).start()
                self.opposite(chip, 1).start()

    def relay(self, block):
        chip, core = lax.div(block, 2), lax.rem(block, 2)
        for way in (0, 1):

            @pl.when((core == self.core) & (self.relation(chip) == way + 1))
            def _(way=way):
                self.opposite(chip, way).wait_recv()
                step = 32

                def add(i, unused):
                    at = pl.ds(pl.multiple_of(i * step, step), step)
                    here = pl.ds(pl.multiple_of(way * self.half + i * step, step), step)
                    self.mine[chip, here, :] = (
                        self.mine[chip, here, :].astype(jnp.float32)
                        + self.relayed[way, at, :].astype(jnp.float32)
                    ).astype(jnp.bfloat16)
                    return unused

                lax.fori_loop(0, self.half // step, add, 0)
                self.home(chip, way, way).start()

    def arrive(self):
        for way in (0, 1):
            for half in (0, 1):
                self.home(self.chip, way, half).wait_recv()

    def total(self, at):
        value = self.mine[self.chip, at, :].astype(jnp.float32)
        return (
            value
            + self.landed[0, at, :].astype(jnp.float32)
            + self.landed[1, at, :].astype(jnp.float32)
        )

    def finish(self):
        for chip in range(4):
            self.aside(chip).wait_send()

            @pl.when(chip != self.chip)
            def _(chip=chip):
                self.home(chip, 0, 0).wait_send()
                self.home(chip, 0, 1).wait_send()


def norm_apply(rows, gain):
    return rows * lax.rsqrt(jnp.mean(rows * rows, axis=-1, keepdims=True) + EPSILON) * gain


def gather(values, axis_name, axis):
    return lax.all_gather(values, axis_name, axis=axis, tiled=True)


def scatter(values, axis_name, axis):
    return lax.psum_scatter(values, axis_name, scatter_dimension=axis, tiled=True)

def once(shape):
    return pl.BlockSpec(
        shape, lambda i: (0,) * len(shape), pipeline_mode=pl.Buffered(buffer_count=1)
    )


def norm_rows(rows, gain):
    return rows * lax.rsqrt(jnp.mean(rows * rows, axis=-1, keepdims=True) + EPSILON) * gain


def lay_out_params(
    taps_ref, rows_ref, gates_ref, resets_ref,
    taps_out, vec_out, wr_out, we_out, keep_out, square, moved,
):
    used, width = rows_ref.shape[1], gates_ref.shape[2]
    columns = vec_out.shape[1]
    taps_out[...] = jnp.zeros_like(taps_out)
    taps_out[:, 0:used] = taps_ref[...]
    vec_out[...] = jnp.zeros_like(vec_out)
    vec_out[3:4, :] = jnp.full((1, columns), 2.0, jnp.float32)
    vec_out[0:4, 0:used] = rows_ref[...]
    decay = vec_out[3:4, :]
    vec_out[3:4, :] = -8.0 * jnp.log1p(jnp.exp(-decay))
    vec_out[4:5, :] = 8.0 * jax.nn.sigmoid(-decay)
    for k, out in enumerate((wr_out, we_out)):
        square[...] = jnp.zeros_like(square)
        square[0:width, 0:width] = gates_ref[k, 1].astype(jnp.float32)
        moved[...] = pltpu.roll(pltpu.roll(square[...], width, 0), width, 1)
        square[...] = jnp.zeros_like(square)
        square[0:width, 0:width] = gates_ref[k, 0].astype(jnp.float32)
        out[...] = (square[...] + moved[...]).astype(jnp.bfloat16)
    resets = resets_ref[...]
    first = lax.broadcasted_iota(jnp.int32, resets.shape, 1) == 0
    one = jnp.where(first | (resets > 0), 0.0, 1.0)
    length = resets.shape[1]
    two = one * pltpu.roll(one, 1, 1)
    three = two * pltpu.roll(one, 2, 1)
    ahead = [pltpu.roll(item, length - k, 1) for k, item in ((1, one), (2, two), (3, three))]
    rows = jnp.concatenate(
        [one, one, two, three, *ahead, one, jnp.zeros((120, length), jnp.float32)], axis=0
    )
    for k in range(length // 128):
        turned = rows[:, k * 128 : (k + 1) * 128].T
        keep_out[k * 128 : (k + 1) * 128, :] = turned[:, 0:8]


def open_body(
    x_ref, mix_ref, ffn_ref, cot, xt_ref, yt_ref, ot_ref,
    taps_ref, rows_ref, gates_ref, resets_ref,
    full, cot_out, xy_full, out_full, mix_out, ffn_out, taps_out, vec_out, wr_out, we_out, keep_out,
    shards, blank, square, moved,
    normed, column, spread, gain_sent, gain_arrived, wide_sent, wide_arrived, wiped, *semaphores,
):
    r, h = lax.axis_index("row"), lax.axis_index("head")
    held_rows, share = shards.shape[1:]
    used, chans = xt_ref.shape[0], out_full.shape[0]

    def slot(full, first):
        def at(origin):
            lanes = pl.ds(pl.multiple_of(origin * share, share), share)
            return full.at[pl.ds(first, held_rows), lanes]

        return at

    lines = [
        LineGather(shards.at[k], slot(dst, first), *semaphores[3 * k : 3 * k + 3])
        for k, (dst, first) in enumerate(((xy_full, 0), (xy_full, chans), (out_full, 0)))
    ]
    wipes = [
        pltpu.make_async_copy(
            blank, dst.at[pl.ds(first + held_rows, chans - held_rows)], wiped.at[k]
        )
        for k, (dst, first) in enumerate(((xy_full, 0), (xy_full, chans), (out_full, 0)))
    ]
    plane = PlaneGather(normed, full, *semaphores[9:12])
    cot_plane = PlaneGather(
        cot, cot_out, *semaphores[12:15], source=pl.ds(0, cot_out.shape[2])
    )
    for k, source in enumerate((xt_ref, yt_ref, ot_ref)):
        shards[k, held_rows - 16 :, :] = jnp.zeros((16, share), jnp.bfloat16)
        shards[k, 0:used, :] = source[...]
    gain_share = mix_ref.shape[1]
    low = lax.broadcasted_iota(jnp.int32, (8, 2 * gain_share), 1) < gain_share
    column[r] = jnp.zeros_like(column[r])
    column[r, 0:1, 0:gain_share] = mix_ref[...].astype(jnp.float32)
    column[r, 1:2, 0:gain_share] = ffn_ref[...].astype(jnp.float32)
    rows = column[r]
    column[r] = jnp.where(low, rows, pltpu.roll(pltpu.roll(rows, gain_share, 1), 7, 0))
    meet(True, "all")

    def up_line(t):
        return send_to(
            column.at[r], column.at[r], gain_sent.at[t], gain_arrived.at[r], "row", t
        )

    def from_line(t):
        return send_to(
            column.at[t], column.at[t], gain_sent.at[t], gain_arrived.at[t], "row", t
        )

    def over_plane(step, owner):
        return send_to(
            column, spread.at[owner], wide_sent.at[step], wide_arrived.at[owner], "head",
            lax.rem(h + step, PLANE),
        )

    for step in range(1, LINE):
        up_line(lax.rem(r + step, LINE)).start()
    for line in lines:
        line.start()
    blank[...] = jnp.zeros_like(blank)
    for wipe in wipes:
        wipe.start()
    for step in range(1, LINE):
        from_line(lax.rem(r + step, LINE)).wait_recv()
    for step in range(1, PLANE):
        over_plane(step, h).start()
    cot_plane.start()
    spread[h] = column[...]
    for step in range(1, PLANE):
        over_plane(step, lax.rem(h + step, PLANE)).wait_recv()

    low = lax.broadcasted_iota(jnp.int32, (1, 2 * gain_share), 1) < gain_share
    for line_place in range(LINE):
        for pair in range(PLANE // 2):
            even = spread[2 * pair, line_place][0:1, :]
            odd = spread[2 * pair + 1, line_place][0:1, :]
            at = (line_place * (PLANE // 2) + pair) * 2 * gain_share
            end = at + 2 * gain_share
            mix_out[0:1, at:end] = jnp.where(low, even, pltpu.roll(odd, gain_share, 1))
            ffn_out[0:1, at:end] = jnp.where(low, pltpu.roll(even, gain_share, 1), odd)

    def make(i, unused):
        at = pl.ds(pl.multiple_of(i * CHUNK, CHUNK), CHUNK)
        normed[at, :] = norm_rows(x_ref[at, :].astype(jnp.float32), mix_out[...]).astype(
            jnp.bfloat16
        )
        return unused

    lax.fori_loop(0, x_ref.shape[0] // CHUNK, make, 0, unroll=UNROLL)
    plane.start()
    lay_out_params(
        taps_ref, rows_ref, gates_ref, resets_ref,
        taps_out, vec_out, wr_out, we_out, keep_out, square, moved,
    )
    cot_plane.relay(0)
    cot_plane.relay(1)
    lines[0].forward()
    cot_plane.rest()
    plane.relay(0)
    plane.relay(1)
    lines[1].forward()
    cot_plane.far_side()
    cot_plane.end()
    plane.rest()
    plane.far_side()
    plane.end()
    lines[2].forward()
    for line in lines:
        line.finish()
    for wipe in wipes:
        wipe.wait()
    for step in range(1, LINE):
        up_line(lax.rem(r + step, LINE)).wait_send()
    for step in range(1, PLANE):
        over_plane(step, h).wait_send()


def open_block(layer_in, gains, cot, weights, params):
    rows, width = layer_in.shape
    used, share = weights[0].shape
    chans, held_rows = -(-used // 128) * 128, -(-used // 16) * 16
    length = params[-1].shape[1]
    tile = (8, 2 * gains[0].shape[1])
    return pl.pallas_call(
        open_body,
        in_specs=[IN_VMEM, IN_VMEM, IN_VMEM, ANYWHERE] + [IN_VMEM] * 7,
        out_specs=[ANYWHERE] * 4 + [IN_VMEM] * 7,
        out_shape=[
            jax.ShapeDtypeStruct((PLANE, rows, width), jnp.bfloat16),
            jax.ShapeDtypeStruct((PLANE, rows, width // 2), jnp.bfloat16),
            jax.ShapeDtypeStruct((2 * chans, width), jnp.bfloat16),
            jax.ShapeDtypeStruct((chans, width), jnp.bfloat16),
            jax.ShapeDtypeStruct((1, width), jnp.float32),
            jax.ShapeDtypeStruct((1, width), jnp.float32),
            jax.ShapeDtypeStruct((4, chans), jnp.float32),
            jax.ShapeDtypeStruct((8, chans), jnp.float32),
            jax.ShapeDtypeStruct((chans, chans), jnp.bfloat16),
            jax.ShapeDtypeStruct((chans, chans), jnp.bfloat16),
            jax.ShapeDtypeStruct((length, 8), jnp.float32),
        ],
        scratch_shapes=[
            pltpu.VMEM((3, held_rows, share), jnp.bfloat16),
            pltpu.VMEM((chans - held_rows, width), jnp.bfloat16),
            pltpu.VMEM((chans, chans), jnp.float32),
            pltpu.VMEM((chans, chans), jnp.float32),
            pltpu.VMEM((rows, width), jnp.bfloat16),
            pltpu.VMEM((LINE,) + tile, jnp.float32),
            pltpu.VMEM((PLANE, LINE) + tile, jnp.float32),
            pltpu.SemaphoreType.DMA((LINE,)),
            pltpu.SemaphoreType.DMA((LINE,)),
            pltpu.SemaphoreType.DMA((PLANE,)),
            pltpu.SemaphoreType.DMA((PLANE,)),
            pltpu.SemaphoreType.DMA((3,)),
            *(LineGather.semaphores * 3),
            *(PlaneGather.semaphores * 2),
        ],
        compiler_params=pltpu.CompilerParams(
            collective_id=0, has_side_effects=True, vmem_limit_bytes=61 * 2**20
        ),
        name="open_block",
    )(layer_in, *gains, cot, *weights, *params)


def forward_linked_body(
    normed_ref, xy_hbm, ow_hbm, taps_ref, vec_ref, wr_ref, we_ref, keep_ref,
    x_hbm, gain_ref, gate_shard, up_shard,
    u_ref, by_ref, before_ref, states_ref, mixed_ref, residual_ref, two_ref, gate_out, up_out,
    xy_ref, ow_ref, x_ref, brought,
    window, conv, conv_low, rate, entry, carry, *links,
):
    step = pl.program_id(0)
    plane = PlaneReduce(*links[:10])
    gate_line = LineGather(gate_shard, lambda t: gate_out.at[t], *links[10:13])
    first_rows = up_shard.at[pl.ds(0, up_out.shape[1])]
    up_line = LineGather(first_rows, lambda t: up_out.at[t], *links[13:16])

    bring = Bring((xy_hbm, ow_hbm, x_hbm), (xy_ref, ow_ref, x_ref), brought)

    @pl.when(step == 0)
    def _():
        bring.start()
        meet(True, "near")
        gate_line.start()
        up_line.start()
        bring.wait(0, 1, 2)

    @pl.when(step > 0)
    def _():
        plane.pass_on(step - 1)

    @pl.when(step > 2)
    def _():
        plane.relay(step - 3)

    forward_step(
        normed_ref, xy_ref, taps_ref, vec_ref, wr_ref, we_ref, keep_ref,
        u_ref, by_ref, before_ref, states_ref, mixed_ref,
        window, conv, conv_low, rate, entry, carry,
    )
    plane.put(step, dot_plain(mixed_ref[...], ow_ref[...]).astype(jnp.bfloat16))

    @pl.when(step == 6)
    def _():
        gate_line.forward()

    @pl.when(step == PLANE - 1)
    def _():
        plane.relay(step - 2)
        plane.pass_on(step)
        plane.relay(step - 1)
        plane.relay(step)
        up_line.forward()
        plane.arrive()

        def make(i, unused):
            at = pl.ds(pl.multiple_of(i * CHUNK, CHUNK), CHUNK)
            residual = x_ref[at, :].astype(jnp.float32) + plane.total(at)
            residual_ref[at, :] = residual
            two_ref[at, :] = norm_rows(residual, gain_ref[...]).astype(jnp.bfloat16)
            return unused

        lax.fori_loop(0, x_ref.shape[0] // CHUNK, make, 0, unroll=UNROLL)
        plane.finish()
        gate_line.finish()
        up_line.finish()


def forward_linked(normed, xy, ow, taps, vec, wr, we, keep, layer_in, gain, gate_shard, up_shard):
    length, width = normed.shape
    chans = ow.shape[0]
    rows = length // PLANE
    share, units = up_shard.shape
    tile = lambda columns: pl.BlockSpec((rows, columns), lambda i: (i, 0))
    return pl.pallas_call(
        forward_linked_body,
        grid=(PLANE,),
        in_specs=[
            tile(width), ANYWHERE, ANYWHERE, once(taps.shape),
            once(vec.shape), once(wr.shape), once(we.shape), tile(keep.shape[1]),
            ANYWHERE, once(gain.shape), ANYWHERE, ANYWHERE,
        ],
        out_specs=[tile(chans)] * 5 + [once((rows, width))] * 2 + [ANYWHERE] * 2,
        out_shape=[
            jax.ShapeDtypeStruct((length, chans), jnp.bfloat16),
            jax.ShapeDtypeStruct((length, chans), jnp.float32),
            jax.ShapeDtypeStruct((length, chans), jnp.float32),
            jax.ShapeDtypeStruct((length, chans), jnp.bfloat16),
            jax.ShapeDtypeStruct((length, chans), jnp.bfloat16),
            jax.ShapeDtypeStruct((rows, width), jnp.float32),
            jax.ShapeDtypeStruct((rows, width), jnp.bfloat16),
            jax.ShapeDtypeStruct((LINE,) + gate_shard.shape, jnp.bfloat16),
            jax.ShapeDtypeStruct((LINE, share // 2, units), jnp.bfloat16),
        ],
        scratch_shapes=[
            *held(xy, ow, layer_in),
            pltpu.VMEM((rows + 8, chans), jnp.float32),
            pltpu.VMEM((rows, chans), jnp.float32),
            pltpu.VMEM((rows, chans), jnp.bfloat16),
            pltpu.VMEM((rows, chans), jnp.float32),
            pltpu.VMEM((rows, chans), jnp.float32),
            pltpu.VMEM((8, chans), jnp.float32),
            *PlaneReduce.buffers(rows, width),
            *PlaneReduce.semaphores,
            *(LineGather.semaphores * 2),
        ],
        compiler_params=pltpu.CompilerParams(
            collective_id=1, has_side_effects=True, vmem_limit_bytes=61 * 2**20
        ),
        name="mixer_forward_linked",
    )(normed, xy, ow, taps, vec, wr, we, keep, layer_in, gain, gate_shard, up_shard)


def ffn_up_body(
    own_two, gate_ref, own_cot, cot_half, up_half, up_shard, down_shard,
    two_out, cot_out, up_out, down_out, gates_out, ups_out, hidden_out, down_parts,
    two, cot, up, gates, ups, hidden, total, copied, brought, *semaphores,
):
    h = lax.axis_index("head")
    rows = own_two.shape[0]
    units = gates.shape[1]
    width, share = own_two.shape[1], up_shard.shape[0]
    half = share // 2
    late_columns = pl.ds(width // 2, width // 2)
    up_line = LineGather(
        up_shard.at[pl.ds(half, half)],
        lambda t: up.at[pl.ds(pl.multiple_of(t * share + half, half), half)],
        *semaphores[0:3],
    )
    down_line = LineGather(down_shard, lambda t: down_out.at[t], *semaphores[3:6])
    two_plane = PlaneGather(own_two, two, *semaphores[6:9])
    cot_plane = PlaneGather(
        own_cot, cot, *semaphores[9:12], source=late_columns, target=late_columns
    )
    inward = [
        pltpu.make_async_copy(up_half.at[t], up.at[pl.ds(t * share, half)], brought.at[t])
        for t in range(LINE)
    ]
    inward.append(
        pltpu.make_async_copy(cot_half, cot.at[:, :, pl.ds(0, width // 2)], brought.at[LINE])
    )
    outward = [
        pltpu.make_async_copy(src, dst, copied.at[k])
        for k, (src, dst) in enumerate(
            (
                (two, two_out), (cot, cot_out), (up, up_out), (gates, gates_out),
                (ups, ups_out), (hidden, hidden_out),
            )
        )
    ]
    meet(True, "near")
    up_line.start()
    down_line.start()
    two_plane.start()
    for copy in inward:
        copy.start()

    def at_block(block):
        return pl.ds(pl.multiple_of(block * rows, rows), rows)

    def make_gates(block):
        gates[at_block(block), :] = dot_plain(two[block], gate_ref[...])

    gates[at_block(h), :] = dot_plain(own_two[...], gate_ref[...])
    two_plane.relay(0)
    two_plane.beside()
    make_gates(two_plane.side)
    two_plane.relay(1)
    cot_plane.start()
    two_plane.rest()
    make_gates(two_plane.x)
    make_gates(two_plane.y)
    up_line.forward()
    two_plane.far_side()
    make_gates(two_plane.far)
    two_plane.end(beside=False)
    outward[0].start()
    cot_plane.relay(0)
    make_gates(across_of(two_plane.side))
    make_gates(along_of(two_plane.side))
    cot_plane.relay(1)
    make_gates(across_of(along_of(two_plane.side)))
    outward[3].start()
    up_line.finish()
    for copy in inward:
        copy.wait()
    outward[2].start()

    def make_hidden(block, unused):
        at = at_block(block)
        ups[at, :] = dot_plain(two[block], up[...])

        def make(i, unused):
            here = pl.ds(pl.multiple_of(block * rows + i * CHUNK, CHUNK), CHUNK)
            hidden[here, :] = (gelu_only(gates[here, :]) * ups[here, :]).astype(jnp.bfloat16)
            return unused

        lax.fori_loop(0, rows // CHUNK, make, 0, unroll=UNROLL)
        return unused

    lax.fori_loop(0, 2, make_hidden, 0)
    cot_plane.rest()
    lax.fori_loop(2, 5, make_hidden, 0)
    cot_plane.far_side()
    down_line.forward()
    lax.fori_loop(5, PLANE, make_hidden, 0)
    outward[4].start()
    outward[5].start()
    cot_plane.end()
    outward[1].start()
    total[...] = contract_first(cot[0], hidden[0:rows, :])

    def add_down(block, unused):
        total[...] += contract_first(cot[block], hidden[at_block(block), :])
        return unused

    lax.fori_loop(1, PLANE, add_down, 0)
    to_parts(total, down_parts)
    down_line.finish()
    for copy in outward:
        copy.wait()


def ffn_up(own_two, gate, own_cot, cot_half, up_half, up_shard, down_shard):
    rows, width = own_two.shape
    share, units = up_shard.shape
    length = rows * PLANE
    group = jax.ShapeDtypeStruct((PLANE, rows, width), jnp.bfloat16)
    weight = jax.ShapeDtypeStruct((LINE, share, units), jnp.bfloat16)
    return pl.pallas_call(
        ffn_up_body,
        in_specs=[IN_VMEM, IN_VMEM] + [ANYWHERE] * 5,
        out_specs=[ANYWHERE] * 7 + [IN_VMEM],
        out_shape=[
            group,
            group,
            jax.ShapeDtypeStruct((width, units), jnp.bfloat16),
            weight,
            jax.ShapeDtypeStruct((length, units), jnp.float32),
            jax.ShapeDtypeStruct((length, units), jnp.float32),
            jax.ShapeDtypeStruct((length, units), jnp.bfloat16),
            weight,
        ],
        scratch_shapes=[
            pltpu.VMEM((PLANE, rows, width), jnp.bfloat16),
            pltpu.VMEM((PLANE, rows, width), jnp.bfloat16),
            pltpu.VMEM((width, units), jnp.bfloat16),
            pltpu.VMEM((length, units), jnp.float32),
            pltpu.VMEM((length, units), jnp.float32),
            pltpu.VMEM((length, units), jnp.bfloat16),
            pltpu.VMEM((width, units), jnp.float32),
            pltpu.SemaphoreType.DMA((6,)),
            pltpu.SemaphoreType.DMA((LINE + 1,)),
            *(LineGather.semaphores * 2),
            *(PlaneGather.semaphores * 2),
        ],
        compiler_params=pltpu.CompilerParams(
            collective_id=2, has_side_effects=True, vmem_limit_bytes=61 * 2**20
        ),
        name="ffn_up",
    )(own_two, gate, own_cot, cot_half, up_half, up_shard, down_shard)
def far_first(step):
    chip = lax.div(lax.axis_index("head"), 2)
    place = lax.div(step, 2)
    x = lax.rem(lax.rem(chip, 2) + 1 - lax.div(place, 2), 2)
    y = lax.rem(lax.div(chip, 2) + 1 + lax.rem(place, 2), 2)
    return 2 * (2 * y + x) + lax.rem(step, 2)


def norm_back(rows, gain, incoming):
    scale = lax.rsqrt(jnp.mean(rows * rows, axis=-1, keepdims=True) + EPSILON)
    scaled = incoming * gain
    inner = jnp.mean(scaled * rows, axis=-1, keepdims=True)
    return scale * scaled - rows * (scale * scale * scale * inner), incoming * rows * scale


def to_parts(total, parts):
    rows = parts.shape[1]
    step = 64

    def move(i, unused):
        at = pl.ds(pl.multiple_of(i * step, step), step)
        for t in range(LINE):
            here = pl.ds(pl.multiple_of(t * rows + i * step, step), step)
            parts[t, at, :] = total[here, :].astype(jnp.bfloat16)
        return unused

    lax.fori_loop(0, rows // step, move, 0)


def to_turned_parts(total, parts, places):
    share = parts.shape[2]
    step = 32
    for first, target, count in places:

        def move(i, unused, first=first, target=target):
            here = pl.ds(pl.multiple_of(first + i * step, step), step)
            at = pl.ds(pl.multiple_of(target + i * step, step), step)
            for t in range(LINE):
                parts[t, at, :] = total[here, t * share : (t + 1) * share].astype(jnp.bfloat16)
            return unused

        lax.fori_loop(0, count // step, move, 0)


def ffn_back_body(
    cot_ref, two_ref, gates_ref, ups_ref, gate_hbm, up_hbm, down_hbm, parts_hbm,
    residual_hbm, own_cot_hbm, gain_ref,
    d_ups_ref, gate_parts, down_out, d_res_ref, d_low_ref, gain_out,
    gate_ref, up_ref, down_ref, parts, brought, late,
    total, d_gates, d_hidden, eight, *links,
):
    step = pl.program_id(0)
    line = LineReduce(parts_hbm, parts, *links[:5])
    plane = PlaneReduce(*links[5:])
    rows = cot_ref.shape[0]

    bring = Bring(
        (down_hbm, gate_hbm, up_hbm, parts_hbm), (down_ref, gate_ref, up_ref, parts), brought
    )
    into_outputs = Bring((residual_hbm, own_cot_hbm), (d_res_ref, d_low_ref), late)

    @pl.when(step == 0)
    def _():
        bring.start()
        meet(True, "near")
        line.start()
        into_outputs.start()
        bring.wait(0, 1, 2, 3)

    @pl.when((step > 2) & (step <= PLANE + 2))
    def _():
        plane.relay(far_first(step - 3))

    @pl.when(step < PLANE)
    def _():
        d_hidden[...] = dot_plain(cot_ref[...], down_ref[...])

        def make(i, unused):
            at = pl.ds(pl.multiple_of(i * CHUNK, CHUNK), CHUNK)
            gelu_gate, slope = gelu_both(gates_ref[at, :])
            through = d_hidden[at, :]
            d_gates[step, at, :] = (through * ups_ref[at, :] * slope).astype(jnp.bfloat16)
            d_ups_ref[at, :] = (through * gelu_gate).astype(jnp.bfloat16)
            return unused

        lax.fori_loop(0, rows // CHUNK, make, 0, unroll=UNROLL)

        @pl.when(step > 0)
        def _():
            plane.pass_on(far_first(step - 1))

        value = contract_last(d_gates[step], gate_ref[...]) + contract_last(
            d_ups_ref[...], up_ref[...]
        )
        plane.put(far_first(step), value.astype(jnp.bfloat16))

    @pl.when(step == PLANE)
    def _():
        total[...] = contract_first(two_ref[...], d_gates[0])

    @pl.when(step > PLANE)
    def _():
        total[...] += contract_first(two_ref[...], d_gates[step - PLANE])

    @pl.when(step == PLANE)
    def _():
        plane.pass_on(far_first(step - 1))

    @pl.when(step == 3)
    def _():
        line.forward()

    @pl.when(step == 2 * PLANE - 1)
    def _():
        to_parts(total, gate_parts)
        plane.arrive()
        into_outputs.wait(0, 1)
        eight[...] = jnp.zeros_like(eight)

        def back(i, unused):
            at = pl.ds(pl.multiple_of(i * CHUNK, CHUNK), CHUNK)
            d_rows, d_gain = norm_back(d_res_ref[at, :], gain_ref[...], plane.total(at))
            d_residual = d_low_ref[at, :].astype(jnp.float32) + d_rows
            d_res_ref[at, :] = d_residual
            d_low_ref[at, :] = d_residual.astype(jnp.bfloat16)
            eight[...] += sum_eight(d_gain)
            return unused

        lax.fori_loop(0, rows // CHUNK, back, 0, unroll=UNROLL)
        gain_out[...] = jnp.sum(eight[...], axis=0, keepdims=True)

        def write(at, value):
            down_out[at, :] = value

        line.finish(write)
        plane.finish()


def ffn_back(
    cot_group, two_group, gates, ups, gate, up, down, parts, residual, own_cot, gain
):
    length, width = cot_group.shape
    units = gate.shape[1]
    rows, share = length // PLANE, width // LINE
    tile = lambda columns: pl.BlockSpec(
        (rows, columns), lambda i: (far_first(jnp.minimum(i, PLANE - 1)), 0)
    )
    later = lambda columns: pl.BlockSpec(
        (rows, columns), lambda i: (far_first(jnp.maximum(i - PLANE, 0)), 0)
    )
    return pl.pallas_call(
        ffn_back_body,
        grid=(2 * PLANE,),
        in_specs=[
            tile(width), later(width), tile(units), tile(units),
            *([ANYWHERE] * 6), once(gain.shape),
        ],
        out_specs=[
            tile(units), once((LINE, share, units)), once((share, units)),
            once((rows, width)), once((rows, width)), once((1, width)),
        ],
        out_shape=[
            jax.ShapeDtypeStruct((length, units), jnp.bfloat16),
            jax.ShapeDtypeStruct((LINE, share, units), jnp.bfloat16),
            jax.ShapeDtypeStruct((share, units), jnp.float32),
            jax.ShapeDtypeStruct((rows, width), jnp.float32),
            jax.ShapeDtypeStruct((rows, width), jnp.bfloat16),
            jax.ShapeDtypeStruct((1, width), jnp.float32),
        ],
        scratch_shapes=[
            *held(gate, up, down, parts),
            pltpu.SemaphoreType.DMA((2,)),
            pltpu.VMEM((width, units), jnp.float32),
            pltpu.VMEM((PLANE, rows, units), jnp.bfloat16),
            pltpu.VMEM((rows, units), jnp.float32),
            pltpu.VMEM((8, width), jnp.float32),
            *LineReduce.buffers(share, units),
            *LineReduce.semaphores,
            *PlaneReduce.buffers(rows, width),
            *PlaneReduce.semaphores,
        ],
        compiler_params=pltpu.CompilerParams(
            collective_id=4, has_side_effects=True, vmem_limit_bytes=63 * 2**20
        ),
        name="ffn_back",
    )(cot_group, two_group, gates, ups, gate, up, down, parts, residual, own_cot, gain)


def turn_body(
    two_ref, d_ups_ref, parts_hbm, block, mixed_hbm, ow_hbm,
    up_parts, out_parts, gate_out, d_mixed_out,
    gate_parts, mixed_ref, ow_ref, brought,
    full, total, out_total, *links,
):
    step = pl.program_id(0)
    line = LineReduce(parts_hbm, gate_parts, *links[:5])
    plane = PlaneGather(block, full, *links[5:])
    rows = two_ref.shape[0]

    bring = Bring(
        (parts_hbm, mixed_hbm, ow_hbm), (gate_parts, mixed_ref, ow_ref), brought
    )

    @pl.when(step == 0)
    def _():
        bring.start()
        meet(True, "near")
        line.start()
        plane.start()
        total[...] = contract_first(two_ref[...], d_ups_ref[...])

    @pl.when(step > 0)
    def _():
        total[...] += contract_first(two_ref[...], d_ups_ref[...])

    @pl.when(step == 3)
    def _():
        plane.relay(0)

    @pl.when(step == PLANE - 2)
    def _():
        bring.wait(0)
        line.forward()
        plane.relay(1)

    @pl.when(step == PLANE - 1)
    def _():
        bring.wait(1, 2)

        def add(owner, start=False):
            at = pl.ds(pl.multiple_of(owner * rows, rows), rows)
            d_mixed_out[at, :] = contract_last(full[owner], ow_ref[...])
            value = contract_first(mixed_ref[at, :], full[owner])
            out_total[...] = value if start else out_total[...] + value

        plane.beside()
        add(plane.side, start=True)
        to_parts(total, up_parts)
        plane.rest()
        add(plane.x)
        add(plane.y)
        plane.far_side()
        add(plane.far)
        plane.end(beside=False)
        add(plane.h)
        add(across_of(plane.side))
        add(along_of(plane.side))
        add(across_of(along_of(plane.side)))
        kept = out_parts.shape[1]
        to_turned_parts(out_total, out_parts, ((0, 0, kept),))

        def write(at, value):
            gate_out[at, :] = value

        line.finish(write)


def turn(two_group, d_ups, gate_parts, block, mixed, ow, kept):
    length, width = two_group.shape
    units, chans = d_ups.shape[1], mixed.shape[1]
    rows, share = length // PLANE, width // LINE
    tile = lambda columns: pl.BlockSpec((rows, columns), lambda i: (i, 0))
    return pl.pallas_call(
        turn_body,
        grid=(PLANE,),
        in_specs=[
            tile(width), tile(units), ANYWHERE, ANYWHERE, ANYWHERE, ANYWHERE,
        ],
        out_specs=[
            once(gate_parts.shape), once((LINE, kept, share)), once((share, units)),
            once((length, chans)),
        ],
        out_shape=[
            jax.ShapeDtypeStruct(gate_parts.shape, jnp.bfloat16),
            jax.ShapeDtypeStruct((LINE, kept, share), jnp.bfloat16),
            jax.ShapeDtypeStruct((share, units), jnp.float32),
            jax.ShapeDtypeStruct((length, chans), jnp.float32),
        ],
        scratch_shapes=[
            *held(gate_parts, mixed, ow),
            pltpu.VMEM((PLANE, rows, width), jnp.bfloat16),
            pltpu.VMEM((width, units), jnp.float32),
            pltpu.VMEM((chans, width), jnp.float32),
            *LineReduce.buffers(share, units),
            *LineReduce.semaphores,
            *PlaneGather.semaphores,
        ],
        compiler_params=pltpu.CompilerParams(
            collective_id=5, has_side_effects=True, vmem_limit_bytes=61 * 2**20
        ),
        name="turn",
    )(two_group, d_ups, gate_parts, block, mixed, ow)


def pack_small(head_width, taps, vec, params, wr, we, small):
    columns = small.shape[1]
    step = 16
    last = (2 * head_width + 7) // 8 * 8

    def move(i, unused):
        at = pl.ds(pl.multiple_of(i * step, step), step)
        shape = (step, columns)
        row = lax.broadcasted_iota(jnp.int32, shape, 0) + i * step
        left = lax.broadcasted_iota(jnp.int32, shape, 1) < head_width
        rate, entry = wr[at, :], we[at, :]
        first = jnp.where(left, rate, pltpu.roll(entry, head_width, 1))
        second = jnp.where(left, pltpu.roll(rate, columns - head_width, 1), entry)
        small[at, :] = jnp.where(row < head_width, first, second).astype(jnp.bfloat16)
        return unused

    lax.fori_loop(0, last // step, move, 0)
    scaled = vec[0:4, :] * jnp.concatenate(
        [jnp.ones((3, columns), jnp.float32), params[4:5, :]], axis=0
    )
    tail = jnp.concatenate([taps[...], scaled], axis=0).astype(jnp.bfloat16)
    here = last // step * step
    rate, entry = wr[here : here + 8, :], we[here : here + 8, :]
    left = lax.broadcasted_iota(jnp.int32, (8, columns), 1) < head_width
    rest = jnp.where(left, pltpu.roll(rate, columns - head_width, 1), entry).astype(jnp.bfloat16)
    small[here : here + 16, :] = jnp.concatenate([rest, tail], axis=0)
    if small.shape[0] > here + 16:
        small[here + 16 :, :] = jnp.zeros_like(small[here + 16 :, :])


def split_gains(mix, ffn, out):
    share = out.shape[2] // 2
    low = lax.broadcasted_iota(jnp.int32, (1, 2 * share), 1) < share
    for r in range(LINE):
        lines = []
        for pair in range(PLANE // 2):
            at = (r * (PLANE // 2) + pair) * 2 * share
            one, two = mix[:, at : at + 2 * share], ffn[:, at : at + 2 * share]
            lines.append(jnp.where(low, one, pltpu.roll(two, share, 1)))
            lines.append(jnp.where(low, pltpu.roll(one, share, 1), two))
        out[r] = jnp.concatenate(lines, axis=0)


def backward_linked_body(
    head_width,
    d_mixed_ref, xy_hbm, taps_ref, vec_ref, wr_ref, we_ref, keep_ref,
    u_ref, u_prev_ref, by_ref, before_ref, states_ref, normed_ref, up_hbm, out_hbm,
    x_hbm, gain_ref, d_residual_hbm, ffn_gain_ref,
    xy_parts, up_out, out_out, in_grad, gains_out, small_out,
    xy_ref, up_parts, out_parts, brought, late,
    out_sum, taps_sum, vec_sum, wr_sum, we_sum, small, small_parts, d_xy, d_all, xy_total, eight, *rest,
):
    scratch, links = rest[:10], rest[10:]
    step = pl.program_id(0)
    block = PLANE - 1 - step
    line = LineReduce(up_hbm, up_parts, *links[:5])
    out_line = LineReduce(out_hbm, out_parts, *links[5:10])
    small_line = LineReduce(small_parts, small_parts, *links[10:15])
    plane = PlaneReduce(*links[15:])

    bring = Bring(
        (xy_hbm, up_hbm, out_hbm), (xy_ref, up_parts, out_parts), brought
    )
    d_residual_ref = xy_total.at[0 : x_hbm.shape[0]]
    bring_late = Bring((x_hbm, d_residual_hbm), (in_grad, d_residual_ref), late)

    @pl.when(step == 0)
    def _():
        bring.start()
        meet(True, "near")
        line.start()
        out_line.start()
        bring.wait(0, 1, 2)

    @pl.when((step > 0) & (step <= PLANE))
    def _():
        plane.pass_on(block + 1)

    @pl.when((step > 2) & (step <= PLANE))
    def _():
        plane.relay(block + 3)

    @pl.when(step == 3)
    def _():
        line.forward()

    @pl.when(step < PLANE)
    def _():
        backward_step(
            step == 0, step == PLANE - 1, d_mixed_ref, taps_ref, vec_ref, wr_ref, we_ref,
            keep_ref, u_ref, u_prev_ref, by_ref, before_ref, states_ref, d_xy,
            taps_sum, vec_sum, wr_sum, we_sum, *scratch,
        )
        d_all[step] = d_xy[...]
        plane.put(block, dot_plain(d_xy[...], xy_ref[...]).astype(jnp.bfloat16))

    @pl.when(step == PLANE)
    def _():
        pack_small(head_width, taps_sum, vec_sum, vec_ref, wr_sum, we_sum, small)
        share = small_parts.shape[1]
        for t in range(LINE):
            small_parts[t] = small[t * share : (t + 1) * share, :]
        small_line.start()
        xy_total[...] = contract_first(d_all[0], normed_ref[...])

    @pl.when(step > PLANE)
    def _():
        xy_total[...] += contract_first(d_all[step - PLANE], normed_ref[...])

    @pl.when(step == PLANE + 2)
    def _():
        plane.relay(1)

    @pl.when(step == PLANE + 4)
    def _():
        out_line.forward()

    @pl.when(step == PLANE + 5)
    def _():
        plane.relay(0)

    @pl.when(step == 2 * PLANE - 1)
    def _():
        small_line.forward()
        kept, chans = out_parts.shape[1], d_xy.shape[1] // 2
        to_turned_parts(xy_total, xy_parts, ((0, 0, kept), (chans, kept, kept)))
        bring_late.start()
        plane.arrive()
        bring_late.wait(0, 1)
        eight[...] = jnp.zeros_like(eight)

        def back(i, unused):
            at = pl.ds(pl.multiple_of(i * CHUNK, CHUNK), CHUNK)
            d_rows, d_gain = norm_back(
                in_grad[at, :].astype(jnp.float32), gain_ref[...], plane.total(at)
            )
            in_grad[at, :] = (xy_total[at, :] + d_rows).astype(jnp.bfloat16)
            eight[...] += sum_eight(d_gain)
            return unused

        lax.fori_loop(0, in_grad.shape[0] // CHUNK, back, 0, unroll=UNROLL)
        split_gains(jnp.sum(eight[...], axis=0, keepdims=True), ffn_gain_ref[...], gains_out)

        def write(at, value):
            up_out[at, :] = value

        def write_out(at, value):
            out_sum[at, :] = value

        def write_small(at, value):
            small_out[at, :] = value.astype(jnp.bfloat16)

        line.finish(write)
        out_line.finish(write_out)
        out_out[...] = out_sum[0 : out_out.shape[0], :]
        small_line.finish(write_small)
        plane.finish()


def backward_linked(
    d_mixed, xy, taps, vec, wr, we, keep, u, by, before, states, normed, up_parts, out_parts,
    layer_in, gain, d_residual, ffn_gain, head_width, used,
):
    length, width = normed.shape
    chans, units = d_mixed.shape[1], up_parts.shape[2]
    rows, share = length // PLANE, width // LINE
    kept = out_parts.shape[1]
    place = lambda i: PLANE - 1 - jnp.minimum(i, PLANE - 1)
    tile = lambda columns: pl.BlockSpec((rows, columns), lambda i: (place(i), 0))
    later = lambda columns: pl.BlockSpec(
        (rows, columns), lambda i: (PLANE - 1 - jnp.maximum(i - PLANE, 0), 0)
    )
    ahead = pl.BlockSpec((16, chans), lambda i: (jnp.maximum(place(i) * (rows // 16) - 1, 0), 0))
    small_share = -(-((2 * head_width + 7) // 8 * 8 + 8) // (LINE * 32)) * 32
    gain_terms = (LINE, PLANE, width // (LINE * PLANE) * 2)
    return pl.pallas_call(
        functools.partial(backward_linked_body, head_width),
        grid=(2 * PLANE,),
        in_specs=[
            tile(chans), ANYWHERE, once(taps.shape), once(vec.shape), once(wr.shape),
            once(we.shape), tile(keep.shape[1]), tile(chans), ahead, tile(chans), tile(chans),
            tile(chans), later(width), ANYWHERE, ANYWHERE,
            ANYWHERE, once(gain.shape), ANYWHERE, once(ffn_gain.shape),
        ],
        out_specs=[
            once((LINE, 2 * kept, share)), once((share, units)), once((used, share)),
            once((rows, width)), once(gain_terms), once((small_share, chans)),
        ],
        out_shape=[
            jax.ShapeDtypeStruct((LINE, 2 * kept, share), jnp.bfloat16),
            jax.ShapeDtypeStruct((share, units), jnp.float32),
            jax.ShapeDtypeStruct((used, share), jnp.float32),
            jax.ShapeDtypeStruct((rows, width), jnp.bfloat16),
            jax.ShapeDtypeStruct(gain_terms, jnp.float32),
            jax.ShapeDtypeStruct((small_share, chans), jnp.bfloat16),
        ],
        scratch_shapes=[
            *held(xy, up_parts, out_parts),
            pltpu.SemaphoreType.DMA((2,)),
            pltpu.VMEM((kept, share), jnp.float32),
            pltpu.VMEM(taps.shape, jnp.float32),
            pltpu.VMEM(vec.shape, jnp.float32),
            pltpu.VMEM(wr.shape, jnp.float32),
            pltpu.VMEM(we.shape, jnp.float32),
            pltpu.VMEM((LINE * small_share, chans), jnp.bfloat16),
            pltpu.VMEM((LINE, small_share, chans), jnp.bfloat16),
            pltpu.VMEM((rows, 2 * chans), jnp.bfloat16),
            pltpu.VMEM((PLANE, rows, 2 * chans), jnp.bfloat16),
            pltpu.VMEM((2 * chans, width), jnp.float32),
            pltpu.VMEM((8, width), jnp.float32),
            pltpu.VMEM((rows + 8, chans), jnp.float32),
            pltpu.VMEM((rows, chans), jnp.float32),
            pltpu.VMEM((rows, chans), jnp.bfloat16),
            pltpu.VMEM((rows, chans), jnp.float32),
            pltpu.VMEM((rows, chans), jnp.float32),
            pltpu.VMEM((rows + 8, chans), jnp.float32),
            pltpu.VMEM((rows, chans), jnp.bfloat16),
            pltpu.VMEM((rows, chans), jnp.bfloat16),
            pltpu.VMEM((8, chans), jnp.float32),
            pltpu.VMEM((64, chans), jnp.float32),
            *LineReduce.buffers(share, units),
            *LineReduce.semaphores,
            *LineReduce.buffers(kept, share),
            *LineReduce.semaphores,
            *LineReduce.buffers(small_share, chans),
            *LineReduce.semaphores,
            *PlaneReduce.buffers(rows, width),
            *PlaneReduce.semaphores,
        ],
        compiler_params=pltpu.CompilerParams(
            collective_id=6, has_side_effects=True, vmem_limit_bytes=61 * 2**20
        ),
        name="mixer_backward_linked",
    )(
        d_mixed, xy, taps, vec, wr, we, keep, u, u, by, before, states, normed,
        up_parts, out_parts, layer_in, gain, d_residual, ffn_gain,
    )


def close_body(
    hidden_ref, down_hbm, xy_hbm, residual_hbm, gains_ref, small,
    layer_out, x_out, y_out, gains_out, small_out,
    down_ref, xy_parts, residual_ref, brought, xy_sum,
    gathered, line_gains, both_gains, plane_gains,
    gain_sent, gain_arrived, wide_sent, wide_arrived, *links,
):
    r, h = lax.axis_index("row"), lax.axis_index("head")
    step = pl.program_id(0)
    xy_line = LineReduce(xy_hbm, xy_parts, *links[0:5])
    small_line = LineGather(small, lambda t: gathered.at[t], *links[5:8])
    plane = PlaneReduce(*links[8:])

    def to_row(t, owner):
        return send_to(
            gains_ref.at[t], line_gains.at[owner], gain_sent.at[t], gain_arrived.at[owner],
            "row", t,
        )

    def over_plane(place, owner):
        return send_to(
            both_gains, plane_gains.at[owner], wide_sent.at[place], wide_arrived.at[owner],
            "head", lax.rem(h + place, PLANE),
        )

    bring = Bring(
        (down_hbm, xy_hbm, residual_hbm), (down_ref, xy_parts, residual_ref), brought
    )

    @pl.when(step == 0)
    def _():
        bring.start()
        meet(True, "all")
        for place in range(1, LINE):
            to_row(lax.rem(r + place, LINE), r).start()
        small_line.start()
        xy_line.start()
        bring.wait(0, 1, 2)

    @pl.when(step > 0)
    def _():
        plane.pass_on(far_first(step - 1))

    @pl.when(step > 2)
    def _():
        plane.relay(far_first(step - 3))

    plane.put(far_first(step), contract_last(hidden_ref[...], down_ref[...]).astype(jnp.bfloat16))

    @pl.when(step == 2)
    def _():
        total = gains_ref[r]
        for place in range(1, LINE):
            t = lax.rem(r + place, LINE)
            to_row(t, t).wait_recv()
            total = total + line_gains[t]
        both_gains[...] = total
        for place in range(1, PLANE):
            over_plane(place, h).start()

    @pl.when(step == PLANE - 1)
    def _():
        small_line.forward()
        xy_line.forward()
        plane.relay(far_first(step - 2))
        plane.pass_on(far_first(step))
        plane.relay(far_first(step - 1))
        plane.relay(far_first(step))
        total = both_gains[...]
        for place in range(1, PLANE):
            owner = lax.rem(h + place, PLANE)
            over_plane(place, owner).wait_recv()
            total = total + plane_gains[owner]
        mine = lax.broadcasted_iota(jnp.int32, total.shape, 0) == h
        gains_out[...] = jnp.sum(jnp.where(mine, total, 0.0), axis=0, keepdims=True)
        plane.arrive()

        def make(i, unused):
            at = pl.ds(pl.multiple_of(i * CHUNK, CHUNK), CHUNK)
            layer_out[at, :] = (residual_ref[at, :] + plane.total(at)).astype(jnp.bfloat16)
            return unused

        lax.fori_loop(0, residual_ref.shape[0] // CHUNK, make, 0)
        def write(at, value):
            xy_sum[at, :] = value

        xy_line.finish(write)
        used, kept = x_out.shape[0], xy_sum.shape[0] // 2
        x_out[...] = xy_sum[0:used, :]
        y_out[...] = xy_sum[kept : kept + used, :]
        small_line.finish()
        small_out[...] = gathered[...].astype(jnp.float32)
        plane.finish()
        for place in range(1, LINE):
            to_row(lax.rem(r + place, LINE), r).wait_send()
        for place in range(1, PLANE):
            over_plane(place, h).wait_send()


def close_block(hidden, down, xy_parts, residual, gains, small, used):
    length, units = hidden.shape
    rows, width = residual.shape
    both, share = xy_parts.shape[1:]
    return pl.pallas_call(
        close_body,
        grid=(PLANE,),
        in_specs=[
            pl.BlockSpec((rows, units), lambda i: (far_first(i), 0)), ANYWHERE,
            ANYWHERE, ANYWHERE, once(gains.shape), once(small.shape),
        ],
        out_specs=[
            once((rows, width)), once((used, share)), once((used, share)), once((1, gains.shape[2])),
            once((LINE,) + small.shape),
        ],
        out_shape=[
            jax.ShapeDtypeStruct((rows, width), jnp.bfloat16),
            jax.ShapeDtypeStruct((used, share), jnp.float32),
            jax.ShapeDtypeStruct((used, share), jnp.float32),
            jax.ShapeDtypeStruct((1, gains.shape[2]), jnp.float32),
            jax.ShapeDtypeStruct((LINE,) + small.shape, jnp.float32),
        ],
        scratch_shapes=[
            *held(down, xy_parts, residual),
            pltpu.VMEM((both, share), jnp.float32),
            pltpu.VMEM((LINE,) + small.shape, jnp.bfloat16),
            pltpu.VMEM(gains.shape, jnp.float32),
            pltpu.VMEM(gains.shape[1:], jnp.float32),
            pltpu.VMEM((PLANE,) + gains.shape[1:], jnp.float32),
            pltpu.SemaphoreType.DMA((LINE,)),
            pltpu.SemaphoreType.DMA((LINE,)),
            pltpu.SemaphoreType.DMA((PLANE,)),
            pltpu.SemaphoreType.DMA((PLANE,)),
            *LineReduce.buffers(both, share), *LineReduce.semaphores,
            *LineGather.semaphores,
            *PlaneReduce.buffers(rows, width), *PlaneReduce.semaphores,
        ],
        compiler_params=pltpu.CompilerParams(
            collective_id=7, has_side_effects=True, vmem_limit_bytes=61 * 2**20
        ),
        name="close_block",
    )(hidden, down, xy_parts, residual, gains, small)


def hand_over_body(*refs):
    count = (len(refs) - 2) // 3
    sources, targets, held = refs[:count], refs[count : 2 * count], refs[2 * count : 3 * count]
    inward, outward = (
        [
            pltpu.make_async_copy(src, dst, done.at[k])
            for k, (src, dst) in enumerate(zip(starts, ends))
        ]
        for starts, ends, done in ((sources, held, refs[-2]), (held, targets, refs[-1]))
    )
    for copy in inward:
        copy.start()
    for first, second in zip(inward, outward):
        first.wait()
        second.start()
    for copy in outward:
        copy.wait()


def hand_over(*arrays):
    return pl.pallas_call(
        hand_over_body,
        in_specs=[ANYWHERE] * len(arrays),
        out_specs=[ANYWHERE] * len(arrays),
        out_shape=[jax.ShapeDtypeStruct(item.shape, item.dtype) for item in arrays],
        scratch_shapes=[pltpu.VMEM(item.shape, item.dtype) for item in arrays]
        + [pltpu.SemaphoreType.DMA((len(arrays),))] * 2,
        compiler_params=pltpu.CompilerParams(vmem_limit_bytes=61 * 2**20),
        name="hand_over",
    )(*arrays)


def mixer_params(
    conv_weight, conv_bias, rate_weight, rate_bias, entry_weight, entry_bias, decay_param, chans
):
    used = conv_bias.shape[0]
    spare = (0, chans - used)
    decay_wide = jnp.pad(decay_param, spare, constant_values=2.0)
    blank = jnp.zeros((chans,), jnp.float32)
    vec = jnp.stack(
        [
            jnp.pad(conv_bias, spare),
            jnp.pad(rate_bias, spare),
            jnp.pad(entry_bias, spare),
            -8.0 * jax.nn.softplus(-decay_wide),
            8.0 * jax.nn.sigmoid(-decay_wide),
            blank,
            blank,
            blank,
        ]
    )
    taps = jnp.pad(conv_weight, ((0, 0), spare))
    return taps, vec, block_diagonal(rate_weight, chans), block_diagonal(entry_weight, chans)


def shards(
    layer_in,
    cotangent,
    mix_gain,
    ffn_gain,
    x_weight,
    y_weight,
    out_weight,
    conv_weight,
    conv_bias,
    rate_weight,
    rate_bias,
    entry_weight,
    entry_bias,
    decay_param,
    gate_weight,
    up_weight,
    down_weight,
    resets,
):
    heads, head_width = rate_weight.shape[:2]
    used = conv_bias.shape[0]
    chans = -(-used // 128) * 128
    widen = lambda values: jnp.pad(values, ((0, 0), (0, chans - used)))
    mix_full = gather(mix_gain, ("row", "head"), 0)
    ffn_full = gather(ffn_gain, ("row", "head"), 0)
    xy_shard = jnp.concatenate([widen(x_weight), widen(y_weight)], axis=1)
    xy_rows = gather(xy_shard, "row", 0).T
    out_rows = gather(widen(out_weight), "row", 0).T
    gate_rows = gather(gate_weight, "row", 0)
    up_rows = gather(up_weight, "row", 0)
    down_rows = gather(down_weight, "row", 0)

    taps, vec, wr, we = mixer_params(
        conv_weight, conv_bias, rate_weight, rate_bias, entry_weight, entry_bias, decay_param, chans
    )
    keep = keep_columns(resets)

    inputs = layer_in.astype(jnp.float32)
    normed_f, norm_back_one = jax.vjp(norm_apply, inputs, mix_full.astype(jnp.float32))
    normed_group = gather(normed_f.astype(jnp.bfloat16), "head", 0)
    u, by, before, states, mixed, part = mixer_forward(
        normed_group, xy_rows, out_rows, taps, vec, wr, we, keep, ROWS
    )
    residual = inputs + scatter(part, "head", 0).astype(jnp.float32)
    normed_two_f, norm_back_two = jax.vjp(norm_apply, residual, ffn_full.astype(jnp.float32))
    cot_group = gather(cotangent, "head", 0)
    two_group = gather(normed_two_f.astype(jnp.bfloat16), "head", 0)
    gates = dot_plain(two_group, gate_rows)
    ups = dot_plain(two_group, up_rows)
    activated, slope = gelu_both(gates)
    hidden = (activated * ups).astype(jnp.bfloat16)
    ffn_part = contract_last(hidden, down_rows).astype(jnp.bfloat16)
    d_hidden = dot_plain(cot_group, down_rows)
    d_gates = (d_hidden * ups * slope).astype(jnp.bfloat16)
    d_ups = (d_hidden * activated).astype(jnp.bfloat16)
    d_two_part = (contract_last(d_gates, gate_rows) + contract_last(d_ups, up_rows)).astype(
        jnp.bfloat16
    )
    gate_grad = scatter(contract_first(two_group, d_gates).astype(jnp.bfloat16), "row", 0)
    up_grad = scatter(contract_first(two_group, d_ups).astype(jnp.bfloat16), "row", 0)
    down_grad = scatter(contract_first(cot_group, hidden).astype(jnp.bfloat16), "row", 0)
    layer_out = (residual + scatter(ffn_part, "head", 0).astype(jnp.float32)).astype(jnp.bfloat16)
    d_two = scatter(d_two_part, "head", 0).astype(jnp.float32)
    d_resid_norm, d_ffn_gain = norm_back_two(d_two)
    d_residual = cotangent.astype(jnp.float32) + d_resid_norm
    d_res_group = gather(d_residual.astype(jnp.bfloat16), "head", 0)
    d_xy, d_part, d_taps, d_vec, d_wr, d_we = mixer_backward(
        d_res_group, xy_rows, out_rows, taps, vec, wr, we, keep, u, by, before, states, ROWS
    )
    out_grad = scatter(contract_first(d_res_group, mixed).astype(jnp.bfloat16), "row", 0)
    xy_grad = scatter(contract_first(normed_group, d_xy).astype(jnp.bfloat16), "row", 0)
    d_normed = scatter(d_part, "head", 0).astype(jnp.float32)
    d_inputs, d_mix_gain = norm_back_one(d_normed)
    layer_in_grad = (d_inputs + d_residual).astype(jnp.bfloat16)

    small = [
        d_taps[:, :used],
        d_vec[0, :used],
        diagonal_blocks(d_wr, heads, head_width),
        d_vec[1, :used],
        diagonal_blocks(d_we, heads, head_width),
        d_vec[2, :used],
        d_vec[3, :used] * (8.0 * jax.nn.sigmoid(-decay_param)),
    ]
    small = [lax.psum(item.astype(jnp.bfloat16), "row").astype(jnp.float32) for item in small]
    mix_part = scatter(d_mix_gain, ("row", "head"), 0)
    ffn_part_grad = scatter(d_ffn_gain, ("row", "head"), 0)
    wide = lambda values: values[:, :used].astype(jnp.float32)
    return (
        layer_out,
        layer_in_grad,
        mix_part,
        ffn_part_grad,
        wide(xy_grad),
        wide(xy_grad[:, chans:]),
        wide(out_grad),
        *small,
        gate_grad.astype(jnp.float32),
        up_grad.astype(jnp.float32),
        down_grad.astype(jnp.float32),
    )

def shards_linked(
    layer_in,
    cotangent,
    mix_gain,
    ffn_gain,
    x_weight,
    y_weight,
    out_weight,
    conv_weight,
    conv_bias,
    rate_weight,
    rate_bias,
    entry_weight,
    entry_bias,
    decay_param,
    gate_weight,
    up_weight,
    down_weight,
    resets,
):
    heads, head_width = rate_weight.shape[:2]
    used = conv_bias.shape[0]
    kept = -(-used // 16) * 16
    flat = lambda values: values.reshape((-1, values.shape[-1]))
    line = lambda values: values.reshape(1, -1)
    vectors = (conv_bias, rate_bias, entry_bias, decay_param)
    place = lax.broadcasted_iota(jnp.int32, (len(vectors), used), 0)
    rows = jnp.zeros((len(vectors), used), jnp.float32)
    for k, vector in enumerate(vectors):
        rows = jnp.where(place == k, vector[None, :], rows)
    (
        normed_group, cot_half, xy_rows, out_rows, mix_full, ffn_full, taps, vec, wr, we, keep,
    ) = open_block(
        layer_in,
        (line(mix_gain), line(ffn_gain)),
        cotangent,
        (x_weight.T, y_weight.T, out_weight.T),
        (
            conv_weight,
            rows,
            jnp.stack([rate_weight, entry_weight]),
            resets,
        ),
    )
    normed_group = flat(normed_group)
    u, by, before, states, mixed, residual, normed_two, gate_rows, up_half = forward_linked(
        normed_group, xy_rows, out_rows, taps, vec, wr, we, keep, layer_in, ffn_full,
        gate_weight, up_weight,
    )
    gate_rows = flat(gate_rows)
    two_group, cot_group, up_rows, down_rows, gates, ups, hidden, down_parts = ffn_up(
        normed_two, gate_rows, cotangent, cot_half, up_half, up_weight, down_weight
    )
    two_group, cot_group, down_rows = map(flat, (two_group, cot_group, down_rows))
    d_ups, gate_parts, down_grad, d_residual, d_low, d_ffn_gain = ffn_back(
        cot_group, two_group, gates, ups, gate_rows, up_rows, down_rows, down_parts, residual,
        cotangent, ffn_full,
    )
    up_parts, out_parts, gate_grad, d_mixed = turn(
        two_group, d_ups, gate_parts, d_low, mixed, out_rows, kept
    )
    xy_parts, up_grad, out_grad, layer_in_grad, gain_terms, small = backward_linked(
        d_mixed, xy_rows, taps, vec, wr, we, keep, u, by, before, states,
        normed_group, up_parts, out_parts, layer_in, mix_full, d_residual, d_ffn_gain,
        head_width, used,
    )
    layer_out, x_grad, y_grad, gain_grads, sums = close_block(
        hidden, down_rows, xy_parts, residual, gain_terms, small, used
    )
    sums = flat(sums)
    share = mix_gain.shape[0]
    ends = -(-used // 8) * 8
    (
        layer_out, layer_in_grad, x_grad, y_grad, out_grad, gate_grad, up_grad, down_grad,
    ) = hand_over(
        layer_out, layer_in_grad, x_grad, y_grad, out_grad, gate_grad, up_grad, down_grad
    )
    gates_end = heads * head_width
    return (
        layer_out,
        layer_in_grad,
        gain_grads[0, :share],
        gain_grads[0, share:],
        x_grad.T,
        y_grad.T,
        out_grad.T,
        sums[ends : ends + 4, :used],
        sums[ends + 4, :used],
        sums[:gates_end, :head_width].reshape(heads, head_width, head_width),
        sums[ends + 5, :used],
        sums[:gates_end, head_width : 2 * head_width].reshape(heads, head_width, head_width),
        sums[ends + 6, :used],
        sums[ends + 7, :used],
        gate_grad,
        up_grad,
        down_grad,
    )


def solution(mesh):
    linked = mesh.shape["row"] == LINE and mesh.shape["head"] == PLANE
    return jax.shard_map(
        shards_linked if linked else shards,
        mesh=mesh,
        in_specs=(
            P(("row", "head"), None),
            P(("row", "head"), None),
            P(("row", "head")),
            P(("row", "head")),
            P("row", "head"),
            P("row", "head"),
            P("row", "head"),
            P(None, "head"),
            P("head"),
            P("head", None, None),
            P("head"),
            P("head", None, None),
            P("head"),
            P("head"),
            P("row", "head"),
            P("row", "head"),
            P("row", "head"),
            P("row", None),
        ),
        out_specs=(
            P(("row", "head"), None),
            P(("row", "head"), None),
            P(("row", "head")),
            P(("row", "head")),
            P("row", "head"),
            P("row", "head"),
            P("row", "head"),
            P(None, "head"),
            P("head"),
            P("head", None, None),
            P("head"),
            P("head", None, None),
            P("head"),
            P("head"),
            P("row", "head"),
            P("row", "head"),
            P("row", "head"),
        ),
        check_vma=False,
    )
```

```python
import functools

import jax
import jax.numpy as jnp
from jax import lax
from jax.experimental import pallas as pl
from jax.experimental.pallas import tpu as pltpu
from jax.sharding import PartitionSpec as P

EPSILON = 1e-06
ROWS = 256
GELU_A = 0.7978845608028654
GELU_B = 0.044715
CHUNK = 16
UNROLL = 4


def gelu_only(x):
    return 0.5 * x * (1.0 + jnp.tanh(GELU_A * (x + GELU_B * x * x * x)))


def gelu_both(x):
    square = x * x
    bent = jnp.tanh(GELU_A * x * (1.0 + GELU_B * square))
    half = 0.5 * (1.0 + bent)
    slope = half + 0.5 * x * (1.0 - bent * bent) * (GELU_A * (1.0 + 3.0 * GELU_B * square))
    return x * half, slope


def one_minus_exp(x, exp_x):
    return -jnp.tanh(0.5 * x) * (1.0 + exp_x)


def dot_plain(left, right):
    return jnp.dot(left, right, preferred_element_type=jnp.float32)


def contract_last(left, right):
    return lax.dot_general(
        left, right, (((1,), (1,)), ((), ())), preferred_element_type=jnp.float32
    )


def contract_first(left, right):
    return lax.dot_general(
        left, right, (((0,), (0,)), ((), ())), preferred_element_type=jnp.float32
    )


def sum_eight(value):
    total = value[0:8, :]
    for k in range(1, value.shape[0] // 8):
        total = total + value[8 * k : 8 * k + 8, :]
    return total


def conv_rows(window, keep, taps, shift):
    rows = window.shape[0] - 8
    total = taps[0:1] * window[8:] + shift
    for offset in range(1, 4):
        total = total + taps[offset : offset + 1] * (
            keep[:, offset : offset + 1] * window[8 - offset : 8 - offset + rows]
        )
    return total


def scan_down(decays, driven, carry):
    rows = decays.shape[0]
    place = lax.broadcasted_iota(jnp.int32, decays.shape, 0)
    step = 1
    while step < rows:
        inside = place >= step
        driven = jnp.where(inside, decays * pltpu.roll(driven, step, 0) + driven, driven)
        decays = jnp.where(inside, decays * pltpu.roll(decays, step, 0), decays)
        step *= 2
    return decays * carry + driven


def scan_up(decays, driven, carry):
    rows = decays.shape[0]
    place = lax.broadcasted_iota(jnp.int32, decays.shape, 0)
    step = 1
    while step < rows:
        inside = place < rows - step
        driven = jnp.where(inside, decays * pltpu.roll(driven, rows - step, 0) + driven, driven)
        decays = jnp.where(inside, decays * pltpu.roll(decays, rows - step, 0), decays)
        step *= 2
    return decays * carry + driven


def forward_step(
    normed_ref, xy_ref, taps_ref, vec_ref, wr_ref, we_ref, keep_ref,
    u_ref, by_ref, before_ref, states_ref, mixed_ref,
    window, conv, conv_low, rate, entry, carry,
):
    rows = normed_ref.shape[0]

    @pl.when(pl.program_id(0) == 0)
    def _():
        window[0:8, :] = jnp.zeros_like(window[0:8, :])
        carry[...] = jnp.zeros_like(carry)

    chans = u_ref.shape[1]
    branches = contract_last(normed_ref[...], xy_ref[...])
    branch_x = branches[:, :chans].astype(jnp.bfloat16)
    u_ref[...] = branch_x
    window[pl.ds(8, rows), :] = branch_x.astype(jnp.float32)
    by_ref[...] = branches[:, chans:]

    def conv_step(j, unused):
        at = pl.multiple_of(j * CHUNK, CHUNK)
        made = conv_rows(
            window[pl.ds(at, CHUNK + 8), :], keep_ref[pl.ds(at, CHUNK), :],
            taps_ref[...], vec_ref[0:1, :],
        )
        conv[pl.ds(at, CHUNK), :] = made
        conv_low[pl.ds(at, CHUNK), :] = made.astype(jnp.bfloat16)
        return unused

    lax.fori_loop(0, rows // CHUNK, conv_step, 0, unroll=2 * UNROLL)
    window[0:8, :] = window[pl.ds(rows, 8), :]
    rate[...] = dot_plain(conv_low[...], wr_ref[...]) + vec_ref[1:2, :]
    entry[...] = dot_plain(conv_low[...], we_ref[...]) + vec_ref[2:3, :]

    def scan_step(j, before):
        at = pl.multiple_of(j * CHUNK, CHUNK)
        here = pl.ds(at, CHUNK)
        carried = keep_ref[here, 0:1]
        log_decay = jax.nn.sigmoid(rate[here, :]) * vec_ref[3:4, :]
        exp_decay = jnp.exp(log_decay)
        lost = one_minus_exp(2.0 * log_decay, exp_decay * exp_decay)
        drop = lost * lax.rsqrt(jnp.maximum(lost, 1e-30))
        scaling = (1.0 - carried) + carried * drop
        driven = scaling * jax.nn.sigmoid(entry[here, :]) * conv[here, :]
        states = scan_down(exp_decay * carried, driven, before)
        first = lax.broadcasted_iota(jnp.int32, states.shape, 0) == 0
        before_ref[here, :] = jnp.where(first, before, pltpu.roll(states, 1, 0))
        states_low = states.astype(jnp.bfloat16)
        states_ref[here, :] = states_low
        mixed_ref[here, :] = (
            states_low.astype(jnp.float32) * gelu_only(by_ref[here, :])
        ).astype(jnp.bfloat16)
        return states[CHUNK - 1 : CHUNK, :]

    carry[0:1, :] = lax.fori_loop(0, rows // CHUNK, scan_step, carry[0:1, :], unroll=2 * UNROLL)


def forward_body(
    normed_ref, xy_ref, ow_ref, taps_ref, vec_ref, wr_ref, we_ref, keep_ref,
    u_ref, by_ref, before_ref, states_ref, mixed_ref, part_ref, *scratch,
):
    forward_step(
        normed_ref, xy_ref, taps_ref, vec_ref, wr_ref, we_ref, keep_ref,
        u_ref, by_ref, before_ref, states_ref, mixed_ref, *scratch,
    )
    part_ref[...] = dot_plain(mixed_ref[...], ow_ref[...]).astype(jnp.bfloat16)


def backward_step(
    first_step, last_step, d_mixed, taps_ref, vec_ref, wr_ref, we_ref, keep_ref,
    u_ref, u_prev_ref, by_ref, before_ref, states_ref,
    d_xy_ref, taps_out, vec_out, wr_out, we_out,
    window, conv, conv_low, rate, entry, d_conv, g_rate, g_entry, carry, sums,
):
    rows, chans = u_ref.shape

    @pl.when(first_step)
    def _():
        d_conv[pl.ds(rows, 8), :] = jnp.zeros_like(d_conv[pl.ds(rows, 8), :])
        carry[...] = jnp.zeros_like(carry)
        sums[...] = jnp.zeros_like(sums)
        wr_out[...] = jnp.zeros_like(wr_out)
        we_out[...] = jnp.zeros_like(we_out)

    @pl.when(jnp.logical_not(first_step))
    def _():
        d_conv[pl.ds(rows, 8), :] = d_conv[0:8, :]

    window[0:8, :] = u_prev_ref[8:16, :].astype(jnp.float32)
    window[pl.ds(8, rows), :] = u_ref[...].astype(jnp.float32)

    def conv_step(j, unused):
        at = pl.multiple_of(j * CHUNK, CHUNK)
        made = conv_rows(
            window[pl.ds(at, CHUNK + 8), :], keep_ref[pl.ds(at, CHUNK), :],
            taps_ref[...], vec_ref[0:1, :],
        )
        conv[pl.ds(at, CHUNK), :] = made
        conv_low[pl.ds(at, CHUNK), :] = made.astype(jnp.bfloat16)
        return unused

    lax.fori_loop(0, rows // CHUNK, conv_step, 0, unroll=2 * UNROLL)
    rate[...] = dot_plain(conv_low[...], wr_ref[...]) + vec_ref[1:2, :]
    entry[...] = dot_plain(conv_low[...], we_ref[...]) + vec_ref[2:3, :]

    def fold(value):
        return sum_eight(value)

    def scan_step(j, after):
        at = pl.multiple_of(rows - CHUNK - j * CHUNK, CHUNK)
        here = pl.ds(at, CHUNK)
        carried = keep_ref[here, 0:1]
        rate_gate = jax.nn.sigmoid(rate[here, :])
        entry_gate = jax.nn.sigmoid(entry[here, :])
        log_decay = rate_gate * vec_ref[3:4, :]
        exp_decay = jnp.exp(log_decay)
        exp_twice = exp_decay * exp_decay
        lost = one_minus_exp(2.0 * log_decay, exp_twice)
        inverse = lax.rsqrt(jnp.maximum(lost, 1e-30))
        drop = lost * inverse
        scaling = (1.0 - carried) + carried * drop
        decays = exp_decay * carried
        gelu_y, slope_y = gelu_both(by_ref[here, :])
        through = d_mixed[here, :]
        d_states = (through * gelu_y).astype(jnp.bfloat16).astype(jnp.float32)
        d_xy_ref[here, chans:] = (
            through * states_ref[here, :].astype(jnp.float32) * slope_y
        ).astype(jnp.bfloat16)
        passed = scan_up(decays, decays * d_states, after)
        last = lax.broadcasted_iota(jnp.int32, passed.shape, 0) == CHUNK - 1
        adjoint = d_states + jnp.where(last, after, pltpu.roll(passed, CHUNK - 1, 0))
        convolved = conv[here, :]
        gated = adjoint * entry_gate
        g_log = adjoint * before_ref[here, :] * decays - gated * convolved * (
            carried * (exp_twice * inverse)
        )
        g_pre_rate = g_log * vec_ref[3:4, :] * (rate_gate * (1.0 - rate_gate))
        direct = gated * scaling
        g_pre_entry = direct * convolved * (1.0 - entry_gate)
        d_conv[here, :] = direct
        g_rate[here, :] = g_pre_rate.astype(jnp.bfloat16)
        g_entry[here, :] = g_pre_entry.astype(jnp.bfloat16)
        sums[8:16, :] += fold(g_pre_rate)
        sums[16:24, :] += fold(g_pre_entry)
        sums[24:32, :] += fold(g_log * rate_gate)
        return passed[0:1, :]

    carry[0:1, :] = lax.fori_loop(0, rows // CHUNK, scan_step, carry[0:1, :], unroll=2 * UNROLL)
    wr_out[...] += contract_first(conv_low[...], g_rate[...])
    we_out[...] += contract_first(conv_low[...], g_entry[...])
    d_conv[0:rows, :] += contract_last(g_rate[...], wr_ref[...]) + contract_last(
        g_entry[...], we_ref[...]
    )

    def back_step(j, unused):
        at = pl.multiple_of(j * CHUNK, CHUNK)
        here = pl.ds(at, CHUNK)
        keep = keep_ref[here, :]
        ahead = d_conv[pl.ds(at, CHUNK + 8), :]
        behind = window[pl.ds(at, CHUNK + 8), :]
        now = ahead[0:CHUNK]
        total = taps_ref[0:1, :] * now
        sums[0:8, :] += fold(now)
        sums[32:40, :] += fold(now * behind[8:])
        for offset in range(1, 4):
            total = total + taps_ref[offset : offset + 1, :] * (
                keep[:, 3 + offset : 4 + offset] * ahead[offset : offset + CHUNK]
            )
            base = 32 + 8 * offset
            sums[base : base + 8, :] += fold(
                now * (keep[:, offset : offset + 1] * behind[8 - offset : 8 - offset + CHUNK])
            )
        d_xy_ref[here, :chans] = total.astype(jnp.bfloat16)
        return unused

    lax.fori_loop(0, rows // CHUNK, back_step, 0, unroll=2 * UNROLL)

    @pl.when(last_step)
    def _():
        vec_out[...] = jnp.zeros_like(vec_out)
        for place in range(4):
            vec_out[place : place + 1, :] = jnp.sum(
                sums[8 * place : 8 * place + 8, :], axis=0, keepdims=True
            )
            taps_out[place : place + 1, :] = jnp.sum(
                sums[32 + 8 * place : 40 + 8 * place, :], axis=0, keepdims=True
            )


def backward_body(
    d_res_ref, xy_ref, ow_ref, taps_ref, vec_ref, wr_ref, we_ref, keep_ref,
    u_ref, u_prev_ref, by_ref, before_ref, states_ref,
    d_xy_ref, part_ref, taps_out, vec_out, wr_out, we_out, d_mixed, *scratch,
):
    step = pl.program_id(0)
    d_mixed[...] = contract_last(d_res_ref[...], ow_ref[...])
    backward_step(
        step == 0, step == pl.num_programs(0) - 1, d_mixed, taps_ref, vec_ref, wr_ref,
        we_ref, keep_ref, u_ref, u_prev_ref, by_ref, before_ref, states_ref, d_xy_ref,
        taps_out, vec_out, wr_out, we_out, *scratch,
    )
    part_ref[...] = dot_plain(d_xy_ref[...], xy_ref[...]).astype(jnp.bfloat16)


def whole(shape):
    return pl.BlockSpec(shape, lambda i: (0,) * len(shape))


def mixer_forward(normed, xy, ow, taps, vec, wr, we, keep, rows):
    length, width = normed.shape
    chans = ow.shape[0]
    tile = lambda columns: pl.BlockSpec((rows, columns), lambda i: (i, 0))
    return pl.pallas_call(
        forward_body,
        grid=(length // rows,),
        in_specs=[
            tile(width), whole(xy.shape), whole(ow.shape), whole(taps.shape),
            whole(vec.shape), whole(wr.shape), whole(we.shape), tile(keep.shape[1]),
        ],
        out_specs=[tile(chans)] * 5 + [tile(width)],
        out_shape=[
            jax.ShapeDtypeStruct((length, chans), jnp.bfloat16),
            jax.ShapeDtypeStruct((length, chans), jnp.float32),
            jax.ShapeDtypeStruct((length, chans), jnp.float32),
            jax.ShapeDtypeStruct((length, chans), jnp.bfloat16),
            jax.ShapeDtypeStruct((length, chans), jnp.bfloat16),
            jax.ShapeDtypeStruct((length, width), jnp.bfloat16),
        ],
        scratch_shapes=[
            pltpu.VMEM((rows + 8, chans), jnp.float32),
            pltpu.VMEM((rows, chans), jnp.float32),
            pltpu.VMEM((rows, chans), jnp.bfloat16),
            pltpu.VMEM((rows, chans), jnp.float32),
            pltpu.VMEM((rows, chans), jnp.float32),
            pltpu.VMEM((8, chans), jnp.float32),
        ],
        compiler_params=pltpu.CompilerParams(vmem_limit_bytes=48 * 2**20),
        cost_estimate=pl.CostEstimate(
            flops=6 * length * width * chans,
            bytes_accessed=4 * length * width + 30 * length * chans,
            transcendentals=6 * length * chans,
        ),
        name="mixer_forward",
    )(normed, xy, ow, taps, vec, wr, we, keep)


def mixer_backward(d_res, xy, ow, taps, vec, wr, we, keep, u, by, before, states, rows):
    length, width = d_res.shape
    chans = ow.shape[0]
    blocks = length // rows
    tile = lambda columns: pl.BlockSpec((rows, columns), lambda i: (blocks - 1 - i, 0))
    ahead = pl.BlockSpec(
        (16, chans), lambda i: (jnp.maximum((blocks - 1 - i) * (rows // 16) - 1, 0), 0)
    )
    return pl.pallas_call(
        backward_body,
        grid=(blocks,),
        in_specs=[
            tile(width), whole(xy.shape), whole(ow.shape), whole(taps.shape),
            whole(vec.shape), whole(wr.shape), whole(we.shape), tile(keep.shape[1]),
            tile(chans), ahead, tile(chans), tile(chans), tile(chans),
        ],
        out_specs=[
            tile(2 * chans), tile(width), whole(taps.shape), whole(vec.shape),
            whole(wr.shape), whole(we.shape),
        ],
        out_shape=[
            jax.ShapeDtypeStruct((length, 2 * chans), jnp.bfloat16),
            jax.ShapeDtypeStruct((length, width), jnp.bfloat16),
            jax.ShapeDtypeStruct(taps.shape, jnp.float32),
            jax.ShapeDtypeStruct(vec.shape, jnp.float32),
            jax.ShapeDtypeStruct(wr.shape, jnp.float32),
            jax.ShapeDtypeStruct(we.shape, jnp.float32),
        ],
        scratch_shapes=[
            pltpu.VMEM((rows, chans), jnp.float32),
            pltpu.VMEM((rows + 8, chans), jnp.float32),
            pltpu.VMEM((rows, chans), jnp.float32),
            pltpu.VMEM((rows, chans), jnp.bfloat16),
            pltpu.VMEM((rows, chans), jnp.float32),
            pltpu.VMEM((rows, chans), jnp.float32),
            pltpu.VMEM((rows + 8, chans), jnp.float32),
            pltpu.VMEM((rows, chans), jnp.bfloat16),
            pltpu.VMEM((rows, chans), jnp.bfloat16),
            pltpu.VMEM((8, chans), jnp.float32),
            pltpu.VMEM((64, chans), jnp.float32),
        ],
        compiler_params=pltpu.CompilerParams(vmem_limit_bytes=48 * 2**20),
        cost_estimate=pl.CostEstimate(
            flops=6 * length * width * chans,
            bytes_accessed=4 * length * width + 30 * length * chans,
            transcendentals=6 * length * chans,
        ),
        name="mixer_backward",
    )(d_res, xy, ow, taps, vec, wr, we, keep, u, u, by, before, states)


def keep_columns(resets):
    length = resets.shape[1]
    position = lax.broadcasted_iota(jnp.int32, resets.shape, 1)
    starts = jnp.maximum(resets, (position == 0).astype(jnp.int32)).astype(jnp.float32)
    carried = (1.0 - starts).reshape(-1)
    seqs = resets.shape[0]

    def back(values, by):
        values = values.reshape(seqs, length)
        return jnp.pad(values, ((0, 0), (by, 0)))[:, :length].reshape(-1)

    def ahead(values, by):
        values = values.reshape(seqs, length)
        return jnp.pad(values, ((0, 0), (0, by)))[:, by:].reshape(-1)

    one = carried
    two = one * back(carried, 1)
    three = two * back(carried, 2)
    return jnp.stack(
        [carried, one, two, three, ahead(one, 1), ahead(two, 2), ahead(three, 3), carried], axis=1
    )


def block_diagonal(blocks, chans):
    heads, width, unused = blocks.shape
    rows = [
        jnp.pad(blocks[h], ((0, 0), (h * width, chans - (h + 1) * width))) for h in range(heads)
    ]
    full = jnp.concatenate(rows, axis=0)
    return jnp.pad(full, ((0, chans - heads * width), (0, 0)))


def diagonal_blocks(full, heads, width):
    return jnp.stack(
        [full[h * width : (h + 1) * width, h * width : (h + 1) * width] for h in range(heads)]
    )


MESH = pl.DeviceIdType.MESH
ANYWHERE = pl.BlockSpec(memory_space=pl.ANY)
IN_VMEM = pl.BlockSpec(memory_space=pltpu.VMEM)
LINE = 4
PLANE = 8
PIECES = 4


def send_to(src, dst, sent, arrived, axis, target):
    return pltpu.make_async_remote_copy(
        src_ref=src,
        dst_ref=dst,
        send_sem=sent,
        recv_sem=arrived,
        device_id={axis: target},
        device_id_type=MESH,
    )


def sibling_of(h):
    return h + 1 - 2 * lax.rem(h, 2)


def across_of(h):
    return h + 2 - 4 * lax.rem(lax.div(h, 2), 2)


def along_of(h):
    return lax.rem(h + 4, PLANE)


def meet(row_line, plane):
    r, h = lax.axis_index("row"), lax.axis_index("head")
    barrier = pltpu.get_barrier_semaphore()
    count = 0
    if row_line:
        for step in range(1, LINE):
            pl.semaphore_signal(
                barrier, inc=1, device_id={"row": lax.rem(r + step, LINE)}, device_id_type=MESH
            )
        count += LINE - 1
    if plane == "all":
        for step in range(1, PLANE):
            pl.semaphore_signal(
                barrier, inc=1, device_id={"head": lax.rem(h + step, PLANE)}, device_id_type=MESH
            )
        count += PLANE - 1
    if plane == "near":
        for target in (sibling_of(h), across_of(h), along_of(h)):
            pl.semaphore_signal(barrier, inc=1, device_id={"head": target}, device_id_type=MESH)
        count += 3
    pl.semaphore_wait(barrier, count)


class Bring:
    def __init__(self, sources, places, semaphores):
        self.copies = [
            pltpu.make_async_copy(src, dst, semaphores.at[k])
            for k, (src, dst) in enumerate(zip(sources, places))
        ]

    def start(self):
        for copy in self.copies:
            copy.start()

    def wait(self, *which):
        for k in which:
            self.copies[k].wait()


def held(*arrays):
    return [pltpu.VMEM(item.shape, item.dtype) for item in arrays] + [
        pltpu.SemaphoreType.DMA((len(arrays),))
    ]


class LineGather:
    semaphores = (
        pltpu.SemaphoreType.DMA((LINE,)),
        pltpu.SemaphoreType.DMA((LINE,)),
        pltpu.SemaphoreType.DMA((2,)),
    )

    def __init__(self, source, slot, sent, arrived, other):
        self.r = lax.axis_index("row")
        self.source, self.slot = source, slot
        self.sent, self.arrived, self.other = sent, arrived, other

    def own(self, t):
        return send_to(
            self.source, self.slot(self.r), self.sent.at[t], self.arrived.at[self.r], "row", t
        )

    def handed(self, origin, target):
        return send_to(
            self.slot(origin), self.slot(origin), self.other.at[0], self.arrived.at[origin],
            "row", target,
        )

    def local(self):
        return pltpu.make_async_copy(self.source, self.slot(self.r), self.other.at[1])

    def start(self):
        for gap in (2, -2, 1, -1):
            t = self.r + gap

            @pl.when((t >= 0) & (t < LINE))
            def _(t=t):
                self.own(t).start()

        self.local().start()

    def forward(self):
        for me, origin, target in ((2, 0, 3), (1, 3, 0)):

            @pl.when(self.r == me)
            def _(origin=origin, target=target):
                copy = self.handed(origin, target)
                copy.wait_recv()
                copy.start()

    def finish(self):
        r = self.r
        for t in range(LINE):
            known = (r == t) | ((r == 2) & (t == 0)) | ((r == 1) & (t == 3))
            near = (r != t) & (r - t < 3) & (t - r < 3)

            @pl.when(jnp.logical_not(known))
            def _(t=t):
                self.handed(t, t).wait_recv()

            @pl.when(near)
            def _(t=t):
                self.own(t).wait_send()

        for me, origin, target in ((2, 0, 3), (1, 3, 0)):

            @pl.when(r == me)
            def _(origin=origin, target=target):
                self.handed(origin, target).wait_send()

        self.local().wait()


class LineReduce:
    semaphores = (
        pltpu.SemaphoreType.DMA((LINE,)),
        pltpu.SemaphoreType.DMA((LINE,)),
        pltpu.SemaphoreType.DMA((2,)),
    )

    @staticmethod
    def buffers(rows, width):
        return [
            pltpu.VMEM((LINE, rows, width), jnp.bfloat16),
            pltpu.VMEM((rows, width), jnp.bfloat16),
        ]

    def __init__(self, source, parts, landed, passed, sent, arrived, other):
        self.r = lax.axis_index("row")
        self.source, self.parts, self.landed, self.passed = source, parts, landed, passed
        self.sent, self.arrived, self.other = sent, arrived, other

    def to_pass(self, me, origin, via):
        return send_to(
            self.source.at[origin], self.passed, self.sent.at[origin], self.other.at[0], "row", via
        )

    def direct(self, t):
        return send_to(
            self.source.at[t], self.landed.at[self.r], self.sent.at[t], self.arrived.at[self.r],
            "row", t,
        )

    def added(self, t):
        return send_to(
            self.passed, self.landed.at[self.r], self.sent.at[t], self.arrived.at[self.r], "row", t
        )

    def plain(self, t):
        r = self.r
        ends = ((r == 0) & (t == 3)) | ((r == 3) & (t == 0))
        added = ((r == 1) & (t == 3)) | ((r == 2) & (t == 0))
        return jnp.logical_not(ends | added | (r == t))

    def start(self):
        for me, end, via in ((0, 3, 1), (3, 0, 2)):

            @pl.when(self.r == me)
            def _(me=me, end=end, via=via):
                self.to_pass(me, end, via).start()

        for gap in (2, -2, 1, -1):
            t = self.r + gap

            @pl.when((t >= 0) & (t < LINE) & self.plain(t))
            def _(t=t):
                self.direct(t).start()

    def forward(self):
        for me, end in ((1, 3), (2, 0)):

            @pl.when(self.r == me)
            def _(me=me, end=end):
                self.to_pass(me, end, end).wait_recv()
                rows = self.passed.shape[0]
                step = 32

                def add(i, unused):
                    at = pl.ds(pl.multiple_of(i * step, step), step)
                    self.passed[at, :] = (
                        self.parts[end, at, :].astype(jnp.float32)
                        + self.passed[at, :].astype(jnp.float32)
                    ).astype(jnp.bfloat16)
                    return unused

                lax.fori_loop(0, rows // step, add, 0)
                self.added(end).start()

    def finish(self, write):
        r = self.r
        for t in range(LINE):

            @pl.when(jnp.logical_not(unsent_to(r, t)))
            def _(t=t):
                send_to(
                    self.source.at[t], self.landed.at[t], self.sent.at[t], self.arrived.at[t],
                    "row", t,
                ).wait_recv()

        def total_of(sources):
            step = 32

            def add(i, unused):
                at = pl.ds(pl.multiple_of(i * step, step), step)
                total = self.parts[r, at, :].astype(jnp.float32)
                for t in sources:
                    total = total + self.landed[t, at, :].astype(jnp.float32)
                write(at, total)
                return unused

            lax.fori_loop(0, self.passed.shape[0] // step, add, 0)

        at_end = (r == 0) | (r == 3)

        @pl.when(at_end)
        def _():
            total_of((1, 2))

        @pl.when(jnp.logical_not(at_end))
        def _():
            total_of((0, 3, 3 - r))

        for me, end, via in ((0, 3, 1), (3, 0, 2)):

            @pl.when(r == me)
            def _(me=me, end=end, via=via):
                self.to_pass(me, end, via).wait_send()

        for t in range(LINE):

            @pl.when(jnp.logical_not(unsent_to(r, t)))
            def _(t=t):
                self.direct(t).wait_send()


def unsent_to(r, t):
    return ((r == 0) & (t == 3)) | ((r == 3) & (t == 0)) | (r == t)


class PlaneGather:
    semaphores = (
        pltpu.SemaphoreType.DMA((PIECES, 7)),
        pltpu.SemaphoreType.DMA((PIECES, 7)),
        pltpu.SemaphoreType.DMA((PIECES,)),
    )
    first = tuple(range(PIECES // 2))
    second = tuple(range(PIECES // 2, PIECES))

    def __init__(self, block, full, sent, arrived, other, source=None, target=None):
        h = lax.axis_index("head")
        self.source, self.target = source, target
        self.h, self.side, self.x, self.y = h, sibling_of(h), across_of(h), along_of(h)
        self.far = across_of(self.y)
        self.block, self.full = block, full
        self.sent, self.arrived, self.other = sent, arrived, other
        self.rows = block.shape[0] // PIECES

    def piece(self, owner, c):
        rows = pl.ds(c * self.rows, self.rows)
        if self.target is None:
            return self.full.at[owner, rows]
        return self.full.at[owner, rows, self.target]

    def mine(self, c):
        rows = pl.ds(c * self.rows, self.rows)
        return self.block.at[rows] if self.source is None else self.block.at[rows, self.source]

    def own(self, c, lane, target):
        return send_to(
            self.mine(c), self.piece(self.h, c),
            self.sent.at[c, lane], self.arrived.at[c, lane], "head", target,
        )

    def hand(self, owner, c, lane, target):
        return send_to(
            self.piece(owner, c), self.piece(owner, c), self.sent.at[c, lane],
            self.arrived.at[c, lane], "head", target,
        )

    def local(self, c):
        return pltpu.make_async_copy(self.mine(c), self.piece(self.h, c), self.other.at[c])

    def start(self):
        for a, b in zip(self.first, self.second):
            self.own(a, 1, self.x).start()
            self.own(b, 2, self.y).start()
        for a, b in zip(self.first, self.second):
            self.own(b, 1, self.x).start()
            self.own(a, 2, self.y).start()
        for c in range(PIECES):
            self.own(c, 0, self.side).start()
            self.local(c).start()

    def relay(self, place):
        a, b = self.first[place], self.second[place]
        self.hand(self.x, a, 1, self.x).wait_recv()
        self.hand(self.x, a, 3, self.y).start()
        self.hand(self.x, a, 4, self.side).start()
        self.hand(self.y, b, 2, self.y).wait_recv()
        self.hand(self.y, b, 3, self.x).start()
        self.hand(self.y, b, 5, self.side).start()

    def rest(self):
        for a, b in zip(self.first, self.second):
            self.hand(self.x, b, 1, self.x).wait_recv()
            self.hand(self.x, b, 4, self.side).start()
            self.hand(self.y, a, 2, self.y).wait_recv()
            self.hand(self.y, a, 5, self.side).start()

    def beside(self):
        for c in range(PIECES):
            self.hand(self.side, c, 0, self.side).wait_recv()

    def far_side(self):
        for pair in zip(self.first, self.second):
            for c in pair:
                self.hand(self.far, c, 3, self.side).wait_recv()
                self.hand(self.far, c, 6, self.side).start()

    def end(self, beside=True):
        side = self.side
        if beside:
            self.beside()
        for c in range(PIECES):
            for owner, lane in (
                (across_of(side), 4), (along_of(side), 5), (across_of(along_of(side)), 6)
            ):
                self.hand(owner, c, lane, side).wait_recv()
        for c in range(PIECES):
            for lane in range(7):
                self.own(c, lane, side).wait_send()
            self.local(c).wait()


class PlaneReduce:
    semaphores = (
        pltpu.SemaphoreType.DMA((4,)),
        pltpu.SemaphoreType.DMA((4,)),
        pltpu.SemaphoreType.DMA((4, 2)),
        pltpu.SemaphoreType.DMA((2, 2)),
        pltpu.SemaphoreType.DMA((2,)),
    )

    @staticmethod
    def buffers(rows, width):
        return [
            pltpu.VMEM((4, rows, width), jnp.bfloat16),
            pltpu.VMEM((4, rows, width), jnp.bfloat16),
            pltpu.VMEM((4, rows, width), jnp.bfloat16),
            pltpu.VMEM((2, rows // 2, width), jnp.bfloat16),
            pltpu.VMEM((2, rows, width), jnp.bfloat16),
        ]

    def __init__(
        self, staged, beside, mine, relayed, landed,
        side_sent, side_arrived, sent, arrived, relay_arrived,
    ):
        h = lax.axis_index("head")
        self.h, self.core, self.chip = h, lax.rem(h, 2), lax.div(h, 2)
        self.staged, self.beside, self.mine = staged, beside, mine
        self.relayed, self.landed = relayed, landed
        self.side_sent, self.side_arrived = side_sent, side_arrived
        self.sent, self.arrived, self.relay_arrived = sent, arrived, relay_arrived
        self.half = mine.shape[1] // 2

    def aside(self, chip):
        return send_to(
            self.staged.at[chip], self.beside.at[chip], self.side_sent.at[chip],
            self.side_arrived.at[chip], "head", sibling_of(self.h),
        )

    def relation(self, chip):
        flip_x = lax.rem(chip + self.chip, 2)
        flip_y = lax.rem(lax.div(chip, 2) + lax.div(self.chip, 2), 2)
        return flip_x + 2 * flip_y

    def part(self, half):
        return pl.ds(half * self.half, self.half)

    def home(self, chip, way, half):
        return send_to(
            self.mine.at[chip, self.part(half)], self.landed.at[way, self.part(half)],
            self.sent.at[chip, half], self.arrived.at[way, half], "head",
            (across_of, along_of)[way](self.h),
        )

    def opposite(self, chip, half):
        return send_to(
            self.mine.at[chip, self.part(half)], self.relayed.at[half], self.sent.at[chip, half],
            self.relay_arrived.at[half], "head", (along_of, across_of)[half](self.h),
        )

    def put(self, block, value):
        chip, core = lax.div(block, 2), lax.rem(block, 2)

        @pl.when(core == self.core)
        def _():
            self.mine[chip] = value

        @pl.when(core != self.core)
        def _():
            self.staged[chip] = value
            self.aside(chip).start()

    def pass_on(self, block):
        chip, core = lax.div(block, 2), lax.rem(block, 2)

        @pl.when(core == self.core)
        def _():
            self.aside(chip).wait_recv()
            step = 32

            def add(i, unused):
                at = pl.ds(pl.multiple_of(i * step, step), step)
                self.mine[chip, at, :] = (
                    self.mine[chip, at, :].astype(jnp.float32)
                    + self.beside[chip, at, :].astype(jnp.float32)
                ).astype(jnp.bfloat16)
                return unused

            lax.fori_loop(0, 2 * self.half // step, add, 0)
            relation = self.relation(chip)

            @pl.when(relation == 1)
            def _():
                self.home(chip, 0, 1).start()

            @pl.when(relation == 2)
            def _():
                self.home(chip, 1, 0).start()

            @pl.when(relation == 3)
            def _():
                self.opposite(chip, 0).start()
                self.opposite(chip, 1).start()

    def relay(self, block):
        chip, core = lax.div(block, 2), lax.rem(block, 2)
        for way in (0, 1):

            @pl.when((core == self.core) & (self.relation(chip) == way + 1))
            def _(way=way):
                self.opposite(chip, way).wait_recv()
                step = 32

                def add(i, unused):
                    at = pl.ds(pl.multiple_of(i * step, step), step)
                    here = pl.ds(pl.multiple_of(way * self.half + i * step, step), step)
                    self.mine[chip, here, :] = (
                        self.mine[chip, here, :].astype(jnp.float32)
                        + self.relayed[way, at, :].astype(jnp.float32)
                    ).astype(jnp.bfloat16)
                    return unused

                lax.fori_loop(0, self.half // step, add, 0)
                self.home(chip, way, way).start()

    def arrive(self):
        for way in (0, 1):
            for half in (0, 1):
                self.home(self.chip, way, half).wait_recv()

    def total(self, at):
        value = self.mine[self.chip, at, :].astype(jnp.float32)
        return (
            value
            + self.landed[0, at, :].astype(jnp.float32)
            + self.landed[1, at, :].astype(jnp.float32)
        )

    def finish(self):
        for chip in range(4):
            self.aside(chip).wait_send()

            @pl.when(chip != self.chip)
            def _(chip=chip):
                self.home(chip, 0, 0).wait_send()
                self.home(chip, 0, 1).wait_send()


def norm_apply(rows, gain):
    return rows * lax.rsqrt(jnp.mean(rows * rows, axis=-1, keepdims=True) + EPSILON) * gain


def gather(values, axis_name, axis):
    return lax.all_gather(values, axis_name, axis=axis, tiled=True)


def scatter(values, axis_name, axis):
    return lax.psum_scatter(values, axis_name, scatter_dimension=axis, tiled=True)

def once(shape):
    return pl.BlockSpec(
        shape, lambda i: (0,) * len(shape), pipeline_mode=pl.Buffered(buffer_count=1)
    )


def norm_rows(rows, gain):
    return rows * lax.rsqrt(jnp.mean(rows * rows, axis=-1, keepdims=True) + EPSILON) * gain


def lay_out_params(
    taps_ref, rows_ref, gates_ref, resets_ref,
    taps_out, vec_out, wr_out, we_out, keep_out, square, moved,
):
    used, width = rows_ref.shape[1], gates_ref.shape[2]
    columns = vec_out.shape[1]
    taps_out[...] = jnp.zeros_like(taps_out)
    taps_out[:, 0:used] = taps_ref[...]
    vec_out[...] = jnp.zeros_like(vec_out)
    vec_out[3:4, :] = jnp.full((1, columns), 2.0, jnp.float32)
    vec_out[0:4, 0:used] = rows_ref[...]
    decay = vec_out[3:4, :]
    vec_out[3:4, :] = -8.0 * jnp.log1p(jnp.exp(-decay))
    vec_out[4:5, :] = 8.0 * jax.nn.sigmoid(-decay)
    for k, out in enumerate((wr_out, we_out)):
        square[...] = jnp.zeros_like(square)
        square[0:width, 0:width] = gates_ref[k, 1].astype(jnp.float32)
        moved[...] = pltpu.roll(pltpu.roll(square[...], width, 0), width, 1)
        square[...] = jnp.zeros_like(square)
        square[0:width, 0:width] = gates_ref[k, 0].astype(jnp.float32)
        out[...] = (square[...] + moved[...]).astype(jnp.bfloat16)
    resets = resets_ref[...]
    first = lax.broadcasted_iota(jnp.int32, resets.shape, 1) == 0
    one = jnp.where(first | (resets > 0), 0.0, 1.0)
    length = resets.shape[1]
    two = one * pltpu.roll(one, 1, 1)
    three = two * pltpu.roll(one, 2, 1)
    ahead = [pltpu.roll(item, length - k, 1) for k, item in ((1, one), (2, two), (3, three))]
    rows = jnp.concatenate(
        [one, one, two, three, *ahead, one, jnp.zeros((120, length), jnp.float32)], axis=0
    )
    for k in range(length // 128):
        turned = rows[:, k * 128 : (k + 1) * 128].T
        keep_out[k * 128 : (k + 1) * 128, :] = turned[:, 0:8]


def open_body(
    x_ref, mix_ref, ffn_ref, cot, xt_ref, yt_ref, ot_ref,
    taps_ref, rows_ref, gates_ref, resets_ref,
    full, cot_out, xy_full, out_full, mix_out, ffn_out, taps_out, vec_out, wr_out, we_out, keep_out,
    shards, blank, square, moved,
    normed, column, spread, gain_sent, gain_arrived, wide_sent, wide_arrived, wiped, *semaphores,
):
    r, h = lax.axis_index("row"), lax.axis_index("head")
    held_rows, share = shards.shape[1:]
    used, chans = xt_ref.shape[0], out_full.shape[0]

    def slot(full, first):
        def at(origin):
            lanes = pl.ds(pl.multiple_of(origin * share, share), share)
            return full.at[pl.ds(first, held_rows), lanes]

        return at

    lines = [
        LineGather(shards.at[k], slot(dst, first), *semaphores[3 * k : 3 * k + 3])
        for k, (dst, first) in enumerate(((xy_full, 0), (xy_full, chans), (out_full, 0)))
    ]
    wipes = [
        pltpu.make_async_copy(
            blank, dst.at[pl.ds(first + held_rows, chans - held_rows)], wiped.at[k]
        )
        for k, (dst, first) in enumerate(((xy_full, 0), (xy_full, chans), (out_full, 0)))
    ]
    plane = PlaneGather(normed, full, *semaphores[9:12])
    cot_plane = PlaneGather(
        cot, cot_out, *semaphores[12:15], source=pl.ds(0, cot_out.shape[2])
    )
    for k, source in enumerate((xt_ref, yt_ref, ot_ref)):
        shards[k, held_rows - 16 :, :] = jnp.zeros((16, share), jnp.bfloat16)
        shards[k, 0:used, :] = source[...]
    gain_share = mix_ref.shape[1]
    low = lax.broadcasted_iota(jnp.int32, (8, 2 * gain_share), 1) < gain_share
    column[r] = jnp.zeros_like(column[r])
    column[r, 0:1, 0:gain_share] = mix_ref[...].astype(jnp.float32)
    column[r, 1:2, 0:gain_share] = ffn_ref[...].astype(jnp.float32)
    rows = column[r]
    column[r] = jnp.where(low, rows, pltpu.roll(pltpu.roll(rows, gain_share, 1), 7, 0))
    meet(True, "all")

    def up_line(t):
        return send_to(
            column.at[r], column.at[r], gain_sent.at[t], gain_arrived.at[r], "row", t
        )

    def from_line(t):
        return send_to(
            column.at[t], column.at[t], gain_sent.at[t], gain_arrived.at[t], "row", t
        )

    def over_plane(step, owner):
        return send_to(
            column, spread.at[owner], wide_sent.at[step], wide_arrived.at[owner], "head",
            lax.rem(h + step, PLANE),
        )

    for step in range(1, LINE):
        up_line(lax.rem(r + step, LINE)).start()
    for line in lines:
        line.start()
    blank[...] = jnp.zeros_like(blank)
    for wipe in wipes:
        wipe.start()
    for step in range(1, LINE):
        from_line(lax.rem(r + step, LINE)).wait_recv()
    for step in range(1, PLANE):
        over_plane(step, h).start()
    cot_plane.start()
    spread[h] = column[...]
    for step in range(1, PLANE):
        over_plane(step, lax.rem(h + step, PLANE)).wait_recv()

    low = lax.broadcasted_iota(jnp.int32, (1, 2 * gain_share), 1) < gain_share
    for line_place in range(LINE):
        for pair in range(PLANE // 2):
            even = spread[2 * pair, line_place][0:1, :]
            odd = spread[2 * pair + 1, line_place][0:1, :]
            at = (line_place * (PLANE // 2) + pair) * 2 * gain_share
            end = at + 2 * gain_share
            mix_out[0:1, at:end] = jnp.where(low, even, pltpu.roll(odd, gain_share, 1))
            ffn_out[0:1, at:end] = jnp.where(low, pltpu.roll(even, gain_share, 1), odd)

    def make(i, unused):
        at = pl.ds(pl.multiple_of(i * CHUNK, CHUNK), CHUNK)
        normed[at, :] = norm_rows(x_ref[at, :].astype(jnp.float32), mix_out[...]).astype(
            jnp.bfloat16
        )
        return unused

    lax.fori_loop(0, x_ref.shape[0] // CHUNK, make, 0, unroll=UNROLL)
    plane.start()
    lay_out_params(
        taps_ref, rows_ref, gates_ref, resets_ref,
        taps_out, vec_out, wr_out, we_out, keep_out, square, moved,
    )
    cot_plane.relay(0)
    cot_plane.relay(1)
    lines[0].forward()
    cot_plane.rest()
    plane.relay(0)
    plane.relay(1)
    lines[1].forward()
    cot_plane.far_side()
    cot_plane.end()
    plane.rest()
    plane.far_side()
    plane.end()
    lines[2].forward()
    for line in lines:
        line.finish()
    for wipe in wipes:
        wipe.wait()
    for step in range(1, LINE):
        up_line(lax.rem(r + step, LINE)).wait_send()
    for step in range(1, PLANE):
        over_plane(step, h).wait_send()


def open_block(layer_in, gains, cot, weights, params):
    rows, width = layer_in.shape
    used, share = weights[0].shape
    chans, held_rows = -(-used // 128) * 128, -(-used // 16) * 16
    length = params[-1].shape[1]
    tile = (8, 2 * gains[0].shape[1])
    return pl.pallas_call(
        open_body,
        in_specs=[IN_VMEM, IN_VMEM, IN_VMEM, ANYWHERE] + [IN_VMEM] * 7,
        out_specs=[ANYWHERE] * 4 + [IN_VMEM] * 7,
        out_shape=[
            jax.ShapeDtypeStruct((PLANE, rows, width), jnp.bfloat16),
            jax.ShapeDtypeStruct((PLANE, rows, width // 2), jnp.bfloat16),
            jax.ShapeDtypeStruct((2 * chans, width), jnp.bfloat16),
            jax.ShapeDtypeStruct((chans, width), jnp.bfloat16),
            jax.ShapeDtypeStruct((1, width), jnp.float32),
            jax.ShapeDtypeStruct((1, width), jnp.float32),
            jax.ShapeDtypeStruct((4, chans), jnp.float32),
            jax.ShapeDtypeStruct((8, chans), jnp.float32),
            jax.ShapeDtypeStruct((chans, chans), jnp.bfloat16),
            jax.ShapeDtypeStruct((chans, chans), jnp.bfloat16),
            jax.ShapeDtypeStruct((length, 8), jnp.float32),
        ],
        scratch_shapes=[
            pltpu.VMEM((3, held_rows, share), jnp.bfloat16),
            pltpu.VMEM((chans - held_rows, width), jnp.bfloat16),
            pltpu.VMEM((chans, chans), jnp.float32),
            pltpu.VMEM((chans, chans), jnp.float32),
            pltpu.VMEM((rows, width), jnp.bfloat16),
            pltpu.VMEM((LINE,) + tile, jnp.float32),
            pltpu.VMEM((PLANE, LINE) + tile, jnp.float32),
            pltpu.SemaphoreType.DMA((LINE,)),
            pltpu.SemaphoreType.DMA((LINE,)),
            pltpu.SemaphoreType.DMA((PLANE,)),
            pltpu.SemaphoreType.DMA((PLANE,)),
            pltpu.SemaphoreType.DMA((3,)),
            *(LineGather.semaphores * 3),
            *(PlaneGather.semaphores * 2),
        ],
        compiler_params=pltpu.CompilerParams(
            collective_id=0, has_side_effects=True, vmem_limit_bytes=61 * 2**20
        ),
        name="open_block",
    )(layer_in, *gains, cot, *weights, *params)


def forward_linked_body(
    normed_ref, xy_hbm, ow_hbm, taps_ref, vec_ref, wr_ref, we_ref, keep_ref,
    x_hbm, gain_ref, gate_shard, up_shard,
    u_ref, by_ref, before_ref, states_ref, mixed_ref, residual_out, two_out, gate_out, up_out,
    xy_ref, ow_ref, x_ref, brought, residual_ref, two_ref, taken,
    window, conv, conv_low, rate, entry, carry, *links,
):
    step = pl.program_id(0)
    plane = PlaneReduce(*links[:10])
    gate_line = LineGather(gate_shard, lambda t: gate_out.at[t], *links[10:13])
    first_rows = up_shard.at[pl.ds(0, up_out.shape[1])]
    up_line = LineGather(first_rows, lambda t: up_out.at[t], *links[13:16])

    take = Bring((residual_ref, two_ref), (residual_out, two_out), taken)
    bring = Bring((xy_hbm, ow_hbm, x_hbm), (xy_ref, ow_ref, x_ref), brought)

    @pl.when(step == 0)
    def _():
        bring.start()
        meet(True, "near")
        gate_line.start()
        up_line.start()
        bring.wait(0, 1, 2)

    @pl.when(step > 0)
    def _():
        plane.pass_on(step - 1)

    @pl.when(step > 2)
    def _():
        plane.relay(step - 3)

    forward_step(
        normed_ref, xy_ref, taps_ref, vec_ref, wr_ref, we_ref, keep_ref,
        u_ref, by_ref, before_ref, states_ref, mixed_ref,
        window, conv, conv_low, rate, entry, carry,
    )
    plane.put(step, dot_plain(mixed_ref[...], ow_ref[...]).astype(jnp.bfloat16))

    @pl.when(step == 6)
    def _():
        gate_line.forward()

    @pl.when(step == PLANE - 1)
    def _():
        plane.relay(step - 2)
        plane.pass_on(step)
        plane.relay(step - 1)
        plane.relay(step)
        up_line.forward()
        plane.arrive()

        def make(i, unused):
            at = pl.ds(pl.multiple_of(i * CHUNK, CHUNK), CHUNK)
            residual = x_ref[at, :].astype(jnp.float32) + plane.total(at)
            residual_ref[at, :] = residual
            two_ref[at, :] = norm_rows(residual, gain_ref[...]).astype(jnp.bfloat16)
            return unused

        lax.fori_loop(0, x_ref.shape[0] // CHUNK, make, 0, unroll=UNROLL)
        take.start()
        plane.finish()
        gate_line.finish()
        up_line.finish()
        take.wait(0, 1)


def forward_linked(normed, xy, ow, taps, vec, wr, we, keep, layer_in, gain, gate_shard, up_shard):
    length, width = normed.shape
    chans = ow.shape[0]
    rows = length // PLANE
    share, units = up_shard.shape
    tile = lambda columns: pl.BlockSpec((rows, columns), lambda i: (i, 0))
    return pl.pallas_call(
        forward_linked_body,
        grid=(PLANE,),
        in_specs=[
            tile(width), ANYWHERE, ANYWHERE, once(taps.shape),
            once(vec.shape), once(wr.shape), once(we.shape), tile(keep.shape[1]),
            ANYWHERE, once(gain.shape), ANYWHERE, ANYWHERE,
        ],
        out_specs=[tile(chans)] * 5 + [ANYWHERE] * 4,
        out_shape=[
            jax.ShapeDtypeStruct((length, chans), jnp.bfloat16),
            jax.ShapeDtypeStruct((length, chans), jnp.float32),
            jax.ShapeDtypeStruct((length, chans), jnp.float32),
            jax.ShapeDtypeStruct((length, chans), jnp.bfloat16),
            jax.ShapeDtypeStruct((length, chans), jnp.bfloat16),
            jax.ShapeDtypeStruct((rows, width), jnp.float32),
            jax.ShapeDtypeStruct((rows, width), jnp.bfloat16),
            jax.ShapeDtypeStruct((LINE,) + gate_shard.shape, jnp.bfloat16),
            jax.ShapeDtypeStruct((LINE, share // 2, units), jnp.bfloat16),
        ],
        scratch_shapes=[
            *held(xy, ow, layer_in),
            pltpu.VMEM((rows, width), jnp.float32),
            pltpu.VMEM((rows, width), jnp.bfloat16),
            pltpu.SemaphoreType.DMA((2,)),
            pltpu.VMEM((rows + 8, chans), jnp.float32),
            pltpu.VMEM((rows, chans), jnp.float32),
            pltpu.VMEM((rows, chans), jnp.bfloat16),
            pltpu.VMEM((rows, chans), jnp.float32),
            pltpu.VMEM((rows, chans), jnp.float32),
            pltpu.VMEM((8, chans), jnp.float32),
            *PlaneReduce.buffers(rows, width),
            *PlaneReduce.semaphores,
            *(LineGather.semaphores * 2),
        ],
        compiler_params=pltpu.CompilerParams(
            collective_id=1, has_side_effects=True, vmem_limit_bytes=61 * 2**20
        ),
        name="mixer_forward_linked",
    )(normed, xy, ow, taps, vec, wr, we, keep, layer_in, gain, gate_shard, up_shard)


def ffn_up_body(
    own_two, gate_ref, own_cot, cot_half, up_half, up_shard, down_shard,
    two_out, cot_out, up_out, down_out, gates_out, ups_out, hidden_out, parts_out,
    two, cot, up, gates, ups, hidden, total, down_parts, copied, brought, *semaphores,
):
    h = lax.axis_index("head")
    rows = own_two.shape[0]
    units = gates.shape[1]
    width, share = own_two.shape[1], up_shard.shape[0]
    half = share // 2
    late_columns = pl.ds(width // 2, width // 2)
    up_line = LineGather(
        up_shard.at[pl.ds(half, half)],
        lambda t: up.at[pl.ds(pl.multiple_of(t * share + half, half), half)],
        *semaphores[0:3],
    )
    down_line = LineGather(down_shard, lambda t: down_out.at[t], *semaphores[3:6])
    two_plane = PlaneGather(own_two, two, *semaphores[6:9])
    cot_plane = PlaneGather(
        own_cot, cot, *semaphores[9:12], source=late_columns, target=late_columns
    )
    inward = [
        pltpu.make_async_copy(up_half.at[t], up.at[pl.ds(t * share, half)], brought.at[t])
        for t in range(LINE)
    ]
    inward.append(
        pltpu.make_async_copy(cot_half, cot.at[:, :, pl.ds(0, width // 2)], brought.at[LINE])
    )
    outward = [
        pltpu.make_async_copy(src, dst, copied.at[k])
        for k, (src, dst) in enumerate(
            (
                (two, two_out), (cot, cot_out), (up, up_out), (gates, gates_out),
                (ups, ups_out), (hidden, hidden_out), (down_parts, parts_out),
            )
        )
    ]
    meet(True, "near")
    up_line.start()
    down_line.start()
    two_plane.start()
    for copy in inward:
        copy.start()

    def at_block(block):
        return pl.ds(pl.multiple_of(block * rows, rows), rows)

    def make_gates(block):
        gates[at_block(block), :] = dot_plain(two[block], gate_ref[...])

    gates[at_block(h), :] = dot_plain(own_two[...], gate_ref[...])
    two_plane.relay(0)
    two_plane.beside()
    make_gates(two_plane.side)
    two_plane.relay(1)
    cot_plane.start()
    two_plane.rest()
    make_gates(two_plane.x)
    make_gates(two_plane.y)
    up_line.forward()
    two_plane.far_side()
    make_gates(two_plane.far)
    two_plane.end(beside=False)
    outward[0].start()
    cot_plane.relay(0)
    make_gates(across_of(two_plane.side))
    make_gates(along_of(two_plane.side))
    cot_plane.relay(1)
    make_gates(across_of(along_of(two_plane.side)))
    outward[3].start()
    up_line.finish()
    for copy in inward:
        copy.wait()
    outward[2].start()

    def make_hidden(block, unused):
        at = at_block(block)
        ups[at, :] = dot_plain(two[block], up[...])

        def make(i, unused):
            here = pl.ds(pl.multiple_of(block * rows + i * CHUNK, CHUNK), CHUNK)
            hidden[here, :] = (gelu_only(gates[here, :]) * ups[here, :]).astype(jnp.bfloat16)
            return unused

        lax.fori_loop(0, rows // CHUNK, make, 0, unroll=UNROLL)
        return unused

    lax.fori_loop(0, 2, make_hidden, 0)
    cot_plane.rest()
    lax.fori_loop(2, 5, make_hidden, 0)
    cot_plane.far_side()
    down_line.forward()
    lax.fori_loop(5, PLANE, make_hidden, 0)
    outward[4].start()
    outward[5].start()
    cot_plane.end()
    outward[1].start()
    total[...] = contract_first(cot[0], hidden[0:rows, :])

    def add_down(block, unused):
        total[...] += contract_first(cot[block], hidden[at_block(block), :])
        return unused

    lax.fori_loop(1, PLANE, add_down, 0)
    to_parts(total, down_parts)
    outward[6].start()
    down_line.finish()
    for copy in outward:
        copy.wait()


def ffn_up(own_two, gate, own_cot, cot_half, up_half, up_shard, down_shard):
    rows, width = own_two.shape
    share, units = up_shard.shape
    length = rows * PLANE
    group = jax.ShapeDtypeStruct((PLANE, rows, width), jnp.bfloat16)
    weight = jax.ShapeDtypeStruct((LINE, share, units), jnp.bfloat16)
    return pl.pallas_call(
        ffn_up_body,
        in_specs=[IN_VMEM, IN_VMEM] + [ANYWHERE] * 5,
        out_specs=[ANYWHERE] * 8,
        out_shape=[
            group,
            group,
            jax.ShapeDtypeStruct((width, units), jnp.bfloat16),
            weight,
            jax.ShapeDtypeStruct((length, units), jnp.float32),
            jax.ShapeDtypeStruct((length, units), jnp.float32),
            jax.ShapeDtypeStruct((length, units), jnp.bfloat16),
            weight,
        ],
        scratch_shapes=[
            pltpu.VMEM((PLANE, rows, width), jnp.bfloat16),
            pltpu.VMEM((PLANE, rows, width), jnp.bfloat16),
            pltpu.VMEM((width, units), jnp.bfloat16),
            pltpu.VMEM((length, units), jnp.float32),
            pltpu.VMEM((length, units), jnp.float32),
            pltpu.VMEM((length, units), jnp.bfloat16),
            pltpu.VMEM((width, units), jnp.float32),
            pltpu.VMEM((LINE, share, units), jnp.bfloat16),
            pltpu.SemaphoreType.DMA((7,)),
            pltpu.SemaphoreType.DMA((LINE + 1,)),
            *(LineGather.semaphores * 2),
            *(PlaneGather.semaphores * 2),
        ],
        compiler_params=pltpu.CompilerParams(
            collective_id=2, has_side_effects=True, vmem_limit_bytes=61 * 2**20
        ),
        name="ffn_up",
    )(own_two, gate, own_cot, cot_half, up_half, up_shard, down_shard)
def far_first(step):
    chip = lax.div(lax.axis_index("head"), 2)
    place = lax.div(step, 2)
    x = lax.rem(lax.rem(chip, 2) + 1 - lax.div(place, 2), 2)
    y = lax.rem(lax.div(chip, 2) + 1 + lax.rem(place, 2), 2)
    return 2 * (2 * y + x) + lax.rem(step, 2)


def norm_back(rows, gain, incoming):
    scale = lax.rsqrt(jnp.mean(rows * rows, axis=-1, keepdims=True) + EPSILON)
    scaled = incoming * gain
    inner = jnp.mean(scaled * rows, axis=-1, keepdims=True)
    return scale * scaled - rows * (scale * scale * scale * inner), incoming * rows * scale


def to_parts(total, parts):
    rows = parts.shape[1]
    step = 64

    def move(i, unused):
        at = pl.ds(pl.multiple_of(i * step, step), step)
        for t in range(LINE):
            here = pl.ds(pl.multiple_of(t * rows + i * step, step), step)
            parts[t, at, :] = total[here, :].astype(jnp.bfloat16)
        return unused

    lax.fori_loop(0, rows // step, move, 0)


def to_turned_parts(total, parts, places):
    share = parts.shape[2]
    step = 32
    for first, target, count in places:

        def move(i, unused, first=first, target=target):
            here = pl.ds(pl.multiple_of(first + i * step, step), step)
            at = pl.ds(pl.multiple_of(target + i * step, step), step)
            for t in range(LINE):
                parts[t, at, :] = total[here, t * share : (t + 1) * share].astype(jnp.bfloat16)
            return unused

        lax.fori_loop(0, count // step, move, 0)


def ffn_back_body(
    cot_ref, two_ref, gates_ref, ups_ref, gate_hbm, up_hbm, down_hbm, parts_hbm,
    residual_hbm, own_cot_hbm, gain_ref,
    d_ups_ref, parts_out, down_out, d_res_ref, d_low_ref, gain_out,
    gate_ref, up_ref, down_ref, parts, brought, late, gate_parts, taken,
    total, d_gates, d_hidden, eight, *links,
):
    step = pl.program_id(0)
    line = LineReduce(parts_hbm, parts, *links[:5])
    plane = PlaneReduce(*links[5:])
    rows = cot_ref.shape[0]

    bring = Bring(
        (down_hbm, gate_hbm, up_hbm, parts_hbm), (down_ref, gate_ref, up_ref, parts), brought
    )
    take = Bring((gate_parts,), (parts_out,), taken)
    into_outputs = Bring((residual_hbm, own_cot_hbm), (d_res_ref, d_low_ref), late)

    @pl.when(step == 0)
    def _():
        bring.start()
        meet(True, "near")
        line.start()
        into_outputs.start()
        bring.wait(0, 1, 2, 3)

    @pl.when((step > 2) & (step <= PLANE + 2))
    def _():
        plane.relay(far_first(step - 3))

    @pl.when(step < PLANE)
    def _():
        d_hidden[...] = dot_plain(cot_ref[...], down_ref[...])

        def make(i, unused):
            at = pl.ds(pl.multiple_of(i * CHUNK, CHUNK), CHUNK)
            gelu_gate, slope = gelu_both(gates_ref[at, :])
            through = d_hidden[at, :]
            d_gates[step, at, :] = (through * ups_ref[at, :] * slope).astype(jnp.bfloat16)
            d_ups_ref[at, :] = (through * gelu_gate).astype(jnp.bfloat16)
            return unused

        lax.fori_loop(0, rows // CHUNK, make, 0, unroll=UNROLL)

        @pl.when(step > 0)
        def _():
            plane.pass_on(far_first(step - 1))

        value = contract_last(d_gates[step], gate_ref[...]) + contract_last(
            d_ups_ref[...], up_ref[...]
        )
        plane.put(far_first(step), value.astype(jnp.bfloat16))

    @pl.when(step == PLANE)
    def _():
        total[...] = contract_first(two_ref[...], d_gates[0])

    @pl.when(step > PLANE)
    def _():
        total[...] += contract_first(two_ref[...], d_gates[step - PLANE])

    @pl.when(step == PLANE)
    def _():
        plane.pass_on(far_first(step - 1))

    @pl.when(step == 3)
    def _():
        line.forward()

    @pl.when(step == 2 * PLANE - 1)
    def _():
        to_parts(total, gate_parts)
        take.start()
        plane.arrive()
        into_outputs.wait(0, 1)
        eight[...] = jnp.zeros_like(eight)

        def back(i, unused):
            at = pl.ds(pl.multiple_of(i * CHUNK, CHUNK), CHUNK)
            d_rows, d_gain = norm_back(d_res_ref[at, :], gain_ref[...], plane.total(at))
            d_residual = d_low_ref[at, :].astype(jnp.float32) + d_rows
            d_res_ref[at, :] = d_residual
            d_low_ref[at, :] = d_residual.astype(jnp.bfloat16)
            eight[...] += sum_eight(d_gain)
            return unused

        lax.fori_loop(0, rows // CHUNK, back, 0, unroll=UNROLL)
        gain_out[...] = jnp.sum(eight[...], axis=0, keepdims=True)

        def write(at, value):
            down_out[at, :] = value

        line.finish(write)
        plane.finish()
        take.wait(0)


def ffn_back(
    cot_group, two_group, gates, ups, gate, up, down, parts, residual, own_cot, gain
):
    length, width = cot_group.shape
    units = gate.shape[1]
    rows, share = length // PLANE, width // LINE
    tile = lambda columns: pl.BlockSpec(
        (rows, columns), lambda i: (far_first(jnp.minimum(i, PLANE - 1)), 0)
    )
    later = lambda columns: pl.BlockSpec(
        (rows, columns), lambda i: (far_first(jnp.maximum(i - PLANE, 0)), 0)
    )
    return pl.pallas_call(
        ffn_back_body,
        grid=(2 * PLANE,),
        in_specs=[
            tile(width), later(width), tile(units), tile(units),
            *([ANYWHERE] * 6), once(gain.shape),
        ],
        out_specs=[
            tile(units), ANYWHERE, once((share, units)),
            once((rows, width)), once((rows, width)), once((1, width)),
        ],
        out_shape=[
            jax.ShapeDtypeStruct((length, units), jnp.bfloat16),
            jax.ShapeDtypeStruct((LINE, share, units), jnp.bfloat16),
            jax.ShapeDtypeStruct((share, units), jnp.float32),
            jax.ShapeDtypeStruct((rows, width), jnp.float32),
            jax.ShapeDtypeStruct((rows, width), jnp.bfloat16),
            jax.ShapeDtypeStruct((1, width), jnp.float32),
        ],
        scratch_shapes=[
            *held(gate, up, down, parts),
            pltpu.SemaphoreType.DMA((2,)),
            *held(parts),
            pltpu.VMEM((width, units), jnp.float32),
            pltpu.VMEM((PLANE, rows, units), jnp.bfloat16),
            pltpu.VMEM((rows, units), jnp.float32),
            pltpu.VMEM((8, width), jnp.float32),
            *LineReduce.buffers(share, units),
            *LineReduce.semaphores,
            *PlaneReduce.buffers(rows, width),
            *PlaneReduce.semaphores,
        ],
        compiler_params=pltpu.CompilerParams(
            collective_id=4, has_side_effects=True, vmem_limit_bytes=63 * 2**20
        ),
        name="ffn_back",
    )(cot_group, two_group, gates, ups, gate, up, down, parts, residual, own_cot, gain)


def turn_body(
    two_ref, d_ups_ref, parts_hbm, block, mixed_hbm, ow_hbm,
    up_hbm, out_hbm, gate_out, d_mixed_hbm,
    gate_parts, mixed_ref, ow_ref, brought, up_parts, out_parts, d_mixed_out, taken,
    full, total, out_total, *links,
):
    step = pl.program_id(0)
    line = LineReduce(parts_hbm, gate_parts, *links[:5])
    plane = PlaneGather(block, full, *links[5:])
    rows = two_ref.shape[0]

    take = Bring(
        (up_parts, out_parts, d_mixed_out), (up_hbm, out_hbm, d_mixed_hbm), taken
    )
    bring = Bring(
        (parts_hbm, mixed_hbm, ow_hbm), (gate_parts, mixed_ref, ow_ref), brought
    )

    @pl.when(step == 0)
    def _():
        bring.start()
        meet(True, "near")
        line.start()
        plane.start()
        total[...] = contract_first(two_ref[...], d_ups_ref[...])

    @pl.when(step > 0)
    def _():
        total[...] += contract_first(two_ref[...], d_ups_ref[...])

    @pl.when(step == 3)
    def _():
        plane.relay(0)

    @pl.when(step == PLANE - 2)
    def _():
        bring.wait(0)
        line.forward()
        plane.relay(1)

    @pl.when(step == PLANE - 1)
    def _():
        bring.wait(1, 2)

        def add(owner, start=False):
            at = pl.ds(pl.multiple_of(owner * rows, rows), rows)
            d_mixed_out[at, :] = contract_last(full[owner], ow_ref[...])
            value = contract_first(mixed_ref[at, :], full[owner])
            out_total[...] = value if start else out_total[...] + value

        plane.beside()
        add(plane.side, start=True)
        to_parts(total, up_parts)
        take.copies[0].start()
        plane.rest()
        add(plane.x)
        add(plane.y)
        plane.far_side()
        add(plane.far)
        plane.end(beside=False)
        add(plane.h)
        add(across_of(plane.side))
        add(along_of(plane.side))
        add(across_of(along_of(plane.side)))
        take.copies[2].start()
        kept = out_parts.shape[1]
        to_turned_parts(out_total, out_parts, ((0, 0, kept),))
        take.copies[1].start()

        def write(at, value):
            gate_out[at, :] = value

        line.finish(write)
        take.wait(0, 1, 2)


def turn(two_group, d_ups, gate_parts, block, mixed, ow, kept):
    length, width = two_group.shape
    units, chans = d_ups.shape[1], mixed.shape[1]
    rows, share = length // PLANE, width // LINE
    tile = lambda columns: pl.BlockSpec((rows, columns), lambda i: (i, 0))
    return pl.pallas_call(
        turn_body,
        grid=(PLANE,),
        in_specs=[
            tile(width), tile(units), ANYWHERE, ANYWHERE, ANYWHERE, ANYWHERE,
        ],
        out_specs=[
            ANYWHERE, ANYWHERE, once((share, units)), ANYWHERE,
        ],
        out_shape=[
            jax.ShapeDtypeStruct(gate_parts.shape, jnp.bfloat16),
            jax.ShapeDtypeStruct((LINE, kept, share), jnp.bfloat16),
            jax.ShapeDtypeStruct((share, units), jnp.float32),
            jax.ShapeDtypeStruct((length, chans), jnp.float32),
        ],
        scratch_shapes=[
            *held(gate_parts, mixed, ow),
            pltpu.VMEM(gate_parts.shape, jnp.bfloat16),
            pltpu.VMEM((LINE, kept, share), jnp.bfloat16),
            pltpu.VMEM((length, chans), jnp.float32),
            pltpu.SemaphoreType.DMA((3,)),
            pltpu.VMEM((PLANE, rows, width), jnp.bfloat16),
            pltpu.VMEM((width, units), jnp.float32),
            pltpu.VMEM((chans, width), jnp.float32),
            *LineReduce.buffers(share, units),
            *LineReduce.semaphores,
            *PlaneGather.semaphores,
        ],
        compiler_params=pltpu.CompilerParams(
            collective_id=5, has_side_effects=True, vmem_limit_bytes=61 * 2**20
        ),
        name="turn",
    )(two_group, d_ups, gate_parts, block, mixed, ow)


def pack_small(head_width, taps, vec, params, wr, we, small):
    columns = small.shape[1]
    step = 16
    last = (2 * head_width + 7) // 8 * 8

    def move(i, unused):
        at = pl.ds(pl.multiple_of(i * step, step), step)
        shape = (step, columns)
        row = lax.broadcasted_iota(jnp.int32, shape, 0) + i * step
        left = lax.broadcasted_iota(jnp.int32, shape, 1) < head_width
        rate, entry = wr[at, :], we[at, :]
        first = jnp.where(left, rate, pltpu.roll(entry, head_width, 1))
        second = jnp.where(left, pltpu.roll(rate, columns - head_width, 1), entry)
        small[at, :] = jnp.where(row < head_width, first, second).astype(jnp.bfloat16)
        return unused

    lax.fori_loop(0, last // step, move, 0)
    scaled = vec[0:4, :] * jnp.concatenate(
        [jnp.ones((3, columns), jnp.float32), params[4:5, :]], axis=0
    )
    tail = jnp.concatenate([taps[...], scaled], axis=0).astype(jnp.bfloat16)
    here = last // step * step
    rate, entry = wr[here : here + 8, :], we[here : here + 8, :]
    left = lax.broadcasted_iota(jnp.int32, (8, columns), 1) < head_width
    rest = jnp.where(left, pltpu.roll(rate, columns - head_width, 1), entry).astype(jnp.bfloat16)
    small[here : here + 16, :] = jnp.concatenate([rest, tail], axis=0)
    if small.shape[0] > here + 16:
        small[here + 16 :, :] = jnp.zeros_like(small[here + 16 :, :])


def split_gains(mix, ffn, out):
    share = out.shape[2] // 2
    low = lax.broadcasted_iota(jnp.int32, (1, 2 * share), 1) < share
    for r in range(LINE):
        lines = []
        for pair in range(PLANE // 2):
            at = (r * (PLANE // 2) + pair) * 2 * share
            one, two = mix[:, at : at + 2 * share], ffn[:, at : at + 2 * share]
            lines.append(jnp.where(low, one, pltpu.roll(two, share, 1)))
            lines.append(jnp.where(low, pltpu.roll(one, share, 1), two))
        out[r] = jnp.concatenate(lines, axis=0)


def backward_linked_body(
    head_width,
    d_mixed_ref, xy_hbm, taps_ref, vec_ref, wr_ref, we_ref, keep_ref,
    u_ref, u_prev_ref, by_ref, before_ref, states_ref, normed_ref, up_hbm, out_hbm,
    x_hbm, gain_ref, d_residual_hbm, ffn_gain_ref,
    parts_out, up_out, out_out, in_grad, gains_out, small_out,
    xy_ref, up_parts, out_parts, brought, late, xy_parts, taken,
    out_sum, taps_sum, vec_sum, wr_sum, we_sum, small, small_parts, d_xy, d_all, xy_total, eight, *rest,
):
    scratch, links = rest[:10], rest[10:]
    step = pl.program_id(0)
    block = PLANE - 1 - step
    line = LineReduce(up_hbm, up_parts, *links[:5])
    out_line = LineReduce(out_hbm, out_parts, *links[5:10])
    small_line = LineReduce(small_parts, small_parts, *links[10:15])
    plane = PlaneReduce(*links[15:])

    bring = Bring(
        (xy_hbm, up_hbm, out_hbm), (xy_ref, up_parts, out_parts), brought
    )
    take = Bring((xy_parts,), (parts_out,), taken)
    d_residual_ref = xy_total.at[0 : x_hbm.shape[0]]
    bring_late = Bring((x_hbm, d_residual_hbm), (in_grad, d_residual_ref), late)

    @pl.when(step == 0)
    def _():
        bring.start()
        meet(True, "near")
        line.start()
        out_line.start()
        bring.wait(0, 1, 2)

    @pl.when((step > 0) & (step <= PLANE))
    def _():
        plane.pass_on(block + 1)

    @pl.when((step > 2) & (step <= PLANE))
    def _():
        plane.relay(block + 3)

    @pl.when(step == 3)
    def _():
        line.forward()

    @pl.when(step < PLANE)
    def _():
        backward_step(
            step == 0, step == PLANE - 1, d_mixed_ref, taps_ref, vec_ref, wr_ref, we_ref,
            keep_ref, u_ref, u_prev_ref, by_ref, before_ref, states_ref, d_xy,
            taps_sum, vec_sum, wr_sum, we_sum, *scratch,
        )
        d_all[step] = d_xy[...]
        plane.put(block, dot_plain(d_xy[...], xy_ref[...]).astype(jnp.bfloat16))

    @pl.when(step == PLANE)
    def _():
        pack_small(head_width, taps_sum, vec_sum, vec_ref, wr_sum, we_sum, small)
        share = small_parts.shape[1]
        for t in range(LINE):
            small_parts[t] = small[t * share : (t + 1) * share, :]
        small_line.start()
        xy_total[...] = contract_first(d_all[0], normed_ref[...])

    @pl.when(step > PLANE)
    def _():
        xy_total[...] += contract_first(d_all[step - PLANE], normed_ref[...])

    @pl.when(step == PLANE + 2)
    def _():
        plane.relay(1)

    @pl.when(step == PLANE + 4)
    def _():
        out_line.forward()

    @pl.when(step == PLANE + 5)
    def _():
        plane.relay(0)

    @pl.when(step == 2 * PLANE - 1)
    def _():
        small_line.forward()
        kept, chans = out_parts.shape[1], d_xy.shape[1] // 2
        to_turned_parts(xy_total, xy_parts, ((0, 0, kept), (chans, kept, kept)))
        bring_late.start()
        take.start()

        def write(at, value):
            up_out[at, :] = value

        line.finish(write)
        plane.arrive()
        bring_late.wait(0, 1)
        eight[...] = jnp.zeros_like(eight)

        def back(i, unused):
            at = pl.ds(pl.multiple_of(i * CHUNK, CHUNK), CHUNK)
            d_rows, d_gain = norm_back(
                in_grad[at, :].astype(jnp.float32), gain_ref[...], plane.total(at)
            )
            in_grad[at, :] = (xy_total[at, :] + d_rows).astype(jnp.bfloat16)
            eight[...] += sum_eight(d_gain)
            return unused

        lax.fori_loop(0, in_grad.shape[0] // CHUNK, back, 0, unroll=UNROLL)
        split_gains(jnp.sum(eight[...], axis=0, keepdims=True), ffn_gain_ref[...], gains_out)

        def write_out(at, value):
            out_sum[at, :] = value

        def write_small(at, value):
            small_out[at, :] = value.astype(jnp.bfloat16)

        out_line.finish(write_out)
        out_out[...] = out_sum[0 : out_out.shape[0], :]
        small_line.finish(write_small)
        plane.finish()
        take.wait(0)


def backward_linked(
    d_mixed, xy, taps, vec, wr, we, keep, u, by, before, states, normed, up_parts, out_parts,
    layer_in, gain, d_residual, ffn_gain, head_width, used,
):
    length, width = normed.shape
    chans, units = d_mixed.shape[1], up_parts.shape[2]
    rows, share = length // PLANE, width // LINE
    kept = out_parts.shape[1]
    place = lambda i: PLANE - 1 - jnp.minimum(i, PLANE - 1)
    tile = lambda columns: pl.BlockSpec((rows, columns), lambda i: (place(i), 0))
    later = lambda columns: pl.BlockSpec(
        (rows, columns), lambda i: (PLANE - 1 - jnp.maximum(i - PLANE, 0), 0)
    )
    ahead = pl.BlockSpec((16, chans), lambda i: (jnp.maximum(place(i) * (rows // 16) - 1, 0), 0))
    small_share = -(-((2 * head_width + 7) // 8 * 8 + 8) // (LINE * 32)) * 32
    gain_terms = (LINE, PLANE, width // (LINE * PLANE) * 2)
    return pl.pallas_call(
        functools.partial(backward_linked_body, head_width),
        grid=(2 * PLANE,),
        in_specs=[
            tile(chans), ANYWHERE, once(taps.shape), once(vec.shape), once(wr.shape),
            once(we.shape), tile(keep.shape[1]), tile(chans), ahead, tile(chans), tile(chans),
            tile(chans), later(width), ANYWHERE, ANYWHERE,
            ANYWHERE, once(gain.shape), ANYWHERE, once(ffn_gain.shape),
        ],
        out_specs=[
            ANYWHERE, once((share, units)), once((used, share)),
            once((rows, width)), once(gain_terms), once((small_share, chans)),
        ],
        out_shape=[
            jax.ShapeDtypeStruct((LINE, 2 * kept, share), jnp.bfloat16),
            jax.ShapeDtypeStruct((share, units), jnp.float32),
            jax.ShapeDtypeStruct((used, share), jnp.float32),
            jax.ShapeDtypeStruct((rows, width), jnp.bfloat16),
            jax.ShapeDtypeStruct(gain_terms, jnp.float32),
            jax.ShapeDtypeStruct((small_share, chans), jnp.bfloat16),
        ],
        scratch_shapes=[
            *held(xy, up_parts, out_parts),
            pltpu.SemaphoreType.DMA((2,)),
            pltpu.VMEM((LINE, 2 * kept, share), jnp.bfloat16),
            pltpu.SemaphoreType.DMA((1,)),
            pltpu.VMEM((kept, share), jnp.float32),
            pltpu.VMEM(taps.shape, jnp.float32),
            pltpu.VMEM(vec.shape, jnp.float32),
            pltpu.VMEM(wr.shape, jnp.float32),
            pltpu.VMEM(we.shape, jnp.float32),
            pltpu.VMEM((LINE * small_share, chans), jnp.bfloat16),
            pltpu.VMEM((LINE, small_share, chans), jnp.bfloat16),
            pltpu.VMEM((rows, 2 * chans), jnp.bfloat16),
            pltpu.VMEM((PLANE, rows, 2 * chans), jnp.bfloat16),
            pltpu.VMEM((2 * chans, width), jnp.float32),
            pltpu.VMEM((8, width), jnp.float32),
            pltpu.VMEM((rows + 8, chans), jnp.float32),
            pltpu.VMEM((rows, chans), jnp.float32),
            pltpu.VMEM((rows, chans), jnp.bfloat16),
            pltpu.VMEM((rows, chans), jnp.float32),
            pltpu.VMEM((rows, chans), jnp.float32),
            pltpu.VMEM((rows + 8, chans), jnp.float32),
            pltpu.VMEM((rows, chans), jnp.bfloat16),
            pltpu.VMEM((rows, chans), jnp.bfloat16),
            pltpu.VMEM((8, chans), jnp.float32),
            pltpu.VMEM((64, chans), jnp.float32),
            *LineReduce.buffers(share, units),
            *LineReduce.semaphores,
            *LineReduce.buffers(kept, share),
            *LineReduce.semaphores,
            *LineReduce.buffers(small_share, chans),
            *LineReduce.semaphores,
            *PlaneReduce.buffers(rows, width),
            *PlaneReduce.semaphores,
        ],
        compiler_params=pltpu.CompilerParams(
            collective_id=6, has_side_effects=True, vmem_limit_bytes=61 * 2**20
        ),
        name="mixer_backward_linked",
    )(
        d_mixed, xy, taps, vec, wr, we, keep, u, u, by, before, states, normed,
        up_parts, out_parts, layer_in, gain, d_residual, ffn_gain,
    )


def close_body(
    hidden_ref, down_hbm, xy_hbm, residual_hbm, gains_ref, small,
    layer_out, x_out, y_out, gains_out, small_out,
    down_ref, xy_parts, residual_ref, brought, xy_sum,
    gathered, line_gains, both_gains, plane_gains,
    gain_sent, gain_arrived, wide_sent, wide_arrived, *links,
):
    r, h = lax.axis_index("row"), lax.axis_index("head")
    step = pl.program_id(0)
    xy_line = LineReduce(xy_hbm, xy_parts, *links[0:5])
    small_line = LineGather(small, lambda t: gathered.at[t], *links[5:8])
    plane = PlaneReduce(*links[8:])

    def to_row(t, owner):
        return send_to(
            gains_ref.at[t], line_gains.at[owner], gain_sent.at[t], gain_arrived.at[owner],
            "row", t,
        )

    def over_plane(place, owner):
        return send_to(
            both_gains, plane_gains.at[owner], wide_sent.at[place], wide_arrived.at[owner],
            "head", lax.rem(h + place, PLANE),
        )

    bring = Bring(
        (down_hbm, xy_hbm, residual_hbm), (down_ref, xy_parts, residual_ref), brought
    )

    @pl.when(step == 0)
    def _():
        bring.start()
        meet(True, "all")
        for place in range(1, LINE):
            to_row(lax.rem(r + place, LINE), r).start()
        small_line.start()
        xy_line.start()
        bring.wait(0, 1, 2)

    @pl.when(step > 0)
    def _():
        plane.pass_on(far_first(step - 1))

    @pl.when(step > 2)
    def _():
        plane.relay(far_first(step - 3))

    plane.put(far_first(step), contract_last(hidden_ref[...], down_ref[...]).astype(jnp.bfloat16))

    @pl.when(step == 2)
    def _():
        total = gains_ref[r]
        for place in range(1, LINE):
            t = lax.rem(r + place, LINE)
            to_row(t, t).wait_recv()
            total = total + line_gains[t]
        both_gains[...] = total
        for place in range(1, PLANE):
            over_plane(place, h).start()

    @pl.when(step == PLANE - 1)
    def _():
        small_line.forward()
        xy_line.forward()
        plane.relay(far_first(step - 2))
        plane.pass_on(far_first(step))
        plane.relay(far_first(step - 1))
        plane.relay(far_first(step))
        total = both_gains[...]
        for place in range(1, PLANE):
            owner = lax.rem(h + place, PLANE)
            over_plane(place, owner).wait_recv()
            total = total + plane_gains[owner]
        mine = lax.broadcasted_iota(jnp.int32, total.shape, 0) == h
        gains_out[...] = jnp.sum(jnp.where(mine, total, 0.0), axis=0, keepdims=True)
        plane.arrive()

        def make(i, unused):
            at = pl.ds(pl.multiple_of(i * CHUNK, CHUNK), CHUNK)
            layer_out[at, :] = (residual_ref[at, :] + plane.total(at)).astype(jnp.bfloat16)
            return unused

        lax.fori_loop(0, residual_ref.shape[0] // CHUNK, make, 0)
        def write(at, value):
            xy_sum[at, :] = value

        xy_line.finish(write)
        used, kept = x_out.shape[0], xy_sum.shape[0] // 2
        x_out[...] = xy_sum[0:used, :]
        y_out[...] = xy_sum[kept : kept + used, :]
        small_line.finish()
        small_out[...] = gathered[...].astype(jnp.float32)
        plane.finish()
        for place in range(1, LINE):
            to_row(lax.rem(r + place, LINE), r).wait_send()
        for place in range(1, PLANE):
            over_plane(place, h).wait_send()


def close_block(hidden, down, xy_parts, residual, gains, small, used):
    length, units = hidden.shape
    rows, width = residual.shape
    both, share = xy_parts.shape[1:]
    return pl.pallas_call(
        close_body,
        grid=(PLANE,),
        in_specs=[
            pl.BlockSpec((rows, units), lambda i: (far_first(i), 0)), ANYWHERE,
            ANYWHERE, ANYWHERE, once(gains.shape), once(small.shape),
        ],
        out_specs=[
            once((rows, width)), once((used, share)), once((used, share)), once((1, gains.shape[2])),
            once((LINE,) + small.shape),
        ],
        out_shape=[
            jax.ShapeDtypeStruct((rows, width), jnp.bfloat16),
            jax.ShapeDtypeStruct((used, share), jnp.float32),
            jax.ShapeDtypeStruct((used, share), jnp.float32),
            jax.ShapeDtypeStruct((1, gains.shape[2]), jnp.float32),
            jax.ShapeDtypeStruct((LINE,) + small.shape, jnp.float32),
        ],
        scratch_shapes=[
            *held(down, xy_parts, residual),
            pltpu.VMEM((both, share), jnp.float32),
            pltpu.VMEM((LINE,) + small.shape, jnp.bfloat16),
            pltpu.VMEM(gains.shape, jnp.float32),
            pltpu.VMEM(gains.shape[1:], jnp.float32),
            pltpu.VMEM((PLANE,) + gains.shape[1:], jnp.float32),
            pltpu.SemaphoreType.DMA((LINE,)),
            pltpu.SemaphoreType.DMA((LINE,)),
            pltpu.SemaphoreType.DMA((PLANE,)),
            pltpu.SemaphoreType.DMA((PLANE,)),
            *LineReduce.buffers(both, share), *LineReduce.semaphores,
            *LineGather.semaphores,
            *PlaneReduce.buffers(rows, width), *PlaneReduce.semaphores,
        ],
        compiler_params=pltpu.CompilerParams(
            collective_id=7, has_side_effects=True, vmem_limit_bytes=61 * 2**20
        ),
        name="close_block",
    )(hidden, down, xy_parts, residual, gains, small)


def hand_over_body(*refs):
    count = (len(refs) - 2) // 3
    sources, targets, held = refs[:count], refs[count : 2 * count], refs[2 * count : 3 * count]
    inward, outward = (
        [
            pltpu.make_async_copy(src, dst, done.at[k])
            for k, (src, dst) in enumerate(zip(starts, ends))
        ]
        for starts, ends, done in ((sources, held, refs[-2]), (held, targets, refs[-1]))
    )
    for copy in inward:
        copy.start()
    for first, second in zip(inward, outward):
        first.wait()
        second.start()
    for copy in outward:
        copy.wait()


def hand_over(*arrays):
    return pl.pallas_call(
        hand_over_body,
        in_specs=[ANYWHERE] * len(arrays),
        out_specs=[ANYWHERE] * len(arrays),
        out_shape=[jax.ShapeDtypeStruct(item.shape, item.dtype) for item in arrays],
        scratch_shapes=[pltpu.VMEM(item.shape, item.dtype) for item in arrays]
        + [pltpu.SemaphoreType.DMA((len(arrays),))] * 2,
        compiler_params=pltpu.CompilerParams(vmem_limit_bytes=61 * 2**20),
        name="hand_over",
    )(*arrays)


def mixer_params(
    conv_weight, conv_bias, rate_weight, rate_bias, entry_weight, entry_bias, decay_param, chans
):
    used = conv_bias.shape[0]
    spare = (0, chans - used)
    decay_wide = jnp.pad(decay_param, spare, constant_values=2.0)
    blank = jnp.zeros((chans,), jnp.float32)
    vec = jnp.stack(
        [
            jnp.pad(conv_bias, spare),
            jnp.pad(rate_bias, spare),
            jnp.pad(entry_bias, spare),
            -8.0 * jax.nn.softplus(-decay_wide),
            8.0 * jax.nn.sigmoid(-decay_wide),
            blank,
            blank,
            blank,
        ]
    )
    taps = jnp.pad(conv_weight, ((0, 0), spare))
    return taps, vec, block_diagonal(rate_weight, chans), block_diagonal(entry_weight, chans)


def shards(
    layer_in,
    cotangent,
    mix_gain,
    ffn_gain,
    x_weight,
    y_weight,
    out_weight,
    conv_weight,
    conv_bias,
    rate_weight,
    rate_bias,
    entry_weight,
    entry_bias,
    decay_param,
    gate_weight,
    up_weight,
    down_weight,
    resets,
):
    heads, head_width = rate_weight.shape[:2]
    used = conv_bias.shape[0]
    chans = -(-used // 128) * 128
    widen = lambda values: jnp.pad(values, ((0, 0), (0, chans - used)))
    mix_full = gather(mix_gain, ("row", "head"), 0)
    ffn_full = gather(ffn_gain, ("row", "head"), 0)
    xy_shard = jnp.concatenate([widen(x_weight), widen(y_weight)], axis=1)
    xy_rows = gather(xy_shard, "row", 0).T
    out_rows = gather(widen(out_weight), "row", 0).T
    gate_rows = gather(gate_weight, "row", 0)
    up_rows = gather(up_weight, "row", 0)
    down_rows = gather(down_weight, "row", 0)

    taps, vec, wr, we = mixer_params(
        conv_weight, conv_bias, rate_weight, rate_bias, entry_weight, entry_bias, decay_param, chans
    )
    keep = keep_columns(resets)

    inputs = layer_in.astype(jnp.float32)
    normed_f, norm_back_one = jax.vjp(norm_apply, inputs, mix_full.astype(jnp.float32))
    normed_group = gather(normed_f.astype(jnp.bfloat16), "head", 0)
    u, by, before, states, mixed, part = mixer_forward(
        normed_group, xy_rows, out_rows, taps, vec, wr, we, keep, ROWS
    )
    residual = inputs + scatter(part, "head", 0).astype(jnp.float32)
    normed_two_f, norm_back_two = jax.vjp(norm_apply, residual, ffn_full.astype(jnp.float32))
    cot_group = gather(cotangent, "head", 0)
    two_group = gather(normed_two_f.astype(jnp.bfloat16), "head", 0)
    gates = dot_plain(two_group, gate_rows)
    ups = dot_plain(two_group, up_rows)
    activated, slope = gelu_both(gates)
    hidden = (activated * ups).astype(jnp.bfloat16)
    ffn_part = contract_last(hidden, down_rows).astype(jnp.bfloat16)
    d_hidden = dot_plain(cot_group, down_rows)
    d_gates = (d_hidden * ups * slope).astype(jnp.bfloat16)
    d_ups = (d_hidden * activated).astype(jnp.bfloat16)
    d_two_part = (contract_last(d_gates, gate_rows) + contract_last(d_ups, up_rows)).astype(
        jnp.bfloat16
    )
    gate_grad = scatter(contract_first(two_group, d_gates).astype(jnp.bfloat16), "row", 0)
    up_grad = scatter(contract_first(two_group, d_ups).astype(jnp.bfloat16), "row", 0)
    down_grad = scatter(contract_first(cot_group, hidden).astype(jnp.bfloat16), "row", 0)
    layer_out = (residual + scatter(ffn_part, "head", 0).astype(jnp.float32)).astype(jnp.bfloat16)
    d_two = scatter(d_two_part, "head", 0).astype(jnp.float32)
    d_resid_norm, d_ffn_gain = norm_back_two(d_two)
    d_residual = cotangent.astype(jnp.float32) + d_resid_norm
    d_res_group = gather(d_residual.astype(jnp.bfloat16), "head", 0)
    d_xy, d_part, d_taps, d_vec, d_wr, d_we = mixer_backward(
        d_res_group, xy_rows, out_rows, taps, vec, wr, we, keep, u, by, before, states, ROWS
    )
    out_grad = scatter(contract_first(d_res_group, mixed).astype(jnp.bfloat16), "row", 0)
    xy_grad = scatter(contract_first(normed_group, d_xy).astype(jnp.bfloat16), "row", 0)
    d_normed = scatter(d_part, "head", 0).astype(jnp.float32)
    d_inputs, d_mix_gain = norm_back_one(d_normed)
    layer_in_grad = (d_inputs + d_residual).astype(jnp.bfloat16)

    small = [
        d_taps[:, :used],
        d_vec[0, :used],
        diagonal_blocks(d_wr, heads, head_width),
        d_vec[1, :used],
        diagonal_blocks(d_we, heads, head_width),
        d_vec[2, :used],
        d_vec[3, :used] * (8.0 * jax.nn.sigmoid(-decay_param)),
    ]
    small = [lax.psum(item.astype(jnp.bfloat16), "row").astype(jnp.float32) for item in small]
    mix_part = scatter(d_mix_gain, ("row", "head"), 0)
    ffn_part_grad = scatter(d_ffn_gain, ("row", "head"), 0)
    wide = lambda values: values[:, :used].astype(jnp.float32)
    return (
        layer_out,
        layer_in_grad,
        mix_part,
        ffn_part_grad,
        wide(xy_grad),
        wide(xy_grad[:, chans:]),
        wide(out_grad),
        *small,
        gate_grad.astype(jnp.float32),
        up_grad.astype(jnp.float32),
        down_grad.astype(jnp.float32),
    )

def shards_linked(
    layer_in,
    cotangent,
    mix_gain,
    ffn_gain,
    x_weight,
    y_weight,
    out_weight,
    conv_weight,
    conv_bias,
    rate_weight,
    rate_bias,
    entry_weight,
    entry_bias,
    decay_param,
    gate_weight,
    up_weight,
    down_weight,
    resets,
):
    heads, head_width = rate_weight.shape[:2]
    used = conv_bias.shape[0]
    kept = -(-used // 16) * 16
    flat = lambda values: values.reshape((-1, values.shape[-1]))
    line = lambda values: values.reshape(1, -1)
    vectors = (conv_bias, rate_bias, entry_bias, decay_param)
    place = lax.broadcasted_iota(jnp.int32, (len(vectors), used), 0)
    rows = jnp.zeros((len(vectors), used), jnp.float32)
    for k, vector in enumerate(vectors):
        rows = jnp.where(place == k, vector[None, :], rows)
    (
        normed_group, cot_half, xy_rows, out_rows, mix_full, ffn_full, taps, vec, wr, we, keep,
    ) = open_block(
        layer_in,
        (line(mix_gain), line(ffn_gain)),
        cotangent,
        (x_weight.T, y_weight.T, out_weight.T),
        (
            conv_weight,
            rows,
            jnp.stack([rate_weight, entry_weight]),
            resets,
        ),
    )
    normed_group = flat(normed_group)
    u, by, before, states, mixed, residual, normed_two, gate_rows, up_half = forward_linked(
        normed_group, xy_rows, out_rows, taps, vec, wr, we, keep, layer_in, ffn_full,
        gate_weight, up_weight,
    )
    gate_rows = flat(gate_rows)
    two_group, cot_group, up_rows, down_rows, gates, ups, hidden, down_parts = ffn_up(
        normed_two, gate_rows, cotangent, cot_half, up_half, up_weight, down_weight
    )
    two_group, cot_group, down_rows = map(flat, (two_group, cot_group, down_rows))
    d_ups, gate_parts, down_grad, d_residual, d_low, d_ffn_gain = ffn_back(
        cot_group, two_group, gates, ups, gate_rows, up_rows, down_rows, down_parts, residual,
        cotangent, ffn_full,
    )
    up_parts, out_parts, gate_grad, d_mixed = turn(
        two_group, d_ups, gate_parts, d_low, mixed, out_rows, kept
    )
    xy_parts, up_grad, out_grad, layer_in_grad, gain_terms, small = backward_linked(
        d_mixed, xy_rows, taps, vec, wr, we, keep, u, by, before, states,
        normed_group, up_parts, out_parts, layer_in, mix_full, d_residual, d_ffn_gain,
        head_width, used,
    )
    layer_out, x_grad, y_grad, gain_grads, sums = close_block(
        hidden, down_rows, xy_parts, residual, gain_terms, small, used
    )
    sums = flat(sums)
    share = mix_gain.shape[0]
    ends = -(-used // 8) * 8
    (
        layer_out, layer_in_grad, x_grad, y_grad, out_grad, gate_grad, up_grad, down_grad,
    ) = hand_over(
        layer_out, layer_in_grad, x_grad, y_grad, out_grad, gate_grad, up_grad, down_grad
    )
    gates_end = heads * head_width
    return (
        layer_out,
        layer_in_grad,
        gain_grads[0, :share],
        gain_grads[0, share:],
        x_grad.T,
        y_grad.T,
        out_grad.T,
        sums[ends : ends + 4, :used],
        sums[ends + 4, :used],
        sums[:gates_end, :head_width].reshape(heads, head_width, head_width),
        sums[ends + 5, :used],
        sums[:gates_end, head_width : 2 * head_width].reshape(heads, head_width, head_width),
        sums[ends + 6, :used],
        sums[ends + 7, :used],
        gate_grad,
        up_grad,
        down_grad,
    )


def solution(mesh):
    linked = mesh.shape["row"] == LINE and mesh.shape["head"] == PLANE
    return jax.shard_map(
        shards_linked if linked else shards,
        mesh=mesh,
        in_specs=(
            P(("row", "head"), None),
            P(("row", "head"), None),
            P(("row", "head")),
            P(("row", "head")),
            P("row", "head"),
            P("row", "head"),
            P("row", "head"),
            P(None, "head"),
            P("head"),
            P("head", None, None),
            P("head"),
            P("head", None, None),
            P("head"),
            P("head"),
            P("row", "head"),
            P("row", "head"),
            P("row", "head"),
            P("row", None),
        ),
        out_specs=(
            P(("row", "head"), None),
            P(("row", "head"), None),
            P(("row", "head")),
            P(("row", "head")),
            P("row", "head"),
            P("row", "head"),
            P("row", "head"),
            P(None, "head"),
            P("head"),
            P("head", None, None),
            P("head"),
            P("head", None, None),
            P("head"),
            P("head"),
            P("row", "head"),
            P("row", "head"),
            P("row", "head"),
        ),
        check_vma=False,
    )
```

```python
import functools

import jax
import jax.numpy as jnp
from jax import lax
from jax.experimental import pallas as pl
from jax.experimental.pallas import tpu as pltpu
from jax.sharding import PartitionSpec as P

EPSILON = 1e-06
ROWS = 256
GELU_A = 0.7978845608028654
GELU_B = 0.044715
CHUNK = 16
UNROLL = 4


def gelu_only(x):
    return 0.5 * x * (1.0 + jnp.tanh(GELU_A * (x + GELU_B * x * x * x)))


def gelu_both(x):
    square = x * x
    bent = jnp.tanh(GELU_A * x * (1.0 + GELU_B * square))
    half = 0.5 * (1.0 + bent)
    slope = half + 0.5 * x * (1.0 - bent * bent) * (GELU_A * (1.0 + 3.0 * GELU_B * square))
    return x * half, slope


def one_minus_exp(x, exp_x):
    return -jnp.tanh(0.5 * x) * (1.0 + exp_x)


def dot_plain(left, right):
    return jnp.dot(left, right, preferred_element_type=jnp.float32)


def contract_last(left, right):
    return lax.dot_general(
        left, right, (((1,), (1,)), ((), ())), preferred_element_type=jnp.float32
    )


def contract_first(left, right):
    return lax.dot_general(
        left, right, (((0,), (0,)), ((), ())), preferred_element_type=jnp.float32
    )


def sum_eight(value):
    total = value[0:8, :]
    for k in range(1, value.shape[0] // 8):
        total = total + value[8 * k : 8 * k + 8, :]
    return total


def conv_rows(window, keep, taps, shift):
    rows = window.shape[0] - 8
    total = taps[0:1] * window[8:] + shift
    for offset in range(1, 4):
        total = total + taps[offset : offset + 1] * (
            keep[:, offset : offset + 1] * window[8 - offset : 8 - offset + rows]
        )
    return total


def scan_down(decays, driven, carry):
    rows = decays.shape[0]
    place = lax.broadcasted_iota(jnp.int32, decays.shape, 0)
    step = 1
    while step < rows:
        inside = place >= step
        driven = jnp.where(inside, decays * pltpu.roll(driven, step, 0) + driven, driven)
        decays = jnp.where(inside, decays * pltpu.roll(decays, step, 0), decays)
        step *= 2
    return decays * carry + driven


def scan_up(decays, driven, carry):
    rows = decays.shape[0]
    place = lax.broadcasted_iota(jnp.int32, decays.shape, 0)
    step = 1
    while step < rows:
        inside = place < rows - step
        driven = jnp.where(inside, decays * pltpu.roll(driven, rows - step, 0) + driven, driven)
        decays = jnp.where(inside, decays * pltpu.roll(decays, rows - step, 0), decays)
        step *= 2
    return decays * carry + driven


def forward_step(
    normed_ref, xy_ref, taps_ref, vec_ref, wr_ref, we_ref, keep_ref,
    u_ref, by_ref, before_ref, states_ref, mixed_ref,
    window, conv, conv_low, rate, entry, carry,
):
    rows = normed_ref.shape[0]

    @pl.when(pl.program_id(0) == 0)
    def _():
        window[0:8, :] = jnp.zeros_like(window[0:8, :])
        carry[...] = jnp.zeros_like(carry)

    chans = u_ref.shape[1]
    branches = contract_last(normed_ref[...], xy_ref[...])
    branch_x = branches[:, :chans].astype(jnp.bfloat16)
    u_ref[...] = branch_x
    window[pl.ds(8, rows), :] = branch_x.astype(jnp.float32)
    by_ref[...] = branches[:, chans:]

    def conv_step(j, unused):
        at = pl.multiple_of(j * CHUNK, CHUNK)
        made = conv_rows(
            window[pl.ds(at, CHUNK + 8), :], keep_ref[pl.ds(at, CHUNK), :],
            taps_ref[...], vec_ref[0:1, :],
        )
        conv[pl.ds(at, CHUNK), :] = made
        conv_low[pl.ds(at, CHUNK), :] = made.astype(jnp.bfloat16)
        return unused

    lax.fori_loop(0, rows // CHUNK, conv_step, 0, unroll=2 * UNROLL)
    window[0:8, :] = window[pl.ds(rows, 8), :]
    rate[...] = dot_plain(conv_low[...], wr_ref[...]) + vec_ref[1:2, :]
    entry[...] = dot_plain(conv_low[...], we_ref[...]) + vec_ref[2:3, :]

    def scan_step(j, before):
        at = pl.multiple_of(j * CHUNK, CHUNK)
        here = pl.ds(at, CHUNK)
        carried = keep_ref[here, 0:1]
        log_decay = jax.nn.sigmoid(rate[here, :]) * vec_ref[3:4, :]
        exp_decay = jnp.exp(log_decay)
        lost = one_minus_exp(2.0 * log_decay, exp_decay * exp_decay)
        drop = lost * lax.rsqrt(jnp.maximum(lost, 1e-30))
        scaling = (1.0 - carried) + carried * drop
        driven = scaling * jax.nn.sigmoid(entry[here, :]) * conv[here, :]
        states = scan_down(exp_decay * carried, driven, before)
        first = lax.broadcasted_iota(jnp.int32, states.shape, 0) == 0
        before_ref[here, :] = jnp.where(first, before, pltpu.roll(states, 1, 0))
        states_low = states.astype(jnp.bfloat16)
        states_ref[here, :] = states_low
        mixed_ref[here, :] = (
            states_low.astype(jnp.float32) * gelu_only(by_ref[here, :])
        ).astype(jnp.bfloat16)
        return states[CHUNK - 1 : CHUNK, :]

    carry[0:1, :] = lax.fori_loop(0, rows // CHUNK, scan_step, carry[0:1, :], unroll=2 * UNROLL)


def forward_body(
    normed_ref, xy_ref, ow_ref, taps_ref, vec_ref, wr_ref, we_ref, keep_ref,
    u_ref, by_ref, before_ref, states_ref, mixed_ref, part_ref, *scratch,
):
    forward_step(
        normed_ref, xy_ref, taps_ref, vec_ref, wr_ref, we_ref, keep_ref,
        u_ref, by_ref, before_ref, states_ref, mixed_ref, *scratch,
    )
    part_ref[...] = dot_plain(mixed_ref[...], ow_ref[...]).astype(jnp.bfloat16)


def backward_step(
    first_step, last_step, d_mixed, taps_ref, vec_ref, wr_ref, we_ref, keep_ref,
    u_ref, u_prev_ref, by_ref, before_ref, states_ref,
    d_xy_ref, taps_out, vec_out, wr_out, we_out,
    window, conv, conv_low, rate, entry, d_conv, g_rate, g_entry, carry, sums,
):
    rows, chans = u_ref.shape

    @pl.when(first_step)
    def _():
        d_conv[pl.ds(rows, 8), :] = jnp.zeros_like(d_conv[pl.ds(rows, 8), :])
        carry[...] = jnp.zeros_like(carry)
        sums[...] = jnp.zeros_like(sums)
        wr_out[...] = jnp.zeros_like(wr_out)
        we_out[...] = jnp.zeros_like(we_out)

    @pl.when(jnp.logical_not(first_step))
    def _():
        d_conv[pl.ds(rows, 8), :] = d_conv[0:8, :]

    window[0:8, :] = u_prev_ref[8:16, :].astype(jnp.float32)
    window[pl.ds(8, rows), :] = u_ref[...].astype(jnp.float32)

    def conv_step(j, unused):
        at = pl.multiple_of(j * CHUNK, CHUNK)
        made = conv_rows(
            window[pl.ds(at, CHUNK + 8), :], keep_ref[pl.ds(at, CHUNK), :],
            taps_ref[...], vec_ref[0:1, :],
        )
        conv[pl.ds(at, CHUNK), :] = made
        conv_low[pl.ds(at, CHUNK), :] = made.astype(jnp.bfloat16)
        return unused

    lax.fori_loop(0, rows // CHUNK, conv_step, 0, unroll=2 * UNROLL)
    rate[...] = dot_plain(conv_low[...], wr_ref[...]) + vec_ref[1:2, :]
    entry[...] = dot_plain(conv_low[...], we_ref[...]) + vec_ref[2:3, :]

    def fold(value):
        return sum_eight(value)

    def scan_step(j, after):
        at = pl.multiple_of(rows - CHUNK - j * CHUNK, CHUNK)
        here = pl.ds(at, CHUNK)
        carried = keep_ref[here, 0:1]
        rate_gate = jax.nn.sigmoid(rate[here, :])
        entry_gate = jax.nn.sigmoid(entry[here, :])
        log_decay = rate_gate * vec_ref[3:4, :]
        exp_decay = jnp.exp(log_decay)
        exp_twice = exp_decay * exp_decay
        lost = one_minus_exp(2.0 * log_decay, exp_twice)
        inverse = lax.rsqrt(jnp.maximum(lost, 1e-30))
        drop = lost * inverse
        scaling = (1.0 - carried) + carried * drop
        decays = exp_decay * carried
        gelu_y, slope_y = gelu_both(by_ref[here, :])
        through = d_mixed[here, :]
        d_states = (through * gelu_y).astype(jnp.bfloat16).astype(jnp.float32)
        d_xy_ref[here, chans:] = (
            through * states_ref[here, :].astype(jnp.float32) * slope_y
        ).astype(jnp.bfloat16)
        passed = scan_up(decays, decays * d_states, after)
        last = lax.broadcasted_iota(jnp.int32, passed.shape, 0) == CHUNK - 1
        adjoint = d_states + jnp.where(last, after, pltpu.roll(passed, CHUNK - 1, 0))
        convolved = conv[here, :]
        gated = adjoint * entry_gate
        g_log = adjoint * before_ref[here, :] * decays - gated * convolved * (
            carried * (exp_twice * inverse)
        )
        g_pre_rate = g_log * vec_ref[3:4, :] * (rate_gate * (1.0 - rate_gate))
        direct = gated * scaling
        g_pre_entry = direct * convolved * (1.0 - entry_gate)
        d_conv[here, :] = direct
        g_rate[here, :] = g_pre_rate.astype(jnp.bfloat16)
        g_entry[here, :] = g_pre_entry.astype(jnp.bfloat16)
        sums[8:16, :] += fold(g_pre_rate)
        sums[16:24, :] += fold(g_pre_entry)
        sums[24:32, :] += fold(g_log * rate_gate)
        return passed[0:1, :]

    carry[0:1, :] = lax.fori_loop(0, rows // CHUNK, scan_step, carry[0:1, :], unroll=2 * UNROLL)
    wr_out[...] += contract_first(conv_low[...], g_rate[...])
    we_out[...] += contract_first(conv_low[...], g_entry[...])
    d_conv[0:rows, :] += contract_last(g_rate[...], wr_ref[...]) + contract_last(
        g_entry[...], we_ref[...]
    )

    def back_step(j, unused):
        at = pl.multiple_of(j * CHUNK, CHUNK)
        here = pl.ds(at, CHUNK)
        keep = keep_ref[here, :]
        ahead = d_conv[pl.ds(at, CHUNK + 8), :]
        behind = window[pl.ds(at, CHUNK + 8), :]
        now = ahead[0:CHUNK]
        total = taps_ref[0:1, :] * now
        sums[0:8, :] += fold(now)
        sums[32:40, :] += fold(now * behind[8:])
        for offset in range(1, 4):
            total = total + taps_ref[offset : offset + 1, :] * (
                keep[:, 3 + offset : 4 + offset] * ahead[offset : offset + CHUNK]
            )
            base = 32 + 8 * offset
            sums[base : base + 8, :] += fold(
                now * (keep[:, offset : offset + 1] * behind[8 - offset : 8 - offset + CHUNK])
            )
        d_xy_ref[here, :chans] = total.astype(jnp.bfloat16)
        return unused

    lax.fori_loop(0, rows // CHUNK, back_step, 0, unroll=2 * UNROLL)

    @pl.when(last_step)
    def _():
        vec_out[...] = jnp.zeros_like(vec_out)
        for place in range(4):
            vec_out[place : place + 1, :] = jnp.sum(
                sums[8 * place : 8 * place + 8, :], axis=0, keepdims=True
            )
            taps_out[place : place + 1, :] = jnp.sum(
                sums[32 + 8 * place : 40 + 8 * place, :], axis=0, keepdims=True
            )


def backward_body(
    d_res_ref, xy_ref, ow_ref, taps_ref, vec_ref, wr_ref, we_ref, keep_ref,
    u_ref, u_prev_ref, by_ref, before_ref, states_ref,
    d_xy_ref, part_ref, taps_out, vec_out, wr_out, we_out, d_mixed, *scratch,
):
    step = pl.program_id(0)
    d_mixed[...] = contract_last(d_res_ref[...], ow_ref[...])
    backward_step(
        step == 0, step == pl.num_programs(0) - 1, d_mixed, taps_ref, vec_ref, wr_ref,
        we_ref, keep_ref, u_ref, u_prev_ref, by_ref, before_ref, states_ref, d_xy_ref,
        taps_out, vec_out, wr_out, we_out, *scratch,
    )
    part_ref[...] = dot_plain(d_xy_ref[...], xy_ref[...]).astype(jnp.bfloat16)


def whole(shape):
    return pl.BlockSpec(shape, lambda i: (0,) * len(shape))


def mixer_forward(normed, xy, ow, taps, vec, wr, we, keep, rows):
    length, width = normed.shape
    chans = ow.shape[0]
    tile = lambda columns: pl.BlockSpec((rows, columns), lambda i: (i, 0))
    return pl.pallas_call(
        forward_body,
        grid=(length // rows,),
        in_specs=[
            tile(width), whole(xy.shape), whole(ow.shape), whole(taps.shape),
            whole(vec.shape), whole(wr.shape), whole(we.shape), tile(keep.shape[1]),
        ],
        out_specs=[tile(chans)] * 5 + [tile(width)],
        out_shape=[
            jax.ShapeDtypeStruct((length, chans), jnp.bfloat16),
            jax.ShapeDtypeStruct((length, chans), jnp.float32),
            jax.ShapeDtypeStruct((length, chans), jnp.float32),
            jax.ShapeDtypeStruct((length, chans), jnp.bfloat16),
            jax.ShapeDtypeStruct((length, chans), jnp.bfloat16),
            jax.ShapeDtypeStruct((length, width), jnp.bfloat16),
        ],
        scratch_shapes=[
            pltpu.VMEM((rows + 8, chans), jnp.float32),
            pltpu.VMEM((rows, chans), jnp.float32),
            pltpu.VMEM((rows, chans), jnp.bfloat16),
            pltpu.VMEM((rows, chans), jnp.float32),
            pltpu.VMEM((rows, chans), jnp.float32),
            pltpu.VMEM((8, chans), jnp.float32),
        ],
        compiler_params=pltpu.CompilerParams(vmem_limit_bytes=48 * 2**20),
        cost_estimate=pl.CostEstimate(
            flops=6 * length * width * chans,
            bytes_accessed=4 * length * width + 30 * length * chans,
            transcendentals=6 * length * chans,
        ),
        name="mixer_forward",
    )(normed, xy, ow, taps, vec, wr, we, keep)


def mixer_backward(d_res, xy, ow, taps, vec, wr, we, keep, u, by, before, states, rows):
    length, width = d_res.shape
    chans = ow.shape[0]
    blocks = length // rows
    tile = lambda columns: pl.BlockSpec((rows, columns), lambda i: (blocks - 1 - i, 0))
    ahead = pl.BlockSpec(
        (16, chans), lambda i: (jnp.maximum((blocks - 1 - i) * (rows // 16) - 1, 0), 0)
    )
    return pl.pallas_call(
        backward_body,
        grid=(blocks,),
        in_specs=[
            tile(width), whole(xy.shape), whole(ow.shape), whole(taps.shape),
            whole(vec.shape), whole(wr.shape), whole(we.shape), tile(keep.shape[1]),
            tile(chans), ahead, tile(chans), tile(chans), tile(chans),
        ],
        out_specs=[
            tile(2 * chans), tile(width), whole(taps.shape), whole(vec.shape),
            whole(wr.shape), whole(we.shape),
        ],
        out_shape=[
            jax.ShapeDtypeStruct((length, 2 * chans), jnp.bfloat16),
            jax.ShapeDtypeStruct((length, width), jnp.bfloat16),
            jax.ShapeDtypeStruct(taps.shape, jnp.float32),
            jax.ShapeDtypeStruct(vec.shape, jnp.float32),
            jax.ShapeDtypeStruct(wr.shape, jnp.float32),
            jax.ShapeDtypeStruct(we.shape, jnp.float32),
        ],
        scratch_shapes=[
            pltpu.VMEM((rows, chans), jnp.float32),
            pltpu.VMEM((rows + 8, chans), jnp.float32),
            pltpu.VMEM((rows, chans), jnp.float32),
            pltpu.VMEM((rows, chans), jnp.bfloat16),
            pltpu.VMEM((rows, chans), jnp.float32),
            pltpu.VMEM((rows, chans), jnp.float32),
            pltpu.VMEM((rows + 8, chans), jnp.float32),
            pltpu.VMEM((rows, chans), jnp.bfloat16),
            pltpu.VMEM((rows, chans), jnp.bfloat16),
            pltpu.VMEM((8, chans), jnp.float32),
            pltpu.VMEM((64, chans), jnp.float32),
        ],
        compiler_params=pltpu.CompilerParams(vmem_limit_bytes=48 * 2**20),
        cost_estimate=pl.CostEstimate(
            flops=6 * length * width * chans,
            bytes_accessed=4 * length * width + 30 * length * chans,
            transcendentals=6 * length * chans,
        ),
        name="mixer_backward",
    )(d_res, xy, ow, taps, vec, wr, we, keep, u, u, by, before, states)


def keep_columns(resets):
    length = resets.shape[1]
    position = lax.broadcasted_iota(jnp.int32, resets.shape, 1)
    starts = jnp.maximum(resets, (position == 0).astype(jnp.int32)).astype(jnp.float32)
    carried = (1.0 - starts).reshape(-1)
    seqs = resets.shape[0]

    def back(values, by):
        values = values.reshape(seqs, length)
        return jnp.pad(values, ((0, 0), (by, 0)))[:, :length].reshape(-1)

    def ahead(values, by):
        values = values.reshape(seqs, length)
        return jnp.pad(values, ((0, 0), (0, by)))[:, by:].reshape(-1)

    one = carried
    two = one * back(carried, 1)
    three = two * back(carried, 2)
    return jnp.stack(
        [carried, one, two, three, ahead(one, 1), ahead(two, 2), ahead(three, 3), carried], axis=1
    )


def block_diagonal(blocks, chans):
    heads, width, unused = blocks.shape
    rows = [
        jnp.pad(blocks[h], ((0, 0), (h * width, chans - (h + 1) * width))) for h in range(heads)
    ]
    full = jnp.concatenate(rows, axis=0)
    return jnp.pad(full, ((0, chans - heads * width), (0, 0)))


def diagonal_blocks(full, heads, width):
    return jnp.stack(
        [full[h * width : (h + 1) * width, h * width : (h + 1) * width] for h in range(heads)]
    )


MESH = pl.DeviceIdType.MESH
ANYWHERE = pl.BlockSpec(memory_space=pl.ANY)
IN_VMEM = pl.BlockSpec(memory_space=pltpu.VMEM)
LINE = 4
PLANE = 8
PIECES = 4


def send_to(src, dst, sent, arrived, axis, target):
    return pltpu.make_async_remote_copy(
        src_ref=src,
        dst_ref=dst,
        send_sem=sent,
        recv_sem=arrived,
        device_id={axis: target},
        device_id_type=MESH,
    )


def sibling_of(h):
    return h + 1 - 2 * lax.rem(h, 2)


def across_of(h):
    return h + 2 - 4 * lax.rem(lax.div(h, 2), 2)


def along_of(h):
    return lax.rem(h + 4, PLANE)


def meet(row_line, plane):
    r, h = lax.axis_index("row"), lax.axis_index("head")
    barrier = pltpu.get_barrier_semaphore()
    count = 0
    if row_line:
        for step in range(1, LINE):
            pl.semaphore_signal(
                barrier, inc=1, device_id={"row": lax.rem(r + step, LINE)}, device_id_type=MESH
            )
        count += LINE - 1
    if plane == "all":
        for step in range(1, PLANE):
            pl.semaphore_signal(
                barrier, inc=1, device_id={"head": lax.rem(h + step, PLANE)}, device_id_type=MESH
            )
        count += PLANE - 1
    if plane == "near":
        for target in (sibling_of(h), across_of(h), along_of(h)):
            pl.semaphore_signal(barrier, inc=1, device_id={"head": target}, device_id_type=MESH)
        count += 3
    pl.semaphore_wait(barrier, count)


class Bring:
    def __init__(self, sources, places, semaphores):
        self.copies = [
            pltpu.make_async_copy(src, dst, semaphores.at[k])
            for k, (src, dst) in enumerate(zip(sources, places))
        ]

    def start(self):
        for copy in self.copies:
            copy.start()

    def wait(self, *which):
        for k in which:
            self.copies[k].wait()


def held(*arrays):
    return [pltpu.VMEM(item.shape, item.dtype) for item in arrays] + [
        pltpu.SemaphoreType.DMA((len(arrays),))
    ]


class LineGather:
    semaphores = (
        pltpu.SemaphoreType.DMA((LINE,)),
        pltpu.SemaphoreType.DMA((LINE,)),
        pltpu.SemaphoreType.DMA((2,)),
    )

    def __init__(self, source, slot, sent, arrived, other):
        self.r = lax.axis_index("row")
        self.source, self.slot = source, slot
        self.sent, self.arrived, self.other = sent, arrived, other

    def own(self, t):
        return send_to(
            self.source, self.slot(self.r), self.sent.at[t], self.arrived.at[self.r], "row", t
        )

    def handed(self, origin, target):
        return send_to(
            self.slot(origin), self.slot(origin), self.other.at[0], self.arrived.at[origin],
            "row", target,
        )

    def local(self):
        return pltpu.make_async_copy(self.source, self.slot(self.r), self.other.at[1])

    def start(self):
        for gap in (2, -2, 1, -1):
            t = self.r + gap

            @pl.when((t >= 0) & (t < LINE))
            def _(t=t):
                self.own(t).start()

        self.local().start()

    def forward(self):
        for me, origin, target in ((2, 0, 3), (1, 3, 0)):

            @pl.when(self.r == me)
            def _(origin=origin, target=target):
                copy = self.handed(origin, target)
                copy.wait_recv()
                copy.start()

    def finish(self):
        r = self.r
        for t in range(LINE):
            known = (r == t) | ((r == 2) & (t == 0)) | ((r == 1) & (t == 3))
            near = (r != t) & (r - t < 3) & (t - r < 3)

            @pl.when(jnp.logical_not(known))
            def _(t=t):
                self.handed(t, t).wait_recv()

            @pl.when(near)
            def _(t=t):
                self.own(t).wait_send()

        for me, origin, target in ((2, 0, 3), (1, 3, 0)):

            @pl.when(r == me)
            def _(origin=origin, target=target):
                self.handed(origin, target).wait_send()

        self.local().wait()


class LineReduce:
    semaphores = (
        pltpu.SemaphoreType.DMA((LINE,)),
        pltpu.SemaphoreType.DMA((LINE,)),
        pltpu.SemaphoreType.DMA((2,)),
    )

    @staticmethod
    def buffers(rows, width):
        return [
            pltpu.VMEM((LINE, rows, width), jnp.bfloat16),
            pltpu.VMEM((rows, width), jnp.bfloat16),
        ]

    def __init__(self, source, parts, landed, passed, sent, arrived, other):
        self.r = lax.axis_index("row")
        self.source, self.parts, self.landed, self.passed = source, parts, landed, passed
        self.sent, self.arrived, self.other = sent, arrived, other

    def to_pass(self, me, origin, via):
        return send_to(
            self.source.at[origin], self.passed, self.sent.at[origin], self.other.at[0], "row", via
        )

    def direct(self, t):
        return send_to(
            self.source.at[t], self.landed.at[self.r], self.sent.at[t], self.arrived.at[self.r],
            "row", t,
        )

    def added(self, t):
        return send_to(
            self.passed, self.landed.at[self.r], self.sent.at[t], self.arrived.at[self.r], "row", t
        )

    def plain(self, t):
        r = self.r
        ends = ((r == 0) & (t == 3)) | ((r == 3) & (t == 0))
        added = ((r == 1) & (t == 3)) | ((r == 2) & (t == 0))
        return jnp.logical_not(ends | added | (r == t))

    def start(self):
        for me, end, via in ((0, 3, 1), (3, 0, 2)):

            @pl.when(self.r == me)
            def _(me=me, end=end, via=via):
                self.to_pass(me, end, via).start()

        for gap in (2, -2, 1, -1):
            t = self.r + gap

            @pl.when((t >= 0) & (t < LINE) & self.plain(t))
            def _(t=t):
                self.direct(t).start()

    def forward(self):
        for me, end in ((1, 3), (2, 0)):

            @pl.when(self.r == me)
            def _(me=me, end=end):
                self.to_pass(me, end, end).wait_recv()
                rows = self.passed.shape[0]
                step = 32

                def add(i, unused):
                    at = pl.ds(pl.multiple_of(i * step, step), step)
                    self.passed[at, :] = (
                        self.parts[end, at, :].astype(jnp.float32)
                        + self.passed[at, :].astype(jnp.float32)
                    ).astype(jnp.bfloat16)
                    return unused

                lax.fori_loop(0, rows // step, add, 0)
                self.added(end).start()

    def finish(self, write):
        r = self.r
        for t in range(LINE):

            @pl.when(jnp.logical_not(unsent_to(r, t)))
            def _(t=t):
                send_to(
                    self.source.at[t], self.landed.at[t], self.sent.at[t], self.arrived.at[t],
                    "row", t,
                ).wait_recv()

        def total_of(sources):
            step = 32

            def add(i, unused):
                at = pl.ds(pl.multiple_of(i * step, step), step)
                total = self.parts[r, at, :].astype(jnp.float32)
                for t in sources:
                    total = total + self.landed[t, at, :].astype(jnp.float32)
                write(at, total)
                return unused

            lax.fori_loop(0, self.passed.shape[0] // step, add, 0)

        at_end = (r == 0) | (r == 3)

        @pl.when(at_end)
        def _():
            total_of((1, 2))

        @pl.when(jnp.logical_not(at_end))
        def _():
            total_of((0, 3, 3 - r))

        for me, end, via in ((0, 3, 1), (3, 0, 2)):

            @pl.when(r == me)
            def _(me=me, end=end, via=via):
                self.to_pass(me, end, via).wait_send()

        for t in range(LINE):

            @pl.when(jnp.logical_not(unsent_to(r, t)))
            def _(t=t):
                self.direct(t).wait_send()


def unsent_to(r, t):
    return ((r == 0) & (t == 3)) | ((r == 3) & (t == 0)) | (r == t)


class PlaneGather:
    semaphores = (
        pltpu.SemaphoreType.DMA((PIECES, 7)),
        pltpu.SemaphoreType.DMA((PIECES, 7)),
        pltpu.SemaphoreType.DMA((PIECES,)),
    )
    first = tuple(range(PIECES // 2))
    second = tuple(range(PIECES // 2, PIECES))

    def __init__(self, block, full, sent, arrived, other, source=None, target=None):
        h = lax.axis_index("head")
        self.source, self.target = source, target
        self.h, self.side, self.x, self.y = h, sibling_of(h), across_of(h), along_of(h)
        self.far = across_of(self.y)
        self.block, self.full = block, full
        self.sent, self.arrived, self.other = sent, arrived, other
        self.rows = block.shape[0] // PIECES

    def piece(self, owner, c):
        rows = pl.ds(c * self.rows, self.rows)
        if self.target is None:
            return self.full.at[owner, rows]
        return self.full.at[owner, rows, self.target]

    def mine(self, c):
        rows = pl.ds(c * self.rows, self.rows)
        return self.block.at[rows] if self.source is None else self.block.at[rows, self.source]

    def own(self, c, lane, target):
        return send_to(
            self.mine(c), self.piece(self.h, c),
            self.sent.at[c, lane], self.arrived.at[c, lane], "head", target,
        )

    def hand(self, owner, c, lane, target):
        return send_to(
            self.piece(owner, c), self.piece(owner, c), self.sent.at[c, lane],
            self.arrived.at[c, lane], "head", target,
        )

    def local(self, c):
        return pltpu.make_async_copy(self.mine(c), self.piece(self.h, c), self.other.at[c])

    def start(self):
        for a, b in zip(self.first, self.second):
            self.own(a, 1, self.x).start()
            self.own(b, 2, self.y).start()
        for a, b in zip(self.first, self.second):
            self.own(b, 1, self.x).start()
            self.own(a, 2, self.y).start()
        for c in range(PIECES):
            self.own(c, 0, self.side).start()
            self.local(c).start()

    def relay(self, place):
        a, b = self.first[place], self.second[place]
        self.hand(self.x, a, 1, self.x).wait_recv()
        self.hand(self.x, a, 3, self.y).start()
        self.hand(self.x, a, 4, self.side).start()
        self.hand(self.y, b, 2, self.y).wait_recv()
        self.hand(self.y, b, 3, self.x).start()
        self.hand(self.y, b, 5, self.side).start()

    def rest(self):
        for a, b in zip(self.first, self.second):
            self.hand(self.x, b, 1, self.x).wait_recv()
            self.hand(self.x, b, 4, self.side).start()
            self.hand(self.y, a, 2, self.y).wait_recv()
            self.hand(self.y, a, 5, self.side).start()

    def beside(self):
        for c in range(PIECES):
            self.hand(self.side, c, 0, self.side).wait_recv()

    def far_side(self):
        for pair in zip(self.first, self.second):
            for c in pair:
                self.hand(self.far, c, 3, self.side).wait_recv()
                self.hand(self.far, c, 6, self.side).start()

    def end(self, beside=True):
        side = self.side
        if beside:
            self.beside()
        for c in range(PIECES):
            for owner, lane in (
                (across_of(side), 4), (along_of(side), 5), (across_of(along_of(side)), 6)
            ):
                self.hand(owner, c, lane, side).wait_recv()
        for c in range(PIECES):
            for lane in range(7):
                self.own(c, lane, side).wait_send()
            self.local(c).wait()


class PlaneReduce:
    semaphores = (
        pltpu.SemaphoreType.DMA((4,)),
        pltpu.SemaphoreType.DMA((4,)),
        pltpu.SemaphoreType.DMA((4, 2)),
        pltpu.SemaphoreType.DMA((2, 2)),
        pltpu.SemaphoreType.DMA((2,)),
    )

    @staticmethod
    def buffers(rows, width):
        return [
            pltpu.VMEM((4, rows, width), jnp.bfloat16),
            pltpu.VMEM((4, rows, width), jnp.bfloat16),
            pltpu.VMEM((4, rows, width), jnp.bfloat16),
            pltpu.VMEM((2, rows // 2, width), jnp.bfloat16),
            pltpu.VMEM((2, rows, width), jnp.bfloat16),
        ]

    def __init__(
        self, staged, beside, mine, relayed, landed,
        side_sent, side_arrived, sent, arrived, relay_arrived,
    ):
        h = lax.axis_index("head")
        self.h, self.core, self.chip = h, lax.rem(h, 2), lax.div(h, 2)
        self.staged, self.beside, self.mine = staged, beside, mine
        self.relayed, self.landed = relayed, landed
        self.side_sent, self.side_arrived = side_sent, side_arrived
        self.sent, self.arrived, self.relay_arrived = sent, arrived, relay_arrived
        self.half = mine.shape[1] // 2

    def aside(self, chip):
        return send_to(
            self.staged.at[chip], self.beside.at[chip], self.side_sent.at[chip],
            self.side_arrived.at[chip], "head", sibling_of(self.h),
        )

    def relation(self, chip):
        flip_x = lax.rem(chip + self.chip, 2)
        flip_y = lax.rem(lax.div(chip, 2) + lax.div(self.chip, 2), 2)
        return flip_x + 2 * flip_y

    def part(self, half):
        return pl.ds(half * self.half, self.half)

    def home(self, chip, way, half):
        return send_to(
            self.mine.at[chip, self.part(half)], self.landed.at[way, self.part(half)],
            self.sent.at[chip, half], self.arrived.at[way, half], "head",
            (across_of, along_of)[way](self.h),
        )

    def opposite(self, chip, half):
        return send_to(
            self.mine.at[chip, self.part(half)], self.relayed.at[half], self.sent.at[chip, half],
            self.relay_arrived.at[half], "head", (along_of, across_of)[half](self.h),
        )

    def put(self, block, value):
        chip, core = lax.div(block, 2), lax.rem(block, 2)

        @pl.when(core == self.core)
        def _():
            self.mine[chip] = value

        @pl.when(core != self.core)
        def _():
            self.staged[chip] = value
            self.aside(chip).start()

    def pass_on(self, block):
        chip, core = lax.div(block, 2), lax.rem(block, 2)

        @pl.when(core == self.core)
        def _():
            self.aside(chip).wait_recv()
            step = 32

            def add(i, unused):
                at = pl.ds(pl.multiple_of(i * step, step), step)
                self.mine[chip, at, :] = (
                    self.mine[chip, at, :].astype(jnp.float32)
                    + self.beside[chip, at, :].astype(jnp.float32)
                ).astype(jnp.bfloat16)
                return unused

            lax.fori_loop(0, 2 * self.half // step, add, 0)
            relation = self.relation(chip)

            @pl.when(relation == 1)
            def _():
                self.home(chip, 0, 1).start()

            @pl.when(relation == 2)
            def _():
                self.home(chip, 1, 0).start()

            @pl.when(relation == 3)
            def _():
                self.opposite(chip, 0).start()
                self.opposite(chip, 1).start()

    def relay(self, block):
        chip, core = lax.div(block, 2), lax.rem(block, 2)
        for way in (0, 1):

            @pl.when((core == self.core) & (self.relation(chip) == way + 1))
            def _(way=way):
                self.opposite(chip, way).wait_recv()
                step = 32

                def add(i, unused):
                    at = pl.ds(pl.multiple_of(i * step, step), step)
                    here = pl.ds(pl.multiple_of(way * self.half + i * step, step), step)
                    self.mine[chip, here, :] = (
                        self.mine[chip, here, :].astype(jnp.float32)
                        + self.relayed[way, at, :].astype(jnp.float32)
                    ).astype(jnp.bfloat16)
                    return unused

                lax.fori_loop(0, self.half // step, add, 0)
                self.home(chip, way, way).start()

    def arrive(self):
        for way in (0, 1):
            for half in (0, 1):
                self.home(self.chip, way, half).wait_recv()

    def total(self, at):
        value = self.mine[self.chip, at, :].astype(jnp.float32)
        return (
            value
            + self.landed[0, at, :].astype(jnp.float32)
            + self.landed[1, at, :].astype(jnp.float32)
        )

    def finish(self):
        for chip in range(4):
            self.aside(chip).wait_send()

            @pl.when(chip != self.chip)
            def _(chip=chip):
                self.home(chip, 0, 0).wait_send()
                self.home(chip, 0, 1).wait_send()


def norm_apply(rows, gain):
    return rows * lax.rsqrt(jnp.mean(rows * rows, axis=-1, keepdims=True) + EPSILON) * gain


def gather(values, axis_name, axis):
    return lax.all_gather(values, axis_name, axis=axis, tiled=True)


def scatter(values, axis_name, axis):
    return lax.psum_scatter(values, axis_name, scatter_dimension=axis, tiled=True)

def once(shape):
    return pl.BlockSpec(
        shape, lambda i: (0,) * len(shape), pipeline_mode=pl.Buffered(buffer_count=1)
    )


def norm_rows(rows, gain):
    return rows * lax.rsqrt(jnp.mean(rows * rows, axis=-1, keepdims=True) + EPSILON) * gain


def lay_out_params(
    taps_ref, rows_ref, gates_ref, resets_ref,
    taps_out, vec_out, wr_out, we_out, keep_out, square, moved,
):
    used, width = rows_ref.shape[1], gates_ref.shape[2]
    columns = vec_out.shape[1]
    taps_out[...] = jnp.zeros_like(taps_out)
    taps_out[:, 0:used] = taps_ref[...]
    vec_out[...] = jnp.zeros_like(vec_out)
    vec_out[3:4, :] = jnp.full((1, columns), 2.0, jnp.float32)
    vec_out[0:4, 0:used] = rows_ref[...]
    decay = vec_out[3:4, :]
    vec_out[3:4, :] = -8.0 * jnp.log1p(jnp.exp(-decay))
    vec_out[4:5, :] = 8.0 * jax.nn.sigmoid(-decay)
    for k, out in enumerate((wr_out, we_out)):
        square[...] = jnp.zeros_like(square)
        square[0:width, 0:width] = gates_ref[k, 1].astype(jnp.float32)
        moved[...] = pltpu.roll(pltpu.roll(square[...], width, 0), width, 1)
        square[...] = jnp.zeros_like(square)
        square[0:width, 0:width] = gates_ref[k, 0].astype(jnp.float32)
        out[...] = (square[...] + moved[...]).astype(jnp.bfloat16)
    resets = resets_ref[...]
    first = lax.broadcasted_iota(jnp.int32, resets.shape, 1) == 0
    one = jnp.where(first | (resets > 0), 0.0, 1.0)
    length = resets.shape[1]
    two = one * pltpu.roll(one, 1, 1)
    three = two * pltpu.roll(one, 2, 1)
    ahead = [pltpu.roll(item, length - k, 1) for k, item in ((1, one), (2, two), (3, three))]
    rows = jnp.concatenate(
        [one, one, two, three, *ahead, one, jnp.zeros((120, length), jnp.float32)], axis=0
    )
    for k in range(length // 128):
        turned = rows[:, k * 128 : (k + 1) * 128].T
        keep_out[k * 128 : (k + 1) * 128, :] = turned[:, 0:8]


def open_body(
    x_hbm, mix_ref, ffn_ref, cot, x_weight, y_weight, out_weight,
    taps_ref, rows_ref, gates_ref, resets_ref,
    full, cot_out, xy_full, out_full, mix_out, ffn_out, taps_out, vec_out, wr_out, we_out, keep_out,
    x_ref, xt_ref, yt_ref, ot_ref, brought, shards, blank, square, moved,
    normed, column, spread, gain_sent, gain_arrived, wide_sent, wide_arrived, wiped, *semaphores,
):
    r, h = lax.axis_index("row"), lax.axis_index("head")
    held_rows, share = shards.shape[1:]
    used, chans = xt_ref.shape[0], out_full.shape[0]

    def slot(full, first):
        def at(origin):
            lanes = pl.ds(pl.multiple_of(origin * share, share), share)
            return full.at[pl.ds(first, held_rows), lanes]

        return at

    lines = [
        LineGather(shards.at[k], slot(dst, first), *semaphores[3 * k : 3 * k + 3])
        for k, (dst, first) in enumerate(((xy_full, 0), (xy_full, chans), (out_full, 0)))
    ]
    wipes = [
        pltpu.make_async_copy(
            blank, dst.at[pl.ds(first + held_rows, chans - held_rows)], wiped.at[k]
        )
        for k, (dst, first) in enumerate(((xy_full, 0), (xy_full, chans), (out_full, 0)))
    ]
    plane = PlaneGather(normed, full, *semaphores[9:12])
    cot_plane = PlaneGather(
        cot, cot_out, *semaphores[12:15], source=pl.ds(0, cot_out.shape[2])
    )
    bring = Bring(
        (x_weight, y_weight, out_weight, x_hbm), (xt_ref, yt_ref, ot_ref, x_ref), brought
    )
    bring.start()
    gain_share = mix_ref.shape[1]
    low = lax.broadcasted_iota(jnp.int32, (8, 2 * gain_share), 1) < gain_share
    column[r] = jnp.zeros_like(column[r])
    column[r, 0:1, 0:gain_share] = mix_ref[...].astype(jnp.float32)
    column[r, 1:2, 0:gain_share] = ffn_ref[...].astype(jnp.float32)
    rows = column[r]
    column[r] = jnp.where(low, rows, pltpu.roll(pltpu.roll(rows, gain_share, 1), 7, 0))
    meet(True, "all")

    def up_line(t):
        return send_to(
            column.at[r], column.at[r], gain_sent.at[t], gain_arrived.at[r], "row", t
        )

    def from_line(t):
        return send_to(
            column.at[t], column.at[t], gain_sent.at[t], gain_arrived.at[t], "row", t
        )

    def over_plane(step, owner):
        return send_to(
            column, spread.at[owner], wide_sent.at[step], wide_arrived.at[owner], "head",
            lax.rem(h + step, PLANE),
        )

    for step in range(1, LINE):
        up_line(lax.rem(r + step, LINE)).start()
    for k, (line, source) in enumerate(zip(lines, (xt_ref, yt_ref, ot_ref))):
        bring.wait(k)
        shards[k, held_rows - 16 :, :] = jnp.zeros((16, share), jnp.bfloat16)
        shards[k, 0:used, :] = source[...]
        line.start()
    blank[...] = jnp.zeros_like(blank)
    for wipe in wipes:
        wipe.start()
    for step in range(1, LINE):
        from_line(lax.rem(r + step, LINE)).wait_recv()
    for step in range(1, PLANE):
        over_plane(step, h).start()
    cot_plane.start()
    spread[h] = column[...]
    for step in range(1, PLANE):
        over_plane(step, lax.rem(h + step, PLANE)).wait_recv()

    low = lax.broadcasted_iota(jnp.int32, (1, 2 * gain_share), 1) < gain_share
    for line_place in range(LINE):
        for pair in range(PLANE // 2):
            even = spread[2 * pair, line_place][0:1, :]
            odd = spread[2 * pair + 1, line_place][0:1, :]
            at = (line_place * (PLANE // 2) + pair) * 2 * gain_share
            end = at + 2 * gain_share
            mix_out[0:1, at:end] = jnp.where(low, even, pltpu.roll(odd, gain_share, 1))
            ffn_out[0:1, at:end] = jnp.where(low, pltpu.roll(even, gain_share, 1), odd)

    bring.wait(3)

    def make(i, unused):
        at = pl.ds(pl.multiple_of(i * CHUNK, CHUNK), CHUNK)
        normed[at, :] = norm_rows(x_ref[at, :].astype(jnp.float32), mix_out[...]).astype(
            jnp.bfloat16
        )
        return unused

    lax.fori_loop(0, x_ref.shape[0] // CHUNK, make, 0, unroll=UNROLL)
    plane.start()
    lay_out_params(
        taps_ref, rows_ref, gates_ref, resets_ref,
        taps_out, vec_out, wr_out, we_out, keep_out, square, moved,
    )
    cot_plane.relay(0)
    cot_plane.relay(1)
    lines[0].forward()
    cot_plane.rest()
    plane.relay(0)
    plane.relay(1)
    lines[1].forward()
    cot_plane.far_side()
    cot_plane.end()
    plane.rest()
    plane.far_side()
    plane.end()
    lines[2].forward()
    for line in lines:
        line.finish()
    for wipe in wipes:
        wipe.wait()
    for step in range(1, LINE):
        up_line(lax.rem(r + step, LINE)).wait_send()
    for step in range(1, PLANE):
        over_plane(step, h).wait_send()


def open_block(layer_in, gains, cot, weights, params):
    rows, width = layer_in.shape
    used, share = weights[0].shape
    chans, held_rows = -(-used // 128) * 128, -(-used // 16) * 16
    length = params[-1].shape[1]
    tile = (8, 2 * gains[0].shape[1])
    return pl.pallas_call(
        open_body,
        in_specs=[ANYWHERE, IN_VMEM, IN_VMEM] + [ANYWHERE] * 4 + [IN_VMEM] * 4,
        out_specs=[ANYWHERE] * 4 + [IN_VMEM] * 7,
        out_shape=[
            jax.ShapeDtypeStruct((PLANE, rows, width), jnp.bfloat16),
            jax.ShapeDtypeStruct((PLANE, rows, width // 2), jnp.bfloat16),
            jax.ShapeDtypeStruct((2 * chans, width), jnp.bfloat16),
            jax.ShapeDtypeStruct((chans, width), jnp.bfloat16),
            jax.ShapeDtypeStruct((1, width), jnp.float32),
            jax.ShapeDtypeStruct((1, width), jnp.float32),
            jax.ShapeDtypeStruct((4, chans), jnp.float32),
            jax.ShapeDtypeStruct((8, chans), jnp.float32),
            jax.ShapeDtypeStruct((chans, chans), jnp.bfloat16),
            jax.ShapeDtypeStruct((chans, chans), jnp.bfloat16),
            jax.ShapeDtypeStruct((length, 8), jnp.float32),
        ],
        scratch_shapes=[
            *held(layer_in, *weights),
            pltpu.VMEM((3, held_rows, share), jnp.bfloat16),
            pltpu.VMEM((chans - held_rows, width), jnp.bfloat16),
            pltpu.VMEM((chans, chans), jnp.float32),
            pltpu.VMEM((chans, chans), jnp.float32),
            pltpu.VMEM((rows, width), jnp.bfloat16),
            pltpu.VMEM((LINE,) + tile, jnp.float32),
            pltpu.VMEM((PLANE, LINE) + tile, jnp.float32),
            pltpu.SemaphoreType.DMA((LINE,)),
            pltpu.SemaphoreType.DMA((LINE,)),
            pltpu.SemaphoreType.DMA((PLANE,)),
            pltpu.SemaphoreType.DMA((PLANE,)),
            pltpu.SemaphoreType.DMA((3,)),
            *(LineGather.semaphores * 3),
            *(PlaneGather.semaphores * 2),
        ],
        compiler_params=pltpu.CompilerParams(
            collective_id=0, has_side_effects=True, vmem_limit_bytes=61 * 2**20
        ),
        name="open_block",
    )(layer_in, *gains, cot, *weights, *params)


def forward_linked_body(
    normed_ref, xy_hbm, ow_hbm, taps_ref, vec_ref, wr_ref, we_ref, keep_ref,
    x_hbm, gain_ref, gate_shard, up_shard,
    u_ref, by_ref, before_ref, states_ref, mixed_ref, residual_out, two_out, gate_out, up_out,
    xy_ref, ow_ref, x_ref, brought, residual_ref, two_ref, taken,
    window, conv, conv_low, rate, entry, carry, *links,
):
    step = pl.program_id(0)
    plane = PlaneReduce(*links[:10])
    gate_line = LineGather(gate_shard, lambda t: gate_out.at[t], *links[10:13])
    first_rows = up_shard.at[pl.ds(0, up_out.shape[1])]
    up_line = LineGather(first_rows, lambda t: up_out.at[t], *links[13:16])

    take = Bring((residual_ref, two_ref), (residual_out, two_out), taken)
    bring = Bring((xy_hbm, ow_hbm, x_hbm), (xy_ref, ow_ref, x_ref), brought)

    @pl.when(step == 0)
    def _():
        bring.start()
        meet(True, "near")
        gate_line.start()
        up_line.start()
        bring.wait(0, 1, 2)

    @pl.when(step > 0)
    def _():
        plane.pass_on(step - 1)

    @pl.when(step > 2)
    def _():
        plane.relay(step - 3)

    forward_step(
        normed_ref, xy_ref, taps_ref, vec_ref, wr_ref, we_ref, keep_ref,
        u_ref, by_ref, before_ref, states_ref, mixed_ref,
        window, conv, conv_low, rate, entry, carry,
    )
    plane.put(step, dot_plain(mixed_ref[...], ow_ref[...]).astype(jnp.bfloat16))

    @pl.when(step == 6)
    def _():
        gate_line.forward()

    @pl.when(step == PLANE - 1)
    def _():
        plane.relay(step - 2)
        plane.pass_on(step)
        plane.relay(step - 1)
        plane.relay(step)
        up_line.forward()
        plane.arrive()

        def make(i, unused):
            at = pl.ds(pl.multiple_of(i * CHUNK, CHUNK), CHUNK)
            residual = x_ref[at, :].astype(jnp.float32) + plane.total(at)
            residual_ref[at, :] = residual
            two_ref[at, :] = norm_rows(residual, gain_ref[...]).astype(jnp.bfloat16)
            return unused

        lax.fori_loop(0, x_ref.shape[0] // CHUNK, make, 0, unroll=UNROLL)
        take.start()
        plane.finish()
        gate_line.finish()
        up_line.finish()
        take.wait(0, 1)


def forward_linked(normed, xy, ow, taps, vec, wr, we, keep, layer_in, gain, gate_shard, up_shard):
    length, width = normed.shape
    chans = ow.shape[0]
    rows = length // PLANE
    share, units = up_shard.shape
    tile = lambda columns: pl.BlockSpec((rows, columns), lambda i: (i, 0))
    return pl.pallas_call(
        forward_linked_body,
        grid=(PLANE,),
        in_specs=[
            tile(width), ANYWHERE, ANYWHERE, once(taps.shape),
            once(vec.shape), once(wr.shape), once(we.shape), tile(keep.shape[1]),
            ANYWHERE, once(gain.shape), ANYWHERE, ANYWHERE,
        ],
        out_specs=[tile(chans)] * 5 + [ANYWHERE] * 4,
        out_shape=[
            jax.ShapeDtypeStruct((length, chans), jnp.bfloat16),
            jax.ShapeDtypeStruct((length, chans), jnp.float32),
            jax.ShapeDtypeStruct((length, chans), jnp.float32),
            jax.ShapeDtypeStruct((length, chans), jnp.bfloat16),
            jax.ShapeDtypeStruct((length, chans), jnp.bfloat16),
            jax.ShapeDtypeStruct((rows, width), jnp.float32),
            jax.ShapeDtypeStruct((rows, width), jnp.bfloat16),
            jax.ShapeDtypeStruct((LINE,) + gate_shard.shape, jnp.bfloat16),
            jax.ShapeDtypeStruct((LINE, share // 2, units), jnp.bfloat16),
        ],
        scratch_shapes=[
            *held(xy, ow, layer_in),
            pltpu.VMEM((rows, width), jnp.float32),
            pltpu.VMEM((rows, width), jnp.bfloat16),
            pltpu.SemaphoreType.DMA((2,)),
            pltpu.VMEM((rows + 8, chans), jnp.float32),
            pltpu.VMEM((rows, chans), jnp.float32),
            pltpu.VMEM((rows, chans), jnp.bfloat16),
            pltpu.VMEM((rows, chans), jnp.float32),
            pltpu.VMEM((rows, chans), jnp.float32),
            pltpu.VMEM((8, chans), jnp.float32),
            *PlaneReduce.buffers(rows, width),
            *PlaneReduce.semaphores,
            *(LineGather.semaphores * 2),
        ],
        compiler_params=pltpu.CompilerParams(
            collective_id=1, has_side_effects=True, vmem_limit_bytes=61 * 2**20
        ),
        name="mixer_forward_linked",
    )(normed, xy, ow, taps, vec, wr, we, keep, layer_in, gain, gate_shard, up_shard)


def ffn_up_body(
    own_two, gate_ref, own_cot, cot_half, up_half, up_shard, down_shard,
    two_out, cot_out, up_out, down_out, gates_out, ups_out, hidden_out, parts_out,
    two, cot, up, gates, ups, hidden, total, down_parts, copied, brought, *semaphores,
):
    h = lax.axis_index("head")
    rows = own_two.shape[0]
    units = gates.shape[1]
    width, share = own_two.shape[1], up_shard.shape[0]
    half = share // 2
    late_columns = pl.ds(width // 2, width // 2)
    up_line = LineGather(
        up_shard.at[pl.ds(half, half)],
        lambda t: up.at[pl.ds(pl.multiple_of(t * share + half, half), half)],
        *semaphores[0:3],
    )
    down_line = LineGather(down_shard, lambda t: down_out.at[t], *semaphores[3:6])
    two_plane = PlaneGather(own_two, two, *semaphores[6:9])
    cot_plane = PlaneGather(
        own_cot, cot, *semaphores[9:12], source=late_columns, target=late_columns
    )
    inward = [
        pltpu.make_async_copy(up_half.at[t], up.at[pl.ds(t * share, half)], brought.at[t])
        for t in range(LINE)
    ]
    inward.append(
        pltpu.make_async_copy(cot_half, cot.at[:, :, pl.ds(0, width // 2)], brought.at[LINE])
    )
    outward = [
        pltpu.make_async_copy(src, dst, copied.at[k])
        for k, (src, dst) in enumerate(
            (
                (two, two_out), (cot, cot_out), (up, up_out), (gates, gates_out),
                (ups, ups_out), (hidden, hidden_out), (down_parts, parts_out),
            )
        )
    ]
    meet(True, "near")
    up_line.start()
    down_line.start()
    two_plane.start()
    for copy in inward:
        copy.start()

    def at_block(block):
        return pl.ds(pl.multiple_of(block * rows, rows), rows)

    def make_gates(block):
        gates[at_block(block), :] = dot_plain(two[block], gate_ref[...])

    gates[at_block(h), :] = dot_plain(own_two[...], gate_ref[...])
    two_plane.relay(0)
    two_plane.beside()
    make_gates(two_plane.side)
    two_plane.relay(1)
    cot_plane.start()
    two_plane.rest()
    make_gates(two_plane.x)
    make_gates(two_plane.y)
    up_line.forward()
    two_plane.far_side()
    make_gates(two_plane.far)
    two_plane.end(beside=False)
    outward[0].start()
    cot_plane.relay(0)
    make_gates(across_of(two_plane.side))
    make_gates(along_of(two_plane.side))
    cot_plane.relay(1)
    make_gates(across_of(along_of(two_plane.side)))
    outward[3].start()
    up_line.finish()
    for copy in inward:
        copy.wait()
    outward[2].start()

    def make_hidden(block, unused):
        at = at_block(block)
        ups[at, :] = dot_plain(two[block], up[...])

        def make(i, unused):
            here = pl.ds(pl.multiple_of(block * rows + i * CHUNK, CHUNK), CHUNK)
            hidden[here, :] = (gelu_only(gates[here, :]) * ups[here, :]).astype(jnp.bfloat16)
            return unused

        lax.fori_loop(0, rows // CHUNK, make, 0, unroll=UNROLL)
        return unused

    lax.fori_loop(0, 2, make_hidden, 0)
    cot_plane.rest()
    lax.fori_loop(2, 5, make_hidden, 0)
    cot_plane.far_side()
    down_line.forward()
    lax.fori_loop(5, PLANE, make_hidden, 0)
    outward[4].start()
    outward[5].start()
    cot_plane.end()
    outward[1].start()
    total[...] = contract_first(cot[0], hidden[0:rows, :])

    def add_down(block, unused):
        total[...] += contract_first(cot[block], hidden[at_block(block), :])
        return unused

    lax.fori_loop(1, PLANE, add_down, 0)
    to_parts(total, down_parts)
    outward[6].start()
    down_line.finish()
    for copy in outward:
        copy.wait()


def ffn_up(own_two, gate, own_cot, cot_half, up_half, up_shard, down_shard):
    rows, width = own_two.shape
    share, units = up_shard.shape
    length = rows * PLANE
    group = jax.ShapeDtypeStruct((PLANE, rows, width), jnp.bfloat16)
    weight = jax.ShapeDtypeStruct((LINE, share, units), jnp.bfloat16)
    return pl.pallas_call(
        ffn_up_body,
        in_specs=[IN_VMEM, IN_VMEM] + [ANYWHERE] * 5,
        out_specs=[ANYWHERE] * 8,
        out_shape=[
            group,
            group,
            jax.ShapeDtypeStruct((width, units), jnp.bfloat16),
            weight,
            jax.ShapeDtypeStruct((length, units), jnp.float32),
            jax.ShapeDtypeStruct((length, units), jnp.float32),
            jax.ShapeDtypeStruct((length, units), jnp.bfloat16),
            weight,
        ],
        scratch_shapes=[
            pltpu.VMEM((PLANE, rows, width), jnp.bfloat16),
            pltpu.VMEM((PLANE, rows, width), jnp.bfloat16),
            pltpu.VMEM((width, units), jnp.bfloat16),
            pltpu.VMEM((length, units), jnp.float32),
            pltpu.VMEM((length, units), jnp.float32),
            pltpu.VMEM((length, units), jnp.bfloat16),
            pltpu.VMEM((width, units), jnp.float32),
            pltpu.VMEM((LINE, share, units), jnp.bfloat16),
            pltpu.SemaphoreType.DMA((7,)),
            pltpu.SemaphoreType.DMA((LINE + 1,)),
            *(LineGather.semaphores * 2),
            *(PlaneGather.semaphores * 2),
        ],
        compiler_params=pltpu.CompilerParams(
            collective_id=2, has_side_effects=True, vmem_limit_bytes=61 * 2**20
        ),
        name="ffn_up",
    )(own_two, gate, own_cot, cot_half, up_half, up_shard, down_shard)
def far_first(step):
    chip = lax.div(lax.axis_index("head"), 2)
    place = lax.div(step, 2)
    x = lax.rem(lax.rem(chip, 2) + 1 - lax.div(place, 2), 2)
    y = lax.rem(lax.div(chip, 2) + 1 + lax.rem(place, 2), 2)
    return 2 * (2 * y + x) + lax.rem(step, 2)


def norm_back(rows, gain, incoming):
    scale = lax.rsqrt(jnp.mean(rows * rows, axis=-1, keepdims=True) + EPSILON)
    scaled = incoming * gain
    inner = jnp.mean(scaled * rows, axis=-1, keepdims=True)
    return scale * scaled - rows * (scale * scale * scale * inner), incoming * rows * scale


def to_parts(total, parts):
    rows = parts.shape[1]
    step = 64

    def move(i, unused):
        at = pl.ds(pl.multiple_of(i * step, step), step)
        for t in range(LINE):
            here = pl.ds(pl.multiple_of(t * rows + i * step, step), step)
            parts[t, at, :] = total[here, :].astype(jnp.bfloat16)
        return unused

    lax.fori_loop(0, rows // step, move, 0)


def to_turned_parts(total, parts, places):
    share = parts.shape[2]
    step = 32
    for first, target, count in places:

        def move(i, unused, first=first, target=target):
            here = pl.ds(pl.multiple_of(first + i * step, step), step)
            at = pl.ds(pl.multiple_of(target + i * step, step), step)
            for t in range(LINE):
                parts[t, at, :] = total[here, t * share : (t + 1) * share].astype(jnp.bfloat16)
            return unused

        lax.fori_loop(0, count // step, move, 0)


def ffn_back_body(
    cot_ref, two_ref, gates_ref, ups_ref, gate_hbm, up_hbm, down_hbm, parts_hbm,
    residual_hbm, own_cot_hbm, gain_ref,
    d_ups_ref, parts_out, down_out, d_res_ref, d_low_ref, gain_out,
    gate_ref, up_ref, down_ref, parts, brought, late, gate_parts, taken,
    total, d_gates, d_hidden, eight, *links,
):
    step = pl.program_id(0)
    line = LineReduce(parts_hbm, parts, *links[:5])
    plane = PlaneReduce(*links[5:])
    rows = cot_ref.shape[0]

    bring = Bring(
        (down_hbm, gate_hbm, up_hbm, parts_hbm), (down_ref, gate_ref, up_ref, parts), brought
    )
    take = Bring((gate_parts,), (parts_out,), taken)
    into_outputs = Bring((residual_hbm, own_cot_hbm), (d_res_ref, d_low_ref), late)

    @pl.when(step == 0)
    def _():
        bring.start()
        meet(True, "near")
        line.start()
        into_outputs.start()
        bring.wait(0, 1, 2, 3)

    @pl.when((step > 2) & (step <= PLANE + 2))
    def _():
        plane.relay(far_first(step - 3))

    @pl.when(step < PLANE)
    def _():
        d_hidden[...] = dot_plain(cot_ref[...], down_ref[...])

        def make(i, unused):
            at = pl.ds(pl.multiple_of(i * CHUNK, CHUNK), CHUNK)
            gelu_gate, slope = gelu_both(gates_ref[at, :])
            through = d_hidden[at, :]
            d_gates[step, at, :] = (through * ups_ref[at, :] * slope).astype(jnp.bfloat16)
            d_ups_ref[at, :] = (through * gelu_gate).astype(jnp.bfloat16)
            return unused

        lax.fori_loop(0, rows // CHUNK, make, 0, unroll=UNROLL)

        @pl.when(step > 0)
        def _():
            plane.pass_on(far_first(step - 1))

        value = contract_last(d_gates[step], gate_ref[...]) + contract_last(
            d_ups_ref[...], up_ref[...]
        )
        plane.put(far_first(step), value.astype(jnp.bfloat16))

    @pl.when(step == PLANE)
    def _():
        total[...] = contract_first(two_ref[...], d_gates[0])

    @pl.when(step > PLANE)
    def _():
        total[...] += contract_first(two_ref[...], d_gates[step - PLANE])

    @pl.when(step == PLANE)
    def _():
        plane.pass_on(far_first(step - 1))

    @pl.when(step == 3)
    def _():
        line.forward()

    @pl.when(step == 2 * PLANE - 1)
    def _():
        to_parts(total, gate_parts)
        take.start()
        plane.arrive()
        into_outputs.wait(0, 1)
        eight[...] = jnp.zeros_like(eight)

        def back(i, unused):
            at = pl.ds(pl.multiple_of(i * CHUNK, CHUNK), CHUNK)
            d_rows, d_gain = norm_back(d_res_ref[at, :], gain_ref[...], plane.total(at))
            d_residual = d_low_ref[at, :].astype(jnp.float32) + d_rows
            d_res_ref[at, :] = d_residual
            d_low_ref[at, :] = d_residual.astype(jnp.bfloat16)
            eight[...] += sum_eight(d_gain)
            return unused

        lax.fori_loop(0, rows // CHUNK, back, 0, unroll=UNROLL)
        gain_out[...] = jnp.sum(eight[...], axis=0, keepdims=True)

        def write(at, value):
            down_out[at, :] = value

        line.finish(write)
        plane.finish()
        take.wait(0)


def ffn_back(
    cot_group, two_group, gates, ups, gate, up, down, parts, residual, own_cot, gain
):
    length, width = cot_group.shape
    units = gate.shape[1]
    rows, share = length // PLANE, width // LINE
    tile = lambda columns: pl.BlockSpec(
        (rows, columns), lambda i: (far_first(jnp.minimum(i, PLANE - 1)), 0)
    )
    later = lambda columns: pl.BlockSpec(
        (rows, columns), lambda i: (far_first(jnp.maximum(i - PLANE, 0)), 0)
    )
    return pl.pallas_call(
        ffn_back_body,
        grid=(2 * PLANE,),
        in_specs=[
            tile(width), later(width), tile(units), tile(units),
            *([ANYWHERE] * 6), once(gain.shape),
        ],
        out_specs=[
            tile(units), ANYWHERE, once((share, units)),
            once((rows, width)), once((rows, width)), once((1, width)),
        ],
        out_shape=[
            jax.ShapeDtypeStruct((length, units), jnp.bfloat16),
            jax.ShapeDtypeStruct((LINE, share, units), jnp.bfloat16),
            jax.ShapeDtypeStruct((share, units), jnp.float32),
            jax.ShapeDtypeStruct((rows, width), jnp.float32),
            jax.ShapeDtypeStruct((rows, width), jnp.bfloat16),
            jax.ShapeDtypeStruct((1, width), jnp.float32),
        ],
        scratch_shapes=[
            *held(gate, up, down, parts),
            pltpu.SemaphoreType.DMA((2,)),
            *held(parts),
            pltpu.VMEM((width, units), jnp.float32),
            pltpu.VMEM((PLANE, rows, units), jnp.bfloat16),
            pltpu.VMEM((rows, units), jnp.float32),
            pltpu.VMEM((8, width), jnp.float32),
            *LineReduce.buffers(share, units),
            *LineReduce.semaphores,
            *PlaneReduce.buffers(rows, width),
            *PlaneReduce.semaphores,
        ],
        compiler_params=pltpu.CompilerParams(
            collective_id=4, has_side_effects=True, vmem_limit_bytes=63 * 2**20
        ),
        name="ffn_back",
    )(cot_group, two_group, gates, ups, gate, up, down, parts, residual, own_cot, gain)


def turn_body(
    two_ref, d_ups_ref, parts_hbm, block, mixed_hbm, ow_hbm,
    up_hbm, out_hbm, gate_out, d_mixed_hbm,
    gate_parts, mixed_ref, ow_ref, brought, up_parts, out_parts, d_mixed_out, taken,
    full, total, out_total, *links,
):
    step = pl.program_id(0)
    line = LineReduce(parts_hbm, gate_parts, *links[:5])
    plane = PlaneGather(block, full, *links[5:])
    rows = two_ref.shape[0]

    take = Bring(
        (up_parts, out_parts, d_mixed_out), (up_hbm, out_hbm, d_mixed_hbm), taken
    )
    bring = Bring(
        (parts_hbm, mixed_hbm, ow_hbm), (gate_parts, mixed_ref, ow_ref), brought
    )

    @pl.when(step == 0)
    def _():
        bring.start()
        meet(True, "near")
        line.start()
        plane.start()
        total[...] = contract_first(two_ref[...], d_ups_ref[...])

    @pl.when(step > 0)
    def _():
        total[...] += contract_first(two_ref[...], d_ups_ref[...])

    @pl.when(step == 3)
    def _():
        plane.relay(0)

    @pl.when(step == PLANE - 2)
    def _():
        bring.wait(0)
        line.forward()
        plane.relay(1)

    @pl.when(step == PLANE - 1)
    def _():
        bring.wait(1, 2)

        def add(owner, start=False):
            at = pl.ds(pl.multiple_of(owner * rows, rows), rows)
            d_mixed_out[at, :] = contract_last(full[owner], ow_ref[...])
            value = contract_first(mixed_ref[at, :], full[owner])
            out_total[...] = value if start else out_total[...] + value

        plane.beside()
        add(plane.side, start=True)
        to_parts(total, up_parts)
        take.copies[0].start()
        plane.rest()
        add(plane.x)
        add(plane.y)
        plane.far_side()
        add(plane.far)
        plane.end(beside=False)
        add(plane.h)
        add(across_of(plane.side))
        add(along_of(plane.side))
        add(across_of(along_of(plane.side)))
        take.copies[2].start()
        kept = out_parts.shape[1]
        to_turned_parts(out_total, out_parts, ((0, 0, kept),))
        take.copies[1].start()

        def write(at, value):
            gate_out[at, :] = value

        line.finish(write)
        take.wait(0, 1, 2)


def turn(two_group, d_ups, gate_parts, block, mixed, ow, kept):
    length, width = two_group.shape
    units, chans = d_ups.shape[1], mixed.shape[1]
    rows, share = length // PLANE, width // LINE
    tile = lambda columns: pl.BlockSpec((rows, columns), lambda i: (i, 0))
    return pl.pallas_call(
        turn_body,
        grid=(PLANE,),
        in_specs=[
            tile(width), tile(units), ANYWHERE, ANYWHERE, ANYWHERE, ANYWHERE,
        ],
        out_specs=[
            ANYWHERE, ANYWHERE, once((share, units)), ANYWHERE,
        ],
        out_shape=[
            jax.ShapeDtypeStruct(gate_parts.shape, jnp.bfloat16),
            jax.ShapeDtypeStruct((LINE, kept, share), jnp.bfloat16),
            jax.ShapeDtypeStruct((share, units), jnp.float32),
            jax.ShapeDtypeStruct((length, chans), jnp.float32),
        ],
        scratch_shapes=[
            *held(gate_parts, mixed, ow),
            pltpu.VMEM(gate_parts.shape, jnp.bfloat16),
            pltpu.VMEM((LINE, kept, share), jnp.bfloat16),
            pltpu.VMEM((length, chans), jnp.float32),
            pltpu.SemaphoreType.DMA((3,)),
            pltpu.VMEM((PLANE, rows, width), jnp.bfloat16),
            pltpu.VMEM((width, units), jnp.float32),
            pltpu.VMEM((chans, width), jnp.float32),
            *LineReduce.buffers(share, units),
            *LineReduce.semaphores,
            *PlaneGather.semaphores,
        ],
        compiler_params=pltpu.CompilerParams(
            collective_id=5, has_side_effects=True, vmem_limit_bytes=61 * 2**20
        ),
        name="turn",
    )(two_group, d_ups, gate_parts, block, mixed, ow)


def pack_small(head_width, taps, vec, params, wr, we, small):
    columns = small.shape[1]
    step = 16
    last = (2 * head_width + 7) // 8 * 8

    def move(i, unused):
        at = pl.ds(pl.multiple_of(i * step, step), step)
        shape = (step, columns)
        row = lax.broadcasted_iota(jnp.int32, shape, 0) + i * step
        left = lax.broadcasted_iota(jnp.int32, shape, 1) < head_width
        rate, entry = wr[at, :], we[at, :]
        first = jnp.where(left, rate, pltpu.roll(entry, head_width, 1))
        second = jnp.where(left, pltpu.roll(rate, columns - head_width, 1), entry)
        small[at, :] = jnp.where(row < head_width, first, second).astype(jnp.bfloat16)
        return unused

    lax.fori_loop(0, last // step, move, 0)
    scaled = vec[0:4, :] * jnp.concatenate(
        [jnp.ones((3, columns), jnp.float32), params[4:5, :]], axis=0
    )
    tail = jnp.concatenate([taps[...], scaled], axis=0).astype(jnp.bfloat16)
    here = last // step * step
    rate, entry = wr[here : here + 8, :], we[here : here + 8, :]
    left = lax.broadcasted_iota(jnp.int32, (8, columns), 1) < head_width
    rest = jnp.where(left, pltpu.roll(rate, columns - head_width, 1), entry).astype(jnp.bfloat16)
    small[here : here + 16, :] = jnp.concatenate([rest, tail], axis=0)
    if small.shape[0] > here + 16:
        small[here + 16 :, :] = jnp.zeros_like(small[here + 16 :, :])


def split_gains(mix, ffn, out):
    share = out.shape[2] // 2
    low = lax.broadcasted_iota(jnp.int32, (1, 2 * share), 1) < share
    for r in range(LINE):
        lines = []
        for pair in range(PLANE // 2):
            at = (r * (PLANE // 2) + pair) * 2 * share
            one, two = mix[:, at : at + 2 * share], ffn[:, at : at + 2 * share]
            lines.append(jnp.where(low, one, pltpu.roll(two, share, 1)))
            lines.append(jnp.where(low, pltpu.roll(one, share, 1), two))
        out[r] = jnp.concatenate(lines, axis=0)


def backward_linked_body(
    head_width,
    d_mixed_ref, xy_hbm, taps_ref, vec_ref, wr_ref, we_ref, keep_ref,
    u_ref, u_prev_ref, by_ref, before_ref, states_ref, normed_ref, up_hbm, out_hbm,
    x_hbm, gain_ref, d_residual_hbm, ffn_gain_ref,
    parts_out, up_out, out_out, in_grad, gains_out, small_out,
    xy_ref, up_parts, out_parts, brought, late, xy_parts, taken,
    out_sum, taps_sum, vec_sum, wr_sum, we_sum, small, small_parts, d_xy, d_all, xy_total, eight, *rest,
):
    scratch, links = rest[:10], rest[10:]
    step = pl.program_id(0)
    block = PLANE - 1 - step
    line = LineReduce(up_hbm, up_parts, *links[:5])
    out_line = LineReduce(out_hbm, out_parts, *links[5:10])
    small_line = LineReduce(small_parts, small_parts, *links[10:15])
    plane = PlaneReduce(*links[15:])

    bring = Bring(
        (xy_hbm, up_hbm, out_hbm), (xy_ref, up_parts, out_parts), brought
    )
    take = Bring((xy_parts,), (parts_out,), taken)
    d_residual_ref = xy_total.at[0 : x_hbm.shape[0]]
    bring_late = Bring((x_hbm, d_residual_hbm), (in_grad, d_residual_ref), late)

    @pl.when(step == 0)
    def _():
        bring.start()
        meet(True, "near")
        line.start()
        out_line.start()
        bring.wait(0, 1, 2)

    @pl.when((step > 0) & (step <= PLANE))
    def _():
        plane.pass_on(block + 1)

    @pl.when((step > 2) & (step <= PLANE))
    def _():
        plane.relay(block + 3)

    @pl.when(step == 3)
    def _():
        line.forward()

    @pl.when(step < PLANE)
    def _():
        backward_step(
            step == 0, step == PLANE - 1, d_mixed_ref, taps_ref, vec_ref, wr_ref, we_ref,
            keep_ref, u_ref, u_prev_ref, by_ref, before_ref, states_ref, d_xy,
            taps_sum, vec_sum, wr_sum, we_sum, *scratch,
        )
        d_all[step] = d_xy[...]
        plane.put(block, dot_plain(d_xy[...], xy_ref[...]).astype(jnp.bfloat16))

    @pl.when(step == PLANE)
    def _():
        pack_small(head_width, taps_sum, vec_sum, vec_ref, wr_sum, we_sum, small)
        share = small_parts.shape[1]
        for t in range(LINE):
            small_parts[t] = small[t * share : (t + 1) * share, :]
        small_line.start()
        xy_total[...] = contract_first(d_all[0], normed_ref[...])

    @pl.when(step > PLANE)
    def _():
        xy_total[...] += contract_first(d_all[step - PLANE], normed_ref[...])

    @pl.when(step == PLANE + 2)
    def _():
        plane.relay(1)

    @pl.when(step == PLANE + 4)
    def _():
        out_line.forward()

    @pl.when(step == PLANE + 5)
    def _():
        plane.relay(0)

    @pl.when(step == 2 * PLANE - 1)
    def _():
        small_line.forward()
        kept, chans = out_parts.shape[1], d_xy.shape[1] // 2
        to_turned_parts(xy_total, xy_parts, ((0, 0, kept), (chans, kept, kept)))
        bring_late.start()
        take.start()

        def write(at, value):
            up_out[at, :] = value

        line.finish(write)
        plane.arrive()
        bring_late.wait(0, 1)
        eight[...] = jnp.zeros_like(eight)

        def back(i, unused):
            at = pl.ds(pl.multiple_of(i * CHUNK, CHUNK), CHUNK)
            d_rows, d_gain = norm_back(
                in_grad[at, :].astype(jnp.float32), gain_ref[...], plane.total(at)
            )
            in_grad[at, :] = (xy_total[at, :] + d_rows).astype(jnp.bfloat16)
            eight[...] += sum_eight(d_gain)
            return unused

        lax.fori_loop(0, in_grad.shape[0] // CHUNK, back, 0, unroll=UNROLL)
        split_gains(jnp.sum(eight[...], axis=0, keepdims=True), ffn_gain_ref[...], gains_out)

        def write_out(at, value):
            out_sum[at, :] = value

        def write_small(at, value):
            small_out[at, :] = value.astype(jnp.bfloat16)

        out_line.finish(write_out)
        out_out[...] = out_sum[0 : out_out.shape[0], :]
        small_line.finish(write_small)
        plane.finish()
        take.wait(0)


def backward_linked(
    d_mixed, xy, taps, vec, wr, we, keep, u, by, before, states, normed, up_parts, out_parts,
    layer_in, gain, d_residual, ffn_gain, head_width, used,
):
    length, width = normed.shape
    chans, units = d_mixed.shape[1], up_parts.shape[2]
    rows, share = length // PLANE, width // LINE
    kept = out_parts.shape[1]
    place = lambda i: PLANE - 1 - jnp.minimum(i, PLANE - 1)
    tile = lambda columns: pl.BlockSpec((rows, columns), lambda i: (place(i), 0))
    later = lambda columns: pl.BlockSpec(
        (rows, columns), lambda i: (PLANE - 1 - jnp.maximum(i - PLANE, 0), 0)
    )
    ahead = pl.BlockSpec((16, chans), lambda i: (jnp.maximum(place(i) * (rows // 16) - 1, 0), 0))
    small_share = -(-((2 * head_width + 7) // 8 * 8 + 8) // (LINE * 32)) * 32
    gain_terms = (LINE, PLANE, width // (LINE * PLANE) * 2)
    return pl.pallas_call(
        functools.partial(backward_linked_body, head_width),
        grid=(2 * PLANE,),
        in_specs=[
            tile(chans), ANYWHERE, once(taps.shape), once(vec.shape), once(wr.shape),
            once(we.shape), tile(keep.shape[1]), tile(chans), ahead, tile(chans), tile(chans),
            tile(chans), later(width), ANYWHERE, ANYWHERE,
            ANYWHERE, once(gain.shape), ANYWHERE, once(ffn_gain.shape),
        ],
        out_specs=[
            ANYWHERE, once((share, units)), once((used, share)),
            once((rows, width)), once(gain_terms), once((small_share, chans)),
        ],
        out_shape=[
            jax.ShapeDtypeStruct((LINE, 2 * kept, share), jnp.bfloat16),
            jax.ShapeDtypeStruct((share, units), jnp.float32),
            jax.ShapeDtypeStruct((used, share), jnp.float32),
            jax.ShapeDtypeStruct((rows, width), jnp.bfloat16),
            jax.ShapeDtypeStruct(gain_terms, jnp.float32),
            jax.ShapeDtypeStruct((small_share, chans), jnp.bfloat16),
        ],
        scratch_shapes=[
            *held(xy, up_parts, out_parts),
            pltpu.SemaphoreType.DMA((2,)),
            pltpu.VMEM((LINE, 2 * kept, share), jnp.bfloat16),
            pltpu.SemaphoreType.DMA((1,)),
            pltpu.VMEM((kept, share), jnp.float32),
            pltpu.VMEM(taps.shape, jnp.float32),
            pltpu.VMEM(vec.shape, jnp.float32),
            pltpu.VMEM(wr.shape, jnp.float32),
            pltpu.VMEM(we.shape, jnp.float32),
            pltpu.VMEM((LINE * small_share, chans), jnp.bfloat16),
            pltpu.VMEM((LINE, small_share, chans), jnp.bfloat16),
            pltpu.VMEM((rows, 2 * chans), jnp.bfloat16),
            pltpu.VMEM((PLANE, rows, 2 * chans), jnp.bfloat16),
            pltpu.VMEM((2 * chans, width), jnp.float32),
            pltpu.VMEM((8, width), jnp.float32),
            pltpu.VMEM((rows + 8, chans), jnp.float32),
            pltpu.VMEM((rows, chans), jnp.float32),
            pltpu.VMEM((rows, chans), jnp.bfloat16),
            pltpu.VMEM((rows, chans), jnp.float32),
            pltpu.VMEM((rows, chans), jnp.float32),
            pltpu.VMEM((rows + 8, chans), jnp.float32),
            pltpu.VMEM((rows, chans), jnp.bfloat16),
            pltpu.VMEM((rows, chans), jnp.bfloat16),
            pltpu.VMEM((8, chans), jnp.float32),
            pltpu.VMEM((64, chans), jnp.float32),
            *LineReduce.buffers(share, units),
            *LineReduce.semaphores,
            *LineReduce.buffers(kept, share),
            *LineReduce.semaphores,
            *LineReduce.buffers(small_share, chans),
            *LineReduce.semaphores,
            *PlaneReduce.buffers(rows, width),
            *PlaneReduce.semaphores,
        ],
        compiler_params=pltpu.CompilerParams(
            collective_id=6, has_side_effects=True, vmem_limit_bytes=61 * 2**20
        ),
        name="mixer_backward_linked",
    )(
        d_mixed, xy, taps, vec, wr, we, keep, u, u, by, before, states, normed,
        up_parts, out_parts, layer_in, gain, d_residual, ffn_gain,
    )


def close_body(
    hidden_ref, down_hbm, xy_hbm, residual_hbm, gains_ref, small,
    layer_out, x_out, y_out, gains_out, small_out,
    down_ref, xy_parts, residual_ref, brought, xy_sum,
    gathered, line_gains, both_gains, plane_gains,
    gain_sent, gain_arrived, wide_sent, wide_arrived, *links,
):
    r, h = lax.axis_index("row"), lax.axis_index("head")
    step = pl.program_id(0)
    xy_line = LineReduce(xy_hbm, xy_parts, *links[0:5])
    small_line = LineGather(small, lambda t: gathered.at[t], *links[5:8])
    plane = PlaneReduce(*links[8:])

    def to_row(t, owner):
        return send_to(
            gains_ref.at[t], line_gains.at[owner], gain_sent.at[t], gain_arrived.at[owner],
            "row", t,
        )

    def over_plane(place, owner):
        return send_to(
            both_gains, plane_gains.at[owner], wide_sent.at[place], wide_arrived.at[owner],
            "head", lax.rem(h + place, PLANE),
        )

    bring = Bring(
        (down_hbm, xy_hbm, residual_hbm), (down_ref, xy_parts, residual_ref), brought
    )

    @pl.when(step == 0)
    def _():
        bring.start()
        meet(True, "all")
        for place in range(1, LINE):
            to_row(lax.rem(r + place, LINE), r).start()
        small_line.start()
        xy_line.start()
        bring.wait(0, 1, 2)

    @pl.when(step > 0)
    def _():
        plane.pass_on(far_first(step - 1))

    @pl.when(step > 2)
    def _():
        plane.relay(far_first(step - 3))

    plane.put(far_first(step), contract_last(hidden_ref[...], down_ref[...]).astype(jnp.bfloat16))

    @pl.when(step == 2)
    def _():
        total = gains_ref[r]
        for place in range(1, LINE):
            t = lax.rem(r + place, LINE)
            to_row(t, t).wait_recv()
            total = total + line_gains[t]
        both_gains[...] = total
        for place in range(1, PLANE):
            over_plane(place, h).start()

    @pl.when(step == PLANE - 1)
    def _():
        small_line.forward()
        xy_line.forward()
        plane.relay(far_first(step - 2))
        plane.pass_on(far_first(step))
        plane.relay(far_first(step - 1))
        plane.relay(far_first(step))
        total = both_gains[...]
        for place in range(1, PLANE):
            owner = lax.rem(h + place, PLANE)
            over_plane(place, owner).wait_recv()
            total = total + plane_gains[owner]
        mine = lax.broadcasted_iota(jnp.int32, total.shape, 0) == h
        gains_out[...] = jnp.sum(jnp.where(mine, total, 0.0), axis=0, keepdims=True)
        plane.arrive()

        def make(i, unused):
            at = pl.ds(pl.multiple_of(i * CHUNK, CHUNK), CHUNK)
            layer_out[at, :] = (residual_ref[at, :] + plane.total(at)).astype(jnp.bfloat16)
            return unused

        lax.fori_loop(0, residual_ref.shape[0] // CHUNK, make, 0)
        def write(at, value):
            xy_sum[at, :] = value

        xy_line.finish(write)
        used, kept = x_out.shape[0], xy_sum.shape[0] // 2
        x_out[...] = xy_sum[0:used, :]
        y_out[...] = xy_sum[kept : kept + used, :]
        small_line.finish()
        small_out[...] = gathered[...].astype(jnp.float32)
        plane.finish()
        for place in range(1, LINE):
            to_row(lax.rem(r + place, LINE), r).wait_send()
        for place in range(1, PLANE):
            over_plane(place, h).wait_send()


def close_block(hidden, down, xy_parts, residual, gains, small, used):
    length, units = hidden.shape
    rows, width = residual.shape
    both, share = xy_parts.shape[1:]
    return pl.pallas_call(
        close_body,
        grid=(PLANE,),
        in_specs=[
            pl.BlockSpec((rows, units), lambda i: (far_first(i), 0)), ANYWHERE,
            ANYWHERE, ANYWHERE, once(gains.shape), once(small.shape),
        ],
        out_specs=[
            once((rows, width)), once((used, share)), once((used, share)), once((1, gains.shape[2])),
            once((LINE,) + small.shape),
        ],
        out_shape=[
            jax.ShapeDtypeStruct((rows, width), jnp.bfloat16),
            jax.ShapeDtypeStruct((used, share), jnp.float32),
            jax.ShapeDtypeStruct((used, share), jnp.float32),
            jax.ShapeDtypeStruct((1, gains.shape[2]), jnp.float32),
            jax.ShapeDtypeStruct((LINE,) + small.shape, jnp.float32),
        ],
        scratch_shapes=[
            *held(down, xy_parts, residual),
            pltpu.VMEM((both, share), jnp.float32),
            pltpu.VMEM((LINE,) + small.shape, jnp.bfloat16),
            pltpu.VMEM(gains.shape, jnp.float32),
            pltpu.VMEM(gains.shape[1:], jnp.float32),
            pltpu.VMEM((PLANE,) + gains.shape[1:], jnp.float32),
            pltpu.SemaphoreType.DMA((LINE,)),
            pltpu.SemaphoreType.DMA((LINE,)),
            pltpu.SemaphoreType.DMA((PLANE,)),
            pltpu.SemaphoreType.DMA((PLANE,)),
            *LineReduce.buffers(both, share), *LineReduce.semaphores,
            *LineGather.semaphores,
            *PlaneReduce.buffers(rows, width), *PlaneReduce.semaphores,
        ],
        compiler_params=pltpu.CompilerParams(
            collective_id=7, has_side_effects=True, vmem_limit_bytes=61 * 2**20
        ),
        name="close_block",
    )(hidden, down, xy_parts, residual, gains, small)


def hand_over_body(*refs):
    count = (len(refs) - 2) // 3
    sources, targets, held = refs[:count], refs[count : 2 * count], refs[2 * count : 3 * count]
    inward, outward = (
        [
            pltpu.make_async_copy(src, dst, done.at[k])
            for k, (src, dst) in enumerate(zip(starts, ends))
        ]
        for starts, ends, done in ((sources, held, refs[-2]), (held, targets, refs[-1]))
    )
    for copy in inward:
        copy.start()
    for first, second in zip(inward, outward):
        first.wait()
        second.start()
    for copy in outward:
        copy.wait()


def hand_over(*arrays):
    return pl.pallas_call(
        hand_over_body,
        in_specs=[ANYWHERE] * len(arrays),
        out_specs=[ANYWHERE] * len(arrays),
        out_shape=[jax.ShapeDtypeStruct(item.shape, item.dtype) for item in arrays],
        scratch_shapes=[pltpu.VMEM(item.shape, item.dtype) for item in arrays]
        + [pltpu.SemaphoreType.DMA((len(arrays),))] * 2,
        compiler_params=pltpu.CompilerParams(vmem_limit_bytes=61 * 2**20),
        name="hand_over",
    )(*arrays)


def mixer_params(
    conv_weight, conv_bias, rate_weight, rate_bias, entry_weight, entry_bias, decay_param, chans
):
    used = conv_bias.shape[0]
    spare = (0, chans - used)
    decay_wide = jnp.pad(decay_param, spare, constant_values=2.0)
    blank = jnp.zeros((chans,), jnp.float32)
    vec = jnp.stack(
        [
            jnp.pad(conv_bias, spare),
            jnp.pad(rate_bias, spare),
            jnp.pad(entry_bias, spare),
            -8.0 * jax.nn.softplus(-decay_wide),
            8.0 * jax.nn.sigmoid(-decay_wide),
            blank,
            blank,
            blank,
        ]
    )
    taps = jnp.pad(conv_weight, ((0, 0), spare))
    return taps, vec, block_diagonal(rate_weight, chans), block_diagonal(entry_weight, chans)


def shards(
    layer_in,
    cotangent,
    mix_gain,
    ffn_gain,
    x_weight,
    y_weight,
    out_weight,
    conv_weight,
    conv_bias,
    rate_weight,
    rate_bias,
    entry_weight,
    entry_bias,
    decay_param,
    gate_weight,
    up_weight,
    down_weight,
    resets,
):
    heads, head_width = rate_weight.shape[:2]
    used = conv_bias.shape[0]
    chans = -(-used // 128) * 128
    widen = lambda values: jnp.pad(values, ((0, 0), (0, chans - used)))
    mix_full = gather(mix_gain, ("row", "head"), 0)
    ffn_full = gather(ffn_gain, ("row", "head"), 0)
    xy_shard = jnp.concatenate([widen(x_weight), widen(y_weight)], axis=1)
    xy_rows = gather(xy_shard, "row", 0).T
    out_rows = gather(widen(out_weight), "row", 0).T
    gate_rows = gather(gate_weight, "row", 0)
    up_rows = gather(up_weight, "row", 0)
    down_rows = gather(down_weight, "row", 0)

    taps, vec, wr, we = mixer_params(
        conv_weight, conv_bias, rate_weight, rate_bias, entry_weight, entry_bias, decay_param, chans
    )
    keep = keep_columns(resets)

    inputs = layer_in.astype(jnp.float32)
    normed_f, norm_back_one = jax.vjp(norm_apply, inputs, mix_full.astype(jnp.float32))
    normed_group = gather(normed_f.astype(jnp.bfloat16), "head", 0)
    u, by, before, states, mixed, part = mixer_forward(
        normed_group, xy_rows, out_rows, taps, vec, wr, we, keep, ROWS
    )
    residual = inputs + scatter(part, "head", 0).astype(jnp.float32)
    normed_two_f, norm_back_two = jax.vjp(norm_apply, residual, ffn_full.astype(jnp.float32))
    cot_group = gather(cotangent, "head", 0)
    two_group = gather(normed_two_f.astype(jnp.bfloat16), "head", 0)
    gates = dot_plain(two_group, gate_rows)
    ups = dot_plain(two_group, up_rows)
    activated, slope = gelu_both(gates)
    hidden = (activated * ups).astype(jnp.bfloat16)
    ffn_part = contract_last(hidden, down_rows).astype(jnp.bfloat16)
    d_hidden = dot_plain(cot_group, down_rows)
    d_gates = (d_hidden * ups * slope).astype(jnp.bfloat16)
    d_ups = (d_hidden * activated).astype(jnp.bfloat16)
    d_two_part = (contract_last(d_gates, gate_rows) + contract_last(d_ups, up_rows)).astype(
        jnp.bfloat16
    )
    gate_grad = scatter(contract_first(two_group, d_gates).astype(jnp.bfloat16), "row", 0)
    up_grad = scatter(contract_first(two_group, d_ups).astype(jnp.bfloat16), "row", 0)
    down_grad = scatter(contract_first(cot_group, hidden).astype(jnp.bfloat16), "row", 0)
    layer_out = (residual + scatter(ffn_part, "head", 0).astype(jnp.float32)).astype(jnp.bfloat16)
    d_two = scatter(d_two_part, "head", 0).astype(jnp.float32)
    d_resid_norm, d_ffn_gain = norm_back_two(d_two)
    d_residual = cotangent.astype(jnp.float32) + d_resid_norm
    d_res_group = gather(d_residual.astype(jnp.bfloat16), "head", 0)
    d_xy, d_part, d_taps, d_vec, d_wr, d_we = mixer_backward(
        d_res_group, xy_rows, out_rows, taps, vec, wr, we, keep, u, by, before, states, ROWS
    )
    out_grad = scatter(contract_first(d_res_group, mixed).astype(jnp.bfloat16), "row", 0)
    xy_grad = scatter(contract_first(normed_group, d_xy).astype(jnp.bfloat16), "row", 0)
    d_normed = scatter(d_part, "head", 0).astype(jnp.float32)
    d_inputs, d_mix_gain = norm_back_one(d_normed)
    layer_in_grad = (d_inputs + d_residual).astype(jnp.bfloat16)

    small = [
        d_taps[:, :used],
        d_vec[0, :used],
        diagonal_blocks(d_wr, heads, head_width),
        d_vec[1, :used],
        diagonal_blocks(d_we, heads, head_width),
        d_vec[2, :used],
        d_vec[3, :used] * (8.0 * jax.nn.sigmoid(-decay_param)),
    ]
    small = [lax.psum(item.astype(jnp.bfloat16), "row").astype(jnp.float32) for item in small]
    mix_part = scatter(d_mix_gain, ("row", "head"), 0)
    ffn_part_grad = scatter(d_ffn_gain, ("row", "head"), 0)
    wide = lambda values: values[:, :used].astype(jnp.float32)
    return (
        layer_out,
        layer_in_grad,
        mix_part,
        ffn_part_grad,
        wide(xy_grad),
        wide(xy_grad[:, chans:]),
        wide(out_grad),
        *small,
        gate_grad.astype(jnp.float32),
        up_grad.astype(jnp.float32),
        down_grad.astype(jnp.float32),
    )

def shards_linked(
    layer_in,
    cotangent,
    mix_gain,
    ffn_gain,
    x_weight,
    y_weight,
    out_weight,
    conv_weight,
    conv_bias,
    rate_weight,
    rate_bias,
    entry_weight,
    entry_bias,
    decay_param,
    gate_weight,
    up_weight,
    down_weight,
    resets,
):
    heads, head_width = rate_weight.shape[:2]
    used = conv_bias.shape[0]
    kept = -(-used // 16) * 16
    flat = lambda values: values.reshape((-1, values.shape[-1]))
    line = lambda values: values.reshape(1, -1)
    vectors = (conv_bias, rate_bias, entry_bias, decay_param)
    place = lax.broadcasted_iota(jnp.int32, (len(vectors), used), 0)
    rows = jnp.zeros((len(vectors), used), jnp.float32)
    for k, vector in enumerate(vectors):
        rows = jnp.where(place == k, vector[None, :], rows)
    (
        normed_group, cot_half, xy_rows, out_rows, mix_full, ffn_full, taps, vec, wr, we, keep,
    ) = open_block(
        layer_in,
        (line(mix_gain), line(ffn_gain)),
        cotangent,
        (x_weight.T, y_weight.T, out_weight.T),
        (
            conv_weight,
            rows,
            jnp.stack([rate_weight, entry_weight]),
            resets,
        ),
    )
    normed_group = flat(normed_group)
    u, by, before, states, mixed, residual, normed_two, gate_rows, up_half = forward_linked(
        normed_group, xy_rows, out_rows, taps, vec, wr, we, keep, layer_in, ffn_full,
        gate_weight, up_weight,
    )
    gate_rows = flat(gate_rows)
    two_group, cot_group, up_rows, down_rows, gates, ups, hidden, down_parts = ffn_up(
        normed_two, gate_rows, cotangent, cot_half, up_half, up_weight, down_weight
    )
    two_group, cot_group, down_rows = map(flat, (two_group, cot_group, down_rows))
    d_ups, gate_parts, down_grad, d_residual, d_low, d_ffn_gain = ffn_back(
        cot_group, two_group, gates, ups, gate_rows, up_rows, down_rows, down_parts, residual,
        cotangent, ffn_full,
    )
    up_parts, out_parts, gate_grad, d_mixed = turn(
        two_group, d_ups, gate_parts, d_low, mixed, out_rows, kept
    )
    xy_parts, up_grad, out_grad, layer_in_grad, gain_terms, small = backward_linked(
        d_mixed, xy_rows, taps, vec, wr, we, keep, u, by, before, states,
        normed_group, up_parts, out_parts, layer_in, mix_full, d_residual, d_ffn_gain,
        head_width, used,
    )
    layer_out, x_grad, y_grad, gain_grads, sums = close_block(
        hidden, down_rows, xy_parts, residual, gain_terms, small, used
    )
    sums = flat(sums)
    share = mix_gain.shape[0]
    ends = -(-used // 8) * 8
    (
        layer_out, layer_in_grad, x_grad, y_grad, out_grad, gate_grad, up_grad, down_grad,
    ) = hand_over(
        layer_out, layer_in_grad, x_grad, y_grad, out_grad, gate_grad, up_grad, down_grad
    )
    gates_end = heads * head_width
    return (
        layer_out,
        layer_in_grad,
        gain_grads[0, :share],
        gain_grads[0, share:],
        x_grad.T,
        y_grad.T,
        out_grad.T,
        sums[ends : ends + 4, :used],
        sums[ends + 4, :used],
        sums[:gates_end, :head_width].reshape(heads, head_width, head_width),
        sums[ends + 5, :used],
        sums[:gates_end, head_width : 2 * head_width].reshape(heads, head_width, head_width),
        sums[ends + 6, :used],
        sums[ends + 7, :used],
        gate_grad,
        up_grad,
        down_grad,
    )


def solution(mesh):
    linked = mesh.shape["row"] == LINE and mesh.shape["head"] == PLANE
    return jax.shard_map(
        shards_linked if linked else shards,
        mesh=mesh,
        in_specs=(
            P(("row", "head"), None),
            P(("row", "head"), None),
            P(("row", "head")),
            P(("row", "head")),
            P("row", "head"),
            P("row", "head"),
            P("row", "head"),
            P(None, "head"),
            P("head"),
            P("head", None, None),
            P("head"),
            P("head", None, None),
            P("head"),
            P("head"),
            P("row", "head"),
            P("row", "head"),
            P("row", "head"),
            P("row", None),
        ),
        out_specs=(
            P(("row", "head"), None),
            P(("row", "head"), None),
            P(("row", "head")),
            P(("row", "head")),
            P("row", "head"),
            P("row", "head"),
            P("row", "head"),
            P(None, "head"),
            P("head"),
            P("head", None, None),
            P("head"),
            P("head", None, None),
            P("head"),
            P("head"),
            P("row", "head"),
            P("row", "head"),
            P("row", "head"),
        ),
        check_vma=False,
    )
```
